256 devices in a mesh: gx: 8 (over x, core), gy: 32 (over y, z).
Axes of the slice: x: 4, y: 4, z: 8, core: 2. Of those that a mesh axis runs over, the one named last changes fastest.
Arguments:
- initial: float32 [64, 256, 512], P('gx', 'gy'), may hold values from -4 to 4
- right_side: float32 [64, 256, 512], P('gx', 'gy'), may hold values from -4 to 4
- phase_map: int32 [64, 256, 512], P('gx', 'gy'), may hold values from 0 to 2
- phase_table: float32 [3], replicated, may hold values from 0.2 to 5
Outputs:
- updated: float32 [64, 256, 512], P('gx', 'gy')
The draws below stay inside these ranges and needn't reach their ends.
All inputs are finite; a program needn't handle non-finite values.
Results may differ from the reference program's by a relative error of at most 0.0001.
Values sent between devices are 32-bit elements; how exact they have to be, the bound alone decides.
No kernel may reach another device: no remote copies, remote signals or barrier semaphores. Data moves between devices by JAX's collectives and lax.ppermute only.
A program may use at most 64 MiB of HBM per device.

```python
import math
import jax
import jax.numpy as jnp

NZ = 512
LEVELS = 3
COARSE_SWEEPS = 8
NPHASE = 3
NX = 64
NY = 256


def draw_right_side(key, part):
    key = jax.random.fold_in(key, 11)
    extent = (NX, NY, NZ)
    return jnp.clip(jax.random.normal(key, extent, jnp.float32), -4.0, 4.0)


def plant(entries, own_key, least, high):
    longest = entries.shape.index(max(entries.shape))
    spots = []
    for shift in (0, 1):
        where = [jax.random.randint(jax.random.fold_in(own_key, axis), (), 0, length) for axis, length in enumerate(entries.shape)]
        where[longest] = (where[longest] + shift) % entries.shape[longest]
        spots.append(tuple(where))
    return entries.at[spots[0]].set(least).at[spots[1]].set(high)


def block_levels(own_key, dims, cuts, low, high):
    gain = 1.0
    for axis_at, blocks in cuts:
        steps = jax.random.uniform(jax.random.fold_in(jax.random.fold_in(own_key, 6), axis_at), (blocks,), jnp.float32, low / len(cuts), high / len(cuts))
        gain = gain * jnp.repeat(jnp.exp(steps), dims[axis_at] // blocks).reshape((-1,) + (1,) * (len(dims) - 1 - axis_at))
    return gain


def bell_draw(stream_key, dims, width, reach, cuts=(), held_as=jnp.bfloat16):
    drawn = width * jax.random.normal(stream_key, dims, jnp.float32)
    if cuts:
        drawn = drawn * block_levels(stream_key, dims, cuts, -0.22, 0.18)
    return jnp.clip(drawn, -reach, reach).astype(held_as)


def setup_inputs(seed: int = 0) -> dict:
    streams_of = jax.random.split(jax.random.key(seed), 5)
    return {
        "initial": bell_draw(streams_of[0], (NX, NY, NZ), 1.0, 4.0, ((0, 8), (1, 32)), jnp.float32),
        "right_side": draw_right_side(jax.random.fold_in(streams_of[4], 71), 0),
        "phase_map": plant(jax.random.randint(streams_of[2], (NX, NY, NZ), 0, NPHASE), jax.random.fold_in(streams_of[2], 1), 0, NPHASE - 1).astype(jnp.int32),
        "phase_table": jnp.clip(jnp.exp(jax.random.uniform(streams_of[3], (NPHASE,), jnp.float32, math.log(0.2), math.log(5.0))), 0.2, 5.0),
    }


OMEGA = 0.8


def neighbours(padded):
    return (padded[2:, 1:-1, 1:-1], padded[:-2, 1:-1, 1:-1], padded[1:-1, 2:, 1:-1],
            padded[1:-1, :-2, 1:-1], padded[1:-1, 1:-1, 2:], padded[1:-1, 1:-1, :-2])


def stencil(values_pad, kappa_pad):
    kappa_mid = kappa_pad[1:-1, 1:-1, 1:-1]
    values_mid = values_pad[1:-1, 1:-1, 1:-1]
    applied = jnp.zeros(kappa_mid.shape, jnp.float32)
    diagonal = jnp.zeros(kappa_mid.shape, jnp.float32)
    for kappa_next, values_next in zip(neighbours(kappa_pad), neighbours(values_pad)):
        face_coef = 0.5 * (kappa_mid + kappa_next)
        diagonal = diagonal + face_coef
        applied = applied + face_coef * (values_mid - values_next)
    return applied, diagonal


def sweep(values, rhs_level, kappa_level):
    applied, diagonal = stencil(jnp.pad(values, 1), jnp.pad(kappa_level, 1))
    return values + OMEGA * (rhs_level - applied) / diagonal


def coarsen(source, factor):
    size_x, size_y, size_z = source.shape
    blocks = source.reshape(size_x // 2, 2, size_y // 2, 2, size_z // 2, 2)
    return factor * jnp.sum(blocks, axis=(1, 3, 5))


def prolong(source):
    return jnp.repeat(jnp.repeat(jnp.repeat(source, 2, 0), 2, 1), 2, 2)


def reference(initial, right_side, phase_map, phase_table):
    conduct = jnp.zeros(phase_map.shape, jnp.float32)
    for phase_index in range(NPHASE):
        conduct = conduct + jnp.where(phase_map == phase_index, phase_table[phase_index], 0.0)
    kappa_levels = [conduct]
    for level_index in range(LEVELS):
        kappa_levels.append(coarsen(kappa_levels[-1], 0.125))
    rhs_levels = [right_side]
    stored_values = []
    values = initial
    for level_index in range(LEVELS):
        kappa_level = kappa_levels[level_index]
        rhs_level = rhs_levels[level_index]
        if level_index == 0:
            values = sweep(values, rhs_level, kappa_level)
        else:
            values = sweep(jnp.zeros_like(rhs_level), rhs_level, kappa_level)
        values = sweep(values, rhs_level, kappa_level)
        applied, diagonal = stencil(jnp.pad(values, 1), jnp.pad(kappa_level, 1))
        stored_values.append(values)
        rhs_levels.append(coarsen(rhs_level - applied, 0.5))
    coarse = jnp.zeros_like(rhs_levels[LEVELS])
    for sweep_index in range(COARSE_SWEEPS):
        coarse = sweep(coarse, rhs_levels[LEVELS], kappa_levels[LEVELS])
    kappa_pad = jnp.pad(kappa_levels[LEVELS], 1)
    applied, diagonal = stencil(jnp.pad(coarse, 1), kappa_pad)
    edge, diagonal = stencil(jnp.pad(jnp.ones_like(coarse), 1), kappa_pad)
    shift = jnp.sum(rhs_levels[LEVELS] - applied) / jnp.sum(edge)
    coarse = coarse + shift
    for level_index in reversed(range(LEVELS)):
        values = stored_values[level_index] + prolong(coarse)
        values = sweep(values, rhs_levels[level_index], kappa_levels[level_index])
        values = sweep(values, rhs_levels[level_index], kappa_levels[level_index])
        coarse = values
    return coarse
```

```python
import functools

import jax
import jax.numpy as jnp
from jax import lax
from jax.experimental import pallas as pl
from jax.experimental.pallas import tpu as pltpu
from jax.sharding import PartitionSpec as P

F32 = jnp.float32
KEEP = 0.2
OMEGA = 0.8
VMEM = pltpu.VMEM
PARAMS = pltpu.CompilerParams(vmem_limit_bytes=48 * 1024 * 1024)


def roll(value, shift, axis):
    return pltpu.roll(value, shift % value.shape[axis], axis)


def iota(shape, dim):
    return lax.broadcasted_iota(jnp.int32, shape, dim)


def pair_sum_matrix():
    return (iota((256, 128), 0) // 2 == iota((256, 128), 1)).astype(F32)


def pair_copy_matrix():
    return (iota((128, 256), 1) // 2 == iota((128, 256), 0)).astype(F32)


def exact_dot(a, b):
    return lax.dot_general(
        a, b, (((1,), (0,)), ((), ())), precision=lax.Precision.HIGHEST, preferred_element_type=F32
    )


def lane_sum(value, matrix):
    width = value.shape[1]
    parts = [exact_dot(value[:, at : at + 256], matrix) for at in range(0, width, 256)]
    return parts[0] if len(parts) == 1 else jnp.concatenate(parts, axis=1)


def lane_copy(value, matrix):
    width = value.shape[1]
    parts = [exact_dot(value[:, at : at + 128], matrix) for at in range(0, width, 128)]
    return parts[0] if len(parts) == 1 else jnp.concatenate(parts, axis=1)


def row_sum(scratch, value):
    rows, width = value.shape
    parts = []
    for c in range(width // 128):
        scratch[c, 0:rows] = value[:, 128 * c : 128 * c + 128]
        first = scratch[c, pl.ds(0, rows // 2, stride=2)]
        parts.append(first + scratch[c, pl.ds(1, rows // 2, stride=2)])
    return parts[0] if len(parts) == 1 else jnp.concatenate(parts, axis=1)


def row_copy(scratch, value):
    rows, width = value.shape
    parts = []
    for c in range(width // 128):
        part = value[:, 128 * c : 128 * c + 128]
        scratch[c, pl.ds(0, rows, stride=2)] = part
        scratch[c, pl.ds(1, rows, stride=2)] = part
        parts.append(scratch[c, 0 : 2 * rows])
    return parts[0] if len(parts) == 1 else jnp.concatenate(parts, axis=1)


def gathered(mid, low, high, cx_low, cx, cy, cz):
    total = cx * high + cx_low * low
    total = total + cy * roll(mid, -1, 0) + roll(cy * mid, 1, 0)
    return total + cz * roll(mid, -1, 1) + roll(cz * mid, 1, 1)


def z_neighbours(mid):
    lane = iota(mid.shape, 1)
    last = mid.shape[1] - 1
    up = jnp.where(lane == last, 0.0, roll(mid, -1, 1))
    down = jnp.where(lane == 0, 0.0, roll(mid, 1, 1))
    return up, down


def diagonal(mid, low, high):
    up, down = z_neighbours(mid)
    total = low + high + roll(mid, -1, 0) + roll(mid, 1, 0) + up + down
    return 3.0 * mid + 0.5 * total


def coupling_y(mid):
    return 0.5 * (mid + roll(mid, -1, 0))


def coupling_z(mid):
    lane = iota(mid.shape, 1)
    return jnp.where(lane == mid.shape[1] - 1, 0.0, 0.5 * (mid + roll(mid, -1, 1)))


def edge_flags(at, grid):
    even = at % 2 == 0
    outside = jnp.logical_or(at == 0, at == grid - 1)
    return even, outside


def start_kernel(where_ref, table_ref, phase_ref, init_ref, rhs_ref, kap_ref, near_ref, far_ref):
    even = where_ref[0] % 2 == 0
    for x in range(8):
        phase = phase_ref[x]
        kap_ref[x] = jnp.where(
            phase == 0, table_ref[0], jnp.where(phase == 1, table_ref[1], table_ref[2])
        )
    for ref, side in ((near_ref, even), (far_ref, jnp.logical_not(even))):
        deep = jnp.where(side, 5, 0)
        shallow = jnp.where(side, 6, 0)
        for i in range(3):
            ref[i] = kap_ref[deep + i]
            ref[3 + i] = init_ref[deep + i]
        for i in range(2):
            ref[6 + i] = rhs_ref[shallow + i]


def place_x(where_ref, grid, own_ref, near_ref, far_ref, first, depth, out_ref, count=8):
    even, outside = edge_flags(where_ref[0], grid)
    near_at = jnp.where(even, depth + count, 0)
    far_at = jnp.where(even, 0, depth + count)
    for x in range(count):
        out_ref[depth + x, 0:8] = own_ref[x]
    for i in range(depth):
        out_ref[near_at + i, 0:8] = near_ref[first + i]
        out_ref[far_at + i, 0:8] = jnp.where(outside, 0.0, far_ref[first + i])


def turn_kernel(
    nx, where_ref, kap_ref, init_ref, rhs_ref, near_ref, far_ref, even_ref, odd_ref, ks, vs, rs
):
    place_x(where_ref, nx, kap_ref, near_ref, far_ref, 0, 3, ks)
    place_x(where_ref, nx, init_ref, near_ref, far_ref, 3, 3, vs)
    place_x(where_ref, nx, rhs_ref, near_ref, far_ref, 6, 2, rs)
    even = where_ref[1] % 2 == 0

    def write(low_ref, high_ref):
        for p in range(12):
            low_ref[p, 0:3] = ks[p + 1, 0:3]
            low_ref[p, 3:6] = vs[p + 1, 0:3]
            low_ref[p, 6:8] = rs[p, 0:2]
            high_ref[p, 0:3] = ks[p + 1, 5:8]
            high_ref[p, 3:6] = vs[p + 1, 5:8]
            high_ref[p, 6:8] = rs[p, 6:8]

    @pl.when(even)
    def _():
        write(odd_ref, even_ref)

    @pl.when(jnp.logical_not(even))
    def _():
        write(even_ref, odd_ref)


def y_tiles(where_ref, grid, even_ref, odd_ref, p):
    even, outside = edge_flags(where_ref[1], grid)
    inner = even_ref[p]
    outer = jnp.where(outside, 0.0, odd_ref[p])
    return jnp.where(even, inner, outer), jnp.where(even, outer, inner)


def down0_kernel(
    nx, ny, where_ref, kap_ref, init_ref, rhs_ref, near_ref, far_ref, even_ref, odd_ref,
    v0_ref, rs, cx, cy, cz, wi, block_ref, mnear_ref, mfar_ref,
    ks, vs, v1, v2, pair, fine, coarse,
):
    zero = jnp.zeros((8, 512), F32)
    for p in range(14):
        ks[p, 8:16] = zero
        vs[p, 8:16] = zero
    for p in range(12):
        rs[p, 8:16] = zero
    place_x(where_ref, nx, kap_ref, near_ref, far_ref, 0, 3, ks)
    place_x(where_ref, nx, init_ref, near_ref, far_ref, 3, 3, vs)
    place_x(where_ref, nx, rhs_ref, near_ref, far_ref, 6, 2, rs)
    for p in range(12):
        high, low = y_tiles(where_ref, ny, even_ref, odd_ref, p)
        ks[p + 1, 8:11] = high[0:3]
        ks[p + 1, 13:16] = low[0:3]
        vs[p + 1, 8:11] = high[3:6]
        vs[p + 1, 13:16] = low[3:6]
        rs[p, 8:10] = high[6:8]
        rs[p, 14:16] = low[6:8]
    cx[0] = 0.5 * (ks[0] + ks[1])
    for p in range(12):
        mid = ks[p + 1]
        cx[p + 1] = 0.5 * (mid + ks[p + 2])
        cy[p] = coupling_y(mid)
        cz[p] = coupling_z(mid)
        diag = diagonal(mid, ks[p], ks[p + 2])
        wi[p] = jnp.where(mid > 0.0, OMEGA / jnp.where(mid > 0.0, diag, 1.0), 0.0)
    for p in range(12):
        mid = vs[p + 1]
        total = gathered(mid, vs[p], vs[p + 2], cx[p], cx[p + 1], cy[p], cz[p])
        v1[p] = KEEP * mid + wi[p] * (rs[p] + total)
    for p in range(1, 11):
        mid = v1[p]
        total = gathered(mid, v1[p - 1], v1[p + 1], cx[p], cx[p + 1], cy[p], cz[p])
        v2[p] = KEEP * mid + wi[p] * (rs[p] + total)
    for p in range(2, 10, 2):
        both = None
        for q in (p, p + 1):
            mid = v2[q]
            total = gathered(mid, v2[q - 1], v2[q + 1], cx[q], cx[q + 1], cy[q], cz[q])
            diag = diagonal(ks[q + 1], ks[q], ks[q + 2])
            rest = (rs[q] + total - diag * mid)[0:8]
            both = rest if both is None else both + rest
            v0_ref[q - 2] = mid[0:8]
        at = 4 * (p // 2 - 1)
        fine[at : at + 4] = row_sum(pair, both)
    for p in range(0, 12, 2):
        at = 16 + 4 * p
        fine[at : at + 8] = row_sum(pair, ks[p + 1] + ks[p + 2])
    coarse[...] = lane_sum(fine[...], pair_sum_matrix())
    for x in range(4):
        half = pl.ds(256 * (x % 2), 256)
        mid = 0.125 * coarse[24 + 8 * x : 32 + 8 * x]
        low = 0.125 * coarse[16 + 8 * x : 24 + 8 * x]
        high = 0.125 * coarse[32 + 8 * x : 40 + 8 * x]
        block_ref[x // 2, 0:4, half] = 0.5 * coarse[4 * x : 4 * x + 4]
        block_ref[x // 2, 4:8, half] = mid[0:4]
        at = 4 * (x // 2)
        block_ref[2, at : at + 4, half] = (OMEGA / diagonal(mid, low, high)[0:4])
    even = where_ref[0] % 2 == 0
    for ref, side in ((mnear_ref, even), (mfar_ref, jnp.logical_not(even))):
        shallow = jnp.where(side, 6, 0)
        for i in range(3):
            ref[i] = block_ref[i]
        for i in range(2):
            ref[3 + i] = v0_ref[shallow + i]


def place_blocks(where_ref, grid, block_ref, near_ref, far_ref, v0_ref, lanes, v0x):
    even, outside = edge_flags(where_ref[0], grid)
    near_at = jnp.where(even, 6, 0)
    far_at = jnp.where(even, 0, 6)
    for i in range(3):
        lanes[3 + i] = block_ref[i]
        lanes[near_at + i] = near_ref[i]
        lanes[far_at + i] = jnp.where(outside, 0.0, far_ref[i])
    near_at = jnp.where(even, 10, 0)
    far_at = jnp.where(even, 0, 10)
    for x in range(8):
        v0x[2 + x, 0:8] = v0_ref[x]
    for i in range(2):
        v0x[near_at + i, 0:8] = near_ref[3 + i]
        v0x[far_at + i, 0:8] = jnp.where(outside, 0.0, far_ref[3 + i])


def turn1_kernel(
    nx, where_ref, block_ref, v0_ref, near_ref, far_ref, even_ref, odd_ref, lanes, v0x
):
    place_blocks(where_ref, nx, block_ref, near_ref, far_ref, v0_ref, lanes, v0x)
    even = where_ref[1] % 2 == 0
    for ref in (even_ref, odd_ref):
        for i in range(9):
            ref[i] = lanes[i]

    def write(low_ref, high_ref):
        for p in range(12):
            at = 2 * (p % 4)
            low_ref[9 + p // 4, at : at + 2] = v0x[p, 0:2]
            high_ref[9 + p // 4, at : at + 2] = v0x[p, 6:8]

    @pl.when(even)
    def _():
        write(odd_ref, even_ref)

    @pl.when(jnp.logical_not(even))
    def _():
        write(even_ref, odd_ref)


def down1_kernel(
    nx, ny, where_ref, block_ref, v0_ref, near_ref, far_ref, even_ref, odd_ref,
    v0x, v1, f1, w1, cx, cy, cz, send_ref,
    lanes, k1, u1, pair, fine,
):
    place_blocks(where_ref, nx, block_ref, near_ref, far_ref, v0_ref, lanes, v0x)
    zero = jnp.zeros((4, 256), F32)
    for b in range(3):
        tiles = [y_tiles(where_ref, ny, even_ref, odd_ref, 3 * b + i) for i in range(3)]
        own = [lanes[3 * b + i] for i in range(3)]
        for x in range(4):
            p = 4 * b + x
            half = slice(256 * (x % 2), 256 * (x % 2) + 256)
            t = x // 2
            wrow = slice(4 * t, 4 * t + 4)
            for ref, pick, row in (
                (f1, t, slice(0, 4)), (k1, t, slice(4, 8)), (w1, 2, wrow)
            ):
                ref[p, 0:4] = own[pick][row, half]
                ref[p, 4:8] = tiles[pick][0][row, half]
                ref[p, 8:12] = zero
                ref[p, 12:16] = tiles[pick][1][row, half]
    for i in range(3):
        high, low = y_tiles(where_ref, ny, even_ref, odd_ref, 9 + i)
        for j in range(4):
            p = 4 * i + j
            v0x[p, 8:10] = high[2 * j : 2 * j + 2]
            v0x[p, 10:14] = jnp.zeros((4, 512), F32)
            v0x[p, 14:16] = low[2 * j : 2 * j + 2]
    for p in range(12):
        u1[p] = w1[p] * f1[p]
        if p < 11:
            cx[p] = 0.5 * (k1[p] + k1[p + 1])
        cy[p] = coupling_y(k1[p])
        cz[p] = coupling_z(k1[p])
    for p in range(1, 11):
        mid = u1[p]
        total = gathered(mid, u1[p - 1], u1[p + 1], cx[p - 1], cx[p], cy[p], cz[p])
        v1[p] = KEEP * mid + w1[p] * (f1[p] + total)
    for p in range(4, 8, 2):
        both = None
        for q in (p, p + 1):
            mid = v1[q]
            total = gathered(mid, v1[q - 1], v1[q + 1], cx[q - 1], cx[q], cy[q], cz[q])
            diag = diagonal(k1[q], k1[q - 1], k1[q + 1])
            rest = (f1[q] + total - diag * mid)[0:8]
            both = rest if both is None else both + rest
        at = p - 4
        fine[at : at + 2] = 0.5 * row_sum(pair, both)[0:2]
        kept = k1[p, 0:8] + k1[p + 1, 0:8]
        fine[4 + at : 6 + at] = 0.125 * row_sum(pair, kept)[0:2]
    tile = lane_sum(fine[...], pair_sum_matrix())
    for i in range(send_ref.shape[0]):
        send_ref[i] = tile


def up_kernel(
    nx, ny, where_ref, mine_ref, other_ref, v1, f1, w1, cx1, cy1, cz1,
    v0x, rs, cx0, cy0, cz0, w0, out_ref,
    f2, k2, cx2, cyi, cyo, cz2, w2, u2, v2, e2, f3, k3, cx3, cy3, cz3, w3, ga, gb,
    small, wide, e1a, e1b, narrow, e0a, e0b,
):
    gx = where_ref[0]
    gy = where_ref[1]
    core = gx % 2
    n2 = 2 * nx
    zero = jnp.zeros((ny, 128), F32)
    row = iota((ny, 128), 0)
    lane = iota((ny, 128), 1)
    last_row = row == ny - 1
    for s in range(2):
        k2[0, s] = zero
        k2[n2 + 1, s] = zero
        u2[0, s] = zero
        u2[n2 + 1, s] = zero
        v2[0, s] = zero
        v2[n2 + 1, s] = zero
    for x in range(nx // 2):
        for ref, which in ((mine_ref, core), (other_ref, 1 - core)):
            for i in range(2):
                p = 4 * x + 2 * which + i + 1
                for s in range(2):
                    f2[p, s] = ref[x, pl.ds(2 * i + s, ny, stride=8)]
                    k2[p, s] = ref[x, pl.ds(4 + 2 * i + s, ny, stride=8)]
    for p in range(n2 + 1):
        for s in range(2):
            cx2[p, s] = 0.5 * (k2[p, s] + k2[p + 1, s])
    diags = {}
    for p in range(1, n2 + 1):
        k_low, k_high = k2[p, 0], k2[p, 1]
        after = jnp.where(last_row, 0.0, roll(k_low, -1, 0))
        before = jnp.where(row == 0, 0.0, roll(k_high, 1, 0))
        cyi[p] = 0.5 * (k_low + k_high)
        cyo[p] = jnp.where(last_row, 0.0, 0.5 * (k_high + after))
        for s, mid, ya, yb in ((0, k_low, k_high, before), (1, k_high, k_low, after)):
            up, down = z_neighbours(mid)
            cz2[p, s] = jnp.where(lane == 127, 0.0, 0.5 * (mid + up))
            diag = 3.0 * mid + 0.5 * (k2[p - 1, s] + k2[p + 1, s] + ya + yb + up + down)
            w2[p, s] = OMEGA / diag
            u2[p, s] = (OMEGA / diag) * f2[p, s]

    def gather2(ref, p):
        low, high = ref[p, 0], ref[p, 1]
        sums = []
        for s, mid in ((0, low), (1, high)):
            total = cx2[p, s] * ref[p + 1, s] + cx2[p - 1, s] * ref[p - 1, s]
            total = total + cz2[p, s] * roll(mid, -1, 1) + roll(cz2[p, s] * mid, 1, 1)
            sums.append(total)
        sums[0] = sums[0] + cyi[p] * high + roll(cyo[p] * high, 1, 0)
        sums[1] = sums[1] + cyi[p] * low + cyo[p] * roll(low, -1, 0)
        return (low, high), sums

    def sweep2(source, target):
        for p in range(1, n2 + 1):
            mids, sums = gather2(source, p)
            for s in range(2):
                target[p, s] = KEEP * mids[s] + w2[p, s] * (f2[p, s] + sums[s])

    sweep2(u2, v2)
    even_lane = lane % 2 == 0

    def pair_lanes(value):
        return value + jnp.where(even_lane, roll(value, -1, 1), roll(value, 1, 1))

    k3[0] = zero
    k3[nx + 1] = zero
    ga[0] = zero
    ga[nx + 1] = zero
    gb[0] = zero
    gb[nx + 1] = zero
    for x in range(nx):
        both = None
        kept = None
        for p in (2 * x + 1, 2 * x + 2):
            mids, sums = gather2(v2, p)
            for s in range(2):
                rest = f2[p, s] + sums[s] - (OMEGA / w2[p, s]) * mids[s]
                both = rest if both is None else both + rest
                kept = k2[p, s] if kept is None else kept + k2[p, s]
        f3[x + 1] = 0.5 * pair_lanes(both)
        k3[x + 1] = 0.125 * pair_lanes(kept)
    for p in range(nx + 1):
        cx3[p] = 0.5 * (k3[p] + k3[p + 1])
    edge_total = zero
    outer = (
        (row == 0).astype(F32) + last_row.astype(F32)
        + (lane < 2).astype(F32) + (lane >= 126).astype(F32)
    )
    for p in range(1, nx + 1):
        mid = k3[p]
        after = jnp.where(last_row, 0.0, roll(mid, -1, 0))
        before = jnp.where(row == 0, 0.0, roll(mid, 1, 0))
        up = jnp.where(lane >= 126, 0.0, roll(mid, -2, 1))
        down = jnp.where(lane < 2, 0.0, roll(mid, 2, 1))
        cy3[p] = jnp.where(last_row, 0.0, 0.5 * (mid + after))
        cz3[p] = jnp.where(lane >= 126, 0.0, 0.5 * (mid + up))
        diag = 3.0 * mid + 0.5 * (k3[p - 1] + k3[p + 1] + after + before + up + down)
        w3[p] = OMEGA / diag
        ga[p] = (OMEGA / diag) * f3[p]
        faces = outer + (1.0 if p == 1 else 0.0) + (1.0 if p == nx else 0.0)
        edge_total = edge_total + 0.5 * mid * faces

    def gather3(ref, p):
        mid = ref[p]
        total = cx3[p] * ref[p + 1] + cx3[p - 1] * ref[p - 1]
        total = total + cy3[p] * roll(mid, -1, 0) + roll(cy3[p] * mid, 1, 0)
        return mid, total + cz3[p] * roll(mid, -2, 1) + roll(cz3[p] * mid, 2, 1)

    source, target = ga, gb
    for _ in range(7):
        for p in range(1, nx + 1):
            mid, total = gather3(source, p)
            target[p] = KEEP * mid + w3[p] * (f3[p] + total)
        source, target = target, source
    rest_total = zero
    for p in range(1, nx + 1):
        mid, total = gather3(source, p)
        rest_total = rest_total + (f3[p] + total - (OMEGA / w3[p]) * mid)

    def whole(value):
        return jnp.sum(jnp.sum(value, axis=0, keepdims=True), axis=1, keepdims=True)

    shift = whole(rest_total) / whole(edge_total)
    for x in range(nx):
        e3 = source[x + 1] + shift
        for p in (2 * x + 1, 2 * x + 2):
            for s in range(2):
                v2[p, s] = v2[p, s] + e3
    sweep2(v2, u2)
    blank = jnp.zeros(e2.shape[2:], F32)
    for p in (0, 1, n2 + 2, n2 + 3):
        for s in range(2):
            e2[p, s] = blank
    for p in range(1, n2 + 1):
        mids, sums = gather2(u2, p)
        for s in range(2):
            e2[p + 1, s, 0:8] = blank[0:8]
            e2[p + 1, s, ny + 8 : ny + 16] = blank[0:8]
            e2[p + 1, s, 8 : ny + 8] = KEEP * mids[s] + w2[p, s] * (f2[p, s] + sums[s])
    copies = pair_copy_matrix()
    for i in range(6):
        small[8 * i + 4 : 8 * i + 6] = jnp.zeros((2, 128), F32)
        for j, step in ((0, 0), (2, 1), (6, -1)):
            for s in range(2):
                small[8 * i + j + s : 8 * i + j + s + 1] = e2[
                    2 * gx + i, s, pl.ds(gy + 8 + step, 1)
                ]
    wide[...] = lane_copy(small[...], copies)
    for i in range(6):
        spread = row_copy(narrow, wide[8 * i : 8 * i + 8])
        for p in (2 * i, 2 * i + 1):
            if 1 <= p <= 10:
                e1a[p] = v1[p] + spread
    for source, target, first, last in ((e1a, e1b, 2, 9), (e1b, e1a, 3, 8)):
        for p in range(first, last + 1):
            mid = source[p]
            total = gathered(
                mid, source[p - 1], source[p + 1], cx1[p - 1], cx1[p], cy1[p], cz1[p]
            )
            target[p] = KEEP * mid + w1[p] * (f1[p] + total)
    row8 = iota((8, 256), 0)
    for i in range(6):
        value = e1a[i + 3]
        wide[8 * i : 8 * i + 8] = jnp.where(row8 == 7, value[8:16], value[0:8])
    doubled = lane_copy(wide[...], copies)
    for i in range(6):
        spread = row_copy(narrow, doubled[8 * i : 8 * i + 8])
        for p in (2 * i, 2 * i + 1):
            e0a[p] = v0x[p] + spread
    for p in range(1, 11):
        mid = e0a[p]
        total = gathered(mid, e0a[p - 1], e0a[p + 1], cx0[p], cx0[p + 1], cy0[p], cz0[p])
        e0b[p] = KEEP * mid + w0[p] * (rs[p] + total)
    for p in range(2, 10):
        mid = e0b[p]
        total = gathered(mid, e0b[p - 1], e0b[p + 1], cx0[p], cx0[p + 1], cy0[p], cz0[p])
        out_ref[p - 2] = (KEEP * mid + w0[p] * (rs[p] + total))[0:8]


def run(kernel, outs, scratch, where, *operands, table=None):
    smem = pl.BlockSpec(memory_space=pltpu.SMEM)
    vmem = pl.BlockSpec(memory_space=VMEM)
    scalars = [where] if table is None else [where, table]
    return pl.pallas_call(
        kernel,
        out_shape=[jax.ShapeDtypeStruct(shape, F32) for shape in outs],
        in_specs=[smem] * len(scalars) + [vmem] * len(operands),
        out_specs=[vmem] * len(outs),
        scratch_shapes=[VMEM(shape, F32) for shape in scratch],
        compiler_params=PARAMS,
    )(*scalars, *operands)


def body(initial, right_side, phase_map, phase_table):
    nx, ny = lax.axis_size("gx"), lax.axis_size("gy")
    where = jnp.stack([lax.axis_index("gx"), lax.axis_index("gy")]).astype(jnp.int32)

    def inner(size):
        return [(i, i ^ 1) for i in range(size)]

    def outer(size):
        return [(i, (i + 1) % size if i % 2 else (i - 1) % size) for i in range(size)]

    def swap(near, far, axis, size):
        return lax.ppermute(near, axis, inner(size)), lax.ppermute(far, axis, outer(size))

    tile0 = (8, 512)
    kappa, near, far = run(
        start_kernel, [(8,) + tile0] * 3, [], where, phase_map, initial, right_side,
        table=phase_table,
    )
    near, far = swap(near, far, "gx", nx)
    even, odd = run(
        functools.partial(turn_kernel, nx), [(12,) + tile0] * 2,
        [(14,) + tile0, (14,) + tile0, (12,) + tile0],
        where, kappa, initial, right_side, near, far,
    )
    even, odd = swap(even, odd, "gy", ny)
    ring0 = (16, 512)
    v0, rs, cx0, cy0, cz0, w0, block, mnear, mfar = run(
        functools.partial(down0_kernel, nx, ny),
        [(8,) + tile0, (12,) + ring0, (13,) + ring0]
        + [(12,) + ring0] * 3
        + [(3,) + tile0, (5,) + tile0, (5,) + tile0],
        [(14,) + ring0, (14,) + ring0, (12,) + ring0, (12,) + ring0, (4, 16, 128), (64, 512), (64, 256)],
        where, kappa, initial, right_side, near, far, even, odd,
    )
    mnear, mfar = swap(mnear, mfar, "gx", nx)
    meven, modd = run(
        functools.partial(turn1_kernel, nx), [(12,) + tile0] * 2,
        [(9,) + tile0, (12,) + tile0],
        where, block, v0, mnear, mfar,
    )
    meven, modd = swap(meven, modd, "gy", ny)
    ring1 = (16, 256)
    v0x, v1, f1, w1, cx1, cy1, cz1, send = run(
        functools.partial(down1_kernel, nx, ny),
        [(12,) + ring0] + [(12,) + ring1] * 6 + [(ny, 8, 128)],
        [(9,) + tile0, (12,) + ring1, (12,) + ring1, (4, 16, 128), (8, 256)],
        where, block, v0, mnear, mfar, meven, modd,
    )
    column = lax.all_to_all(send, "gy", 0, 0).reshape(1, ny * 8, 128)
    groups = [list(range(0, nx, 2)), list(range(1, nx, 2))]
    mine = lax.all_to_all(
        jnp.broadcast_to(column, (nx // 2, ny * 8, 128)), "gx", 0, 0, axis_index_groups=groups
    )
    other = lax.ppermute(mine, "gx", inner(nx))
    n2 = 2 * nx
    pair2 = (n2 + 2, 2, ny, 128)
    one2 = (n2 + 2, ny, 128)
    one3 = (nx + 2, ny, 128)
    (out,) = run(
        functools.partial(up_kernel, nx, ny), [(8,) + tile0],
        [pair2, pair2, pair2, one2, one2, pair2, pair2, pair2, pair2, (n2 + 4, 2, ny + 16, 128)]
        + [one3] * 8
        + [(48, 128), (48, 256), (12,) + ring1, (12,) + ring1, (4, 16, 128), (12,) + ring0, (12,) + ring0],
        where, mine, other, v1, f1, w1, cx1, cy1, cz1, v0x, rs, cx0, cy0, cz0, w0,
    )
    return out


def solution(mesh):
    return jax.shard_map(
        body,
        mesh=mesh,
        in_specs=(P("gx", "gy", None), P("gx", "gy", None), P("gx", "gy", None), P()),
        out_specs=P("gx", "gy", None),
        check_vma=False,
    )
```

```python
import functools

import jax
import jax.numpy as jnp
from jax import lax
from jax.experimental import pallas as pl
from jax.experimental.pallas import tpu as pltpu
from jax.sharding import PartitionSpec as P

F32 = jnp.float32
KEEP = 0.2
OMEGA = 0.8
VMEM = pltpu.VMEM
PARAMS = pltpu.CompilerParams(vmem_limit_bytes=48 * 1024 * 1024)


def roll(value, shift, axis):
    return pltpu.roll(value, shift % value.shape[axis], axis)


def iota(shape, dim):
    return lax.broadcasted_iota(jnp.int32, shape, dim)


def pair_sum_matrix():
    return (iota((256, 128), 0) // 2 == iota((256, 128), 1)).astype(F32)


def pair_copy_matrix():
    return (iota((128, 256), 1) // 2 == iota((128, 256), 0)).astype(F32)


def exact_dot(a, b):
    return lax.dot_general(
        a, b, (((1,), (0,)), ((), ())), precision=lax.Precision.HIGHEST, preferred_element_type=F32
    )


def lane_sum(value, matrix):
    width = value.shape[1]
    parts = [exact_dot(value[:, at : at + 256], matrix) for at in range(0, width, 256)]
    return parts[0] if len(parts) == 1 else jnp.concatenate(parts, axis=1)


def lane_copy(value, matrix):
    width = value.shape[1]
    parts = [exact_dot(value[:, at : at + 128], matrix) for at in range(0, width, 128)]
    return parts[0] if len(parts) == 1 else jnp.concatenate(parts, axis=1)


def row_sum(scratch, value):
    rows, width = value.shape
    parts = []
    for c in range(width // 128):
        scratch[c, 0:rows] = value[:, 128 * c : 128 * c + 128]
        first = scratch[c, pl.ds(0, rows // 2, stride=2)]
        parts.append(first + scratch[c, pl.ds(1, rows // 2, stride=2)])
    return parts[0] if len(parts) == 1 else jnp.concatenate(parts, axis=1)


def row_copy(scratch, value):
    rows, width = value.shape
    parts = []
    for c in range(width // 128):
        part = value[:, 128 * c : 128 * c + 128]
        scratch[c, pl.ds(0, rows, stride=2)] = part
        scratch[c, pl.ds(1, rows, stride=2)] = part
        parts.append(scratch[c, 0 : 2 * rows])
    return parts[0] if len(parts) == 1 else jnp.concatenate(parts, axis=1)


def gathered(mid, low, high, cx_low, cx, cy, cz):
    total = cx * high + cx_low * low
    total = total + cy * roll(mid, -1, 0) + roll(cy * mid, 1, 0)
    return total + cz * roll(mid, -1, 1) + roll(cz * mid, 1, 1)


def z_neighbours(mid):
    lane = iota(mid.shape, 1)
    last = mid.shape[1] - 1
    up = jnp.where(lane == last, 0.0, roll(mid, -1, 1))
    down = jnp.where(lane == 0, 0.0, roll(mid, 1, 1))
    return up, down


def diagonal(mid, low, high):
    up, down = z_neighbours(mid)
    total = low + high + roll(mid, -1, 0) + roll(mid, 1, 0) + up + down
    return 3.0 * mid + 0.5 * total


def coupling_y(mid):
    return 0.5 * (mid + roll(mid, -1, 0))


def coupling_z(mid):
    lane = iota(mid.shape, 1)
    return jnp.where(lane == mid.shape[1] - 1, 0.0, 0.5 * (mid + roll(mid, -1, 1)))


def edge_flags(at, grid):
    even = at % 2 == 0
    outside = jnp.logical_or(at == 0, at == grid - 1)
    return even, outside


def start_kernel(
    where_ref, table_hbm, phase_hbm, init_hbm, rhs_hbm,
    kap_ref, init_ref, rhs_ref, near_ref, far_ref, yeven_ref, yodd_ref,
    table_ref, phase_ref, sems,
):
    copies = [
        pltpu.make_async_copy(source, target, sems.at[i])
        for i, (source, target) in enumerate(
            ((table_hbm, table_ref), (phase_hbm, phase_ref), (init_hbm, init_ref), (rhs_hbm, rhs_ref))
        )
    ]
    for copy in copies:
        copy.start()
    for copy in copies:
        copy.wait()
    even = where_ref[0] % 2 == 0
    for x in range(8):
        phase = phase_ref[x]
        kap_ref[x] = jnp.where(
            phase == 0, table_ref[0], jnp.where(phase == 1, table_ref[1], table_ref[2])
        )
    for ref, side in ((near_ref, even), (far_ref, jnp.logical_not(even))):
        deep = jnp.where(side, 5, 0)
        shallow = jnp.where(side, 6, 0)
        for i in range(3):
            ref[i] = kap_ref[deep + i]
            ref[3 + i] = init_ref[deep + i]
        for i in range(2):
            ref[6 + i] = rhs_ref[shallow + i]

    def write(low_ref, high_ref):
        for x in range(8):
            low_ref[x, 0:3] = kap_ref[x, 0:3]
            low_ref[x, 3:6] = init_ref[x, 0:3]
            low_ref[x, 6:8] = rhs_ref[x, 0:2]
            high_ref[x, 0:3] = kap_ref[x, 5:8]
            high_ref[x, 3:6] = init_ref[x, 5:8]
            high_ref[x, 6:8] = rhs_ref[x, 6:8]

    by_parity(where_ref, yeven_ref, yodd_ref, write)


def by_parity(where_ref, even_ref, odd_ref, write):
    even = where_ref[1] % 2 == 0

    @pl.when(even)
    def _():
        write(odd_ref, even_ref)

    @pl.when(jnp.logical_not(even))
    def _():
        write(even_ref, odd_ref)


def place_x(where_ref, grid, own_ref, near_ref, far_ref, first, depth, out_ref, count=8):
    even, outside = edge_flags(where_ref[0], grid)
    near_at = jnp.where(even, depth + count, 0)
    far_at = jnp.where(even, 0, depth + count)
    for x in range(count):
        out_ref[depth + x, 0:8] = own_ref[x]
    for i in range(depth):
        out_ref[near_at + i, 0:8] = near_ref[first + i]
        out_ref[far_at + i, 0:8] = jnp.where(outside, 0.0, far_ref[first + i])


def y_tiles(where_ref, grid, even_ref, odd_ref, p):
    even, outside = edge_flags(where_ref[1], grid)
    inner = even_ref[p]
    outer = jnp.where(outside, 0.0, odd_ref[p])
    return jnp.where(even, inner, outer), jnp.where(even, outer, inner)


def corner_kernel(ny, where_ref, yeven_ref, yodd_ref, near_ref, far_ref):
    even = where_ref[0] % 2 == 0
    for ref, side in ((near_ref, even), (far_ref, jnp.logical_not(even))):
        for i in range(2):
            high, low = y_tiles(where_ref, ny, yeven_ref, yodd_ref, jnp.where(side, 7 - i, i))
            ref[i] = high
            ref[2 + i] = low


def down0_kernel(
    nx, ny, where_ref, kap_ref, init_ref, rhs_ref, near_ref, far_ref, even_ref, odd_ref,
    cnear_ref, cfar_ref,
    v0_ref, rs, cx, cy, cz, wi, block_ref, mnear_ref, mfar_ref, meven_ref, modd_ref,
    ks, vs, v1, v2, pair, fine, coarse,
):
    zero = jnp.zeros((8, 512), F32)
    for p in range(14):
        ks[p, 8:16] = zero
        vs[p, 8:16] = zero
    for p in range(12):
        rs[p, 8:16] = zero
    place_x(where_ref, nx, kap_ref, near_ref, far_ref, 0, 3, ks)
    place_x(where_ref, nx, init_ref, near_ref, far_ref, 3, 3, vs)
    place_x(where_ref, nx, rhs_ref, near_ref, far_ref, 6, 2, rs)

    def place(p, high, low):
        ks[p + 1, 8:11] = high[0:3]
        ks[p + 1, 13:16] = low[0:3]
        vs[p + 1, 8:11] = high[3:6]
        vs[p + 1, 13:16] = low[3:6]
        rs[p, 8:10] = high[6:8]
        rs[p, 14:16] = low[6:8]

    for x in range(8):
        place(x + 2, *y_tiles(where_ref, ny, even_ref, odd_ref, x))
    even, outside = edge_flags(where_ref[0], nx)
    for i in range(2):
        place(jnp.where(even, 10 + i, 1 - i), cnear_ref[i], cnear_ref[2 + i])
        place(
            jnp.where(even, 1 - i, 10 + i),
            jnp.where(outside, 0.0, cfar_ref[i]),
            jnp.where(outside, 0.0, cfar_ref[2 + i]),
        )
    cx[0] = 0.5 * (ks[0] + ks[1])
    for p in range(12):
        mid = ks[p + 1]
        cx[p + 1] = 0.5 * (mid + ks[p + 2])
        cy[p] = coupling_y(mid)
        cz[p] = coupling_z(mid)
        diag = diagonal(mid, ks[p], ks[p + 2])
        wi[p] = jnp.where(mid > 0.0, OMEGA / jnp.where(mid > 0.0, diag, 1.0), 0.0)
    for p in range(12):
        mid = vs[p + 1]
        total = gathered(mid, vs[p], vs[p + 2], cx[p], cx[p + 1], cy[p], cz[p])
        v1[p] = KEEP * mid + wi[p] * (rs[p] + total)
    for p in range(1, 11):
        mid = v1[p]
        total = gathered(mid, v1[p - 1], v1[p + 1], cx[p], cx[p + 1], cy[p], cz[p])
        v2[p] = KEEP * mid + wi[p] * (rs[p] + total)
    for p in range(2, 10, 2):
        both = None
        for q in (p, p + 1):
            mid = v2[q]
            total = gathered(mid, v2[q - 1], v2[q + 1], cx[q], cx[q + 1], cy[q], cz[q])
            diag = diagonal(ks[q + 1], ks[q], ks[q + 2])
            rest = (rs[q] + total - diag * mid)[0:8]
            both = rest if both is None else both + rest
            v0_ref[q - 2] = mid[0:8]
        at = 4 * (p // 2 - 1)
        fine[at : at + 4] = row_sum(pair, both)
    for p in range(0, 12, 2):
        at = 16 + 4 * p
        fine[at : at + 8] = row_sum(pair, ks[p + 1] + ks[p + 2])
    coarse[...] = lane_sum(fine[...], pair_sum_matrix())
    for x in range(4):
        half = pl.ds(256 * (x % 2), 256)
        mid = 0.125 * coarse[24 + 8 * x : 32 + 8 * x]
        low = 0.125 * coarse[16 + 8 * x : 24 + 8 * x]
        high = 0.125 * coarse[32 + 8 * x : 40 + 8 * x]
        block_ref[x // 2, 0:4, half] = 0.5 * coarse[4 * x : 4 * x + 4]
        block_ref[x // 2, 4:8, half] = mid[0:4]
        at = 4 * (x // 2)
        block_ref[2, at : at + 4, half] = (OMEGA / diagonal(mid, low, high)[0:4])
    for ref, side in ((mnear_ref, even), (mfar_ref, jnp.logical_not(even))):
        shallow = jnp.where(side, 6, 0)
        for i in range(3):
            ref[i] = block_ref[i]
        for i in range(2):
            ref[3 + i] = v0_ref[shallow + i]

    def write(low_ref, high_ref):
        for i in range(3):
            low_ref[i] = block_ref[i]
            high_ref[i] = block_ref[i]
        for x in range(8):
            at = 2 * (x % 4)
            low_ref[3 + x // 4, at : at + 2] = v0_ref[x, 0:2]
            high_ref[3 + x // 4, at : at + 2] = v0_ref[x, 6:8]

    by_parity(where_ref, meven_ref, modd_ref, write)


def corner1_kernel(ny, where_ref, meven_ref, modd_ref, near_ref, far_ref):
    tiles = [y_tiles(where_ref, ny, meven_ref, modd_ref, i) for i in range(5)]
    for ref in (near_ref, far_ref):
        for i in range(3):
            ref[i] = tiles[i][0]
            ref[3 + i] = tiles[i][1]
        ref[6] = jnp.zeros((8, 512), F32)

    def write(low_ref, high_ref):
        low_ref[6, 0:2] = tiles[3][0][0:2]
        low_ref[6, 2:4] = tiles[3][1][0:2]
        high_ref[6, 0:2] = tiles[4][0][6:8]
        high_ref[6, 2:4] = tiles[4][1][6:8]

    even = where_ref[0] % 2 == 0

    @pl.when(even)
    def _():
        write(far_ref, near_ref)

    @pl.when(jnp.logical_not(even))
    def _():
        write(near_ref, far_ref)


def down1_kernel(
    nx, ny, where_ref, block_ref, v0_ref, near_ref, far_ref, meven_ref, modd_ref,
    cnear_ref, cfar_ref,
    v0x, v1, f1, w1, cx, cy, cz, send_ref,
    k1, u1, pair, fine,
):
    even, outside = edge_flags(where_ref[0], nx)

    def inside(value):
        return jnp.where(outside, 0.0, value)

    near = [near_ref[i] for i in range(3)]
    far = [inside(far_ref[i]) for i in range(3)]
    cnear = [cnear_ref[i] for i in range(7)]
    cfar = [inside(cfar_ref[i]) for i in range(7)]
    mine = [y_tiles(where_ref, ny, meven_ref, modd_ref, i) for i in range(5)]

    def pick(a, b):
        return [jnp.where(even, p, q) for p, q in zip(a, b)]

    blocks = (
        (pick(far, near), pick(cfar[0:3], cnear[0:3]), pick(cfar[3:6], cnear[3:6])),
        ([block_ref[i] for i in range(3)], [t[0] for t in mine], [t[1] for t in mine]),
        (pick(near, far), pick(cnear[0:3], cfar[0:3]), pick(cnear[3:6], cfar[3:6])),
    )
    zero = jnp.zeros((4, 256), F32)
    for b in range(3):
        for x in range(4):
            p = 4 * b + x
            half = slice(256 * (x % 2), 256 * (x % 2) + 256)
            t = x // 2
            for ref, at, row in (
                (f1, t, slice(0, 4)), (k1, t, slice(4, 8)), (w1, 2, slice(4 * t, 4 * t + 4))
            ):
                ref[p, 0:4] = blocks[b][0][at][row, half]
                ref[p, 4:8] = blocks[b][1][at][row, half]
                ref[p, 8:12] = zero
                ref[p, 12:16] = blocks[b][2][at][row, half]
    blank = jnp.zeros((8, 512), F32)
    for p in range(12):
        v0x[p, 8:16] = blank
    for x in range(8):
        v0x[2 + x, 0:8] = v0_ref[x]
        at = 2 * (x % 4)
        v0x[2 + x, 8:10] = mine[3 + x // 4][0][at : at + 2]
        v0x[2 + x, 14:16] = mine[3 + x // 4][1][at : at + 2]
    near_at = jnp.where(even, 10, 0)
    far_at = jnp.where(even, 0, 10)
    for i in range(2):
        v0x[near_at + i, 0:8] = near_ref[3 + i]
        v0x[far_at + i, 0:8] = inside(far_ref[3 + i])
    for at, tile in ((jnp.where(even, 10, 1), cnear[6]), (jnp.where(even, 1, 10), cfar[6])):
        v0x[at, 8:10] = tile[0:2]
        v0x[at, 14:16] = tile[2:4]
    for p in range(12):
        u1[p] = w1[p] * f1[p]
        if p < 11:
            cx[p] = 0.5 * (k1[p] + k1[p + 1])
        cy[p] = coupling_y(k1[p])
        cz[p] = coupling_z(k1[p])
    for p in range(1, 11):
        mid = u1[p]
        total = gathered(mid, u1[p - 1], u1[p + 1], cx[p - 1], cx[p], cy[p], cz[p])
        v1[p] = KEEP * mid + w1[p] * (f1[p] + total)
    for p in range(4, 8, 2):
        both = None
        for q in (p, p + 1):
            mid = v1[q]
            total = gathered(mid, v1[q - 1], v1[q + 1], cx[q - 1], cx[q], cy[q], cz[q])
            diag = diagonal(k1[q], k1[q - 1], k1[q + 1])
            rest = (f1[q] + total - diag * mid)[0:8]
            both = rest if both is None else both + rest
        at = p - 4
        fine[at : at + 2] = 0.5 * row_sum(pair, both)[0:2]
        kept = k1[p, 0:8] + k1[p + 1, 0:8]
        fine[4 + at : 6 + at] = 0.125 * row_sum(pair, kept)[0:2]
    tile = lane_sum(fine[...], pair_sum_matrix())
    for i in range(send_ref.shape[0]):
        send_ref[i] = tile


def up_kernel(
    nx, ny, where_ref, mine_ref, other_ref, v1, f1, w1, cx1, cy1, cz1,
    v0x, rs, cx0, cy0, cz0, w0, out_ref,
    f2, k2, cx2, cyi, cyo, cz2, w2, u2, v2, e2, f3, k3, cx3, cy3, cz3, w3, ga, gb,
    small, wide, e1a, e1b, narrow, e0a, e0b,
):
    gx = where_ref[0]
    gy = where_ref[1]
    core = gx % 2
    n2 = 2 * nx
    zero = jnp.zeros((ny, 128), F32)
    row = iota((ny, 128), 0)
    lane = iota((ny, 128), 1)
    last_row = row == ny - 1
    for s in range(2):
        k2[0, s] = zero
        k2[n2 + 1, s] = zero
        u2[0, s] = zero
        u2[n2 + 1, s] = zero
        v2[0, s] = zero
        v2[n2 + 1, s] = zero
    for x in range(nx // 2):
        for ref, which in ((mine_ref, core), (other_ref, 1 - core)):
            for i in range(2):
                p = 4 * x + 2 * which + i + 1
                for s in range(2):
                    f2[p, s] = ref[x, pl.ds(2 * i + s, ny, stride=8)]
                    k2[p, s] = ref[x, pl.ds(4 + 2 * i + s, ny, stride=8)]
    for p in range(n2 + 1):
        for s in range(2):
            cx2[p, s] = 0.5 * (k2[p, s] + k2[p + 1, s])
    diags = {}
    for p in range(1, n2 + 1):
        k_low, k_high = k2[p, 0], k2[p, 1]
        after = jnp.where(last_row, 0.0, roll(k_low, -1, 0))
        before = jnp.where(row == 0, 0.0, roll(k_high, 1, 0))
        cyi[p] = 0.5 * (k_low + k_high)
        cyo[p] = jnp.where(last_row, 0.0, 0.5 * (k_high + after))
        for s, mid, ya, yb in ((0, k_low, k_high, before), (1, k_high, k_low, after)):
            up, down = z_neighbours(mid)
            cz2[p, s] = jnp.where(lane == 127, 0.0, 0.5 * (mid + up))
            diag = 3.0 * mid + 0.5 * (k2[p - 1, s] + k2[p + 1, s] + ya + yb + up + down)
            w2[p, s] = OMEGA / diag
            u2[p, s] = (OMEGA / diag) * f2[p, s]

    def gather2(ref, p):
        low, high = ref[p, 0], ref[p, 1]
        sums = []
        for s, mid in ((0, low), (1, high)):
            total = cx2[p, s] * ref[p + 1, s] + cx2[p - 1, s] * ref[p - 1, s]
            total = total + cz2[p, s] * roll(mid, -1, 1) + roll(cz2[p, s] * mid, 1, 1)
            sums.append(total)
        sums[0] = sums[0] + cyi[p] * high + roll(cyo[p] * high, 1, 0)
        sums[1] = sums[1] + cyi[p] * low + cyo[p] * roll(low, -1, 0)
        return (low, high), sums

    def sweep2(source, target):
        for p in range(1, n2 + 1):
            mids, sums = gather2(source, p)
            for s in range(2):
                target[p, s] = KEEP * mids[s] + w2[p, s] * (f2[p, s] + sums[s])

    sweep2(u2, v2)
    even_lane = lane % 2 == 0

    def pair_lanes(value):
        return value + jnp.where(even_lane, roll(value, -1, 1), roll(value, 1, 1))

    k3[0] = zero
    k3[nx + 1] = zero
    ga[0] = zero
    ga[nx + 1] = zero
    gb[0] = zero
    gb[nx + 1] = zero
    for x in range(nx):
        both = None
        kept = None
        for p in (2 * x + 1, 2 * x + 2):
            mids, sums = gather2(v2, p)
            for s in range(2):
                rest = f2[p, s] + sums[s] - (OMEGA / w2[p, s]) * mids[s]
                both = rest if both is None else both + rest
                kept = k2[p, s] if kept is None else kept + k2[p, s]
        f3[x + 1] = 0.5 * pair_lanes(both)
        k3[x + 1] = 0.125 * pair_lanes(kept)
    for p in range(nx + 1):
        cx3[p] = 0.5 * (k3[p] + k3[p + 1])
    edge_total = zero
    outer = (
        (row == 0).astype(F32) + last_row.astype(F32)
        + (lane < 2).astype(F32) + (lane >= 126).astype(F32)
    )
    for p in range(1, nx + 1):
        mid = k3[p]
        after = jnp.where(last_row, 0.0, roll(mid, -1, 0))
        before = jnp.where(row == 0, 0.0, roll(mid, 1, 0))
        up = jnp.where(lane >= 126, 0.0, roll(mid, -2, 1))
        down = jnp.where(lane < 2, 0.0, roll(mid, 2, 1))
        cy3[p] = jnp.where(last_row, 0.0, 0.5 * (mid + after))
        cz3[p] = jnp.where(lane >= 126, 0.0, 0.5 * (mid + up))
        diag = 3.0 * mid + 0.5 * (k3[p - 1] + k3[p + 1] + after + before + up + down)
        w3[p] = OMEGA / diag
        ga[p] = (OMEGA / diag) * f3[p]
        faces = outer + (1.0 if p == 1 else 0.0) + (1.0 if p == nx else 0.0)
        edge_total = edge_total + 0.5 * mid * faces

    def gather3(ref, p):
        mid = ref[p]
        total = cx3[p] * ref[p + 1] + cx3[p - 1] * ref[p - 1]
        total = total + cy3[p] * roll(mid, -1, 0) + roll(cy3[p] * mid, 1, 0)
        return mid, total + cz3[p] * roll(mid, -2, 1) + roll(cz3[p] * mid, 2, 1)

    source, target = ga, gb
    for _ in range(7):
        for p in range(1, nx + 1):
            mid, total = gather3(source, p)
            target[p] = KEEP * mid + w3[p] * (f3[p] + total)
        source, target = target, source
    rest_total = zero
    for p in range(1, nx + 1):
        mid, total = gather3(source, p)
        rest_total = rest_total + (f3[p] + total - (OMEGA / w3[p]) * mid)

    def whole(value):
        return jnp.sum(jnp.sum(value, axis=0, keepdims=True), axis=1, keepdims=True)

    shift = whole(rest_total) / whole(edge_total)
    for x in range(nx):
        e3 = source[x + 1] + shift
        for p in (2 * x + 1, 2 * x + 2):
            for s in range(2):
                v2[p, s] = v2[p, s] + e3
    sweep2(v2, u2)
    blank = jnp.zeros(e2.shape[2:], F32)
    for p in (0, 1, n2 + 2, n2 + 3):
        for s in range(2):
            e2[p, s] = blank
    for p in range(1, n2 + 1):
        mids, sums = gather2(u2, p)
        for s in range(2):
            e2[p + 1, s, 0:8] = blank[0:8]
            e2[p + 1, s, ny + 8 : ny + 16] = blank[0:8]
            e2[p + 1, s, 8 : ny + 8] = KEEP * mids[s] + w2[p, s] * (f2[p, s] + sums[s])
    copies = pair_copy_matrix()
    for i in range(6):
        small[8 * i + 4 : 8 * i + 6] = jnp.zeros((2, 128), F32)
        for j, step in ((0, 0), (2, 1), (6, -1)):
            for s in range(2):
                small[8 * i + j + s : 8 * i + j + s + 1] = e2[
                    2 * gx + i, s, pl.ds(gy + 8 + step, 1)
                ]
    wide[...] = lane_copy(small[...], copies)
    for i in range(6):
        spread = row_copy(narrow, wide[8 * i : 8 * i + 8])
        for p in (2 * i, 2 * i + 1):
            if 1 <= p <= 10:
                e1a[p] = v1[p] + spread
    for source, target, first, last in ((e1a, e1b, 2, 9), (e1b, e1a, 3, 8)):
        for p in range(first, last + 1):
            mid = source[p]
            total = gathered(
                mid, source[p - 1], source[p + 1], cx1[p - 1], cx1[p], cy1[p], cz1[p]
            )
            target[p] = KEEP * mid + w1[p] * (f1[p] + total)
    row8 = iota((8, 256), 0)
    for i in range(6):
        value = e1a[i + 3]
        wide[8 * i : 8 * i + 8] = jnp.where(row8 == 7, value[8:16], value[0:8])
    doubled = lane_copy(wide[...], copies)
    for i in range(6):
        spread = row_copy(narrow, doubled[8 * i : 8 * i + 8])
        for p in (2 * i, 2 * i + 1):
            e0a[p] = v0x[p] + spread
    for p in range(1, 11):
        mid = e0a[p]
        total = gathered(mid, e0a[p - 1], e0a[p + 1], cx0[p], cx0[p + 1], cy0[p], cz0[p])
        e0b[p] = KEEP * mid + w0[p] * (rs[p] + total)
    for p in range(2, 10):
        mid = e0b[p]
        total = gathered(mid, e0b[p - 1], e0b[p + 1], cx0[p], cx0[p + 1], cy0[p], cz0[p])
        out_ref[p - 2] = (KEEP * mid + w0[p] * (rs[p] + total))[0:8]


def run(kernel, outs, scratch, where, *operands, space=VMEM):
    return pl.pallas_call(
        kernel,
        out_shape=[jax.ShapeDtypeStruct(shape, F32) for shape in outs],
        in_specs=[pl.BlockSpec(memory_space=pltpu.SMEM)]
        + [pl.BlockSpec(memory_space=space)] * len(operands),
        out_specs=[pl.BlockSpec(memory_space=VMEM)] * len(outs),
        scratch_shapes=[VMEM(s, F32) if isinstance(s, tuple) else s for s in scratch],
        compiler_params=PARAMS,
    )(where, *operands)


def body(initial, right_side, phase_map, phase_table):
    nx, ny = lax.axis_size("gx"), lax.axis_size("gy")
    where = jnp.stack([lax.axis_index("gx"), lax.axis_index("gy")]).astype(jnp.int32)

    def inner(size):
        return [(i, i ^ 1) for i in range(size)]

    def outer(size):
        return [(i, (i + 1) % size if i % 2 else (i - 1) % size) for i in range(size)]

    def swap(near, far, axis, size):
        return lax.ppermute(near, axis, inner(size)), lax.ppermute(far, axis, outer(size))

    tile0 = (8, 512)
    ring0 = (16, 512)
    ring1 = (16, 256)
    kappa, init, rhs, near, far, yeven, yodd = run(
        start_kernel, [(8,) + tile0] * 7,
        [pltpu.SMEM((3,), F32), VMEM((8,) + tile0, jnp.int32), pltpu.SemaphoreType.DMA((4,))],
        where, phase_table, phase_map, initial, right_side, space=pl.ANY,
    )
    yeven, yodd = swap(yeven, yodd, "gy", ny)
    near, far = swap(near, far, "gx", nx)
    cnear, cfar = run(
        functools.partial(corner_kernel, ny), [(4,) + tile0] * 2, [], where, yeven, yodd
    )
    cnear, cfar = swap(cnear, cfar, "gx", nx)
    v0, rs, cx0, cy0, cz0, w0, block, mnear, mfar, meven, modd = run(
        functools.partial(down0_kernel, nx, ny),
        [(8,) + tile0, (12,) + ring0, (13,) + ring0]
        + [(12,) + ring0] * 3
        + [(3,) + tile0]
        + [(5,) + tile0] * 4,
        [(14,) + ring0, (14,) + ring0, (12,) + ring0, (12,) + ring0, (4, 16, 128), (64, 512), (64, 256)],
        where, kappa, init, rhs, near, far, yeven, yodd, cnear, cfar,
    )
    meven, modd = swap(meven, modd, "gy", ny)
    mnear, mfar = swap(mnear, mfar, "gx", nx)
    cnear, cfar = run(
        functools.partial(corner1_kernel, ny), [(7,) + tile0] * 2, [], where, meven, modd
    )
    cnear, cfar = swap(cnear, cfar, "gx", nx)
    v0x, v1, f1, w1, cx1, cy1, cz1, send = run(
        functools.partial(down1_kernel, nx, ny),
        [(12,) + ring0] + [(12,) + ring1] * 6 + [(ny, 8, 128)],
        [(12,) + ring1, (12,) + ring1, (4, 16, 128), (8, 256)],
        where, block, v0, mnear, mfar, meven, modd, cnear, cfar,
    )
    column = lax.all_to_all(send, "gy", 0, 0).reshape(1, ny * 8, 128)
    groups = [list(range(0, nx, 2)), list(range(1, nx, 2))]
    mine = lax.all_to_all(
        jnp.broadcast_to(column, (nx // 2, ny * 8, 128)), "gx", 0, 0, axis_index_groups=groups
    )
    other = lax.ppermute(mine, "gx", inner(nx))
    n2 = 2 * nx
    pair2 = (n2 + 2, 2, ny, 128)
    one2 = (n2 + 2, ny, 128)
    one3 = (nx + 2, ny, 128)
    (out,) = run(
        functools.partial(up_kernel, nx, ny), [(8,) + tile0],
        [pair2, pair2, pair2, one2, one2, pair2, pair2, pair2, pair2, (n2 + 4, 2, ny + 16, 128)]
        + [one3] * 8
        + [(48, 128), (48, 256), (12,) + ring1, (12,) + ring1, (4, 16, 128), (12,) + ring0, (12,) + ring0],
        where, mine, other, v1, f1, w1, cx1, cy1, cz1, v0x, rs, cx0, cy0, cz0, w0,
    )
    return out


def solution(mesh):
    return jax.shard_map(
        body,
        mesh=mesh,
        in_specs=(P("gx", "gy", None), P("gx", "gy", None), P("gx", "gy", None), P()),
        out_specs=P("gx", "gy", None),
        check_vma=False,
    )
```

```python
import functools

import jax
import jax.numpy as jnp
from jax import lax
from jax.experimental import pallas as pl
from jax.experimental.pallas import tpu as pltpu
from jax.sharding import PartitionSpec as P

F32 = jnp.float32
KEEP = 0.2
OMEGA = 0.8
VMEM = pltpu.VMEM
PARAMS = pltpu.CompilerParams(vmem_limit_bytes=48 * 1024 * 1024)


def roll(value, shift, axis):
    return pltpu.roll(value, shift % value.shape[axis], axis)


def iota(shape, dim):
    return lax.broadcasted_iota(jnp.int32, shape, dim)


def pair_sum_matrix():
    return (iota((256, 128), 0) // 2 == iota((256, 128), 1)).astype(F32)


def pair_copy_matrix():
    return (iota((128, 256), 1) // 2 == iota((128, 256), 0)).astype(F32)


def exact_dot(a, b):
    return lax.dot_general(
        a, b, (((1,), (0,)), ((), ())), precision=lax.Precision.HIGHEST, preferred_element_type=F32
    )


def lane_sum(value, matrix):
    width = value.shape[1]
    parts = [exact_dot(value[:, at : at + 256], matrix) for at in range(0, width, 256)]
    return parts[0] if len(parts) == 1 else jnp.concatenate(parts, axis=1)


def lane_copy(value, matrix):
    width = value.shape[1]
    parts = [exact_dot(value[:, at : at + 128], matrix) for at in range(0, width, 128)]
    return parts[0] if len(parts) == 1 else jnp.concatenate(parts, axis=1)


def row_sum(scratch, value):
    rows, width = value.shape
    parts = []
    for c in range(width // 128):
        scratch[c, 0:rows] = value[:, 128 * c : 128 * c + 128]
        first = scratch[c, pl.ds(0, rows // 2, stride=2)]
        parts.append(first + scratch[c, pl.ds(1, rows // 2, stride=2)])
    return parts[0] if len(parts) == 1 else jnp.concatenate(parts, axis=1)


def row_copy(scratch, value):
    rows, width = value.shape
    parts = []
    for c in range(width // 128):
        part = value[:, 128 * c : 128 * c + 128]
        scratch[c, pl.ds(0, rows, stride=2)] = part
        scratch[c, pl.ds(1, rows, stride=2)] = part
        parts.append(scratch[c, 0 : 2 * rows])
    return parts[0] if len(parts) == 1 else jnp.concatenate(parts, axis=1)


def gathered(mid, low, high, cx_low, cx, cy, cz):
    total = cx * high + cx_low * low
    total = total + cy * roll(mid, -1, 0) + roll(cy * mid, 1, 0)
    return total + cz * roll(mid, -1, 1) + roll(cz * mid, 1, 1)


def z_neighbours(mid):
    lane = iota(mid.shape, 1)
    last = mid.shape[1] - 1
    up = jnp.where(lane == last, 0.0, roll(mid, -1, 1))
    down = jnp.where(lane == 0, 0.0, roll(mid, 1, 1))
    return up, down


def diagonal(mid, low, high):
    up, down = z_neighbours(mid)
    total = low + high + roll(mid, -1, 0) + roll(mid, 1, 0) + up + down
    return 3.0 * mid + 0.5 * total


def coupling_y(mid):
    return 0.5 * (mid + roll(mid, -1, 0))


def coupling_z(mid):
    lane = iota(mid.shape, 1)
    return jnp.where(lane == mid.shape[1] - 1, 0.0, 0.5 * (mid + roll(mid, -1, 1)))


def edge_flags(at, grid):
    even = at % 2 == 0
    outside = jnp.logical_or(at == 0, at == grid - 1)
    return even, outside


def start_kernel(
    where_ref, table_hbm, phase_hbm, init_hbm, rhs_hbm,
    kap_ref, init_ref, rhs_ref, near_ref, far_ref, yeven_ref, yodd_ref,
    table_ref, phase_ref, sems,
):
    copies = [
        pltpu.make_async_copy(source, target, sems.at[i])
        for i, (source, target) in enumerate(
            ((table_hbm, table_ref), (phase_hbm, phase_ref), (init_hbm, init_ref), (rhs_hbm, rhs_ref))
        )
    ]
    for copy in copies:
        copy.start()
    for copy in copies:
        copy.wait()
    even = where_ref[0] % 2 == 0
    for x in range(8):
        phase = phase_ref[x]
        kap_ref[x] = jnp.where(
            phase == 0, table_ref[0], jnp.where(phase == 1, table_ref[1], table_ref[2])
        )
    for ref, side in ((near_ref, even), (far_ref, jnp.logical_not(even))):
        deep = jnp.where(side, 5, 0)
        shallow = jnp.where(side, 6, 0)
        for i in range(3):
            ref[i] = kap_ref[deep + i]
            ref[3 + i] = init_ref[deep + i]
        for i in range(2):
            ref[6 + i] = rhs_ref[shallow + i]

    def write(low_ref, high_ref):
        for x in range(8):
            low_ref[x, 0:3] = kap_ref[x, 0:3]
            low_ref[x, 3:6] = init_ref[x, 0:3]
            low_ref[x, 6:8] = rhs_ref[x, 0:2]
            high_ref[x, 0:3] = kap_ref[x, 5:8]
            high_ref[x, 3:6] = init_ref[x, 5:8]
            high_ref[x, 6:8] = rhs_ref[x, 6:8]

    by_parity(where_ref, yeven_ref, yodd_ref, write)


def by_parity(where_ref, even_ref, odd_ref, write):
    even = where_ref[1] % 2 == 0

    @pl.when(even)
    def _():
        write(odd_ref, even_ref)

    @pl.when(jnp.logical_not(even))
    def _():
        write(even_ref, odd_ref)


def place_x(where_ref, grid, own_ref, near_ref, far_ref, first, depth, out_ref, count=8):
    even, outside = edge_flags(where_ref[0], grid)
    near_at = jnp.where(even, depth + count, 0)
    far_at = jnp.where(even, 0, depth + count)
    for x in range(count):
        out_ref[depth + x, 0:8] = own_ref[x]
    for i in range(depth):
        out_ref[near_at + i, 0:8] = near_ref[first + i]
        out_ref[far_at + i, 0:8] = jnp.where(outside, 0.0, far_ref[first + i])


def y_tiles(where_ref, grid, even_ref, odd_ref, p):
    even, outside = edge_flags(where_ref[1], grid)
    inner = even_ref[p]
    outer = jnp.where(outside, 0.0, odd_ref[p])
    return jnp.where(even, inner, outer), jnp.where(even, outer, inner)


def corner_messages(nx, ny, yeven, yodd):
    even = lax.axis_index("gx") % 2 == 0
    high, low = both_tiles(ny, yeven, yodd)
    top = jnp.concatenate([high[7:8], high[6:7], low[7:8], low[6:7]], axis=0)
    bottom = jnp.concatenate([high[0:2], low[0:2]], axis=0)
    return jnp.where(even, top, bottom), jnp.where(even, bottom, top)


def both_tiles(ny, yeven, yodd):
    at = lax.axis_index("gy")
    even, outside = edge_flags(at, ny)
    outer = jnp.where(outside, 0.0, yodd)
    return jnp.where(even, yeven, outer), jnp.where(even, outer, yeven)


def down0_kernel(
    nx, ny, where_ref, kap_ref, init_ref, rhs_ref, near_ref, far_ref, even_ref, odd_ref,
    cnear_ref, cfar_ref,
    v0_ref, rs, cx, cy, cz, wi, block_ref, mnear_ref, mfar_ref, meven_ref, modd_ref,
    ks, vs, v1, v2, pair, fine, coarse,
):
    zero = jnp.zeros((8, 512), F32)
    for p in range(14):
        ks[p, 8:16] = zero
        vs[p, 8:16] = zero
    for p in range(12):
        rs[p, 8:16] = zero
    place_x(where_ref, nx, kap_ref, near_ref, far_ref, 0, 3, ks)
    place_x(where_ref, nx, init_ref, near_ref, far_ref, 3, 3, vs)
    place_x(where_ref, nx, rhs_ref, near_ref, far_ref, 6, 2, rs)

    def place(p, high, low):
        ks[p + 1, 8:11] = high[0:3]
        ks[p + 1, 13:16] = low[0:3]
        vs[p + 1, 8:11] = high[3:6]
        vs[p + 1, 13:16] = low[3:6]
        rs[p, 8:10] = high[6:8]
        rs[p, 14:16] = low[6:8]

    for x in range(8):
        place(x + 2, *y_tiles(where_ref, ny, even_ref, odd_ref, x))
    even, outside = edge_flags(where_ref[0], nx)
    for i in range(2):
        place(jnp.where(even, 10 + i, 1 - i), cnear_ref[i], cnear_ref[2 + i])
        place(
            jnp.where(even, 1 - i, 10 + i),
            jnp.where(outside, 0.0, cfar_ref[i]),
            jnp.where(outside, 0.0, cfar_ref[2 + i]),
        )
    cx[0] = 0.5 * (ks[0] + ks[1])
    for p in range(12):
        mid = ks[p + 1]
        cx[p + 1] = 0.5 * (mid + ks[p + 2])
        cy[p] = coupling_y(mid)
        cz[p] = coupling_z(mid)
        diag = diagonal(mid, ks[p], ks[p + 2])
        wi[p] = jnp.where(mid > 0.0, OMEGA / jnp.where(mid > 0.0, diag, 1.0), 0.0)
    for p in range(12):
        mid = vs[p + 1]
        total = gathered(mid, vs[p], vs[p + 2], cx[p], cx[p + 1], cy[p], cz[p])
        v1[p] = KEEP * mid + wi[p] * (rs[p] + total)
    for p in range(1, 11):
        mid = v1[p]
        total = gathered(mid, v1[p - 1], v1[p + 1], cx[p], cx[p + 1], cy[p], cz[p])
        v2[p] = KEEP * mid + wi[p] * (rs[p] + total)
    for p in range(2, 10, 2):
        both = None
        for q in (p, p + 1):
            mid = v2[q]
            total = gathered(mid, v2[q - 1], v2[q + 1], cx[q], cx[q + 1], cy[q], cz[q])
            diag = diagonal(ks[q + 1], ks[q], ks[q + 2])
            rest = (rs[q] + total - diag * mid)[0:8]
            both = rest if both is None else both + rest
            v0_ref[q - 2] = mid[0:8]
        at = 4 * (p // 2 - 1)
        fine[at : at + 4] = row_sum(pair, both)
    for p in range(0, 12, 2):
        at = 16 + 4 * p
        fine[at : at + 8] = row_sum(pair, ks[p + 1] + ks[p + 2])
    coarse[...] = lane_sum(fine[...], pair_sum_matrix())
    for x in range(4):
        half = pl.ds(256 * (x % 2), 256)
        mid = 0.125 * coarse[24 + 8 * x : 32 + 8 * x]
        low = 0.125 * coarse[16 + 8 * x : 24 + 8 * x]
        high = 0.125 * coarse[32 + 8 * x : 40 + 8 * x]
        block_ref[x // 2, 0:4, half] = 0.5 * coarse[4 * x : 4 * x + 4]
        block_ref[x // 2, 4:8, half] = mid[0:4]
        at = 4 * (x // 2)
        block_ref[2, at : at + 4, half] = (OMEGA / diagonal(mid, low, high)[0:4])
    for ref, side in ((mnear_ref, even), (mfar_ref, jnp.logical_not(even))):
        shallow = jnp.where(side, 6, 0)
        for i in range(3):
            ref[i] = block_ref[i]
        for i in range(2):
            ref[3 + i] = v0_ref[shallow + i]

    def write(low_ref, high_ref):
        for i in range(3):
            low_ref[i] = block_ref[i]
            high_ref[i] = block_ref[i]
        for x in range(8):
            at = 2 * (x % 4)
            low_ref[3 + x // 4, at : at + 2] = v0_ref[x, 0:2]
            high_ref[3 + x // 4, at : at + 2] = v0_ref[x, 6:8]

    by_parity(where_ref, meven_ref, modd_ref, write)


def corner1_message(ny, meven, modd):
    high, low = both_tiles(ny, meven, modd)
    rows = [high[4:5, 6:8], low[4:5, 6:8], high[3:4, 0:2], low[3:4, 0:2]]
    return jnp.concatenate([high[0:3], low[0:3], jnp.concatenate(rows, axis=1)], axis=0)


def down1_kernel(
    nx, ny, where_ref, block_ref, v0_ref, near_ref, far_ref, meven_ref, modd_ref,
    cnear_ref, cfar_ref,
    v0x, v1, f1, w1, cx, cy, cz, send_ref,
    k1, u1, pair, fine,
):
    even, outside = edge_flags(where_ref[0], nx)

    def inside(value):
        return jnp.where(outside, 0.0, value)

    near = [near_ref[i] for i in range(3)]
    far = [inside(far_ref[i]) for i in range(3)]
    cnear = [cnear_ref[i] for i in range(7)]
    cfar = [inside(cfar_ref[i]) for i in range(7)]
    mine = [y_tiles(where_ref, ny, meven_ref, modd_ref, i) for i in range(5)]

    def pick(a, b):
        return [jnp.where(even, p, q) for p, q in zip(a, b)]

    blocks = (
        (pick(far, near), pick(cfar[0:3], cnear[0:3]), pick(cfar[3:6], cnear[3:6])),
        ([block_ref[i] for i in range(3)], [t[0] for t in mine], [t[1] for t in mine]),
        (pick(near, far), pick(cnear[0:3], cfar[0:3]), pick(cnear[3:6], cfar[3:6])),
    )
    zero = jnp.zeros((4, 256), F32)
    for b in range(3):
        for x in range(4):
            p = 4 * b + x
            half = slice(256 * (x % 2), 256 * (x % 2) + 256)
            t = x // 2
            for ref, at, row in (
                (f1, t, slice(0, 4)), (k1, t, slice(4, 8)), (w1, 2, slice(4 * t, 4 * t + 4))
            ):
                ref[p, 0:4] = blocks[b][0][at][row, half]
                ref[p, 4:8] = blocks[b][1][at][row, half]
                ref[p, 8:12] = zero
                ref[p, 12:16] = blocks[b][2][at][row, half]
    blank = jnp.zeros((8, 512), F32)
    for p in range(12):
        v0x[p, 8:16] = blank
    for x in range(8):
        v0x[2 + x, 0:8] = v0_ref[x]
        at = 2 * (x % 4)
        v0x[2 + x, 8:10] = mine[3 + x // 4][0][at : at + 2]
        v0x[2 + x, 14:16] = mine[3 + x // 4][1][at : at + 2]
    near_at = jnp.where(even, 10, 0)
    far_at = jnp.where(even, 0, 10)
    for i in range(2):
        v0x[near_at + i, 0:8] = near_ref[3 + i]
        v0x[far_at + i, 0:8] = inside(far_ref[3 + i])
    low_tile = jnp.where(even, cfar[6], cnear[6])
    high_tile = jnp.where(even, cnear[6], cfar[6])
    for at, tile, row in ((1, low_tile, 0), (10, high_tile, 4)):
        v0x[at, 8:10] = tile[row : row + 2]
        v0x[at, 14:16] = tile[row + 2 : row + 4]
    for p in range(12):
        u1[p] = w1[p] * f1[p]
        if p < 11:
            cx[p] = 0.5 * (k1[p] + k1[p + 1])
        cy[p] = coupling_y(k1[p])
        cz[p] = coupling_z(k1[p])
    for p in range(1, 11):
        mid = u1[p]
        total = gathered(mid, u1[p - 1], u1[p + 1], cx[p - 1], cx[p], cy[p], cz[p])
        v1[p] = KEEP * mid + w1[p] * (f1[p] + total)
    for p in range(4, 8, 2):
        both = None
        for q in (p, p + 1):
            mid = v1[q]
            total = gathered(mid, v1[q - 1], v1[q + 1], cx[q - 1], cx[q], cy[q], cz[q])
            diag = diagonal(k1[q], k1[q - 1], k1[q + 1])
            rest = (f1[q] + total - diag * mid)[0:8]
            both = rest if both is None else both + rest
        at = p - 4
        fine[at : at + 2] = 0.5 * row_sum(pair, both)[0:2]
        kept = k1[p, 0:8] + k1[p + 1, 0:8]
        fine[4 + at : 6 + at] = 0.125 * row_sum(pair, kept)[0:2]
    tile = lane_sum(fine[...], pair_sum_matrix())
    for i in range(send_ref.shape[0]):
        send_ref[i] = tile


def up_kernel(
    nx, ny, where_ref, mine_ref, other_ref, v1, f1, w1, cx1, cy1, cz1,
    v0x, rs, cx0, cy0, cz0, w0, out_ref,
    f2, k2, cx2, cyi, cyo, cz2, w2, d2, u2, v2, e2, f3, k3, cx3, cy3, cz3, w3, edge3, ga, gb,
    small, wide, e1a, e1b, narrow, e0a, e0b,
):
    gx = where_ref[0]
    gy = where_ref[1]
    core = gx % 2
    n2 = 2 * nx
    zero = jnp.zeros((ny, 128), F32)
    row = iota((ny, 128), 0)
    lane = iota((ny, 128), 1)
    last_row = row == ny - 1
    for s in range(2):
        k2[0, s] = zero
        k2[n2 + 1, s] = zero
        u2[0, s] = zero
        u2[n2 + 1, s] = zero
        v2[0, s] = zero
        v2[n2 + 1, s] = zero
    for x in range(nx // 2):
        for ref, which in ((mine_ref, core), (other_ref, 1 - core)):
            for i in range(2):
                p = 4 * x + 2 * which + i + 1
                for s in range(2):
                    f2[p, s] = ref[x, pl.ds(2 * i + s, ny, stride=8)]
                    k2[p, s] = ref[x, pl.ds(4 + 2 * i + s, ny, stride=8)]
    for p in range(n2 + 1):
        for s in range(2):
            cx2[p, s] = 0.5 * (k2[p, s] + k2[p + 1, s])
    for p in range(1, n2 + 1):
        k_low, k_high = k2[p, 0], k2[p, 1]
        after = jnp.where(last_row, 0.0, roll(k_low, -1, 0))
        before = jnp.where(row == 0, 0.0, roll(k_high, 1, 0))
        cyi[p] = 0.5 * (k_low + k_high)
        cyo[p] = jnp.where(last_row, 0.0, 0.5 * (k_high + after))
        for s, mid, ya, yb in ((0, k_low, k_high, before), (1, k_high, k_low, after)):
            up, down = z_neighbours(mid)
            cz2[p, s] = jnp.where(lane == 127, 0.0, 0.5 * (mid + up))
            diag = 3.0 * mid + 0.5 * (k2[p - 1, s] + k2[p + 1, s] + ya + yb + up + down)
            scale = OMEGA / diag
            d2[p, s] = diag
            w2[p, s] = scale
            u2[p, s] = scale * f2[p, s]

    def gather2(ref, p):
        low, high = ref[p, 0], ref[p, 1]
        sums = []
        for s, mid in ((0, low), (1, high)):
            total = cx2[p, s] * ref[p + 1, s] + cx2[p - 1, s] * ref[p - 1, s]
            total = total + cz2[p, s] * roll(mid, -1, 1) + roll(cz2[p, s] * mid, 1, 1)
            sums.append(total)
        sums[0] = sums[0] + cyi[p] * high + roll(cyo[p] * high, 1, 0)
        sums[1] = sums[1] + cyi[p] * low + cyo[p] * roll(low, -1, 0)
        return (low, high), sums

    def sweep2(source, target):
        for p in range(1, n2 + 1):
            mids, sums = gather2(source, p)
            for s in range(2):
                target[p, s] = KEEP * mids[s] + w2[p, s] * (f2[p, s] + sums[s])

    sweep2(u2, v2)
    even_lane = lane % 2 == 0

    def pair_lanes(value):
        return value + jnp.where(even_lane, roll(value, -1, 1), roll(value, 1, 1))

    k3[0] = zero
    k3[nx + 1] = zero
    ga[0] = zero
    ga[nx + 1] = zero
    gb[0] = zero
    gb[nx + 1] = zero
    for x in range(nx):
        both = None
        kept = None
        for p in (2 * x + 1, 2 * x + 2):
            mids, sums = gather2(v2, p)
            for s in range(2):
                rest = f2[p, s] + sums[s] - d2[p, s] * mids[s]
                both = rest if both is None else both + rest
                kept = k2[p, s] if kept is None else kept + k2[p, s]
        f3[x + 1] = 0.5 * pair_lanes(both)
        k3[x + 1] = 0.125 * pair_lanes(kept)
    for p in range(nx + 1):
        cx3[p] = 0.5 * (k3[p] + k3[p + 1])
    edge_total = zero
    rest_total = zero
    outer = (
        (row == 0).astype(F32) + last_row.astype(F32)
        + (lane < 2).astype(F32) + (lane >= 126).astype(F32)
    )
    for p in range(1, nx + 1):
        mid = k3[p]
        after = jnp.where(last_row, 0.0, roll(mid, -1, 0))
        before = jnp.where(row == 0, 0.0, roll(mid, 1, 0))
        up = jnp.where(lane >= 126, 0.0, roll(mid, -2, 1))
        down = jnp.where(lane < 2, 0.0, roll(mid, 2, 1))
        cy3[p] = jnp.where(last_row, 0.0, 0.5 * (mid + after))
        cz3[p] = jnp.where(lane >= 126, 0.0, 0.5 * (mid + up))
        diag = 3.0 * mid + 0.5 * (k3[p - 1] + k3[p + 1] + after + before + up + down)
        scale = OMEGA / diag
        w3[p] = scale
        ga[p] = scale * f3[p]
        faces = outer + (1.0 if p == 1 else 0.0) + (1.0 if p == nx else 0.0)
        edge = 0.5 * mid * faces
        edge3[p] = edge
        edge_total = edge_total + edge
        rest_total = rest_total + f3[p]

    def gather3(ref, p):
        mid = ref[p]
        total = cx3[p] * ref[p + 1] + cx3[p - 1] * ref[p - 1]
        total = total + cy3[p] * roll(mid, -1, 0) + roll(cy3[p] * mid, 1, 0)
        return mid, total + cz3[p] * roll(mid, -2, 1) + roll(cz3[p] * mid, 2, 1)

    source, target = ga, gb
    for _ in range(7):
        for p in range(1, nx + 1):
            mid, total = gather3(source, p)
            target[p] = KEEP * mid + w3[p] * (f3[p] + total)
        source, target = target, source
    for p in range(1, nx + 1):
        rest_total = rest_total - edge3[p] * source[p]

    def whole(value):
        return jnp.sum(jnp.sum(value, axis=0, keepdims=True), axis=1, keepdims=True)

    shift = whole(rest_total) / whole(edge_total)
    first_row = jnp.clip(gy - 3, 0, ny - 8)
    rows = pl.ds(first_row, 8)
    no_wrap = iota((8, 128), 0) < 7
    planes = []
    for j in range(10):
        x = 2 * gx - 4 + j
        planes.append((jnp.logical_and(x >= 0, x < n2), jnp.clip(x, 0, n2 - 1)))
    level = []
    for ok, q in planes:
        e3 = source[q // 2 + 1, rows] + shift
        level.append([jnp.where(ok, v2[q + 1, s, rows] + e3, 0.0) for s in range(2)])
    for first, last in ((1, 8), (2, 7)):
        done = list(level)
        for j in range(first, last + 1):
            ok, q = planes[j]
            low, high = level[j]
            inner = cyi[q + 1, rows]
            after = jnp.where(no_wrap, cyo[q + 1, rows], 0.0)
            sums = [inner * high + roll(after * high, 1, 0), inner * low + after * roll(low, -1, 0)]
            for s in range(2):
                mid = level[j][s]
                cz = cz2[q + 1, s, rows]
                total = sums[s] + cz * roll(mid, -1, 1) + roll(cz * mid, 1, 1)
                total = total + cx2[q + 1, s, rows] * level[j + 1][s]
                total = total + cx2[q, s, rows] * level[j - 1][s]
                value = KEEP * mid + w2[q + 1, s, rows] * (f2[q + 1, s, rows] + total)
                done[j] = [jnp.where(ok, value, 0.0)] if s == 0 else done[j] + [jnp.where(ok, value, 0.0)]
        level = done
    copies = pair_copy_matrix()
    at = gy - first_row
    steps = (
        (0, at, None),
        (2, jnp.minimum(at + 1, 7), gy < ny - 1),
        (6, jnp.maximum(at - 1, 0), gy > 0),
    )
    for i in range(6):
        small[8 * i + 4 : 8 * i + 6] = jnp.zeros((2, 128), F32)
        for s in range(2):
            e2[i, s] = level[i + 2][s]
            for j, r, ok in steps:
                line = e2[i, s, pl.ds(r, 1)]
                small[8 * i + j + s : 8 * i + j + s + 1] = (
                    line if ok is None else jnp.where(ok, line, 0.0)
                )
    wide[...] = lane_copy(small[...], copies)
    for i in range(6):
        spread = row_copy(narrow, wide[8 * i : 8 * i + 8])
        for p in (2 * i, 2 * i + 1):
            if 1 <= p <= 10:
                e1a[p] = v1[p] + spread
    for source, target, first, last in ((e1a, e1b, 2, 9), (e1b, e1a, 3, 8)):
        for p in range(first, last + 1):
            mid = source[p]
            total = gathered(
                mid, source[p - 1], source[p + 1], cx1[p - 1], cx1[p], cy1[p], cz1[p]
            )
            target[p] = KEEP * mid + w1[p] * (f1[p] + total)
    row8 = iota((8, 256), 0)
    for i in range(6):
        value = e1a[i + 3]
        wide[8 * i : 8 * i + 8] = jnp.where(row8 == 7, value[8:16], value[0:8])
    doubled = lane_copy(wide[...], copies)
    for i in range(6):
        spread = row_copy(narrow, doubled[8 * i : 8 * i + 8])
        for p in (2 * i, 2 * i + 1):
            e0a[p] = v0x[p] + spread
    for p in range(1, 11):
        mid = e0a[p]
        total = gathered(mid, e0a[p - 1], e0a[p + 1], cx0[p], cx0[p + 1], cy0[p], cz0[p])
        e0b[p] = KEEP * mid + w0[p] * (rs[p] + total)
    for p in range(2, 10):
        mid = e0b[p]
        total = gathered(mid, e0b[p - 1], e0b[p + 1], cx0[p], cx0[p + 1], cy0[p], cz0[p])
        out_ref[p - 2] = (KEEP * mid + w0[p] * (rs[p] + total))[0:8]


def run(kernel, outs, scratch, where, *operands, space=VMEM):
    return pl.pallas_call(
        kernel,
        out_shape=[jax.ShapeDtypeStruct(shape, F32) for shape in outs],
        in_specs=[pl.BlockSpec(memory_space=pltpu.SMEM)]
        + [pl.BlockSpec(memory_space=space)] * len(operands),
        out_specs=[pl.BlockSpec(memory_space=VMEM)] * len(outs),
        scratch_shapes=[VMEM(s, F32) if isinstance(s, tuple) else s for s in scratch],
        compiler_params=PARAMS,
    )(where, *operands)


def body(initial, right_side, phase_map, phase_table):
    nx, ny = lax.axis_size("gx"), lax.axis_size("gy")
    where = jnp.stack([lax.axis_index("gx"), lax.axis_index("gy")]).astype(jnp.int32)

    def inner(size):
        return [(i, i ^ 1) for i in range(size)]

    def outer(size):
        return [(i, (i + 1) % size if i % 2 else (i - 1) % size) for i in range(size)]

    def swap(near, far, axis, size):
        return lax.ppermute(near, axis, inner(size)), lax.ppermute(far, axis, outer(size))

    inputs = [
        pltpu.with_memory_space_constraint(value, pltpu.HBM)
        for value in (phase_table, phase_map, initial, right_side)
    ]
    tile0 = (8, 512)
    ring0 = (16, 512)
    ring1 = (16, 256)
    kappa, init, rhs, near, far, yeven, yodd = run(
        start_kernel, [(8,) + tile0] * 7,
        [pltpu.SMEM((3,), F32), VMEM((8,) + tile0, jnp.int32), pltpu.SemaphoreType.DMA((4,))],
        where, *inputs, space=pltpu.HBM,
    )
    yeven, yodd = swap(yeven, yodd, "gy", ny)
    near, far = swap(near, far, "gx", nx)
    near, far, yeven, yodd = lax.optimization_barrier((near, far, yeven, yodd))
    cnear, cfar = swap(*corner_messages(nx, ny, yeven, yodd), "gx", nx)
    v0, rs, cx0, cy0, cz0, w0, block, mnear, mfar, meven, modd = run(
        functools.partial(down0_kernel, nx, ny),
        [(8,) + tile0, (12,) + ring0, (13,) + ring0]
        + [(12,) + ring0] * 3
        + [(3,) + tile0]
        + [(5,) + tile0] * 4,
        [(14,) + ring0, (14,) + ring0, (12,) + ring0, (12,) + ring0, (4, 16, 128), (64, 512), (64, 256)],
        where, kappa, init, rhs, near, far, yeven, yodd, cnear, cfar,
    )
    meven, modd = swap(meven, modd, "gy", ny)
    mnear, mfar = swap(mnear, mfar, "gx", nx)
    mnear, mfar, meven, modd = lax.optimization_barrier((mnear, mfar, meven, modd))
    corner = corner1_message(ny, meven, modd)
    cnear, cfar = swap(corner, corner, "gx", nx)
    v0x, v1, f1, w1, cx1, cy1, cz1, send = run(
        functools.partial(down1_kernel, nx, ny),
        [(12,) + ring0] + [(12,) + ring1] * 6 + [(ny, 8, 128)],
        [(12,) + ring1, (12,) + ring1, (4, 16, 128), (8, 256)],
        where, block, v0, mnear, mfar, meven, modd, cnear, cfar,
    )
    column = lax.all_to_all(send, "gy", 0, 0).reshape(1, ny * 8, 128)
    groups = [list(range(0, nx, 2)), list(range(1, nx, 2))]
    mine = lax.all_to_all(
        jnp.broadcast_to(column, (nx // 2, ny * 8, 128)), "gx", 0, 0, axis_index_groups=groups
    )
    other = lax.ppermute(mine, "gx", inner(nx))
    n2 = 2 * nx
    pair2 = (n2 + 2, 2, ny, 128)
    one2 = (n2 + 2, ny, 128)
    one3 = (nx + 2, ny, 128)
    (out,) = run(
        functools.partial(up_kernel, nx, ny), [(8,) + tile0],
        [pair2, pair2, pair2, one2, one2, pair2, pair2, pair2, pair2, pair2, (6, 2, 8, 128)]
        + [one3] * 9
        + [(48, 128), (48, 256), (12,) + ring1, (12,) + ring1, (4, 16, 128), (12,) + ring0, (12,) + ring0],
        where, mine, other, v1, f1, w1, cx1, cy1, cz1, v0x, rs, cx0, cy0, cz0, w0,
    )
    return out


def solution(mesh):
    return jax.shard_map(
        body,
        mesh=mesh,
        in_specs=(P("gx", "gy", None), P("gx", "gy", None), P("gx", "gy", None), P()),
        out_specs=P("gx", "gy", None),
        check_vma=False,
    )
```

```python
import functools

import jax
import jax.numpy as jnp
from jax import lax
from jax.experimental import pallas as pl
from jax.experimental.pallas import tpu as pltpu
from jax.sharding import PartitionSpec as P

F32 = jnp.float32
KEEP = 0.2
OMEGA = 0.8
VMEM = pltpu.VMEM
PARAMS = pltpu.CompilerParams(vmem_limit_bytes=48 * 1024 * 1024)


def roll(value, shift, axis):
    return pltpu.roll(value, shift % value.shape[axis], axis)


def iota(shape, dim):
    return lax.broadcasted_iota(jnp.int32, shape, dim)


def pair_sum_matrix():
    return (iota((256, 128), 0) // 2 == iota((256, 128), 1)).astype(F32)


def pair_copy_matrix():
    return (iota((128, 256), 1) // 2 == iota((128, 256), 0)).astype(F32)


def exact_dot(a, b):
    return lax.dot_general(
        a, b, (((1,), (0,)), ((), ())), precision=lax.Precision.HIGHEST, preferred_element_type=F32
    )


def lane_sum(value, matrix):
    width = value.shape[1]
    parts = [exact_dot(value[:, at : at + 256], matrix) for at in range(0, width, 256)]
    return parts[0] if len(parts) == 1 else jnp.concatenate(parts, axis=1)


def lane_copy(value, matrix):
    width = value.shape[1]
    parts = [exact_dot(value[:, at : at + 128], matrix) for at in range(0, width, 128)]
    return parts[0] if len(parts) == 1 else jnp.concatenate(parts, axis=1)


def row_sum(scratch, value):
    rows, width = value.shape
    parts = []
    for c in range(width // 128):
        scratch[c, 0:rows] = value[:, 128 * c : 128 * c + 128]
        first = scratch[c, pl.ds(0, rows // 2, stride=2)]
        parts.append(first + scratch[c, pl.ds(1, rows // 2, stride=2)])
    return parts[0] if len(parts) == 1 else jnp.concatenate(parts, axis=1)


def row_copy(scratch, value):
    rows, width = value.shape
    parts = []
    for c in range(width // 128):
        part = value[:, 128 * c : 128 * c + 128]
        scratch[c, pl.ds(0, rows, stride=2)] = part
        scratch[c, pl.ds(1, rows, stride=2)] = part
        parts.append(scratch[c, 0 : 2 * rows])
    return parts[0] if len(parts) == 1 else jnp.concatenate(parts, axis=1)


def gathered(mid, low, high, cx_low, cx, cy, cz):
    total = cx * high + cx_low * low
    total = total + cy * roll(mid, -1, 0) + roll(cy * mid, 1, 0)
    return total + cz * roll(mid, -1, 1) + roll(cz * mid, 1, 1)


def z_neighbours(mid):
    lane = iota(mid.shape, 1)
    last = mid.shape[1] - 1
    up = jnp.where(lane == last, 0.0, roll(mid, -1, 1))
    down = jnp.where(lane == 0, 0.0, roll(mid, 1, 1))
    return up, down


def diagonal(mid, low, high):
    up, down = z_neighbours(mid)
    total = low + high + roll(mid, -1, 0) + roll(mid, 1, 0) + up + down
    return 3.0 * mid + 0.5 * total


def coupling_y(mid):
    return 0.5 * (mid + roll(mid, -1, 0))


def coupling_z(mid):
    lane = iota(mid.shape, 1)
    return jnp.where(lane == mid.shape[1] - 1, 0.0, 0.5 * (mid + roll(mid, -1, 1)))


def edge_flags(at, grid):
    even = at % 2 == 0
    outside = jnp.logical_or(at == 0, at == grid - 1)
    return even, outside


def start_kernel(
    where_ref, table_hbm, phase_hbm, init_hbm, rhs_hbm,
    kap_ref, init_ref, rhs_ref, near_ref, far_ref, yeven_ref, yodd_ref,
    table_ref, phase_ref, sems,
):
    copies = [
        pltpu.make_async_copy(source, target, sems.at[i])
        for i, (source, target) in enumerate(
            ((table_hbm, table_ref), (phase_hbm, phase_ref), (init_hbm, init_ref), (rhs_hbm, rhs_ref))
        )
    ]
    for copy in copies:
        copy.start()
    for copy in copies:
        copy.wait()
    even = where_ref[0] % 2 == 0
    for x in range(8):
        phase = phase_ref[x]
        kap_ref[x] = jnp.where(
            phase == 0, table_ref[0], jnp.where(phase == 1, table_ref[1], table_ref[2])
        )
    for ref, side in ((near_ref, even), (far_ref, jnp.logical_not(even))):
        deep = jnp.where(side, 5, 0)
        shallow = jnp.where(side, 6, 0)
        for i in range(3):
            ref[i] = kap_ref[deep + i]
            ref[3 + i] = init_ref[deep + i]
        for i in range(2):
            ref[6 + i] = rhs_ref[shallow + i]

    def write(low_ref, high_ref):
        for x in range(8):
            low_ref[x, 0:3] = kap_ref[x, 0:3]
            low_ref[x, 3:6] = init_ref[x, 0:3]
            low_ref[x, 6:8] = rhs_ref[x, 0:2]
            high_ref[x, 0:3] = kap_ref[x, 5:8]
            high_ref[x, 3:6] = init_ref[x, 5:8]
            high_ref[x, 6:8] = rhs_ref[x, 6:8]

    by_parity(where_ref, yeven_ref, yodd_ref, write)


def by_parity(where_ref, even_ref, odd_ref, write):
    even = where_ref[1] % 2 == 0

    @pl.when(even)
    def _():
        write(odd_ref, even_ref)

    @pl.when(jnp.logical_not(even))
    def _():
        write(even_ref, odd_ref)


def place_x(where_ref, grid, own_ref, near_ref, far_ref, first, depth, out_ref, count=8):
    even, outside = edge_flags(where_ref[0], grid)
    near_at = jnp.where(even, depth + count, 0)
    far_at = jnp.where(even, 0, depth + count)
    for x in range(count):
        out_ref[depth + x, 0:8] = own_ref[x]
    for i in range(depth):
        out_ref[near_at + i, 0:8] = near_ref[first + i]
        out_ref[far_at + i, 0:8] = jnp.where(outside, 0.0, far_ref[first + i])


def y_tiles(where_ref, grid, even_ref, odd_ref, p):
    even, outside = edge_flags(where_ref[1], grid)
    inner = even_ref[p]
    outer = jnp.where(outside, 0.0, odd_ref[p])
    return jnp.where(even, inner, outer), jnp.where(even, outer, inner)


def corner_messages(nx, ny, yeven, yodd):
    even = lax.axis_index("gx") % 2 == 0
    high, low = both_tiles(ny, yeven, yodd)
    top = jnp.concatenate([high[7:8], high[6:7], low[7:8], low[6:7]], axis=0)
    bottom = jnp.concatenate([high[0:2], low[0:2]], axis=0)
    return jnp.where(even, top, bottom), jnp.where(even, bottom, top)


def both_tiles(ny, yeven, yodd):
    at = lax.axis_index("gy")
    even, outside = edge_flags(at, ny)
    outer = jnp.where(outside, 0.0, yodd)
    return jnp.where(even, yeven, outer), jnp.where(even, outer, yeven)


def down0_kernel(
    nx, ny, where_ref, kap_ref, init_ref, rhs_ref, near_ref, far_ref, even_ref, odd_ref,
    cnear_ref, cfar_ref,
    v0_ref, rs, cx, cy, cz, wi, block_ref, mnear_ref, mfar_ref, meven_ref, modd_ref,
    ks, vs, v1, v2, pair, fine, coarse,
):
    zero = jnp.zeros((8, 512), F32)
    for p in range(14):
        ks[p, 8:16] = zero
        vs[p, 8:16] = zero
    for p in range(12):
        rs[p, 8:16] = zero
    place_x(where_ref, nx, kap_ref, near_ref, far_ref, 0, 3, ks)
    place_x(where_ref, nx, init_ref, near_ref, far_ref, 3, 3, vs)
    place_x(where_ref, nx, rhs_ref, near_ref, far_ref, 6, 2, rs)

    def place(p, high, low):
        ks[p + 1, 8:11] = high[0:3]
        ks[p + 1, 13:16] = low[0:3]
        vs[p + 1, 8:11] = high[3:6]
        vs[p + 1, 13:16] = low[3:6]
        rs[p, 8:10] = high[6:8]
        rs[p, 14:16] = low[6:8]

    for x in range(8):
        place(x + 2, *y_tiles(where_ref, ny, even_ref, odd_ref, x))
    even, outside = edge_flags(where_ref[0], nx)
    for i in range(2):
        place(jnp.where(even, 10 + i, 1 - i), cnear_ref[i], cnear_ref[2 + i])
        place(
            jnp.where(even, 1 - i, 10 + i),
            jnp.where(outside, 0.0, cfar_ref[i]),
            jnp.where(outside, 0.0, cfar_ref[2 + i]),
        )
    cx[0] = 0.5 * (ks[0] + ks[1])
    for p in range(12):
        mid = ks[p + 1]
        cx[p + 1] = 0.5 * (mid + ks[p + 2])
        cy[p] = coupling_y(mid)
        cz[p] = coupling_z(mid)
        diag = diagonal(mid, ks[p], ks[p + 2])
        wi[p] = jnp.where(mid > 0.0, OMEGA / jnp.where(mid > 0.0, diag, 1.0), 0.0)
    for p in range(12):
        mid = vs[p + 1]
        total = gathered(mid, vs[p], vs[p + 2], cx[p], cx[p + 1], cy[p], cz[p])
        v1[p] = KEEP * mid + wi[p] * (rs[p] + total)
    for p in range(1, 11):
        mid = v1[p]
        total = gathered(mid, v1[p - 1], v1[p + 1], cx[p], cx[p + 1], cy[p], cz[p])
        v2[p] = KEEP * mid + wi[p] * (rs[p] + total)
    for p in range(2, 10, 2):
        both = None
        for q in (p, p + 1):
            mid = v2[q]
            total = gathered(mid, v2[q - 1], v2[q + 1], cx[q], cx[q + 1], cy[q], cz[q])
            diag = diagonal(ks[q + 1], ks[q], ks[q + 2])
            rest = (rs[q] + total - diag * mid)[0:8]
            both = rest if both is None else both + rest
            v0_ref[q - 2] = mid[0:8]
        at = 4 * (p // 2 - 1)
        fine[at : at + 4] = row_sum(pair, both)
    for p in range(0, 12, 2):
        at = 16 + 4 * p
        fine[at : at + 8] = row_sum(pair, ks[p + 1] + ks[p + 2])
    coarse[...] = lane_sum(fine[...], pair_sum_matrix())
    for x in range(4):
        half = pl.ds(256 * (x % 2), 256)
        mid = 0.125 * coarse[24 + 8 * x : 32 + 8 * x]
        low = 0.125 * coarse[16 + 8 * x : 24 + 8 * x]
        high = 0.125 * coarse[32 + 8 * x : 40 + 8 * x]
        block_ref[x // 2, 0:4, half] = 0.5 * coarse[4 * x : 4 * x + 4]
        block_ref[x // 2, 4:8, half] = mid[0:4]
        at = 4 * (x // 2)
        block_ref[2, at : at + 4, half] = (OMEGA / diagonal(mid, low, high)[0:4])
    for ref, side in ((mnear_ref, even), (mfar_ref, jnp.logical_not(even))):
        shallow = jnp.where(side, 6, 0)
        for i in range(3):
            ref[i] = block_ref[i]
        for i in range(2):
            ref[3 + i] = v0_ref[shallow + i]

    def write(low_ref, high_ref):
        for i in range(3):
            low_ref[i] = block_ref[i]
            high_ref[i] = block_ref[i]
        for x in range(8):
            at = 2 * (x % 4)
            low_ref[3 + x // 4, at : at + 2] = v0_ref[x, 0:2]
            high_ref[3 + x // 4, at : at + 2] = v0_ref[x, 6:8]

    by_parity(where_ref, meven_ref, modd_ref, write)


def corner1_message(ny, meven, modd):
    high, low = both_tiles(ny, meven, modd)
    rows = [high[4:5, 6:8], low[4:5, 6:8], high[3:4, 0:2], low[3:4, 0:2]]
    return jnp.concatenate([high[0:3], low[0:3], jnp.concatenate(rows, axis=1)], axis=0)


def down1_kernel(
    nx, ny, where_ref, block_ref, v0_ref, near_ref, far_ref, meven_ref, modd_ref,
    cnear_ref, cfar_ref,
    v0x, v1, f1, w1, cx, cy, cz, send_ref,
    k1, u1, pair, fine,
):
    even, outside = edge_flags(where_ref[0], nx)

    def inside(value):
        return jnp.where(outside, 0.0, value)

    near = [near_ref[i] for i in range(3)]
    far = [inside(far_ref[i]) for i in range(3)]
    cnear = [cnear_ref[i] for i in range(7)]
    cfar = [inside(cfar_ref[i]) for i in range(7)]
    mine = [y_tiles(where_ref, ny, meven_ref, modd_ref, i) for i in range(5)]

    def pick(a, b):
        return [jnp.where(even, p, q) for p, q in zip(a, b)]

    blocks = (
        (pick(far, near), pick(cfar[0:3], cnear[0:3]), pick(cfar[3:6], cnear[3:6])),
        ([block_ref[i] for i in range(3)], [t[0] for t in mine], [t[1] for t in mine]),
        (pick(near, far), pick(cnear[0:3], cfar[0:3]), pick(cnear[3:6], cfar[3:6])),
    )
    zero = jnp.zeros((4, 256), F32)
    for b in range(3):
        for x in range(4):
            p = 4 * b + x
            half = slice(256 * (x % 2), 256 * (x % 2) + 256)
            t = x // 2
            for ref, at, row in (
                (f1, t, slice(0, 4)), (k1, t, slice(4, 8)), (w1, 2, slice(4 * t, 4 * t + 4))
            ):
                ref[p, 0:4] = blocks[b][0][at][row, half]
                ref[p, 4:8] = blocks[b][1][at][row, half]
                ref[p, 8:12] = zero
                ref[p, 12:16] = blocks[b][2][at][row, half]
    blank = jnp.zeros((8, 512), F32)
    for p in range(12):
        v0x[p, 8:16] = blank
    for x in range(8):
        v0x[2 + x, 0:8] = v0_ref[x]
        at = 2 * (x % 4)
        v0x[2 + x, 8:10] = mine[3 + x // 4][0][at : at + 2]
        v0x[2 + x, 14:16] = mine[3 + x // 4][1][at : at + 2]
    near_at = jnp.where(even, 10, 0)
    far_at = jnp.where(even, 0, 10)
    for i in range(2):
        v0x[near_at + i, 0:8] = near_ref[3 + i]
        v0x[far_at + i, 0:8] = inside(far_ref[3 + i])
    low_tile = jnp.where(even, cfar[6], cnear[6])
    high_tile = jnp.where(even, cnear[6], cfar[6])
    for at, tile, row in ((1, low_tile, 0), (10, high_tile, 4)):
        v0x[at, 8:10] = tile[row : row + 2]
        v0x[at, 14:16] = tile[row + 2 : row + 4]
    for p in range(12):
        u1[p] = w1[p] * f1[p]
        if p < 11:
            cx[p] = 0.5 * (k1[p] + k1[p + 1])
        cy[p] = coupling_y(k1[p])
        cz[p] = coupling_z(k1[p])
    for p in range(1, 11):
        mid = u1[p]
        total = gathered(mid, u1[p - 1], u1[p + 1], cx[p - 1], cx[p], cy[p], cz[p])
        v1[p] = KEEP * mid + w1[p] * (f1[p] + total)
    for p in range(4, 8, 2):
        both = None
        for q in (p, p + 1):
            mid = v1[q]
            total = gathered(mid, v1[q - 1], v1[q + 1], cx[q - 1], cx[q], cy[q], cz[q])
            diag = diagonal(k1[q], k1[q - 1], k1[q + 1])
            rest = (f1[q] + total - diag * mid)[0:8]
            both = rest if both is None else both + rest
        at = p - 4
        fine[at : at + 2] = 0.5 * row_sum(pair, both)[0:2]
        kept = k1[p, 0:8] + k1[p + 1, 0:8]
        fine[4 + at : 6 + at] = 0.125 * row_sum(pair, kept)[0:2]
    tile = lane_sum(fine[...], pair_sum_matrix())
    for i in range(send_ref.shape[0]):
        send_ref[i] = tile


def up_kernel(
    nx, ny, where_ref, mine_ref, other_ref, v1, f1, w1, cx1, cy1, cz1,
    v0x, rs, cx0, cy0, cz0, w0, out_ref,
    f2, k2, cx2, cyi, cyo, cz2, w2, d2, u2, v2, e2, f3, k3, cx3, cy3, cz3, w3, edge3, ga, gb,
    small, wide, e1a, e1b, narrow, e0a, e0b,
):
    gx = where_ref[0]
    gy = where_ref[1]
    core = gx % 2
    n2 = 2 * nx
    zero = jnp.zeros((ny, 128), F32)
    row = iota((ny, 128), 0)
    lane = iota((ny, 128), 1)
    last_row = row == ny - 1
    for s in range(2):
        k2[0, s] = zero
        k2[n2 + 1, s] = zero
        u2[0, s] = zero
        u2[n2 + 1, s] = zero
        v2[0, s] = zero
        v2[n2 + 1, s] = zero
    for x in range(nx // 2):
        for ref, which in ((mine_ref, core), (other_ref, 1 - core)):
            for i in range(2):
                p = 4 * x + 2 * which + i + 1
                for s in range(2):
                    f2[p, s] = ref[x, pl.ds(2 * i + s, ny, stride=8)]
                    k2[p, s] = ref[x, pl.ds(4 + 2 * i + s, ny, stride=8)]
    for p in range(n2 + 1):
        for s in range(2):
            cx2[p, s] = 0.5 * (k2[p, s] + k2[p + 1, s])
    for p in range(1, n2 + 1):
        k_low, k_high = k2[p, 0], k2[p, 1]
        after = jnp.where(last_row, 0.0, roll(k_low, -1, 0))
        before = jnp.where(row == 0, 0.0, roll(k_high, 1, 0))
        cyi[p] = 0.5 * (k_low + k_high)
        cyo[p] = jnp.where(last_row, 0.0, 0.5 * (k_high + after))
        for s, mid, ya, yb in ((0, k_low, k_high, before), (1, k_high, k_low, after)):
            up, down = z_neighbours(mid)
            cz2[p, s] = jnp.where(lane == 127, 0.0, 0.5 * (mid + up))
            diag = 3.0 * mid + 0.5 * (k2[p - 1, s] + k2[p + 1, s] + ya + yb + up + down)
            scale = OMEGA / diag
            d2[p, s] = diag
            w2[p, s] = scale
            u2[p, s] = scale * f2[p, s]

    def gather2(ref, p):
        low, high = ref[p, 0], ref[p, 1]
        sums = []
        for s, mid in ((0, low), (1, high)):
            total = cx2[p, s] * ref[p + 1, s] + cx2[p - 1, s] * ref[p - 1, s]
            total = total + cz2[p, s] * roll(mid, -1, 1) + roll(cz2[p, s] * mid, 1, 1)
            sums.append(total)
        sums[0] = sums[0] + cyi[p] * high + roll(cyo[p] * high, 1, 0)
        sums[1] = sums[1] + cyi[p] * low + cyo[p] * roll(low, -1, 0)
        return (low, high), sums

    def sweep2(source, target):
        for p in range(1, n2 + 1):
            mids, sums = gather2(source, p)
            for s in range(2):
                target[p, s] = KEEP * mids[s] + w2[p, s] * (f2[p, s] + sums[s])

    sweep2(u2, v2)
    even_lane = lane % 2 == 0

    def pair_lanes(value):
        return value + jnp.where(even_lane, roll(value, -1, 1), roll(value, 1, 1))

    k3[0] = zero
    k3[nx + 1] = zero
    ga[0] = zero
    ga[nx + 1] = zero
    gb[0] = zero
    gb[nx + 1] = zero
    for x in range(nx):
        both = None
        kept = None
        for p in (2 * x + 1, 2 * x + 2):
            mids, sums = gather2(v2, p)
            for s in range(2):
                rest = f2[p, s] + sums[s] - d2[p, s] * mids[s]
                both = rest if both is None else both + rest
                kept = k2[p, s] if kept is None else kept + k2[p, s]
        f3[x + 1] = 0.5 * pair_lanes(both)
        k3[x + 1] = 0.125 * pair_lanes(kept)
    for p in range(nx + 1):
        cx3[p] = 0.5 * (k3[p] + k3[p + 1])
    edge_total = zero
    rest_total = zero
    outer = (
        (row == 0).astype(F32) + last_row.astype(F32)
        + (lane < 2).astype(F32) + (lane >= 126).astype(F32)
    )
    for p in range(1, nx + 1):
        mid = k3[p]
        after = jnp.where(last_row, 0.0, roll(mid, -1, 0))
        before = jnp.where(row == 0, 0.0, roll(mid, 1, 0))
        up = jnp.where(lane >= 126, 0.0, roll(mid, -2, 1))
        down = jnp.where(lane < 2, 0.0, roll(mid, 2, 1))
        cy3[p] = jnp.where(last_row, 0.0, 0.5 * (mid + after))
        cz3[p] = jnp.where(lane >= 126, 0.0, 0.5 * (mid + up))
        diag = 3.0 * mid + 0.5 * (k3[p - 1] + k3[p + 1] + after + before + up + down)
        scale = OMEGA / diag
        w3[p] = scale
        ga[p] = scale * f3[p]
        faces = outer + (1.0 if p == 1 else 0.0) + (1.0 if p == nx else 0.0)
        edge = 0.5 * mid * faces
        edge3[p] = edge
        edge_total = edge_total + edge
        rest_total = rest_total + f3[p]

    def gather3(ref, p):
        mid = ref[p]
        total = cx3[p] * ref[p + 1] + cx3[p - 1] * ref[p - 1]
        total = total + cy3[p] * roll(mid, -1, 0) + roll(cy3[p] * mid, 1, 0)
        return mid, total + cz3[p] * roll(mid, -2, 1) + roll(cz3[p] * mid, 2, 1)

    source, target = ga, gb
    for _ in range(7):
        for p in range(1, nx + 1):
            mid, total = gather3(source, p)
            target[p] = KEEP * mid + w3[p] * (f3[p] + total)
        source, target = target, source
    for p in range(1, nx + 1):
        rest_total = rest_total - edge3[p] * source[p]

    def whole(value):
        return jnp.sum(jnp.sum(value, axis=0, keepdims=True), axis=1, keepdims=True)

    shift = whole(rest_total) / whole(edge_total)
    first_row = jnp.clip(gy - 3, 0, ny - 8)
    rows = pl.ds(first_row, 8)
    no_wrap = iota((8, 128), 0) < 7
    planes = []
    for j in range(10):
        x = 2 * gx - 4 + j
        planes.append((jnp.logical_and(x >= 0, x < n2), jnp.clip(x, 0, n2 - 1)))
    level = []
    for ok, q in planes:
        e3 = source[q // 2 + 1, rows] + shift
        level.append([jnp.where(ok, v2[q + 1, s, rows] + e3, 0.0) for s in range(2)])
    for first, last in ((1, 8), (2, 7)):
        done = list(level)
        for j in range(first, last + 1):
            ok, q = planes[j]
            low, high = level[j]
            inner = cyi[q + 1, rows]
            after = jnp.where(no_wrap, cyo[q + 1, rows], 0.0)
            sums = [inner * high + roll(after * high, 1, 0), inner * low + after * roll(low, -1, 0)]
            for s in range(2):
                mid = level[j][s]
                cz = cz2[q + 1, s, rows]
                total = sums[s] + cz * roll(mid, -1, 1) + roll(cz * mid, 1, 1)
                total = total + cx2[q + 1, s, rows] * level[j + 1][s]
                total = total + cx2[q, s, rows] * level[j - 1][s]
                value = KEEP * mid + w2[q + 1, s, rows] * (f2[q + 1, s, rows] + total)
                done[j] = [jnp.where(ok, value, 0.0)] if s == 0 else done[j] + [jnp.where(ok, value, 0.0)]
        level = done
    copies = pair_copy_matrix()
    at = gy - first_row
    steps = (
        (0, at, None),
        (2, jnp.minimum(at + 1, 7), gy < ny - 1),
        (6, jnp.maximum(at - 1, 0), gy > 0),
    )
    for i in range(6):
        small[8 * i + 4 : 8 * i + 6] = jnp.zeros((2, 128), F32)
        for s in range(2):
            e2[i, s] = level[i + 2][s]
            for j, r, ok in steps:
                line = e2[i, s, pl.ds(r, 1)]
                small[8 * i + j + s : 8 * i + j + s + 1] = (
                    line if ok is None else jnp.where(ok, line, 0.0)
                )
    wide[...] = lane_copy(small[...], copies)
    for i in range(6):
        spread = row_copy(narrow, wide[8 * i : 8 * i + 8])
        for p in (2 * i, 2 * i + 1):
            if 1 <= p <= 10:
                e1a[p] = v1[p] + spread
    for source, target, first, last in ((e1a, e1b, 2, 9), (e1b, e1a, 3, 8)):
        for p in range(first, last + 1):
            mid = source[p]
            total = gathered(
                mid, source[p - 1], source[p + 1], cx1[p - 1], cx1[p], cy1[p], cz1[p]
            )
            target[p] = KEEP * mid + w1[p] * (f1[p] + total)
    row8 = iota((8, 256), 0)
    for i in range(6):
        value = e1a[i + 3]
        wide[8 * i : 8 * i + 8] = jnp.where(row8 == 7, value[8:16], value[0:8])
    doubled = lane_copy(wide[...], copies)
    for i in range(6):
        spread = row_copy(narrow, doubled[8 * i : 8 * i + 8])
        for p in (2 * i, 2 * i + 1):
            e0a[p] = v0x[p] + spread
    for p in range(1, 11):
        mid = e0a[p]
        total = gathered(mid, e0a[p - 1], e0a[p + 1], cx0[p], cx0[p + 1], cy0[p], cz0[p])
        e0b[p] = KEEP * mid + w0[p] * (rs[p] + total)
    for p in range(2, 10):
        mid = e0b[p]
        total = gathered(mid, e0b[p - 1], e0b[p + 1], cx0[p], cx0[p + 1], cy0[p], cz0[p])
        out_ref[p - 2] = (KEEP * mid + w0[p] * (rs[p] + total))[0:8]


def run(kernel, outs, scratch, where, *operands, space=VMEM):
    return pl.pallas_call(
        kernel,
        out_shape=[jax.ShapeDtypeStruct(shape, F32) for shape in outs],
        in_specs=[pl.BlockSpec(memory_space=pltpu.SMEM)]
        + [pl.BlockSpec(memory_space=space)] * len(operands),
        out_specs=[pl.BlockSpec(memory_space=VMEM)] * len(outs),
        scratch_shapes=[VMEM(s, F32) if isinstance(s, tuple) else s for s in scratch],
        compiler_params=PARAMS,
    )(where, *operands)


def body(initial, right_side, phase_map, phase_table):
    nx, ny = lax.axis_size("gx"), lax.axis_size("gy")
    where = jnp.stack([lax.axis_index("gx"), lax.axis_index("gy")]).astype(jnp.int32)

    def inner(size):
        return [(i, i ^ 1) for i in range(size)]

    def outer(size):
        ends = (0, size - 1)
        return [(i, i if i in ends else i + 1 if i % 2 else i - 1) for i in range(size)]

    def swap(near, far, axis, size):
        return lax.ppermute(near, axis, inner(size)), lax.ppermute(far, axis, outer(size))

    inputs = [
        pltpu.with_memory_space_constraint(value, pltpu.HBM)
        for value in (phase_table, phase_map, initial, right_side)
    ]
    tile0 = (8, 512)
    ring0 = (16, 512)
    ring1 = (16, 256)
    kappa, init, rhs, near, far, yeven, yodd = run(
        start_kernel, [(8,) + tile0] * 7,
        [pltpu.SMEM((3,), F32), VMEM((8,) + tile0, jnp.int32), pltpu.SemaphoreType.DMA((4,))],
        where, *inputs, space=pltpu.HBM,
    )
    yeven, yodd = swap(yeven, yodd, "gy", ny)
    near, far = swap(near, far, "gx", nx)
    near, far, yeven, yodd = lax.optimization_barrier((near, far, yeven, yodd))
    cnear, cfar = swap(*corner_messages(nx, ny, yeven, yodd), "gx", nx)
    v0, rs, cx0, cy0, cz0, w0, block, mnear, mfar, meven, modd = run(
        functools.partial(down0_kernel, nx, ny),
        [(8,) + tile0, (12,) + ring0, (13,) + ring0]
        + [(12,) + ring0] * 3
        + [(3,) + tile0]
        + [(5,) + tile0] * 4,
        [(14,) + ring0, (14,) + ring0, (12,) + ring0, (12,) + ring0, (4, 16, 128), (64, 512), (64, 256)],
        where, kappa, init, rhs, near, far, yeven, yodd, cnear, cfar,
    )
    meven, modd = swap(meven, modd, "gy", ny)
    mnear, mfar = swap(mnear, mfar, "gx", nx)
    mnear, mfar, meven, modd = lax.optimization_barrier((mnear, mfar, meven, modd))
    corner = corner1_message(ny, meven, modd)
    cnear, cfar = swap(corner, corner, "gx", nx)
    v0x, v1, f1, w1, cx1, cy1, cz1, send = run(
        functools.partial(down1_kernel, nx, ny),
        [(12,) + ring0] + [(12,) + ring1] * 6 + [(nx // 2 * ny, 8, 128)],
        [(12,) + ring1, (12,) + ring1, (4, 16, 128), (8, 256)],
        where, block, v0, mnear, mfar, meven, modd, cnear, cfar,
    )
    groups = [[x * ny + y for x in range(c, nx, 2) for y in range(ny)] for c in range(2)]
    mine = lax.all_to_all(send, ("gx", "gy"), 0, 0, axis_index_groups=groups)
    mine = mine.reshape(nx // 2, ny * 8, 128)
    other = lax.ppermute(mine, "gx", inner(nx))
    n2 = 2 * nx
    pair2 = (n2 + 2, 2, ny, 128)
    one2 = (n2 + 2, ny, 128)
    one3 = (nx + 2, ny, 128)
    (out,) = run(
        functools.partial(up_kernel, nx, ny), [(8,) + tile0],
        [pair2, pair2, pair2, one2, one2, pair2, pair2, pair2, pair2, pair2, (6, 2, 8, 128)]
        + [one3] * 9
        + [(48, 128), (48, 256), (12,) + ring1, (12,) + ring1, (4, 16, 128), (12,) + ring0, (12,) + ring0],
        where, mine, other, v1, f1, w1, cx1, cy1, cz1, v0x, rs, cx0, cy0, cz0, w0,
    )
    return out


def solution(mesh):
    return jax.shard_map(
        body,
        mesh=mesh,
        in_specs=(P("gx", "gy", None), P("gx", "gy", None), P("gx", "gy", None), P()),
        out_specs=P("gx", "gy", None),
        check_vma=False,
    )
```

```python
import functools

import jax
import jax.numpy as jnp
from jax import lax
from jax.experimental import pallas as pl
from jax.experimental.pallas import tpu as pltpu
from jax.sharding import PartitionSpec as P

F32 = jnp.float32
KEEP = 0.2
OMEGA = 0.8
VMEM = pltpu.VMEM
PARAMS = pltpu.CompilerParams(vmem_limit_bytes=48 * 1024 * 1024)


def roll(value, shift, axis):
    return pltpu.roll(value, shift % value.shape[axis], axis)


def iota(shape, dim):
    return lax.broadcasted_iota(jnp.int32, shape, dim)


def pair_sum_matrix():
    return (iota((256, 128), 0) // 2 == iota((256, 128), 1)).astype(F32)


def pair_copy_matrix():
    return (iota((128, 256), 1) // 2 == iota((128, 256), 0)).astype(F32)


def exact_dot(a, b):
    return lax.dot_general(
        a, b, (((1,), (0,)), ((), ())), precision=lax.Precision.HIGHEST, preferred_element_type=F32
    )


def lane_sum(value, matrix):
    width = value.shape[1]
    parts = [exact_dot(value[:, at : at + 256], matrix) for at in range(0, width, 256)]
    return parts[0] if len(parts) == 1 else jnp.concatenate(parts, axis=1)


def lane_copy(value, matrix):
    width = value.shape[1]
    parts = [exact_dot(value[:, at : at + 128], matrix) for at in range(0, width, 128)]
    return parts[0] if len(parts) == 1 else jnp.concatenate(parts, axis=1)


def row_sum(scratch, value):
    rows, width = value.shape
    parts = []
    for c in range(width // 128):
        scratch[c, 0:rows] = value[:, 128 * c : 128 * c + 128]
        first = scratch[c, pl.ds(0, rows // 2, stride=2)]
        parts.append(first + scratch[c, pl.ds(1, rows // 2, stride=2)])
    return parts[0] if len(parts) == 1 else jnp.concatenate(parts, axis=1)


def row_copy(scratch, value):
    rows, width = value.shape
    parts = []
    for c in range(width // 128):
        part = value[:, 128 * c : 128 * c + 128]
        scratch[c, pl.ds(0, rows, stride=2)] = part
        scratch[c, pl.ds(1, rows, stride=2)] = part
        parts.append(scratch[c, 0 : 2 * rows])
    return parts[0] if len(parts) == 1 else jnp.concatenate(parts, axis=1)


def gathered(mid, low, high, cx_low, cx, cy, cz):
    total = cx * high + cx_low * low
    total = total + cy * roll(mid, -1, 0) + roll(cy * mid, 1, 0)
    return total + cz * roll(mid, -1, 1) + roll(cz * mid, 1, 1)


def z_neighbours(mid):
    lane = iota(mid.shape, 1)
    last = mid.shape[1] - 1
    up = jnp.where(lane == last, 0.0, roll(mid, -1, 1))
    down = jnp.where(lane == 0, 0.0, roll(mid, 1, 1))
    return up, down


def diagonal(mid, low, high):
    up, down = z_neighbours(mid)
    total = low + high + roll(mid, -1, 0) + roll(mid, 1, 0) + up + down
    return 3.0 * mid + 0.5 * total


def coupling_y(mid):
    return 0.5 * (mid + roll(mid, -1, 0))


def coupling_z(mid):
    lane = iota(mid.shape, 1)
    return jnp.where(lane == mid.shape[1] - 1, 0.0, 0.5 * (mid + roll(mid, -1, 1)))


def edge_flags(at, grid):
    even = at % 2 == 0
    outside = jnp.logical_or(at == 0, at == grid - 1)
    return even, outside


def start_kernel(
    where_ref, table_hbm, phase_hbm, init_hbm, rhs_hbm,
    kap_ref, init_ref, rhs_ref, near_ref, far_ref, yeven_ref, yodd_ref,
    table_ref, phase_ref, sems,
):
    copies = [
        pltpu.make_async_copy(source, target, sems.at[i])
        for i, (source, target) in enumerate(
            ((table_hbm, table_ref), (phase_hbm, phase_ref), (init_hbm, init_ref), (rhs_hbm, rhs_ref))
        )
    ]
    for copy in copies:
        copy.start()
    for copy in copies:
        copy.wait()
    even = where_ref[0] % 2 == 0
    for x in range(8):
        phase = phase_ref[x]
        kap_ref[x] = jnp.where(
            phase == 0, table_ref[0], jnp.where(phase == 1, table_ref[1], table_ref[2])
        )
    for ref, side in ((near_ref, even), (far_ref, jnp.logical_not(even))):
        deep = jnp.where(side, 5, 0)
        shallow = jnp.where(side, 6, 0)
        for i in range(3):
            ref[i] = kap_ref[deep + i]
            ref[3 + i] = init_ref[deep + i]
        for i in range(2):
            ref[6 + i] = rhs_ref[shallow + i]

    def write(low_ref, high_ref):
        for x in range(8):
            low_ref[x, 0:3] = kap_ref[x, 0:3]
            low_ref[x, 3:6] = init_ref[x, 0:3]
            low_ref[x, 6:8] = rhs_ref[x, 0:2]
            high_ref[x, 0:3] = kap_ref[x, 5:8]
            high_ref[x, 3:6] = init_ref[x, 5:8]
            high_ref[x, 6:8] = rhs_ref[x, 6:8]

    by_parity(where_ref, yeven_ref, yodd_ref, write)


def by_parity(where_ref, even_ref, odd_ref, write):
    even = where_ref[1] % 2 == 0

    @pl.when(even)
    def _():
        write(odd_ref, even_ref)

    @pl.when(jnp.logical_not(even))
    def _():
        write(even_ref, odd_ref)


def place_x(where_ref, grid, own_ref, near_ref, far_ref, first, depth, out_ref, count=8):
    even, outside = edge_flags(where_ref[0], grid)
    near_at = jnp.where(even, depth + count, 0)
    far_at = jnp.where(even, 0, depth + count)
    for x in range(count):
        out_ref[depth + x, 0:8] = own_ref[x]
    for i in range(depth):
        out_ref[near_at + i, 0:8] = near_ref[first + i]
        out_ref[far_at + i, 0:8] = jnp.where(outside, 0.0, far_ref[first + i])


def y_tiles(where_ref, grid, even_ref, odd_ref, p):
    even, outside = edge_flags(where_ref[1], grid)
    inner = even_ref[p]
    outer = jnp.where(outside, 0.0, odd_ref[p])
    return jnp.where(even, inner, outer), jnp.where(even, outer, inner)


def corner_messages(nx, ny, yeven, yodd):
    even = lax.axis_index("gx") % 2 == 0
    high, low = both_tiles(ny, yeven, yodd)
    top = jnp.concatenate([high[7:8], high[6:7], low[7:8], low[6:7]], axis=0)
    bottom = jnp.concatenate([high[0:2], low[0:2]], axis=0)
    return jnp.where(even, top, bottom), jnp.where(even, bottom, top)


def both_tiles(ny, yeven, yodd):
    at = lax.axis_index("gy")
    even, outside = edge_flags(at, ny)
    outer = jnp.where(outside, 0.0, yodd)
    return jnp.where(even, yeven, outer), jnp.where(even, outer, yeven)


def down0_kernel(
    nx, ny, where_ref, kap_ref, init_ref, rhs_ref, near_ref, far_ref, even_ref, odd_ref,
    cnear_ref, cfar_ref,
    v0_ref, rs, cx, cy, cz, wi, block_ref, mnear_ref, mfar_ref, meven_ref, modd_ref,
    ks, vs, v1, v2, pair, fine, coarse,
):
    zero = jnp.zeros((8, 512), F32)
    for p in range(14):
        ks[p, 8:16] = zero
        vs[p, 8:16] = zero
    for p in range(12):
        rs[p, 8:16] = zero
    place_x(where_ref, nx, kap_ref, near_ref, far_ref, 0, 3, ks)
    place_x(where_ref, nx, init_ref, near_ref, far_ref, 3, 3, vs)
    place_x(where_ref, nx, rhs_ref, near_ref, far_ref, 6, 2, rs)

    def place(p, high, low):
        ks[p + 1, 8:11] = high[0:3]
        ks[p + 1, 13:16] = low[0:3]
        vs[p + 1, 8:11] = high[3:6]
        vs[p + 1, 13:16] = low[3:6]
        rs[p, 8:10] = high[6:8]
        rs[p, 14:16] = low[6:8]

    for x in range(8):
        place(x + 2, *y_tiles(where_ref, ny, even_ref, odd_ref, x))
    even, outside = edge_flags(where_ref[0], nx)
    for i in range(2):
        place(jnp.where(even, 10 + i, 1 - i), cnear_ref[i], cnear_ref[2 + i])
        place(
            jnp.where(even, 1 - i, 10 + i),
            jnp.where(outside, 0.0, cfar_ref[i]),
            jnp.where(outside, 0.0, cfar_ref[2 + i]),
        )
    cx[0] = 0.5 * (ks[0] + ks[1])
    for p in range(12):
        mid = ks[p + 1]
        cx[p + 1] = 0.5 * (mid + ks[p + 2])
        cy[p] = coupling_y(mid)
        cz[p] = coupling_z(mid)
        diag = diagonal(mid, ks[p], ks[p + 2])
        wi[p] = jnp.where(mid > 0.0, OMEGA / jnp.where(mid > 0.0, diag, 1.0), 0.0)
    for p in range(12):
        mid = vs[p + 1]
        total = gathered(mid, vs[p], vs[p + 2], cx[p], cx[p + 1], cy[p], cz[p])
        v1[p] = KEEP * mid + wi[p] * (rs[p] + total)
    for p in range(1, 11):
        mid = v1[p]
        total = gathered(mid, v1[p - 1], v1[p + 1], cx[p], cx[p + 1], cy[p], cz[p])
        v2[p] = KEEP * mid + wi[p] * (rs[p] + total)
    for p in range(2, 10, 2):
        both = None
        for q in (p, p + 1):
            mid = v2[q]
            total = gathered(mid, v2[q - 1], v2[q + 1], cx[q], cx[q + 1], cy[q], cz[q])
            diag = diagonal(ks[q + 1], ks[q], ks[q + 2])
            rest = (rs[q] + total - diag * mid)[0:8]
            both = rest if both is None else both + rest
            v0_ref[q - 2] = mid[0:8]
        at = 4 * (p // 2 - 1)
        fine[at : at + 4] = row_sum(pair, both)
    for p in range(0, 12, 2):
        at = 16 + 4 * p
        fine[at : at + 8] = row_sum(pair, ks[p + 1] + ks[p + 2])
    coarse[...] = lane_sum(fine[...], pair_sum_matrix())
    for x in range(4):
        half = pl.ds(256 * (x % 2), 256)
        mid = 0.125 * coarse[24 + 8 * x : 32 + 8 * x]
        low = 0.125 * coarse[16 + 8 * x : 24 + 8 * x]
        high = 0.125 * coarse[32 + 8 * x : 40 + 8 * x]
        block_ref[x // 2, 0:4, half] = 0.5 * coarse[4 * x : 4 * x + 4]
        block_ref[x // 2, 4:8, half] = mid[0:4]
        at = 4 * (x // 2)
        block_ref[2, at : at + 4, half] = (OMEGA / diagonal(mid, low, high)[0:4])
    for ref, side in ((mnear_ref, even), (mfar_ref, jnp.logical_not(even))):
        shallow = jnp.where(side, 6, 0)
        for i in range(3):
            ref[i] = block_ref[i]
        for i in range(2):
            ref[3 + i] = v0_ref[shallow + i]

    def write(low_ref, high_ref):
        for i in range(3):
            low_ref[i] = block_ref[i]
            high_ref[i] = block_ref[i]
        for x in range(8):
            at = 2 * (x % 4)
            low_ref[3 + x // 4, at : at + 2] = v0_ref[x, 0:2]
            high_ref[3 + x // 4, at : at + 2] = v0_ref[x, 6:8]

    by_parity(where_ref, meven_ref, modd_ref, write)


def corner1_message(ny, meven, modd):
    high, low = both_tiles(ny, meven, modd)
    rows = [high[4:5, 6:8], low[4:5, 6:8], high[3:4, 0:2], low[3:4, 0:2]]
    return jnp.concatenate([high[0:3], low[0:3], jnp.concatenate(rows, axis=1)], axis=0)


def down1_kernel(
    nx, ny, where_ref, block_ref, v0_ref, near_ref, far_ref, meven_ref, modd_ref,
    cnear_ref, cfar_ref,
    v0x, v1, f1, w1, cx, cy, cz, send_ref,
    k1, u1, pair, fine,
):
    even, outside = edge_flags(where_ref[0], nx)

    def inside(value):
        return jnp.where(outside, 0.0, value)

    near = [near_ref[i] for i in range(3)]
    far = [inside(far_ref[i]) for i in range(3)]
    cnear = [cnear_ref[i] for i in range(7)]
    cfar = [inside(cfar_ref[i]) for i in range(7)]
    mine = [y_tiles(where_ref, ny, meven_ref, modd_ref, i) for i in range(5)]

    def pick(a, b):
        return [jnp.where(even, p, q) for p, q in zip(a, b)]

    blocks = (
        (pick(far, near), pick(cfar[0:3], cnear[0:3]), pick(cfar[3:6], cnear[3:6])),
        ([block_ref[i] for i in range(3)], [t[0] for t in mine], [t[1] for t in mine]),
        (pick(near, far), pick(cnear[0:3], cfar[0:3]), pick(cnear[3:6], cfar[3:6])),
    )
    zero = jnp.zeros((4, 256), F32)
    for b in range(3):
        for x in range(4):
            p = 4 * b + x
            half = slice(256 * (x % 2), 256 * (x % 2) + 256)
            t = x // 2
            for ref, at, row in (
                (f1, t, slice(0, 4)), (k1, t, slice(4, 8)), (w1, 2, slice(4 * t, 4 * t + 4))
            ):
                ref[p, 0:4] = blocks[b][0][at][row, half]
                ref[p, 4:8] = blocks[b][1][at][row, half]
                ref[p, 8:12] = zero
                ref[p, 12:16] = blocks[b][2][at][row, half]
    blank = jnp.zeros((8, 512), F32)
    for p in range(12):
        v0x[p, 8:16] = blank
    for x in range(8):
        v0x[2 + x, 0:8] = v0_ref[x]
        at = 2 * (x % 4)
        v0x[2 + x, 8:10] = mine[3 + x // 4][0][at : at + 2]
        v0x[2 + x, 14:16] = mine[3 + x // 4][1][at : at + 2]
    near_at = jnp.where(even, 10, 0)
    far_at = jnp.where(even, 0, 10)
    for i in range(2):
        v0x[near_at + i, 0:8] = near_ref[3 + i]
        v0x[far_at + i, 0:8] = inside(far_ref[3 + i])
    low_tile = jnp.where(even, cfar[6], cnear[6])
    high_tile = jnp.where(even, cnear[6], cfar[6])
    for at, tile, row in ((1, low_tile, 0), (10, high_tile, 4)):
        v0x[at, 8:10] = tile[row : row + 2]
        v0x[at, 14:16] = tile[row + 2 : row + 4]
    for p in range(12):
        u1[p] = w1[p] * f1[p]
        if p < 11:
            cx[p] = 0.5 * (k1[p] + k1[p + 1])
        cy[p] = coupling_y(k1[p])
        cz[p] = coupling_z(k1[p])
    for p in range(1, 11):
        mid = u1[p]
        total = gathered(mid, u1[p - 1], u1[p + 1], cx[p - 1], cx[p], cy[p], cz[p])
        v1[p] = KEEP * mid + w1[p] * (f1[p] + total)
    for p in range(4, 8, 2):
        both = None
        for q in (p, p + 1):
            mid = v1[q]
            total = gathered(mid, v1[q - 1], v1[q + 1], cx[q - 1], cx[q], cy[q], cz[q])
            diag = diagonal(k1[q], k1[q - 1], k1[q + 1])
            rest = (f1[q] + total - diag * mid)[0:8]
            both = rest if both is None else both + rest
        at = p - 4
        fine[at : at + 2] = 0.5 * row_sum(pair, both)[0:2]
        kept = k1[p, 0:8] + k1[p + 1, 0:8]
        fine[4 + at : 6 + at] = 0.125 * row_sum(pair, kept)[0:2]
    tile = lane_sum(fine[...], pair_sum_matrix())
    for i in range(send_ref.shape[0]):
        send_ref[i] = tile


def up_kernel(
    nx, ny, where_ref, mine_ref, other_ref, v1, f1, w1, cx1, cy1, cz1,
    v0x, rs, cx0, cy0, cz0, w0, out_ref,
    f2, k2, cx2, cyi, cyo, cz2, w2, d2, u2, v2, e2, f3, k3, cx3, cy3, cz3, w3, edge3, ga, gb,
    small, wide, e1a, e1b, narrow, e0a, e0b,
):
    gx = where_ref[0]
    gy = where_ref[1]
    core = gx % 2
    n2 = 2 * nx
    zero = jnp.zeros((ny, 128), F32)
    row = iota((ny, 128), 0)
    lane = iota((ny, 128), 1)
    last_row = row == ny - 1
    for s in range(2):
        k2[0, s] = zero
        k2[n2 + 1, s] = zero
        u2[0, s] = zero
        u2[n2 + 1, s] = zero
        v2[0, s] = zero
        v2[n2 + 1, s] = zero
    for x in range(nx // 2):
        for ref, which in ((mine_ref, core), (other_ref, 1 - core)):
            for i in range(2):
                p = 4 * x + 2 * which + i + 1
                for s in range(2):
                    f2[p, s] = ref[x, pl.ds(2 * i + s, ny, stride=8)]
                    k2[p, s] = ref[x, pl.ds(4 + 2 * i + s, ny, stride=8)]
    for p in range(n2 + 1):
        for s in range(2):
            cx2[p, s] = 0.5 * (k2[p, s] + k2[p + 1, s])
    for p in range(1, n2 + 1):
        k_low, k_high = k2[p, 0], k2[p, 1]
        after = jnp.where(last_row, 0.0, roll(k_low, -1, 0))
        before = jnp.where(row == 0, 0.0, roll(k_high, 1, 0))
        cyi[p] = 0.5 * (k_low + k_high)
        cyo[p] = jnp.where(last_row, 0.0, 0.5 * (k_high + after))
        for s, mid, ya, yb in ((0, k_low, k_high, before), (1, k_high, k_low, after)):
            up, down = z_neighbours(mid)
            cz2[p, s] = jnp.where(lane == 127, 0.0, 0.5 * (mid + up))
            diag = 3.0 * mid + 0.5 * (k2[p - 1, s] + k2[p + 1, s] + ya + yb + up + down)
            scale = OMEGA / diag
            d2[p, s] = diag
            w2[p, s] = scale
            u2[p, s] = scale * f2[p, s]

    def gather2(ref, p):
        low, high = ref[p, 0], ref[p, 1]
        sums = []
        for s, mid in ((0, low), (1, high)):
            total = cx2[p, s] * ref[p + 1, s] + cx2[p - 1, s] * ref[p - 1, s]
            total = total + cz2[p, s] * roll(mid, -1, 1) + roll(cz2[p, s] * mid, 1, 1)
            sums.append(total)
        sums[0] = sums[0] + cyi[p] * high + roll(cyo[p] * high, 1, 0)
        sums[1] = sums[1] + cyi[p] * low + cyo[p] * roll(low, -1, 0)
        return (low, high), sums

    def sweep2(source, target):
        for p in range(1, n2 + 1):
            mids, sums = gather2(source, p)
            for s in range(2):
                target[p, s] = KEEP * mids[s] + w2[p, s] * (f2[p, s] + sums[s])

    sweep2(u2, v2)
    even_lane = lane % 2 == 0

    def pair_lanes(value):
        return value + jnp.where(even_lane, roll(value, -1, 1), roll(value, 1, 1))

    k3[0] = zero
    k3[nx + 1] = zero
    ga[0] = zero
    ga[nx + 1] = zero
    gb[0] = zero
    gb[nx + 1] = zero
    for x in range(nx):
        both = None
        kept = None
        for p in (2 * x + 1, 2 * x + 2):
            mids, sums = gather2(v2, p)
            for s in range(2):
                rest = f2[p, s] + sums[s] - d2[p, s] * mids[s]
                both = rest if both is None else both + rest
                kept = k2[p, s] if kept is None else kept + k2[p, s]
        f3[x + 1] = 0.5 * pair_lanes(both)
        k3[x + 1] = 0.125 * pair_lanes(kept)
    for p in range(nx + 1):
        cx3[p] = 0.5 * (k3[p] + k3[p + 1])
    edge_total = zero
    rest_total = zero
    outer = (
        (row == 0).astype(F32) + last_row.astype(F32)
        + (lane < 2).astype(F32) + (lane >= 126).astype(F32)
    )
    for p in range(1, nx + 1):
        mid = k3[p]
        after = jnp.where(last_row, 0.0, roll(mid, -1, 0))
        before = jnp.where(row == 0, 0.0, roll(mid, 1, 0))
        up = jnp.where(lane >= 126, 0.0, roll(mid, -2, 1))
        down = jnp.where(lane < 2, 0.0, roll(mid, 2, 1))
        cy3[p] = jnp.where(last_row, 0.0, 0.5 * (mid + after))
        cz3[p] = jnp.where(lane >= 126, 0.0, 0.5 * (mid + up))
        diag = 3.0 * mid + 0.5 * (k3[p - 1] + k3[p + 1] + after + before + up + down)
        scale = OMEGA / diag
        w3[p] = scale
        ga[p] = scale * f3[p]
        faces = outer + (1.0 if p == 1 else 0.0) + (1.0 if p == nx else 0.0)
        edge = 0.5 * mid * faces
        edge3[p] = edge
        edge_total = edge_total + edge
        rest_total = rest_total + f3[p]

    def gather3(ref, p):
        mid = ref[p]
        total = cx3[p] * ref[p + 1] + cx3[p - 1] * ref[p - 1]
        total = total + cy3[p] * roll(mid, -1, 0) + roll(cy3[p] * mid, 1, 0)
        return mid, total + cz3[p] * roll(mid, -2, 1) + roll(cz3[p] * mid, 2, 1)

    source, target = ga, gb
    for _ in range(7):
        for p in range(1, nx + 1):
            mid, total = gather3(source, p)
            target[p] = KEEP * mid + w3[p] * (f3[p] + total)
        source, target = target, source
    for p in range(1, nx + 1):
        rest_total = rest_total - edge3[p] * source[p]

    def whole(value):
        return jnp.sum(jnp.sum(value, axis=0, keepdims=True), axis=1, keepdims=True)

    shift = whole(rest_total) / whole(edge_total)
    first_row = jnp.clip(gy - 3, 0, ny - 8)
    rows = pl.ds(first_row, 8)
    no_wrap = iota((8, 128), 0) < 7
    planes = []
    for j in range(10):
        x = 2 * gx - 4 + j
        planes.append((jnp.logical_and(x >= 0, x < n2), jnp.clip(x, 0, n2 - 1)))
    level = []
    for ok, q in planes:
        e3 = source[q // 2 + 1, rows] + shift
        level.append([jnp.where(ok, v2[q + 1, s, rows] + e3, 0.0) for s in range(2)])
    for first, last in ((1, 8), (2, 7)):
        done = list(level)
        for j in range(first, last + 1):
            ok, q = planes[j]
            low, high = level[j]
            inner = cyi[q + 1, rows]
            after = jnp.where(no_wrap, cyo[q + 1, rows], 0.0)
            sums = [inner * high + roll(after * high, 1, 0), inner * low + after * roll(low, -1, 0)]
            for s in range(2):
                mid = level[j][s]
                cz = cz2[q + 1, s, rows]
                total = sums[s] + cz * roll(mid, -1, 1) + roll(cz * mid, 1, 1)
                total = total + cx2[q + 1, s, rows] * level[j + 1][s]
                total = total + cx2[q, s, rows] * level[j - 1][s]
                value = KEEP * mid + w2[q + 1, s, rows] * (f2[q + 1, s, rows] + total)
                done[j] = [jnp.where(ok, value, 0.0)] if s == 0 else done[j] + [jnp.where(ok, value, 0.0)]
        level = done
    copies = pair_copy_matrix()
    at = gy - first_row
    steps = (
        (0, at, None),
        (2, jnp.minimum(at + 1, 7), gy < ny - 1),
        (6, jnp.maximum(at - 1, 0), gy > 0),
    )
    for i in range(6):
        small[8 * i + 4 : 8 * i + 6] = jnp.zeros((2, 128), F32)
        for s in range(2):
            e2[i, s] = level[i + 2][s]
            for j, r, ok in steps:
                line = e2[i, s, pl.ds(r, 1)]
                small[8 * i + j + s : 8 * i + j + s + 1] = (
                    line if ok is None else jnp.where(ok, line, 0.0)
                )
    wide[...] = lane_copy(small[...], copies)
    for i in range(6):
        spread = row_copy(narrow, wide[8 * i : 8 * i + 8])
        for p in (2 * i, 2 * i + 1):
            if 1 <= p <= 10:
                e1a[p] = v1[p] + spread
    for source, target, first, last in ((e1a, e1b, 2, 9), (e1b, e1a, 3, 8)):
        for p in range(first, last + 1):
            mid = source[p]
            total = gathered(
                mid, source[p - 1], source[p + 1], cx1[p - 1], cx1[p], cy1[p], cz1[p]
            )
            target[p] = KEEP * mid + w1[p] * (f1[p] + total)
    row8 = iota((8, 256), 0)
    for i in range(6):
        value = e1a[i + 3]
        wide[8 * i : 8 * i + 8] = jnp.where(row8 == 7, value[8:16], value[0:8])
    doubled = lane_copy(wide[...], copies)
    for i in range(6):
        spread = row_copy(narrow, doubled[8 * i : 8 * i + 8])
        for p in (2 * i, 2 * i + 1):
            e0a[p] = v0x[p] + spread
    for p in range(1, 11):
        mid = e0a[p]
        total = gathered(mid, e0a[p - 1], e0a[p + 1], cx0[p], cx0[p + 1], cy0[p], cz0[p])
        e0b[p] = KEEP * mid + w0[p] * (rs[p] + total)
    for p in range(2, 10):
        mid = e0b[p]
        total = gathered(mid, e0b[p - 1], e0b[p + 1], cx0[p], cx0[p + 1], cy0[p], cz0[p])
        out_ref[p - 2] = (KEEP * mid + w0[p] * (rs[p] + total))[0:8]


def run(kernel, outs, scratch, where, *operands, space=VMEM):
    return pl.pallas_call(
        kernel,
        out_shape=[jax.ShapeDtypeStruct(shape, F32) for shape in outs],
        in_specs=[pl.BlockSpec(memory_space=pltpu.SMEM)]
        + [pl.BlockSpec(memory_space=space)] * len(operands),
        out_specs=[pl.BlockSpec(memory_space=VMEM)] * len(outs),
        scratch_shapes=[VMEM(s, F32) if isinstance(s, tuple) else s for s in scratch],
        compiler_params=PARAMS,
    )(where, *operands)


def body(initial, right_side, phase_map, phase_table):
    nx, ny = lax.axis_size("gx"), lax.axis_size("gy")
    where = jnp.stack([lax.axis_index("gx"), lax.axis_index("gy")]).astype(jnp.int32)

    def pairs(partner):
        return [
            (x * ny + y, px * ny + py)
            for x in range(nx)
            for y in range(ny)
            for px, py in [partner(x, y)]
        ]

    def beyond(at, size):
        other = at + 1 if at % 2 else at - 1
        return other if 0 <= other < size else None

    def far_x(x, y):
        other = beyond(x, nx)
        return (x, y ^ 1) if other is None else (other, y)

    def far_y(x, y):
        other = beyond(y, ny)
        return (x ^ 1, y) if other is None else (x, other)

    both = ("gx", "gy")

    def swap_x(near, far):
        return (
            lax.ppermute(near, both, pairs(lambda x, y: (x ^ 1, y))),
            lax.ppermute(far, both, pairs(far_x)),
        )

    def swap_y(near, far):
        return (
            lax.ppermute(near, both, pairs(lambda x, y: (x, y ^ 1))),
            lax.ppermute(far, both, pairs(far_y)),
        )

    inputs = [
        pltpu.with_memory_space_constraint(value, pltpu.HBM)
        for value in (phase_table, phase_map, initial, right_side)
    ]
    tile0 = (8, 512)
    ring0 = (16, 512)
    ring1 = (16, 256)
    kappa, init, rhs, near, far, yeven, yodd = run(
        start_kernel, [(8,) + tile0] * 7,
        [pltpu.SMEM((3,), F32), VMEM((8,) + tile0, jnp.int32), pltpu.SemaphoreType.DMA((4,))],
        where, *inputs, space=pltpu.HBM,
    )
    yeven, yodd = swap_y(yeven, yodd)
    near, far = swap_x(near, far)
    near, far, yeven, yodd = lax.optimization_barrier((near, far, yeven, yodd))
    cnear, cfar = swap_x(*corner_messages(nx, ny, yeven, yodd))
    v0, rs, cx0, cy0, cz0, w0, block, mnear, mfar, meven, modd = run(
        functools.partial(down0_kernel, nx, ny),
        [(8,) + tile0, (12,) + ring0, (13,) + ring0]
        + [(12,) + ring0] * 3
        + [(3,) + tile0]
        + [(5,) + tile0] * 4,
        [(14,) + ring0, (14,) + ring0, (12,) + ring0, (12,) + ring0, (4, 16, 128), (64, 512), (64, 256)],
        where, kappa, init, rhs, near, far, yeven, yodd, cnear, cfar,
    )
    meven, modd = swap_y(meven, modd)
    mnear, mfar = swap_x(mnear, mfar)
    mnear, mfar, meven, modd = lax.optimization_barrier((mnear, mfar, meven, modd))
    corner = corner1_message(ny, meven, modd)
    cnear, cfar = swap_x(corner, corner)
    v0x, v1, f1, w1, cx1, cy1, cz1, send = run(
        functools.partial(down1_kernel, nx, ny),
        [(12,) + ring0] + [(12,) + ring1] * 6 + [(ny, 8, 128)],
        [(12,) + ring1, (12,) + ring1, (4, 16, 128), (8, 256)],
        where, block, v0, mnear, mfar, meven, modd, cnear, cfar,
    )
    column = lax.all_to_all(send, "gy", 0, 0).reshape(1, ny * 8, 128)
    groups = [list(range(0, nx, 2)), list(range(1, nx, 2))]
    mine = lax.all_to_all(
        jnp.broadcast_to(column, (nx // 2, ny * 8, 128)), "gx", 0, 0, axis_index_groups=groups
    )
    other = lax.ppermute(mine, both, pairs(lambda x, y: (x ^ 1, y)))
    n2 = 2 * nx
    pair2 = (n2 + 2, 2, ny, 128)
    one2 = (n2 + 2, ny, 128)
    one3 = (nx + 2, ny, 128)
    (out,) = run(
        functools.partial(up_kernel, nx, ny), [(8,) + tile0],
        [pair2, pair2, pair2, one2, one2, pair2, pair2, pair2, pair2, pair2, (6, 2, 8, 128)]
        + [one3] * 9
        + [(48, 128), (48, 256), (12,) + ring1, (12,) + ring1, (4, 16, 128), (12,) + ring0, (12,) + ring0],
        where, mine, other, v1, f1, w1, cx1, cy1, cz1, v0x, rs, cx0, cy0, cz0, w0,
    )
    return out


def solution(mesh):
    return jax.shard_map(
        body,
        mesh=mesh,
        in_specs=(P("gx", "gy", None), P("gx", "gy", None), P("gx", "gy", None), P()),
        out_specs=P("gx", "gy", None),
        check_vma=False,
    )
```

```python
import functools

import jax
import jax.numpy as jnp
from jax import lax
from jax.experimental import pallas as pl
from jax.experimental.pallas import tpu as pltpu
from jax.sharding import PartitionSpec as P

F32 = jnp.float32
KEEP = 0.2
OMEGA = 0.8
VMEM = pltpu.VMEM
PARAMS = pltpu.CompilerParams(vmem_limit_bytes=48 * 1024 * 1024)


def roll(value, shift, axis):
    return pltpu.roll(value, shift % value.shape[axis], axis)


def iota(shape, dim):
    return lax.broadcasted_iota(jnp.int32, shape, dim)


def pair_sum_matrix():
    return (iota((256, 128), 0) // 2 == iota((256, 128), 1)).astype(F32)


def pair_copy_matrix():
    return (iota((128, 256), 1) // 2 == iota((128, 256), 0)).astype(F32)


def exact_dot(a, b):
    return lax.dot_general(
        a, b, (((1,), (0,)), ((), ())), precision=lax.Precision.HIGHEST, preferred_element_type=F32
    )


def lane_sum(value, matrix):
    width = value.shape[1]
    parts = [exact_dot(value[:, at : at + 256], matrix) for at in range(0, width, 256)]
    return parts[0] if len(parts) == 1 else jnp.concatenate(parts, axis=1)


def lane_copy(value, matrix):
    width = value.shape[1]
    parts = [exact_dot(value[:, at : at + 128], matrix) for at in range(0, width, 128)]
    return parts[0] if len(parts) == 1 else jnp.concatenate(parts, axis=1)


def row_sum(scratch, value):
    rows, width = value.shape
    parts = []
    for c in range(width // 128):
        scratch[c, 0:rows] = value[:, 128 * c : 128 * c + 128]
        first = scratch[c, pl.ds(0, rows // 2, stride=2)]
        parts.append(first + scratch[c, pl.ds(1, rows // 2, stride=2)])
    return parts[0] if len(parts) == 1 else jnp.concatenate(parts, axis=1)


def row_copy(scratch, value):
    rows, width = value.shape
    parts = []
    for c in range(width // 128):
        part = value[:, 128 * c : 128 * c + 128]
        scratch[c, pl.ds(0, rows, stride=2)] = part
        scratch[c, pl.ds(1, rows, stride=2)] = part
        parts.append(scratch[c, 0 : 2 * rows])
    return parts[0] if len(parts) == 1 else jnp.concatenate(parts, axis=1)


def gathered(mid, low, high, cx_low, cx, cy, cz):
    total = cx * high + cx_low * low
    total = total + cy * roll(mid, -1, 0) + roll(cy * mid, 1, 0)
    return total + cz * roll(mid, -1, 1) + roll(cz * mid, 1, 1)


def z_neighbours(mid):
    lane = iota(mid.shape, 1)
    last = mid.shape[1] - 1
    up = jnp.where(lane == last, 0.0, roll(mid, -1, 1))
    down = jnp.where(lane == 0, 0.0, roll(mid, 1, 1))
    return up, down


def diagonal(mid, low, high):
    up, down = z_neighbours(mid)
    total = low + high + roll(mid, -1, 0) + roll(mid, 1, 0) + up + down
    return 3.0 * mid + 0.5 * total


def coupling_y(mid):
    return 0.5 * (mid + roll(mid, -1, 0))


def coupling_z(mid):
    lane = iota(mid.shape, 1)
    return jnp.where(lane == mid.shape[1] - 1, 0.0, 0.5 * (mid + roll(mid, -1, 1)))


def edge_flags(at, grid):
    even = at % 2 == 0
    outside = jnp.logical_or(at == 0, at == grid - 1)
    return even, outside


def start_kernel(
    where_ref, table_hbm, phase_hbm, init_hbm, rhs_hbm,
    kap_ref, init_ref, rhs_ref, near_ref, far_ref, yeven_ref, yodd_ref,
    table_ref, phase_ref, sems,
):
    copies = [
        pltpu.make_async_copy(source, target, sems.at[i])
        for i, (source, target) in enumerate(
            ((table_hbm, table_ref), (phase_hbm, phase_ref), (init_hbm, init_ref), (rhs_hbm, rhs_ref))
        )
    ]
    for copy in copies:
        copy.start()
    for copy in copies:
        copy.wait()
    even = where_ref[0] % 2 == 0
    for x in range(8):
        phase = phase_ref[x]
        kap_ref[x] = jnp.where(
            phase == 0, table_ref[0], jnp.where(phase == 1, table_ref[1], table_ref[2])
        )
    for ref, side in ((near_ref, even), (far_ref, jnp.logical_not(even))):
        deep = jnp.where(side, 5, 0)
        shallow = jnp.where(side, 6, 0)
        for i in range(3):
            ref[i] = kap_ref[deep + i]
            ref[3 + i] = init_ref[deep + i]
        for i in range(2):
            ref[6 + i] = rhs_ref[shallow + i]

    def write(low_ref, high_ref):
        for x in range(8):
            low_ref[x, 0:3] = kap_ref[x, 0:3]
            low_ref[x, 3:6] = init_ref[x, 0:3]
            low_ref[x, 6:8] = rhs_ref[x, 0:2]
            high_ref[x, 0:3] = kap_ref[x, 5:8]
            high_ref[x, 3:6] = init_ref[x, 5:8]
            high_ref[x, 6:8] = rhs_ref[x, 6:8]

    by_parity(where_ref, yeven_ref, yodd_ref, write)


def by_parity(where_ref, even_ref, odd_ref, write):
    even = where_ref[1] % 2 == 0

    @pl.when(even)
    def _():
        write(odd_ref, even_ref)

    @pl.when(jnp.logical_not(even))
    def _():
        write(even_ref, odd_ref)


def y_tiles(where_ref, grid, even_ref, odd_ref, p):
    even, outside = edge_flags(where_ref[1], grid)
    inner = even_ref[p]
    outer = jnp.where(outside, 0.0, odd_ref[p])
    return jnp.where(even, inner, outer), jnp.where(even, outer, inner)


def corner_messages(nx, ny, yeven, yodd):
    even = lax.axis_index("gx") % 2 == 0
    high, low = both_tiles(ny, yeven, yodd)
    top = jnp.concatenate([high[7:8], high[6:7], low[7:8], low[6:7]], axis=0)
    bottom = jnp.concatenate([high[0:2], low[0:2]], axis=0)
    return jnp.where(even, top, bottom), jnp.where(even, bottom, top)


def both_tiles(ny, yeven, yodd):
    at = lax.axis_index("gy")
    even, outside = edge_flags(at, ny)
    outer = jnp.where(outside, 0.0, yodd)
    return jnp.where(even, yeven, outer), jnp.where(even, outer, yeven)


class Planes:
    def __init__(self, middle, outer, first, count):
        self.middle, self.outer, self.first, self.count = middle, outer, first, count

    def find(self, p):
        if p < self.first:
            return self.outer, p
        if p < self.first + self.count:
            return self.middle, p - self.first
        return self.outer, p - self.count

    def __getitem__(self, p):
        ref, at = self.find(p)
        return ref[at]

    def __setitem__(self, p, value):
        ref, at = self.find(p)
        ref[at] = value


def setup0(ks, cx, cy, cz, wi, planes, faces):
    for p in faces:
        cx[p] = 0.5 * (ks[p] + ks[p + 1])
    for p in planes:
        mid = ks[p]
        cy[p] = coupling_y(mid)
        cz[p] = coupling_z(mid)
        diag = diagonal(mid, ks[p - 1], ks[p + 1])
        wi[p] = jnp.where(mid > 0.0, OMEGA / jnp.where(mid > 0.0, diag, 1.0), 0.0)


def sweep0(source, target, rs, cx, cy, cz, wi, planes):
    for p in planes:
        mid = source[p]
        total = gathered(mid, source[p - 1], source[p + 1], cx[p - 1], cx[p], cy[p], cz[p])
        target[p] = KEEP * mid + wi[p] * (rs[p] + total)


def rest0(v2, rs, ks, cx, cy, cz, p):
    mid = v2[p]
    total = gathered(mid, v2[p - 1], v2[p + 1], cx[p - 1], cx[p], cy[p], cz[p])
    diag = diagonal(ks[p], ks[p - 1], ks[p + 1])
    return (rs[p] + total - diag * mid)[0:8]


def add_y_halo(ks, vs, rs, p, high, low):
    zero = jnp.zeros((8, 512), F32)
    ks[p, 8:16] = zero
    vs[p, 8:16] = zero
    rs[p, 8:16] = zero
    ks[p, 8:11] = high[0:3]
    ks[p, 13:16] = low[0:3]
    vs[p, 8:11] = high[3:6]
    vs[p, 13:16] = low[3:6]
    rs[p, 8:10] = high[6:8]
    rs[p, 14:16] = low[6:8]


def early0_kernel(
    ny, where_ref, kap_ref, init_ref, rhs_ref, even_ref, odd_ref,
    ks, vs, rs, cx, cy, cz, wi, v1, v2, rest,
):
    for x in range(8):
        ks[x, 0:8] = kap_ref[x]
        vs[x, 0:8] = init_ref[x]
        rs[x, 0:8] = rhs_ref[x]
        add_y_halo(ks, vs, rs, x, *y_tiles(where_ref, ny, even_ref, odd_ref, x))
    ks, vs, rs = (Planes(ref, None, 3, 8) for ref in (ks, vs, rs))
    cx = Planes(cx, None, 3, 7)
    cy, cz, wi, v1 = (Planes(ref, None, 4, 6) for ref in (cy, cz, wi, v1))
    v2 = Planes(v2, None, 5, 4)
    setup0(ks, cx, cy, cz, wi, range(4, 10), range(3, 10))
    sweep0(vs, v1, rs, cx, cy, cz, wi, range(4, 10))
    sweep0(v1, v2, rs, cx, cy, cz, wi, range(5, 9))
    for p in (6, 7):
        rest[p - 6] = rest0(v2, rs, ks, cx, cy, cz, p)


def down0_kernel(
    nx, ny, where_ref, near_ref, far_ref, cnear_ref, cfar_ref,
    ks_own, vs_own, rs_own, cx_own, cy_own, cz_own, wi_own, v1_own, v2_own, rest_own,
    v0_ref, rs, cx, cy, cz, wi, block_ref, mnear_ref, mfar_ref, meven_ref, modd_ref,
    ks, vs, v1, v2, pair, fine, coarse,
):
    even, outside = edge_flags(where_ref[0], nx)
    for i in range(3):
        near_at = jnp.where(even, 3 + i, i)
        far_at = jnp.where(even, i, 3 + i)
        for ref, first in ((ks, 0), (vs, 3)):
            ref[near_at, 0:8] = near_ref[first + i]
            ref[far_at, 0:8] = jnp.where(outside, 0.0, far_ref[first + i])
    for i in range(2):
        rs[jnp.where(even, 3 + i, 1 + i), 0:8] = near_ref[6 + i]
        rs[jnp.where(even, 1 + i, 3 + i), 0:8] = jnp.where(outside, 0.0, far_ref[6 + i])
    zero = jnp.zeros((8, 512), F32)
    for p in (0, 5):
        ks[p, 8:16] = zero
        vs[p, 8:16] = zero
        rs[p, 8:16] = zero
    rs[0, 0:8] = zero
    rs[5, 0:8] = zero
    for i in range(2):
        add_y_halo(ks, vs, rs, jnp.where(even, 3 + i, 2 - i), cnear_ref[i], cnear_ref[2 + i])
        add_y_halo(
            ks, vs, rs, jnp.where(even, 2 - i, 3 + i),
            jnp.where(outside, 0.0, cfar_ref[i]), jnp.where(outside, 0.0, cfar_ref[2 + i]),
        )
    ks, vs, rs = (Planes(a, b, 3, 8) for a, b in ((ks_own, ks), (vs_own, vs), (rs_own, rs)))
    cx = Planes(cx_own, cx, 3, 7)
    cy, cz, wi, v1 = (
        Planes(a, b, 4, 6) for a, b in ((cy_own, cy), (cz_own, cz), (wi_own, wi), (v1_own, v1))
    )
    v2 = Planes(v2_own, v2, 5, 4)
    setup0(ks, cx, cy, cz, wi, (1, 2, 3, 10, 11, 12), (0, 1, 2, 10, 11, 12))
    sweep0(vs, v1, rs, cx, cy, cz, wi, (1, 2, 3, 10, 11, 12))
    sweep0(v1, v2, rs, cx, cy, cz, wi, (2, 3, 4, 9, 10, 11))
    for p in range(3, 11, 2):
        both = None
        for q in (p, p + 1):
            rest = rest_own[q - 6] if q in (6, 7) else rest0(v2, rs, ks, cx, cy, cz, q)
            both = rest if both is None else both + rest
            v0_ref[q - 3] = v2[q][0:8]
        at = 2 * (p - 3)
        fine[at : at + 4] = row_sum(pair, both)
    for p in range(1, 13, 2):
        at = 12 + 4 * p
        fine[at : at + 8] = row_sum(pair, ks[p] + ks[p + 1])
    coarse[...] = lane_sum(fine[...], pair_sum_matrix())
    for x in range(4):
        half = pl.ds(256 * (x % 2), 256)
        mid = 0.125 * coarse[24 + 8 * x : 32 + 8 * x]
        low = 0.125 * coarse[16 + 8 * x : 24 + 8 * x]
        high = 0.125 * coarse[32 + 8 * x : 40 + 8 * x]
        block_ref[x // 2, 0:4, half] = 0.5 * coarse[4 * x : 4 * x + 4]
        block_ref[x // 2, 4:8, half] = mid[0:4]
        at = 4 * (x // 2)
        block_ref[2, at : at + 4, half] = (OMEGA / diagonal(mid, low, high)[0:4])
    for ref, side in ((mnear_ref, even), (mfar_ref, jnp.logical_not(even))):
        shallow = jnp.where(side, 6, 0)
        for i in range(3):
            ref[i] = block_ref[i]
        for i in range(2):
            ref[3 + i] = v0_ref[shallow + i]

    def write(low_ref, high_ref):
        for i in range(3):
            low_ref[i] = block_ref[i]
            high_ref[i] = block_ref[i]
        for x in range(8):
            at = 2 * (x % 4)
            low_ref[3 + x // 4, at : at + 2] = v0_ref[x, 0:2]
            high_ref[3 + x // 4, at : at + 2] = v0_ref[x, 6:8]

    by_parity(where_ref, meven_ref, modd_ref, write)


def corner1_message(ny, meven, modd):
    high, low = both_tiles(ny, meven, modd)
    rows = [high[4:5, 6:8], low[4:5, 6:8], high[3:4, 0:2], low[3:4, 0:2]]
    return jnp.concatenate([high[0:3], low[0:3], jnp.concatenate(rows, axis=1)], axis=0)


def down1_kernel(
    nx, ny, where_ref, block_ref, v0_ref, near_ref, far_ref, meven_ref, modd_ref,
    cnear_ref, cfar_ref,
    v0x, v1, f1, w1, cx, cy, cz, send_ref,
    k1, u1, pair, fine,
):
    even, outside = edge_flags(where_ref[0], nx)

    def inside(value):
        return jnp.where(outside, 0.0, value)

    near = [near_ref[i] for i in range(3)]
    far = [inside(far_ref[i]) for i in range(3)]
    cnear = [cnear_ref[i] for i in range(7)]
    cfar = [inside(cfar_ref[i]) for i in range(7)]
    mine = [y_tiles(where_ref, ny, meven_ref, modd_ref, i) for i in range(5)]

    def pick(a, b):
        return [jnp.where(even, p, q) for p, q in zip(a, b)]

    blocks = (
        (pick(far, near), pick(cfar[0:3], cnear[0:3]), pick(cfar[3:6], cnear[3:6])),
        ([block_ref[i] for i in range(3)], [t[0] for t in mine], [t[1] for t in mine]),
        (pick(near, far), pick(cnear[0:3], cfar[0:3]), pick(cnear[3:6], cfar[3:6])),
    )
    zero = jnp.zeros((4, 256), F32)
    for b in range(3):
        for x in range(4):
            p = 4 * b + x
            half = slice(256 * (x % 2), 256 * (x % 2) + 256)
            t = x // 2
            for ref, at, row in (
                (f1, t, slice(0, 4)), (k1, t, slice(4, 8)), (w1, 2, slice(4 * t, 4 * t + 4))
            ):
                ref[p, 0:4] = blocks[b][0][at][row, half]
                ref[p, 4:8] = blocks[b][1][at][row, half]
                ref[p, 8:12] = zero
                ref[p, 12:16] = blocks[b][2][at][row, half]
    blank = jnp.zeros((8, 512), F32)
    for p in range(12):
        v0x[p, 8:16] = blank
    for x in range(8):
        v0x[2 + x, 0:8] = v0_ref[x]
        at = 2 * (x % 4)
        v0x[2 + x, 8:10] = mine[3 + x // 4][0][at : at + 2]
        v0x[2 + x, 14:16] = mine[3 + x // 4][1][at : at + 2]
    near_at = jnp.where(even, 10, 0)
    far_at = jnp.where(even, 0, 10)
    for i in range(2):
        v0x[near_at + i, 0:8] = near_ref[3 + i]
        v0x[far_at + i, 0:8] = inside(far_ref[3 + i])
    low_tile = jnp.where(even, cfar[6], cnear[6])
    high_tile = jnp.where(even, cnear[6], cfar[6])
    for at, tile, row in ((1, low_tile, 0), (10, high_tile, 4)):
        v0x[at, 8:10] = tile[row : row + 2]
        v0x[at, 14:16] = tile[row + 2 : row + 4]
    for p in range(12):
        u1[p] = w1[p] * f1[p]
        if p < 11:
            cx[p] = 0.5 * (k1[p] + k1[p + 1])
        cy[p] = coupling_y(k1[p])
        cz[p] = coupling_z(k1[p])
    for p in range(1, 11):
        mid = u1[p]
        total = gathered(mid, u1[p - 1], u1[p + 1], cx[p - 1], cx[p], cy[p], cz[p])
        v1[p] = KEEP * mid + w1[p] * (f1[p] + total)
    for p in range(4, 8, 2):
        both = None
        for q in (p, p + 1):
            mid = v1[q]
            total = gathered(mid, v1[q - 1], v1[q + 1], cx[q - 1], cx[q], cy[q], cz[q])
            diag = diagonal(k1[q], k1[q - 1], k1[q + 1])
            rest = (f1[q] + total - diag * mid)[0:8]
            both = rest if both is None else both + rest
        at = p - 4
        fine[at : at + 2] = 0.5 * row_sum(pair, both)[0:2]
        kept = k1[p, 0:8] + k1[p + 1, 0:8]
        fine[4 + at : 6 + at] = 0.125 * row_sum(pair, kept)[0:2]
    tile = lane_sum(fine[...], pair_sum_matrix())
    for i in range(send_ref.shape[0]):
        send_ref[i] = tile


def up_kernel(
    nx, ny, where_ref, *refs
):
    half = nx // 2
    columns = (refs[:half], refs[half : 2 * half])
    own, far = refs[nx : nx + 5], refs[nx + 5 : nx + 10]
    rs = Planes(own[0], far[0], 3, 8)
    cx0 = Planes(own[1], far[1], 3, 7)
    cy0, cz0, w0 = (Planes(a, b, 4, 6) for a, b in zip(own[2:], far[2:]))
    up_levels(nx, ny, where_ref, columns, rs, cx0, cy0, cz0, w0, *refs[nx + 10 :])


def up_levels(
    nx, ny, where_ref, columns, rs, cx0, cy0, cz0, w0, v1, f1, w1, cx1, cy1, cz1, v0x, out_ref,
    f2, k2, cx2, cyi, cyo, cz2, w2, d2, u2, v2, e2, f3, k3, cx3, cy3, cz3, w3, edge3, ga, gb,
    small, wide, e1a, e1b, narrow, e0a, e0b,
):
    gx = where_ref[0]
    gy = where_ref[1]
    core = gx % 2
    n2 = 2 * nx
    zero = jnp.zeros((ny, 128), F32)
    row = iota((ny, 128), 0)
    lane = iota((ny, 128), 1)
    last_row = row == ny - 1
    for s in range(2):
        k2[0, s] = zero
        k2[n2 + 1, s] = zero
        u2[0, s] = zero
        u2[n2 + 1, s] = zero
        v2[0, s] = zero
        v2[n2 + 1, s] = zero
    for j in range(nx // 2):
        chip = (gx // 2) ^ j
        for refs, which in ((columns[0], core), (columns[1], 1 - core)):
            for i in range(2):
                p = 4 * chip + 2 * which + i + 1
                for s in range(2):
                    f2[p, s] = refs[j][pl.ds(2 * i + s, ny, stride=8)]
                    k2[p, s] = refs[j][pl.ds(4 + 2 * i + s, ny, stride=8)]
    for p in range(n2 + 1):
        for s in range(2):
            cx2[p, s] = 0.5 * (k2[p, s] + k2[p + 1, s])
    for p in range(1, n2 + 1):
        k_low, k_high = k2[p, 0], k2[p, 1]
        after = jnp.where(last_row, 0.0, roll(k_low, -1, 0))
        before = jnp.where(row == 0, 0.0, roll(k_high, 1, 0))
        cyi[p] = 0.5 * (k_low + k_high)
        cyo[p] = jnp.where(last_row, 0.0, 0.5 * (k_high + after))
        for s, mid, ya, yb in ((0, k_low, k_high, before), (1, k_high, k_low, after)):
            up, down = z_neighbours(mid)
            cz2[p, s] = jnp.where(lane == 127, 0.0, 0.5 * (mid + up))
            diag = 3.0 * mid + 0.5 * (k2[p - 1, s] + k2[p + 1, s] + ya + yb + up + down)
            scale = OMEGA / diag
            d2[p, s] = diag
            w2[p, s] = scale
            u2[p, s] = scale * f2[p, s]

    def gather2(ref, p):
        low, high = ref[p, 0], ref[p, 1]
        sums = []
        for s, mid in ((0, low), (1, high)):
            total = cx2[p, s] * ref[p + 1, s] + cx2[p - 1, s] * ref[p - 1, s]
            total = total + cz2[p, s] * roll(mid, -1, 1) + roll(cz2[p, s] * mid, 1, 1)
            sums.append(total)
        sums[0] = sums[0] + cyi[p] * high + roll(cyo[p] * high, 1, 0)
        sums[1] = sums[1] + cyi[p] * low + cyo[p] * roll(low, -1, 0)
        return (low, high), sums

    def sweep2(source, target):
        for p in range(1, n2 + 1):
            mids, sums = gather2(source, p)
            for s in range(2):
                target[p, s] = KEEP * mids[s] + w2[p, s] * (f2[p, s] + sums[s])

    sweep2(u2, v2)
    even_lane = lane % 2 == 0

    def pair_lanes(value):
        return value + jnp.where(even_lane, roll(value, -1, 1), roll(value, 1, 1))

    k3[0] = zero
    k3[nx + 1] = zero
    ga[0] = zero
    ga[nx + 1] = zero
    gb[0] = zero
    gb[nx + 1] = zero
    for x in range(nx):
        both = None
        kept = None
        for p in (2 * x + 1, 2 * x + 2):
            mids, sums = gather2(v2, p)
            for s in range(2):
                rest = f2[p, s] + sums[s] - d2[p, s] * mids[s]
                both = rest if both is None else both + rest
                kept = k2[p, s] if kept is None else kept + k2[p, s]
        f3[x + 1] = 0.5 * pair_lanes(both)
        k3[x + 1] = 0.125 * pair_lanes(kept)
    for p in range(nx + 1):
        cx3[p] = 0.5 * (k3[p] + k3[p + 1])
    edge_total = zero
    rest_total = zero
    outer = (
        (row == 0).astype(F32) + last_row.astype(F32)
        + (lane < 2).astype(F32) + (lane >= 126).astype(F32)
    )
    for p in range(1, nx + 1):
        mid = k3[p]
        after = jnp.where(last_row, 0.0, roll(mid, -1, 0))
        before = jnp.where(row == 0, 0.0, roll(mid, 1, 0))
        up = jnp.where(lane >= 126, 0.0, roll(mid, -2, 1))
        down = jnp.where(lane < 2, 0.0, roll(mid, 2, 1))
        cy3[p] = jnp.where(last_row, 0.0, 0.5 * (mid + after))
        cz3[p] = jnp.where(lane >= 126, 0.0, 0.5 * (mid + up))
        diag = 3.0 * mid + 0.5 * (k3[p - 1] + k3[p + 1] + after + before + up + down)
        scale = OMEGA / diag
        w3[p] = scale
        ga[p] = scale * f3[p]
        faces = outer + (1.0 if p == 1 else 0.0) + (1.0 if p == nx else 0.0)
        edge = 0.5 * mid * faces
        edge3[p] = edge
        edge_total = edge_total + edge
        rest_total = rest_total + f3[p]

    def gather3(ref, p):
        mid = ref[p]
        total = cx3[p] * ref[p + 1] + cx3[p - 1] * ref[p - 1]
        total = total + cy3[p] * roll(mid, -1, 0) + roll(cy3[p] * mid, 1, 0)
        return mid, total + cz3[p] * roll(mid, -2, 1) + roll(cz3[p] * mid, 2, 1)

    source, target = ga, gb
    for _ in range(7):
        for p in range(1, nx + 1):
            mid, total = gather3(source, p)
            target[p] = KEEP * mid + w3[p] * (f3[p] + total)
        source, target = target, source
    for p in range(1, nx + 1):
        rest_total = rest_total - edge3[p] * source[p]

    def whole(value):
        return jnp.sum(jnp.sum(value, axis=0, keepdims=True), axis=1, keepdims=True)

    shift = whole(rest_total) / whole(edge_total)
    first_row = jnp.clip(gy - 3, 0, ny - 8)
    rows = pl.ds(first_row, 8)
    no_wrap = iota((8, 128), 0) < 7
    planes = []
    for j in range(10):
        x = 2 * gx - 4 + j
        planes.append((jnp.logical_and(x >= 0, x < n2), jnp.clip(x, 0, n2 - 1)))
    level = []
    for ok, q in planes:
        e3 = source[q // 2 + 1, rows] + shift
        level.append([jnp.where(ok, v2[q + 1, s, rows] + e3, 0.0) for s in range(2)])
    for first, last in ((1, 8), (2, 7)):
        done = list(level)
        for j in range(first, last + 1):
            ok, q = planes[j]
            low, high = level[j]
            inner = cyi[q + 1, rows]
            after = jnp.where(no_wrap, cyo[q + 1, rows], 0.0)
            sums = [inner * high + roll(after * high, 1, 0), inner * low + after * roll(low, -1, 0)]
            for s in range(2):
                mid = level[j][s]
                cz = cz2[q + 1, s, rows]
                total = sums[s] + cz * roll(mid, -1, 1) + roll(cz * mid, 1, 1)
                total = total + cx2[q + 1, s, rows] * level[j + 1][s]
                total = total + cx2[q, s, rows] * level[j - 1][s]
                value = KEEP * mid + w2[q + 1, s, rows] * (f2[q + 1, s, rows] + total)
                done[j] = [jnp.where(ok, value, 0.0)] if s == 0 else done[j] + [jnp.where(ok, value, 0.0)]
        level = done
    copies = pair_copy_matrix()
    at = gy - first_row
    steps = (
        (0, at, None),
        (2, jnp.minimum(at + 1, 7), gy < ny - 1),
        (6, jnp.maximum(at - 1, 0), gy > 0),
    )
    for i in range(6):
        small[8 * i + 4 : 8 * i + 6] = jnp.zeros((2, 128), F32)
        for s in range(2):
            e2[i, s] = level[i + 2][s]
            for j, r, ok in steps:
                line = e2[i, s, pl.ds(r, 1)]
                small[8 * i + j + s : 8 * i + j + s + 1] = (
                    line if ok is None else jnp.where(ok, line, 0.0)
                )
    wide[...] = lane_copy(small[...], copies)
    for i in range(6):
        spread = row_copy(narrow, wide[8 * i : 8 * i + 8])
        for p in (2 * i, 2 * i + 1):
            if 1 <= p <= 10:
                e1a[p] = v1[p] + spread
    for source, target, first, last in ((e1a, e1b, 2, 9), (e1b, e1a, 3, 8)):
        for p in range(first, last + 1):
            mid = source[p]
            total = gathered(
                mid, source[p - 1], source[p + 1], cx1[p - 1], cx1[p], cy1[p], cz1[p]
            )
            target[p] = KEEP * mid + w1[p] * (f1[p] + total)
    row8 = iota((8, 256), 0)
    for i in range(6):
        value = e1a[i + 3]
        wide[8 * i : 8 * i + 8] = jnp.where(row8 == 7, value[8:16], value[0:8])
    doubled = lane_copy(wide[...], copies)
    for i in range(6):
        spread = row_copy(narrow, doubled[8 * i : 8 * i + 8])
        for p in (2 * i, 2 * i + 1):
            e0a[p] = v0x[p] + spread
    for p in range(1, 11):
        mid = e0a[p]
        total = gathered(
            mid, e0a[p - 1], e0a[p + 1], cx0[p], cx0[p + 1], cy0[p + 1], cz0[p + 1]
        )
        e0b[p] = KEEP * mid + w0[p + 1] * (rs[p + 1] + total)
    for p in range(2, 10):
        mid = e0b[p]
        total = gathered(
            mid, e0b[p - 1], e0b[p + 1], cx0[p], cx0[p + 1], cy0[p + 1], cz0[p + 1]
        )
        out_ref[p - 2] = (KEEP * mid + w0[p + 1] * (rs[p + 1] + total))[0:8]


def run(kernel, outs, scratch, where, *operands, space=VMEM, cost=None):
    return pl.pallas_call(
        kernel,
        out_shape=[jax.ShapeDtypeStruct(shape, F32) for shape in outs],
        in_specs=[pl.BlockSpec(memory_space=pltpu.SMEM)]
        + [pl.BlockSpec(memory_space=space)] * len(operands),
        out_specs=[pl.BlockSpec(memory_space=VMEM)] * len(outs),
        scratch_shapes=[VMEM(s, F32) if isinstance(s, tuple) else s for s in scratch],
        compiler_params=PARAMS,
        cost_estimate=cost,
    )(where, *operands)


def body(initial, right_side, phase_map, phase_table):
    nx, ny = lax.axis_size("gx"), lax.axis_size("gy")
    where = jnp.stack([lax.axis_index("gx"), lax.axis_index("gy")]).astype(jnp.int32)

    def pairs(partner):
        return [
            (x * ny + y, px * ny + py)
            for x in range(nx)
            for y in range(ny)
            for px, py in [partner(x, y)]
        ]

    def beyond(at, size):
        other = at + 1 if at % 2 else at - 1
        return other if 0 <= other < size else None

    def far_x(x, y):
        other = beyond(x, nx)
        return (x, y ^ 1) if other is None else (other, y)

    def far_y(x, y):
        other = beyond(y, ny)
        return (x ^ 1, y) if other is None else (x, other)

    both = ("gx", "gy")

    def swap_x(near, far):
        return (
            lax.ppermute(near, both, pairs(lambda x, y: (x ^ 1, y))),
            lax.ppermute(far, both, pairs(far_x)),
        )

    def swap_y(near, far):
        return (
            lax.ppermute(near, both, pairs(lambda x, y: (x, y ^ 1))),
            lax.ppermute(far, both, pairs(far_y)),
        )

    inputs = [
        pltpu.with_memory_space_constraint(value, pltpu.HBM)
        for value in (phase_table, phase_map, initial, right_side)
    ]
    early_cost = pl.CostEstimate(flops=20_000_000, bytes_accessed=4_000_000, transcendentals=0)
    tile0 = (8, 512)
    ring0 = (16, 512)
    ring1 = (16, 256)
    kappa, init, rhs, near, far, yeven, yodd = run(
        start_kernel, [(8,) + tile0] * 7,
        [pltpu.SMEM((3,), F32), VMEM((8,) + tile0, jnp.int32), pltpu.SemaphoreType.DMA((4,))],
        where, *inputs, space=pltpu.HBM,
    )
    yeven, yodd = swap_y(yeven, yodd)
    near, far = swap_x(near, far)
    near, far, yeven, yodd = lax.optimization_barrier((near, far, yeven, yodd))
    cnear, cfar = swap_x(*corner_messages(nx, ny, yeven, yodd))
    ksx, vsx, rsx, cxx, cyx, czx, wix, v1x, v2x, restx = run(
        functools.partial(early0_kernel, ny),
        [(8,) + ring0] * 3 + [(7,) + ring0] + [(6,) + ring0] * 4 + [(4,) + ring0, (2,) + tile0],
        [], where, kappa, init, rhs, yeven, yodd, cost=early_cost,
    )
    v0, rs, cx0, cy0, cz0, w0, block, mnear, mfar, meven, modd = run(
        functools.partial(down0_kernel, nx, ny),
        [(8,) + tile0]
        + [(6,) + ring0, (6,) + ring0]
        + [(8,) + ring0] * 3
        + [(3,) + tile0]
        + [(5,) + tile0] * 4,
        [(6,) + ring0] * 2 + [(8,) + ring0, (10,) + ring0, (4, 16, 128), (64, 512), (64, 256)],
        where, near, far, cnear, cfar,
        ksx, vsx, rsx, cxx, cyx, czx, wix, v1x, v2x, restx,
    )
    meven, modd = swap_y(meven, modd)
    mnear, mfar = swap_x(mnear, mfar)
    mnear, mfar, meven, modd = lax.optimization_barrier((mnear, mfar, meven, modd))
    corner = corner1_message(ny, meven, modd)
    cnear, cfar = swap_x(corner, corner)
    v0x, v1, f1, w1, cx1, cy1, cz1, send = run(
        functools.partial(down1_kernel, nx, ny),
        [(12,) + ring0] + [(12,) + ring1] * 6 + [(ny, 8, 128)],
        [(12,) + ring1, (12,) + ring1, (4, 16, 128), (8, 256)],
        where, block, v0, mnear, mfar, meven, modd, cnear, cfar,
    )
    column = lax.all_to_all(send, "gy", 0, 0).reshape(ny * 8, 128)

    def chips_apart(j):
        return pairs(lambda x, y: (((x // 2) ^ j) * 2 + x % 2, y))

    mine = [column] + [lax.ppermute(column, both, chips_apart(j)) for j in range(1, nx // 2)]
    other = [lax.ppermute(c, both, pairs(lambda x, y: (x ^ 1, y))) for c in mine]
    n2 = 2 * nx
    pair2 = (n2 + 2, 2, ny, 128)
    one2 = (n2 + 2, ny, 128)
    one3 = (nx + 2, ny, 128)
    (out,) = run(
        functools.partial(up_kernel, nx, ny), [(8,) + tile0],
        [pair2, pair2, pair2, one2, one2, pair2, pair2, pair2, pair2, pair2, (6, 2, 8, 128)]
        + [one3] * 9
        + [(48, 128), (48, 256), (12,) + ring1, (12,) + ring1, (4, 16, 128), (12,) + ring0, (12,) + ring0],
        where, *mine, *other, rsx, cxx, cyx, czx, wix, rs, cx0, cy0, cz0, w0,
        v1, f1, w1, cx1, cy1, cz1, v0x,
    )
    return out


def solution(mesh):
    return jax.shard_map(
        body,
        mesh=mesh,
        in_specs=(P("gx", "gy", None), P("gx", "gy", None), P("gx", "gy", None), P()),
        out_specs=P("gx", "gy", None),
        check_vma=False,
    )
```

```python
import functools

import jax
import jax.numpy as jnp
from jax import lax
from jax.experimental import pallas as pl
from jax.experimental.pallas import tpu as pltpu
from jax.sharding import PartitionSpec as P

F32 = jnp.float32
KEEP = 0.2
OMEGA = 0.8
VMEM = pltpu.VMEM
PARAMS = pltpu.CompilerParams(vmem_limit_bytes=48 * 1024 * 1024)


def roll(value, shift, axis):
    return pltpu.roll(value, shift % value.shape[axis], axis)


def iota(shape, dim):
    return lax.broadcasted_iota(jnp.int32, shape, dim)


def pair_sum_matrix():
    return (iota((256, 128), 0) // 2 == iota((256, 128), 1)).astype(F32)


def pair_copy_matrix():
    return (iota((128, 256), 1) // 2 == iota((128, 256), 0)).astype(F32)


def exact_dot(a, b):
    return lax.dot_general(
        a, b, (((1,), (0,)), ((), ())), precision=lax.Precision.HIGHEST, preferred_element_type=F32
    )


def lane_sum(value, matrix):
    width = value.shape[1]
    parts = [exact_dot(value[:, at : at + 256], matrix) for at in range(0, width, 256)]
    return parts[0] if len(parts) == 1 else jnp.concatenate(parts, axis=1)


def lane_copy(value, matrix):
    width = value.shape[1]
    parts = [exact_dot(value[:, at : at + 128], matrix) for at in range(0, width, 128)]
    return parts[0] if len(parts) == 1 else jnp.concatenate(parts, axis=1)


def row_sum(scratch, value):
    rows, width = value.shape
    parts = []
    for c in range(width // 128):
        scratch[c, 0:rows] = value[:, 128 * c : 128 * c + 128]
        first = scratch[c, pl.ds(0, rows // 2, stride=2)]
        parts.append(first + scratch[c, pl.ds(1, rows // 2, stride=2)])
    return parts[0] if len(parts) == 1 else jnp.concatenate(parts, axis=1)


def row_copy(scratch, value):
    rows, width = value.shape
    parts = []
    for c in range(width // 128):
        part = value[:, 128 * c : 128 * c + 128]
        scratch[c, pl.ds(0, rows, stride=2)] = part
        scratch[c, pl.ds(1, rows, stride=2)] = part
        parts.append(scratch[c, 0 : 2 * rows])
    return parts[0] if len(parts) == 1 else jnp.concatenate(parts, axis=1)


def gathered(mid, low, high, cx_low, cx, cy, cz):
    total = cx * high + cx_low * low
    total = total + cy * roll(mid, -1, 0) + roll(cy * mid, 1, 0)
    return total + cz * roll(mid, -1, 1) + roll(cz * mid, 1, 1)


def z_neighbours(mid):
    lane = iota(mid.shape, 1)
    last = mid.shape[1] - 1
    up = jnp.where(lane == last, 0.0, roll(mid, -1, 1))
    down = jnp.where(lane == 0, 0.0, roll(mid, 1, 1))
    return up, down


def diagonal(mid, low, high):
    up, down = z_neighbours(mid)
    total = low + high + roll(mid, -1, 0) + roll(mid, 1, 0) + up + down
    return 3.0 * mid + 0.5 * total


def coupling_y(mid):
    return 0.5 * (mid + roll(mid, -1, 0))


def coupling_z(mid):
    lane = iota(mid.shape, 1)
    return jnp.where(lane == mid.shape[1] - 1, 0.0, 0.5 * (mid + roll(mid, -1, 1)))


def edge_flags(at, grid):
    even = at % 2 == 0
    outside = jnp.logical_or(at == 0, at == grid - 1)
    return even, outside


def start_kernel(
    where_ref, table_hbm, phase_hbm, init_hbm, rhs_hbm,
    kap_ref, init_ref, rhs_ref, near_ref, far_ref, yeven_ref, yodd_ref,
    table_ref, phase_ref, sems,
):
    copies = [
        pltpu.make_async_copy(source, target, sems.at[i])
        for i, (source, target) in enumerate(
            ((table_hbm, table_ref), (phase_hbm, phase_ref), (init_hbm, init_ref), (rhs_hbm, rhs_ref))
        )
    ]
    for copy in copies:
        copy.start()
    for copy in copies:
        copy.wait()
    even = where_ref[0] % 2 == 0
    for x in range(8):
        phase = phase_ref[x]
        kap_ref[x] = jnp.where(
            phase == 0, table_ref[0], jnp.where(phase == 1, table_ref[1], table_ref[2])
        )
    for ref, side in ((near_ref, even), (far_ref, jnp.logical_not(even))):
        deep = jnp.where(side, 5, 0)
        shallow = jnp.where(side, 6, 0)
        for i in range(3):
            ref[i] = kap_ref[deep + i]
            ref[3 + i] = init_ref[deep + i]
        for i in range(2):
            ref[6 + i] = rhs_ref[shallow + i]

    def write(low_ref, high_ref):
        for x in range(8):
            low_ref[x, 0:3] = kap_ref[x, 0:3]
            low_ref[x, 3:6] = init_ref[x, 0:3]
            low_ref[x, 6:8] = rhs_ref[x, 0:2]
            high_ref[x, 0:3] = kap_ref[x, 5:8]
            high_ref[x, 3:6] = init_ref[x, 5:8]
            high_ref[x, 6:8] = rhs_ref[x, 6:8]

    by_parity(where_ref, yeven_ref, yodd_ref, write)


def by_parity(where_ref, even_ref, odd_ref, write):
    even = where_ref[1] % 2 == 0

    @pl.when(even)
    def _():
        write(odd_ref, even_ref)

    @pl.when(jnp.logical_not(even))
    def _():
        write(even_ref, odd_ref)


def y_tiles(where_ref, grid, even_ref, odd_ref, p):
    even, outside = edge_flags(where_ref[1], grid)
    inner = even_ref[p]
    outer = jnp.where(outside, 0.0, odd_ref[p])
    return jnp.where(even, inner, outer), jnp.where(even, outer, inner)


def corner_messages(nx, ny, yeven, yodd):
    even = lax.axis_index("gx") % 2 == 0
    high, low = both_tiles(ny, yeven, yodd)
    top = jnp.concatenate([high[7:8], high[6:7], low[7:8], low[6:7]], axis=0)
    bottom = jnp.concatenate([high[0:2], low[0:2]], axis=0)
    return jnp.where(even, top, bottom), jnp.where(even, bottom, top)


def both_tiles(ny, yeven, yodd):
    at = lax.axis_index("gy")
    even, outside = edge_flags(at, ny)
    outer = jnp.where(outside, 0.0, yodd)
    return jnp.where(even, yeven, outer), jnp.where(even, outer, yeven)


class Planes:
    def __init__(self, middle, outer, first, count):
        self.middle, self.outer, self.first, self.count = middle, outer, first, count

    def find(self, p):
        if p < self.first:
            return self.outer, p
        if p < self.first + self.count:
            return self.middle, p - self.first
        return self.outer, p - self.count

    def __getitem__(self, p):
        ref, at = self.find(p)
        return ref[at]

    def __setitem__(self, p, value):
        ref, at = self.find(p)
        ref[at] = value


def setup0(ks, cx, cy, cz, wi, planes, faces):
    for p in faces:
        cx[p] = 0.5 * (ks[p] + ks[p + 1])
    for p in planes:
        mid = ks[p]
        cy[p] = coupling_y(mid)
        cz[p] = coupling_z(mid)
        diag = diagonal(mid, ks[p - 1], ks[p + 1])
        wi[p] = jnp.where(mid > 0.0, OMEGA / jnp.where(mid > 0.0, diag, 1.0), 0.0)


def sweep0(source, target, rs, cx, cy, cz, wi, planes):
    for p in planes:
        mid = source[p]
        total = gathered(mid, source[p - 1], source[p + 1], cx[p - 1], cx[p], cy[p], cz[p])
        target[p] = KEEP * mid + wi[p] * (rs[p] + total)


def rest0(v2, rs, ks, cx, cy, cz, p):
    mid = v2[p]
    total = gathered(mid, v2[p - 1], v2[p + 1], cx[p - 1], cx[p], cy[p], cz[p])
    diag = diagonal(ks[p], ks[p - 1], ks[p + 1])
    return (rs[p] + total - diag * mid)[0:8]


def add_y_halo(ks, vs, rs, p, high, low):
    zero = jnp.zeros((8, 512), F32)
    ks[p, 8:16] = zero
    vs[p, 8:16] = zero
    rs[p, 8:16] = zero
    ks[p, 8:11] = high[0:3]
    ks[p, 13:16] = low[0:3]
    vs[p, 8:11] = high[3:6]
    vs[p, 13:16] = low[3:6]
    rs[p, 8:10] = high[6:8]
    rs[p, 14:16] = low[6:8]


def early0_kernel(
    ny, where_ref, kap_ref, init_ref, rhs_ref, even_ref, odd_ref,
    ks, vs, rs, cx, cy, cz, wi, v1, v2, rest,
):
    for x in range(8):
        ks[x, 0:8] = kap_ref[x]
        vs[x, 0:8] = init_ref[x]
        rs[x, 0:8] = rhs_ref[x]
        add_y_halo(ks, vs, rs, x, *y_tiles(where_ref, ny, even_ref, odd_ref, x))
    ks, vs, rs = (Planes(ref, None, 3, 8) for ref in (ks, vs, rs))
    cx = Planes(cx, None, 3, 7)
    cy, cz, wi, v1 = (Planes(ref, None, 4, 6) for ref in (cy, cz, wi, v1))
    v2 = Planes(v2, None, 5, 4)
    setup0(ks, cx, cy, cz, wi, range(4, 10), range(3, 10))
    sweep0(vs, v1, rs, cx, cy, cz, wi, range(4, 10))
    sweep0(v1, v2, rs, cx, cy, cz, wi, range(5, 9))
    for p in (6, 7):
        rest[p - 6] = rest0(v2, rs, ks, cx, cy, cz, p)


def down0_kernel(
    nx, ny, where_ref, near_ref, far_ref, cnear_ref, cfar_ref,
    ks_own, vs_own, rs_own, cx_own, cy_own, cz_own, wi_own, v1_own, v2_own, rest_own,
    v0_ref, rs, cx, cy, cz, wi, block_ref, mnear_ref, mfar_ref, meven_ref, modd_ref,
    ks, vs, v1, v2, pair, fine, coarse,
):
    even, outside = edge_flags(where_ref[0], nx)
    for i in range(3):
        near_at = jnp.where(even, 3 + i, i)
        far_at = jnp.where(even, i, 3 + i)
        for ref, first in ((ks, 0), (vs, 3)):
            ref[near_at, 0:8] = near_ref[first + i]
            ref[far_at, 0:8] = jnp.where(outside, 0.0, far_ref[first + i])
    for i in range(2):
        rs[jnp.where(even, 3 + i, 1 + i), 0:8] = near_ref[6 + i]
        rs[jnp.where(even, 1 + i, 3 + i), 0:8] = jnp.where(outside, 0.0, far_ref[6 + i])
    zero = jnp.zeros((8, 512), F32)
    for p in (0, 5):
        ks[p, 8:16] = zero
        vs[p, 8:16] = zero
        rs[p, 8:16] = zero
    rs[0, 0:8] = zero
    rs[5, 0:8] = zero
    for i in range(2):
        add_y_halo(ks, vs, rs, jnp.where(even, 3 + i, 2 - i), cnear_ref[i], cnear_ref[2 + i])
        add_y_halo(
            ks, vs, rs, jnp.where(even, 2 - i, 3 + i),
            jnp.where(outside, 0.0, cfar_ref[i]), jnp.where(outside, 0.0, cfar_ref[2 + i]),
        )
    ks, vs, rs = (Planes(a, b, 3, 8) for a, b in ((ks_own, ks), (vs_own, vs), (rs_own, rs)))
    cx = Planes(cx_own, cx, 3, 7)
    cy, cz, wi, v1 = (
        Planes(a, b, 4, 6) for a, b in ((cy_own, cy), (cz_own, cz), (wi_own, wi), (v1_own, v1))
    )
    v2 = Planes(v2_own, v2, 5, 4)
    setup0(ks, cx, cy, cz, wi, (1, 2, 3, 10, 11, 12), (0, 1, 2, 10, 11, 12))
    sweep0(vs, v1, rs, cx, cy, cz, wi, (1, 2, 3, 10, 11, 12))
    sweep0(v1, v2, rs, cx, cy, cz, wi, (2, 3, 4, 9, 10, 11))
    for p in range(3, 11, 2):
        both = None
        for q in (p, p + 1):
            rest = rest_own[q - 6] if q in (6, 7) else rest0(v2, rs, ks, cx, cy, cz, q)
            both = rest if both is None else both + rest
            v0_ref[q - 3] = v2[q][0:8]
        at = 2 * (p - 3)
        fine[at : at + 4] = row_sum(pair, both)
    for p in range(1, 13, 2):
        at = 12 + 4 * p
        fine[at : at + 8] = row_sum(pair, ks[p] + ks[p + 1])
    coarse[...] = lane_sum(fine[...], pair_sum_matrix())
    for x in range(4):
        half = pl.ds(256 * (x % 2), 256)
        mid = 0.125 * coarse[24 + 8 * x : 32 + 8 * x]
        low = 0.125 * coarse[16 + 8 * x : 24 + 8 * x]
        high = 0.125 * coarse[32 + 8 * x : 40 + 8 * x]
        block_ref[x // 2, 0:4, half] = 0.5 * coarse[4 * x : 4 * x + 4]
        block_ref[x // 2, 4:8, half] = mid[0:4]
        at = 4 * (x // 2)
        block_ref[2, at : at + 4, half] = (OMEGA / diagonal(mid, low, high)[0:4])
    for ref, side in ((mnear_ref, even), (mfar_ref, jnp.logical_not(even))):
        shallow = jnp.where(side, 6, 0)
        for i in range(3):
            ref[i] = block_ref[i]
        for i in range(2):
            ref[3 + i] = v0_ref[shallow + i]

    def write(low_ref, high_ref):
        for i in range(3):
            low_ref[i] = block_ref[i]
            high_ref[i] = block_ref[i]
        for x in range(8):
            at = 2 * (x % 4)
            low_ref[3 + x // 4, at : at + 2] = v0_ref[x, 0:2]
            high_ref[3 + x // 4, at : at + 2] = v0_ref[x, 6:8]

    by_parity(where_ref, meven_ref, modd_ref, write)


def corner1_message(ny, meven, modd):
    high, low = both_tiles(ny, meven, modd)
    rows = [high[4:5, 6:8], low[4:5, 6:8], high[3:4, 0:2], low[3:4, 0:2]]
    return jnp.concatenate([high[0:3], low[0:3], jnp.concatenate(rows, axis=1)], axis=0)


def down1_kernel(
    nx, ny, where_ref, block_ref, v0_ref, near_ref, far_ref, meven_ref, modd_ref,
    cnear_ref, cfar_ref,
    v0x, v1, f1, w1, cx, cy, cz, send_ref,
    k1, u1, pair, fine,
):
    even, outside = edge_flags(where_ref[0], nx)

    def inside(value):
        return jnp.where(outside, 0.0, value)

    near = [near_ref[i] for i in range(3)]
    far = [inside(far_ref[i]) for i in range(3)]
    cnear = [cnear_ref[i] for i in range(7)]
    cfar = [inside(cfar_ref[i]) for i in range(7)]
    mine = [y_tiles(where_ref, ny, meven_ref, modd_ref, i) for i in range(5)]

    def pick(a, b):
        return [jnp.where(even, p, q) for p, q in zip(a, b)]

    blocks = (
        (pick(far, near), pick(cfar[0:3], cnear[0:3]), pick(cfar[3:6], cnear[3:6])),
        ([block_ref[i] for i in range(3)], [t[0] for t in mine], [t[1] for t in mine]),
        (pick(near, far), pick(cnear[0:3], cfar[0:3]), pick(cnear[3:6], cfar[3:6])),
    )
    zero = jnp.zeros((4, 256), F32)
    for b in range(3):
        for x in range(4):
            p = 4 * b + x
            half = slice(256 * (x % 2), 256 * (x % 2) + 256)
            t = x // 2
            for ref, at, row in (
                (f1, t, slice(0, 4)), (k1, t, slice(4, 8)), (w1, 2, slice(4 * t, 4 * t + 4))
            ):
                ref[p, 0:4] = blocks[b][0][at][row, half]
                ref[p, 4:8] = blocks[b][1][at][row, half]
                ref[p, 8:12] = zero
                ref[p, 12:16] = blocks[b][2][at][row, half]
    blank = jnp.zeros((8, 512), F32)
    for p in range(12):
        v0x[p, 8:16] = blank
    for x in range(8):
        v0x[2 + x, 0:8] = v0_ref[x]
        at = 2 * (x % 4)
        v0x[2 + x, 8:10] = mine[3 + x // 4][0][at : at + 2]
        v0x[2 + x, 14:16] = mine[3 + x // 4][1][at : at + 2]
    near_at = jnp.where(even, 10, 0)
    far_at = jnp.where(even, 0, 10)
    for i in range(2):
        v0x[near_at + i, 0:8] = near_ref[3 + i]
        v0x[far_at + i, 0:8] = inside(far_ref[3 + i])
    low_tile = jnp.where(even, cfar[6], cnear[6])
    high_tile = jnp.where(even, cnear[6], cfar[6])
    for at, tile, row in ((1, low_tile, 0), (10, high_tile, 4)):
        v0x[at, 8:10] = tile[row : row + 2]
        v0x[at, 14:16] = tile[row + 2 : row + 4]
    for p in range(12):
        u1[p] = w1[p] * f1[p]
        if p < 11:
            cx[p] = 0.5 * (k1[p] + k1[p + 1])
        cy[p] = coupling_y(k1[p])
        cz[p] = coupling_z(k1[p])
    for p in range(1, 11):
        mid = u1[p]
        total = gathered(mid, u1[p - 1], u1[p + 1], cx[p - 1], cx[p], cy[p], cz[p])
        v1[p] = KEEP * mid + w1[p] * (f1[p] + total)
    for p in range(4, 8, 2):
        both = None
        for q in (p, p + 1):
            mid = v1[q]
            total = gathered(mid, v1[q - 1], v1[q + 1], cx[q - 1], cx[q], cy[q], cz[q])
            diag = diagonal(k1[q], k1[q - 1], k1[q + 1])
            rest = (f1[q] + total - diag * mid)[0:8]
            both = rest if both is None else both + rest
        at = p - 4
        fine[at : at + 2] = 0.5 * row_sum(pair, both)[0:2]
        kept = k1[p, 0:8] + k1[p + 1, 0:8]
        fine[4 + at : 6 + at] = 0.125 * row_sum(pair, kept)[0:2]
    tile = lane_sum(fine[...], pair_sum_matrix())
    for i in range(send_ref.shape[0]):
        send_ref[i] = tile


def up_kernel(
    nx, ny, where_ref, *refs
):
    half = nx // 2
    columns = (refs[:half], refs[half : 2 * half])
    own, far = refs[nx : nx + 5], refs[nx + 5 : nx + 10]
    rs = Planes(own[0], far[0], 3, 8)
    cx0 = Planes(own[1], far[1], 3, 7)
    cy0, cz0, w0 = (Planes(a, b, 4, 6) for a, b in zip(own[2:], far[2:]))
    up_levels(nx, ny, where_ref, columns, rs, cx0, cy0, cz0, w0, *refs[nx + 10 :])


def up_levels(
    nx, ny, where_ref, columns, rs, cx0, cy0, cz0, w0, v1, f1, w1, cx1, cy1, cz1, v0x, out_ref,
    f2, k2, cx2, cyi, cyo, cz2, w2, d2, u2, v2, e2, f3, k3, cx3, cy3, cz3, w3, edge3, ga, gb,
    small, wide, e1a, e1b, narrow, e0a, e0b,
):
    gx = where_ref[0]
    gy = where_ref[1]
    core = gx % 2
    n2 = 2 * nx
    zero = jnp.zeros((ny, 128), F32)
    row = iota((ny, 128), 0)
    lane = iota((ny, 128), 1)
    last_row = row == ny - 1
    for s in range(2):
        k2[0, s] = zero
        k2[n2 + 1, s] = zero
        u2[0, s] = zero
        u2[n2 + 1, s] = zero
        v2[0, s] = zero
        v2[n2 + 1, s] = zero
    for j in range(nx // 2):
        chip = (gx // 2) ^ j
        for refs, which in ((columns[0], core), (columns[1], 1 - core)):
            for i in range(2):
                p = 4 * chip + 2 * which + i + 1
                for s in range(2):
                    f2[p, s] = refs[j][2 * i + s]
                    k2[p, s] = refs[j][4 + 2 * i + s]
    for p in range(n2 + 1):
        for s in range(2):
            cx2[p, s] = 0.5 * (k2[p, s] + k2[p + 1, s])
    for p in range(1, n2 + 1):
        k_low, k_high = k2[p, 0], k2[p, 1]
        after = jnp.where(last_row, 0.0, roll(k_low, -1, 0))
        before = jnp.where(row == 0, 0.0, roll(k_high, 1, 0))
        cyi[p] = 0.5 * (k_low + k_high)
        cyo[p] = jnp.where(last_row, 0.0, 0.5 * (k_high + after))
        for s, mid, ya, yb in ((0, k_low, k_high, before), (1, k_high, k_low, after)):
            up, down = z_neighbours(mid)
            cz2[p, s] = jnp.where(lane == 127, 0.0, 0.5 * (mid + up))
            diag = 3.0 * mid + 0.5 * (k2[p - 1, s] + k2[p + 1, s] + ya + yb + up + down)
            scale = OMEGA / diag
            d2[p, s] = diag
            w2[p, s] = scale
            u2[p, s] = scale * f2[p, s]

    def gather2(ref, p):
        low, high = ref[p, 0], ref[p, 1]
        sums = []
        for s, mid in ((0, low), (1, high)):
            total = cx2[p, s] * ref[p + 1, s] + cx2[p - 1, s] * ref[p - 1, s]
            total = total + cz2[p, s] * roll(mid, -1, 1) + roll(cz2[p, s] * mid, 1, 1)
            sums.append(total)
        sums[0] = sums[0] + cyi[p] * high + roll(cyo[p] * high, 1, 0)
        sums[1] = sums[1] + cyi[p] * low + cyo[p] * roll(low, -1, 0)
        return (low, high), sums

    def sweep2(source, target):
        for p in range(1, n2 + 1):
            mids, sums = gather2(source, p)
            for s in range(2):
                target[p, s] = KEEP * mids[s] + w2[p, s] * (f2[p, s] + sums[s])

    sweep2(u2, v2)
    even_lane = lane % 2 == 0

    def pair_lanes(value):
        return value + jnp.where(even_lane, roll(value, -1, 1), roll(value, 1, 1))

    k3[0] = zero
    k3[nx + 1] = zero
    ga[0] = zero
    ga[nx + 1] = zero
    gb[0] = zero
    gb[nx + 1] = zero
    for x in range(nx):
        both = None
        kept = None
        for p in (2 * x + 1, 2 * x + 2):
            mids, sums = gather2(v2, p)
            for s in range(2):
                rest = f2[p, s] + sums[s] - d2[p, s] * mids[s]
                both = rest if both is None else both + rest
                kept = k2[p, s] if kept is None else kept + k2[p, s]
        f3[x + 1] = 0.5 * pair_lanes(both)
        k3[x + 1] = 0.125 * pair_lanes(kept)
    for p in range(nx + 1):
        cx3[p] = 0.5 * (k3[p] + k3[p + 1])
    edge_total = zero
    rest_total = zero
    outer = (
        (row == 0).astype(F32) + last_row.astype(F32)
        + (lane < 2).astype(F32) + (lane >= 126).astype(F32)
    )
    for p in range(1, nx + 1):
        mid = k3[p]
        after = jnp.where(last_row, 0.0, roll(mid, -1, 0))
        before = jnp.where(row == 0, 0.0, roll(mid, 1, 0))
        up = jnp.where(lane >= 126, 0.0, roll(mid, -2, 1))
        down = jnp.where(lane < 2, 0.0, roll(mid, 2, 1))
        cy3[p] = jnp.where(last_row, 0.0, 0.5 * (mid + after))
        cz3[p] = jnp.where(lane >= 126, 0.0, 0.5 * (mid + up))
        diag = 3.0 * mid + 0.5 * (k3[p - 1] + k3[p + 1] + after + before + up + down)
        scale = OMEGA / diag
        w3[p] = scale
        ga[p] = scale * f3[p]
        faces = outer + (1.0 if p == 1 else 0.0) + (1.0 if p == nx else 0.0)
        edge = 0.5 * mid * faces
        edge3[p] = edge
        edge_total = edge_total + edge
        rest_total = rest_total + f3[p]

    def gather3(ref, p):
        mid = ref[p]
        total = cx3[p] * ref[p + 1] + cx3[p - 1] * ref[p - 1]
        total = total + cy3[p] * roll(mid, -1, 0) + roll(cy3[p] * mid, 1, 0)
        return mid, total + cz3[p] * roll(mid, -2, 1) + roll(cz3[p] * mid, 2, 1)

    source, target = ga, gb
    for _ in range(7):
        for p in range(1, nx + 1):
            mid, total = gather3(source, p)
            target[p] = KEEP * mid + w3[p] * (f3[p] + total)
        source, target = target, source
    for p in range(1, nx + 1):
        rest_total = rest_total - edge3[p] * source[p]

    def whole(value):
        return jnp.sum(jnp.sum(value, axis=0, keepdims=True), axis=1, keepdims=True)

    shift = whole(rest_total) / whole(edge_total)
    first_row = jnp.clip(gy - 3, 0, ny - 8)
    rows = pl.ds(first_row, 8)
    no_wrap = iota((8, 128), 0) < 7
    planes = []
    for j in range(10):
        x = 2 * gx - 4 + j
        planes.append((jnp.logical_and(x >= 0, x < n2), jnp.clip(x, 0, n2 - 1)))
    level = []
    for ok, q in planes:
        e3 = source[q // 2 + 1, rows] + shift
        level.append([jnp.where(ok, v2[q + 1, s, rows] + e3, 0.0) for s in range(2)])
    for first, last in ((1, 8), (2, 7)):
        done = list(level)
        for j in range(first, last + 1):
            ok, q = planes[j]
            low, high = level[j]
            inner = cyi[q + 1, rows]
            after = jnp.where(no_wrap, cyo[q + 1, rows], 0.0)
            sums = [inner * high + roll(after * high, 1, 0), inner * low + after * roll(low, -1, 0)]
            for s in range(2):
                mid = level[j][s]
                cz = cz2[q + 1, s, rows]
                total = sums[s] + cz * roll(mid, -1, 1) + roll(cz * mid, 1, 1)
                total = total + cx2[q + 1, s, rows] * level[j + 1][s]
                total = total + cx2[q, s, rows] * level[j - 1][s]
                value = KEEP * mid + w2[q + 1, s, rows] * (f2[q + 1, s, rows] + total)
                done[j] = [jnp.where(ok, value, 0.0)] if s == 0 else done[j] + [jnp.where(ok, value, 0.0)]
        level = done
    copies = pair_copy_matrix()
    at = gy - first_row
    steps = (
        (0, at, None),
        (2, jnp.minimum(at + 1, 7), gy < ny - 1),
        (6, jnp.maximum(at - 1, 0), gy > 0),
    )
    for i in range(6):
        small[8 * i + 4 : 8 * i + 6] = jnp.zeros((2, 128), F32)
        for s in range(2):
            e2[i, s] = level[i + 2][s]
            for j, r, ok in steps:
                line = e2[i, s, pl.ds(r, 1)]
                small[8 * i + j + s : 8 * i + j + s + 1] = (
                    line if ok is None else jnp.where(ok, line, 0.0)
                )
    wide[...] = lane_copy(small[...], copies)
    for i in range(6):
        spread = row_copy(narrow, wide[8 * i : 8 * i + 8])
        for p in (2 * i, 2 * i + 1):
            if 1 <= p <= 10:
                e1a[p] = v1[p] + spread
    for source, target, first, last in ((e1a, e1b, 2, 9), (e1b, e1a, 3, 8)):
        for p in range(first, last + 1):
            mid = source[p]
            total = gathered(
                mid, source[p - 1], source[p + 1], cx1[p - 1], cx1[p], cy1[p], cz1[p]
            )
            target[p] = KEEP * mid + w1[p] * (f1[p] + total)
    row8 = iota((8, 256), 0)
    for i in range(6):
        value = e1a[i + 3]
        wide[8 * i : 8 * i + 8] = jnp.where(row8 == 7, value[8:16], value[0:8])
    doubled = lane_copy(wide[...], copies)
    for i in range(6):
        spread = row_copy(narrow, doubled[8 * i : 8 * i + 8])
        for p in (2 * i, 2 * i + 1):
            e0a[p] = v0x[p] + spread
    for p in range(1, 11):
        mid = e0a[p]
        total = gathered(
            mid, e0a[p - 1], e0a[p + 1], cx0[p], cx0[p + 1], cy0[p + 1], cz0[p + 1]
        )
        e0b[p] = KEEP * mid + w0[p + 1] * (rs[p + 1] + total)
    for p in range(2, 10):
        mid = e0b[p]
        total = gathered(
            mid, e0b[p - 1], e0b[p + 1], cx0[p], cx0[p + 1], cy0[p + 1], cz0[p + 1]
        )
        out_ref[p - 2] = (KEEP * mid + w0[p + 1] * (rs[p + 1] + total))[0:8]


def run(kernel, outs, scratch, where, *operands, space=VMEM, cost=None):
    return pl.pallas_call(
        kernel,
        out_shape=[jax.ShapeDtypeStruct(shape, F32) for shape in outs],
        in_specs=[pl.BlockSpec(memory_space=pltpu.SMEM)]
        + [pl.BlockSpec(memory_space=space)] * len(operands),
        out_specs=[pl.BlockSpec(memory_space=VMEM)] * len(outs),
        scratch_shapes=[VMEM(s, F32) if isinstance(s, tuple) else s for s in scratch],
        compiler_params=PARAMS,
        cost_estimate=cost,
    )(where, *operands)


def body(initial, right_side, phase_map, phase_table):
    nx, ny = lax.axis_size("gx"), lax.axis_size("gy")
    where = jnp.stack([lax.axis_index("gx"), lax.axis_index("gy")]).astype(jnp.int32)

    def pairs(partner):
        return [
            (x * ny + y, px * ny + py)
            for x in range(nx)
            for y in range(ny)
            for px, py in [partner(x, y)]
        ]

    def beyond(at, size):
        other = at + 1 if at % 2 else at - 1
        return other if 0 <= other < size else None

    def far_x(x, y):
        other = beyond(x, nx)
        return (x, y ^ 1) if other is None else (other, y)

    def far_y(x, y):
        other = beyond(y, ny)
        return (x ^ 1, y) if other is None else (x, other)

    both = ("gx", "gy")

    def swap_x(near, far):
        return (
            lax.ppermute(near, both, pairs(lambda x, y: (x ^ 1, y))),
            lax.ppermute(far, both, pairs(far_x)),
        )

    def swap_y(near, far):
        return (
            lax.ppermute(near, both, pairs(lambda x, y: (x, y ^ 1))),
            lax.ppermute(far, both, pairs(far_y)),
        )

    inputs = [
        pltpu.with_memory_space_constraint(value, pltpu.HBM)
        for value in (phase_table, phase_map, initial, right_side)
    ]
    early_cost = pl.CostEstimate(flops=20_000_000, bytes_accessed=4_000_000, transcendentals=0)
    tile0 = (8, 512)
    ring0 = (16, 512)
    ring1 = (16, 256)
    kappa, init, rhs, near, far, yeven, yodd = run(
        start_kernel, [(8,) + tile0] * 7,
        [pltpu.SMEM((3,), F32), VMEM((8,) + tile0, jnp.int32), pltpu.SemaphoreType.DMA((4,))],
        where, *inputs, space=pltpu.HBM,
    )
    yeven, yodd = swap_y(yeven, yodd)
    near, far = swap_x(near, far)
    yodd, yeven, far, near = lax.optimization_barrier((yodd, yeven, far, near))
    cnear, cfar = swap_x(*corner_messages(nx, ny, yeven, yodd))
    ksx, vsx, rsx, cxx, cyx, czx, wix, v1x, v2x, restx = run(
        functools.partial(early0_kernel, ny),
        [(8,) + ring0] * 3 + [(7,) + ring0] + [(6,) + ring0] * 4 + [(4,) + ring0, (2,) + tile0],
        [], where, kappa, init, rhs, yeven, yodd, cost=early_cost,
    )
    v0, rs, cx0, cy0, cz0, w0, block, mnear, mfar, meven, modd = run(
        functools.partial(down0_kernel, nx, ny),
        [(8,) + tile0]
        + [(6,) + ring0, (6,) + ring0]
        + [(8,) + ring0] * 3
        + [(3,) + tile0]
        + [(5,) + tile0] * 4,
        [(6,) + ring0] * 2 + [(8,) + ring0, (10,) + ring0, (4, 16, 128), (64, 512), (64, 256)],
        where, near, far, cnear, cfar,
        ksx, vsx, rsx, cxx, cyx, czx, wix, v1x, v2x, restx,
    )
    meven, modd = swap_y(meven, modd)
    mnear, mfar = swap_x(mnear, mfar)
    modd, meven, mfar, mnear = lax.optimization_barrier((modd, meven, mfar, mnear))
    corner = corner1_message(ny, meven, modd)
    cnear, cfar = swap_x(corner, corner)
    v0x, v1, f1, w1, cx1, cy1, cz1, send = run(
        functools.partial(down1_kernel, nx, ny),
        [(12,) + ring0] + [(12,) + ring1] * 6 + [(ny, 8, 128)],
        [(12,) + ring1, (12,) + ring1, (4, 16, 128), (8, 256)],
        where, block, v0, mnear, mfar, meven, modd, cnear, cfar,
    )
    column = jnp.transpose(lax.all_to_all(send, "gy", 0, 0), (1, 0, 2))

    def chips_apart(j):
        return pairs(lambda x, y: (((x // 2) ^ j) * 2 + x % 2, y))

    mine = [column] + [lax.ppermute(column, both, chips_apart(j)) for j in range(1, nx // 2)]
    other = [lax.ppermute(c, both, pairs(lambda x, y: (x ^ 1, y))) for c in mine]
    n2 = 2 * nx
    pair2 = (n2 + 2, 2, ny, 128)
    one2 = (n2 + 2, ny, 128)
    one3 = (nx + 2, ny, 128)
    (out,) = run(
        functools.partial(up_kernel, nx, ny), [(8,) + tile0],
        [pair2, pair2, pair2, one2, one2, pair2, pair2, pair2, pair2, pair2, (6, 2, 8, 128)]
        + [one3] * 9
        + [(48, 128), (48, 256), (12,) + ring1, (12,) + ring1, (4, 16, 128), (12,) + ring0, (12,) + ring0],
        where, *mine, *other, rsx, cxx, cyx, czx, wix, rs, cx0, cy0, cz0, w0,
        v1, f1, w1, cx1, cy1, cz1, v0x,
    )
    return out


def solution(mesh):
    return jax.shard_map(
        body,
        mesh=mesh,
        in_specs=(P("gx", "gy", None), P("gx", "gy", None), P("gx", "gy", None), P()),
        out_specs=P("gx", "gy", None),
        check_vma=False,
    )
```

```python
import functools

import jax
import jax.numpy as jnp
from jax import lax
from jax.experimental import pallas as pl
from jax.experimental.pallas import tpu as pltpu
from jax.sharding import PartitionSpec as P

F32 = jnp.float32
KEEP = 0.2
OMEGA = 0.8
VMEM = pltpu.VMEM
PARAMS = pltpu.CompilerParams(vmem_limit_bytes=48 * 1024 * 1024)


def roll(value, shift, axis):
    return pltpu.roll(value, shift % value.shape[axis], axis)


def iota(shape, dim):
    return lax.broadcasted_iota(jnp.int32, shape, dim)


def pair_sum_matrix():
    return (iota((256, 128), 0) // 2 == iota((256, 128), 1)).astype(F32)


def pair_copy_matrix():
    return (iota((128, 256), 1) // 2 == iota((128, 256), 0)).astype(F32)


def exact_dot(a, b):
    return lax.dot_general(
        a, b, (((1,), (0,)), ((), ())), precision=lax.Precision.HIGHEST, preferred_element_type=F32
    )


def lane_sum(value, matrix):
    width = value.shape[1]
    parts = [exact_dot(value[:, at : at + 256], matrix) for at in range(0, width, 256)]
    return parts[0] if len(parts) == 1 else jnp.concatenate(parts, axis=1)


def lane_copy(value, matrix):
    width = value.shape[1]
    parts = [exact_dot(value[:, at : at + 128], matrix) for at in range(0, width, 128)]
    return parts[0] if len(parts) == 1 else jnp.concatenate(parts, axis=1)


def row_sum(scratch, value):
    rows, width = value.shape
    parts = []
    for c in range(width // 128):
        scratch[c, 0:rows] = value[:, 128 * c : 128 * c + 128]
        first = scratch[c, pl.ds(0, rows // 2, stride=2)]
        parts.append(first + scratch[c, pl.ds(1, rows // 2, stride=2)])
    return parts[0] if len(parts) == 1 else jnp.concatenate(parts, axis=1)


def row_copy(scratch, value):
    rows, width = value.shape
    parts = []
    for c in range(width // 128):
        part = value[:, 128 * c : 128 * c + 128]
        scratch[c, pl.ds(0, rows, stride=2)] = part
        scratch[c, pl.ds(1, rows, stride=2)] = part
        parts.append(scratch[c, 0 : 2 * rows])
    return parts[0] if len(parts) == 1 else jnp.concatenate(parts, axis=1)


def gathered(mid, low, high, cx_low, cx, cy, cz):
    total = cx * high + cx_low * low
    total = total + cy * roll(mid, -1, 0) + roll(cy * mid, 1, 0)
    return total + cz * roll(mid, -1, 1) + roll(cz * mid, 1, 1)


def z_neighbours(mid):
    lane = iota(mid.shape, 1)
    last = mid.shape[1] - 1
    up = jnp.where(lane == last, 0.0, roll(mid, -1, 1))
    down = jnp.where(lane == 0, 0.0, roll(mid, 1, 1))
    return up, down


def diagonal(mid, low, high):
    up, down = z_neighbours(mid)
    total = low + high + roll(mid, -1, 0) + roll(mid, 1, 0) + up + down
    return 3.0 * mid + 0.5 * total


def coupling_y(mid):
    return 0.5 * (mid + roll(mid, -1, 0))


def coupling_z(mid):
    lane = iota(mid.shape, 1)
    return jnp.where(lane == mid.shape[1] - 1, 0.0, 0.5 * (mid + roll(mid, -1, 1)))


def edge_flags(at, grid):
    even = at % 2 == 0
    outside = jnp.logical_or(at == 0, at == grid - 1)
    return even, outside


def start_kernel(
    where_ref, table_hbm, phase_hbm, init_hbm, rhs_hbm,
    kap_ref, init_ref, rhs_ref, near_ref, far_ref, yeven_ref, yodd_ref,
    table_ref, phase_ref, sems,
):
    copies = [
        pltpu.make_async_copy(source, target, sems.at[i])
        for i, (source, target) in enumerate(
            ((table_hbm, table_ref), (phase_hbm, phase_ref), (init_hbm, init_ref), (rhs_hbm, rhs_ref))
        )
    ]
    for copy in copies:
        copy.start()
    for copy in copies:
        copy.wait()
    even = where_ref[0] % 2 == 0
    for x in range(8):
        phase = phase_ref[x]
        kap_ref[x] = jnp.where(
            phase == 0, table_ref[0], jnp.where(phase == 1, table_ref[1], table_ref[2])
        )
    for ref, side in ((near_ref, even), (far_ref, jnp.logical_not(even))):
        deep = jnp.where(side, 5, 0)
        shallow = jnp.where(side, 6, 0)
        for i in range(3):
            ref[i] = kap_ref[deep + i]
            ref[3 + i] = init_ref[deep + i]
        for i in range(2):
            ref[6 + i] = rhs_ref[shallow + i]

    def write(low_ref, high_ref):
        for x in range(8):
            low_ref[x, 0:3] = kap_ref[x, 0:3]
            low_ref[x, 3:6] = init_ref[x, 0:3]
            low_ref[x, 6:8] = rhs_ref[x, 0:2]
            high_ref[x, 0:3] = kap_ref[x, 5:8]
            high_ref[x, 3:6] = init_ref[x, 5:8]
            high_ref[x, 6:8] = rhs_ref[x, 6:8]

    by_parity(where_ref, yeven_ref, yodd_ref, write)


def by_parity(where_ref, even_ref, odd_ref, write):
    even = where_ref[1] % 2 == 0

    @pl.when(even)
    def _():
        write(odd_ref, even_ref)

    @pl.when(jnp.logical_not(even))
    def _():
        write(even_ref, odd_ref)


def y_tiles(where_ref, grid, even_ref, odd_ref, p):
    even, outside = edge_flags(where_ref[1], grid)
    inner = even_ref[p]
    outer = jnp.where(outside, 0.0, odd_ref[p])
    return jnp.where(even, inner, outer), jnp.where(even, outer, inner)


def corner_messages(nx, ny, yeven, yodd):
    even = lax.axis_index("gx") % 2 == 0
    high, low = both_tiles(ny, yeven, yodd)
    top = jnp.concatenate([high[7:8], high[6:7], low[7:8], low[6:7]], axis=0)
    bottom = jnp.concatenate([high[0:2], low[0:2]], axis=0)
    return jnp.where(even, top, bottom), jnp.where(even, bottom, top)


def both_tiles(ny, yeven, yodd):
    at = lax.axis_index("gy")
    even, outside = edge_flags(at, ny)
    outer = jnp.where(outside, 0.0, yodd)
    return jnp.where(even, yeven, outer), jnp.where(even, outer, yeven)


class Planes:
    def __init__(self, middle, outer, first, count):
        self.middle, self.outer, self.first, self.count = middle, outer, first, count

    def find(self, p):
        if p < self.first:
            return self.outer, p
        if p < self.first + self.count:
            return self.middle, p - self.first
        return self.outer, p - self.count

    def __getitem__(self, p):
        ref, at = self.find(p)
        return ref[at]

    def __setitem__(self, p, value):
        ref, at = self.find(p)
        ref[at] = value


def setup0(ks, cx, cy, cz, wi, planes, faces):
    for p in faces:
        cx[p] = 0.5 * (ks[p] + ks[p + 1])
    for p in planes:
        mid = ks[p]
        cy[p] = coupling_y(mid)
        cz[p] = coupling_z(mid)
        diag = diagonal(mid, ks[p - 1], ks[p + 1])
        wi[p] = jnp.where(mid > 0.0, OMEGA / jnp.where(mid > 0.0, diag, 1.0), 0.0)


def sweep0(source, target, rs, cx, cy, cz, wi, planes):
    for p in planes:
        mid = source[p]
        total = gathered(mid, source[p - 1], source[p + 1], cx[p - 1], cx[p], cy[p], cz[p])
        target[p] = KEEP * mid + wi[p] * (rs[p] + total)


def rest0(v2, rs, ks, cx, cy, cz, p):
    mid = v2[p]
    total = gathered(mid, v2[p - 1], v2[p + 1], cx[p - 1], cx[p], cy[p], cz[p])
    diag = diagonal(ks[p], ks[p - 1], ks[p + 1])
    return (rs[p] + total - diag * mid)[0:8]


def add_y_halo(ks, vs, rs, p, high, low):
    zero = jnp.zeros((8, 512), F32)
    ks[p, 8:16] = zero
    vs[p, 8:16] = zero
    rs[p, 8:16] = zero
    ks[p, 8:11] = high[0:3]
    ks[p, 13:16] = low[0:3]
    vs[p, 8:11] = high[3:6]
    vs[p, 13:16] = low[3:6]
    rs[p, 8:10] = high[6:8]
    rs[p, 14:16] = low[6:8]


def early0_kernel(
    ny, where_ref, kap_ref, init_ref, rhs_ref, even_ref, odd_ref,
    ks, vs, rs, cx, cy, cz, wi, v1, v2, rest, kc,
    pair, fine,
):
    for x in range(8):
        ks[x, 0:8] = kap_ref[x]
        vs[x, 0:8] = init_ref[x]
        rs[x, 0:8] = rhs_ref[x]
        add_y_halo(ks, vs, rs, x, *y_tiles(where_ref, ny, even_ref, odd_ref, x))
    ks, vs, rs = (Planes(ref, None, 3, 8) for ref in (ks, vs, rs))
    cx = Planes(cx, None, 3, 7)
    cy, cz, wi, v1 = (Planes(ref, None, 4, 6) for ref in (cy, cz, wi, v1))
    v2 = Planes(v2, None, 5, 4)
    setup0(ks, cx, cy, cz, wi, range(4, 10), range(3, 10))
    sweep0(vs, v1, rs, cx, cy, cz, wi, range(4, 10))
    sweep0(v1, v2, rs, cx, cy, cz, wi, range(5, 9))
    for p in (6, 7):
        rest[p - 6] = rest0(v2, rs, ks, cx, cy, cz, p)
    for x in range(4):
        fine[8 * x : 8 * x + 8] = row_sum(pair, ks[2 * x + 3] + ks[2 * x + 4])
    kc[...] = 0.125 * lane_sum(fine[...], pair_sum_matrix())


def down0_kernel(
    nx, ny, where_ref, near_ref, far_ref, cnear_ref, cfar_ref,
    ks_own, vs_own, rs_own, cx_own, cy_own, cz_own, wi_own, v1_own, v2_own, rest_own, kc,
    v0_ref, rs, cx, cy, cz, wi, block_ref, mnear_ref, mfar_ref, meven_ref, modd_ref,
    ks, vs, v1, v2, pair, fine, coarse,
):
    even, outside = edge_flags(where_ref[0], nx)
    for i in range(3):
        near_at = jnp.where(even, 3 + i, i)
        far_at = jnp.where(even, i, 3 + i)
        for ref, first in ((ks, 0), (vs, 3)):
            ref[near_at, 0:8] = near_ref[first + i]
            ref[far_at, 0:8] = jnp.where(outside, 0.0, far_ref[first + i])
    for i in range(2):
        rs[jnp.where(even, 3 + i, 1 + i), 0:8] = near_ref[6 + i]
        rs[jnp.where(even, 1 + i, 3 + i), 0:8] = jnp.where(outside, 0.0, far_ref[6 + i])
    zero = jnp.zeros((8, 512), F32)
    for p in (0, 5):
        ks[p, 8:16] = zero
        vs[p, 8:16] = zero
        rs[p, 8:16] = zero
    rs[0, 0:8] = zero
    rs[5, 0:8] = zero
    for i in range(2):
        add_y_halo(ks, vs, rs, jnp.where(even, 3 + i, 2 - i), cnear_ref[i], cnear_ref[2 + i])
        add_y_halo(
            ks, vs, rs, jnp.where(even, 2 - i, 3 + i),
            jnp.where(outside, 0.0, cfar_ref[i]), jnp.where(outside, 0.0, cfar_ref[2 + i]),
        )
    ks, vs, rs = (Planes(a, b, 3, 8) for a, b in ((ks_own, ks), (vs_own, vs), (rs_own, rs)))
    cx = Planes(cx_own, cx, 3, 7)
    cy, cz, wi, v1 = (
        Planes(a, b, 4, 6) for a, b in ((cy_own, cy), (cz_own, cz), (wi_own, wi), (v1_own, v1))
    )
    v2 = Planes(v2_own, v2, 5, 4)
    setup0(ks, cx, cy, cz, wi, (1, 2, 3, 10, 11, 12), (0, 1, 2, 10, 11, 12))
    sweep0(vs, v1, rs, cx, cy, cz, wi, (1, 2, 3, 10, 11, 12))
    sweep0(v1, v2, rs, cx, cy, cz, wi, (2, 3, 4, 9, 10, 11))
    for p in range(3, 11, 2):
        both = None
        for q in (p, p + 1):
            rest = rest_own[q - 6] if q in (6, 7) else rest0(v2, rs, ks, cx, cy, cz, q)
            both = rest if both is None else both + rest
            v0_ref[q - 3] = v2[q][0:8]
        at = 2 * (p - 3)
        fine[at : at + 4] = row_sum(pair, both)
    fine[16:24] = row_sum(pair, ks[1] + ks[2])
    fine[24:32] = row_sum(pair, ks[11] + ks[12])
    coarse[...] = lane_sum(fine[...], pair_sum_matrix())
    kept = [0.125 * coarse[16:24]] + [kc[8 * x : 8 * x + 8] for x in range(4)]
    kept.append(0.125 * coarse[24:32])
    for x in range(4):
        half = pl.ds(256 * (x % 2), 256)
        mid = kept[x + 1]
        block_ref[x // 2, 0:4, half] = 0.5 * coarse[4 * x : 4 * x + 4]
        block_ref[x // 2, 4:8, half] = mid[0:4]
        at = 4 * (x // 2)
        block_ref[2, at : at + 4, half] = (OMEGA / diagonal(mid, kept[x], kept[x + 2])[0:4])
    for ref, side in ((mnear_ref, even), (mfar_ref, jnp.logical_not(even))):
        shallow = jnp.where(side, 6, 0)
        for i in range(3):
            ref[i] = block_ref[i]
        for i in range(2):
            ref[3 + i] = v0_ref[shallow + i]

    def write(low_ref, high_ref):
        for i in range(3):
            low_ref[i] = block_ref[i]
            high_ref[i] = block_ref[i]
        for x in range(8):
            at = 2 * (x % 4)
            low_ref[3 + x // 4, at : at + 2] = v0_ref[x, 0:2]
            high_ref[3 + x // 4, at : at + 2] = v0_ref[x, 6:8]

    by_parity(where_ref, meven_ref, modd_ref, write)


def corner1_message(ny, meven, modd):
    high, low = both_tiles(ny, meven, modd)
    rows = [high[4:5, 6:8], low[4:5, 6:8], high[3:4, 0:2], low[3:4, 0:2]]
    return jnp.concatenate([high[0:3], low[0:3], jnp.concatenate(rows, axis=1)], axis=0)


def down1_kernel(
    nx, ny, where_ref, block_ref, v0_ref, near_ref, far_ref, meven_ref, modd_ref,
    cnear_ref, cfar_ref,
    v0x, v1, f1, w1, cx, cy, cz, send_ref,
    k1, u1, pair, fine,
):
    even, outside = edge_flags(where_ref[0], nx)

    def inside(value):
        return jnp.where(outside, 0.0, value)

    near = [near_ref[i] for i in range(3)]
    far = [inside(far_ref[i]) for i in range(3)]
    cnear = [cnear_ref[i] for i in range(7)]
    cfar = [inside(cfar_ref[i]) for i in range(7)]
    mine = [y_tiles(where_ref, ny, meven_ref, modd_ref, i) for i in range(5)]

    def pick(a, b):
        return [jnp.where(even, p, q) for p, q in zip(a, b)]

    blocks = (
        (pick(far, near), pick(cfar[0:3], cnear[0:3]), pick(cfar[3:6], cnear[3:6])),
        ([block_ref[i] for i in range(3)], [t[0] for t in mine], [t[1] for t in mine]),
        (pick(near, far), pick(cnear[0:3], cfar[0:3]), pick(cnear[3:6], cfar[3:6])),
    )
    zero = jnp.zeros((4, 256), F32)
    for b in range(3):
        for x in range(4):
            p = 4 * b + x
            half = slice(256 * (x % 2), 256 * (x % 2) + 256)
            t = x // 2
            for ref, at, row in (
                (f1, t, slice(0, 4)), (k1, t, slice(4, 8)), (w1, 2, slice(4 * t, 4 * t + 4))
            ):
                ref[p, 0:4] = blocks[b][0][at][row, half]
                ref[p, 4:8] = blocks[b][1][at][row, half]
                ref[p, 8:12] = zero
                ref[p, 12:16] = blocks[b][2][at][row, half]
    blank = jnp.zeros((8, 512), F32)
    for p in range(12):
        v0x[p, 8:16] = blank
    for x in range(8):
        v0x[2 + x, 0:8] = v0_ref[x]
        at = 2 * (x % 4)
        v0x[2 + x, 8:10] = mine[3 + x // 4][0][at : at + 2]
        v0x[2 + x, 14:16] = mine[3 + x // 4][1][at : at + 2]
    near_at = jnp.where(even, 10, 0)
    far_at = jnp.where(even, 0, 10)
    for i in range(2):
        v0x[near_at + i, 0:8] = near_ref[3 + i]
        v0x[far_at + i, 0:8] = inside(far_ref[3 + i])
    low_tile = jnp.where(even, cfar[6], cnear[6])
    high_tile = jnp.where(even, cnear[6], cfar[6])
    for at, tile, row in ((1, low_tile, 0), (10, high_tile, 4)):
        v0x[at, 8:10] = tile[row : row + 2]
        v0x[at, 14:16] = tile[row + 2 : row + 4]
    for p in range(12):
        u1[p] = w1[p] * f1[p]
        if p < 11:
            cx[p] = 0.5 * (k1[p] + k1[p + 1])
        cy[p] = coupling_y(k1[p])
        cz[p] = coupling_z(k1[p])
    for p in range(1, 11):
        mid = u1[p]
        total = gathered(mid, u1[p - 1], u1[p + 1], cx[p - 1], cx[p], cy[p], cz[p])
        v1[p] = KEEP * mid + w1[p] * (f1[p] + total)
    for p in range(4, 8, 2):
        both = None
        for q in (p, p + 1):
            mid = v1[q]
            total = gathered(mid, v1[q - 1], v1[q + 1], cx[q - 1], cx[q], cy[q], cz[q])
            diag = diagonal(k1[q], k1[q - 1], k1[q + 1])
            rest = (f1[q] + total - diag * mid)[0:8]
            both = rest if both is None else both + rest
        at = p - 4
        fine[at : at + 2] = 0.5 * row_sum(pair, both)[0:2]
        kept = k1[p, 0:8] + k1[p + 1, 0:8]
        fine[4 + at : 6 + at] = 0.125 * row_sum(pair, kept)[0:2]
    tile = lane_sum(fine[...], pair_sum_matrix())
    for i in range(send_ref.shape[0]):
        send_ref[i] = tile


def up_kernel(
    nx, ny, where_ref, *refs
):
    half = nx // 2
    columns = (refs[:half], refs[half : 2 * half])
    own, far = refs[nx : nx + 5], refs[nx + 5 : nx + 10]
    rs = Planes(own[0], far[0], 3, 8)
    cx0 = Planes(own[1], far[1], 3, 7)
    cy0, cz0, w0 = (Planes(a, b, 4, 6) for a, b in zip(own[2:], far[2:]))
    up_levels(nx, ny, where_ref, columns, rs, cx0, cy0, cz0, w0, *refs[nx + 10 :])


def up_levels(
    nx, ny, where_ref, columns, rs, cx0, cy0, cz0, w0, v1, f1, w1, cx1, cy1, cz1, v0x, out_ref,
    f2, k2, cx2, cyi, cyo, cz2, w2, d2, u2, v2, e2, f3, k3, cx3, cy3, cz3, w3, edge3, ga, gb,
    small, wide, e1a, e1b, narrow, e0a, e0b,
):
    gx = where_ref[0]
    gy = where_ref[1]
    core = gx % 2
    n2 = 2 * nx
    zero = jnp.zeros((ny, 128), F32)
    row = iota((ny, 128), 0)
    lane = iota((ny, 128), 1)
    last_row = row == ny - 1
    for s in range(2):
        k2[0, s] = zero
        k2[n2 + 1, s] = zero
        u2[0, s] = zero
        u2[n2 + 1, s] = zero
        v2[0, s] = zero
        v2[n2 + 1, s] = zero
    for j in range(nx // 2):
        chip = (gx // 2) ^ j
        for refs, which in ((columns[0], core), (columns[1], 1 - core)):
            for i in range(2):
                p = 4 * chip + 2 * which + i + 1
                for s in range(2):
                    f2[p, s] = refs[j][2 * i + s]
                    k2[p, s] = refs[j][4 + 2 * i + s]
    for p in range(n2 + 1):
        for s in range(2):
            cx2[p, s] = 0.5 * (k2[p, s] + k2[p + 1, s])
    for p in range(1, n2 + 1):
        k_low, k_high = k2[p, 0], k2[p, 1]
        after = jnp.where(last_row, 0.0, roll(k_low, -1, 0))
        before = jnp.where(row == 0, 0.0, roll(k_high, 1, 0))
        cyi[p] = 0.5 * (k_low + k_high)
        cyo[p] = jnp.where(last_row, 0.0, 0.5 * (k_high + after))
        for s, mid, ya, yb in ((0, k_low, k_high, before), (1, k_high, k_low, after)):
            up, down = z_neighbours(mid)
            cz2[p, s] = jnp.where(lane == 127, 0.0, 0.5 * (mid + up))
            diag = 3.0 * mid + 0.5 * (k2[p - 1, s] + k2[p + 1, s] + ya + yb + up + down)
            scale = OMEGA / diag
            d2[p, s] = diag
            w2[p, s] = scale
            u2[p, s] = scale * f2[p, s]

    def gather2(ref, p):
        low, high = ref[p, 0], ref[p, 1]
        sums = []
        for s, mid in ((0, low), (1, high)):
            total = cx2[p, s] * ref[p + 1, s] + cx2[p - 1, s] * ref[p - 1, s]
            total = total + cz2[p, s] * roll(mid, -1, 1) + roll(cz2[p, s] * mid, 1, 1)
            sums.append(total)
        sums[0] = sums[0] + cyi[p] * high + roll(cyo[p] * high, 1, 0)
        sums[1] = sums[1] + cyi[p] * low + cyo[p] * roll(low, -1, 0)
        return (low, high), sums

    def sweep2(source, target):
        for p in range(1, n2 + 1):
            mids, sums = gather2(source, p)
            for s in range(2):
                target[p, s] = KEEP * mids[s] + w2[p, s] * (f2[p, s] + sums[s])

    sweep2(u2, v2)
    even_lane = lane % 2 == 0

    def pair_lanes(value):
        return value + jnp.where(even_lane, roll(value, -1, 1), roll(value, 1, 1))

    k3[0] = zero
    k3[nx + 1] = zero
    ga[0] = zero
    ga[nx + 1] = zero
    gb[0] = zero
    gb[nx + 1] = zero
    for x in range(nx):
        both = None
        kept = None
        for p in (2 * x + 1, 2 * x + 2):
            mids, sums = gather2(v2, p)
            for s in range(2):
                rest = f2[p, s] + sums[s] - d2[p, s] * mids[s]
                both = rest if both is None else both + rest
                kept = k2[p, s] if kept is None else kept + k2[p, s]
        f3[x + 1] = 0.5 * pair_lanes(both)
        k3[x + 1] = 0.125 * pair_lanes(kept)
    for p in range(nx + 1):
        cx3[p] = 0.5 * (k3[p] + k3[p + 1])
    edge_total = zero
    rest_total = zero
    outer = (
        (row == 0).astype(F32) + last_row.astype(F32)
        + (lane < 2).astype(F32) + (lane >= 126).astype(F32)
    )
    for p in range(1, nx + 1):
        mid = k3[p]
        after = jnp.where(last_row, 0.0, roll(mid, -1, 0))
        before = jnp.where(row == 0, 0.0, roll(mid, 1, 0))
        up = jnp.where(lane >= 126, 0.0, roll(mid, -2, 1))
        down = jnp.where(lane < 2, 0.0, roll(mid, 2, 1))
        cy3[p] = jnp.where(last_row, 0.0, 0.5 * (mid + after))
        cz3[p] = jnp.where(lane >= 126, 0.0, 0.5 * (mid + up))
        diag = 3.0 * mid + 0.5 * (k3[p - 1] + k3[p + 1] + after + before + up + down)
        scale = OMEGA / diag
        w3[p] = scale
        ga[p] = scale * f3[p]
        faces = outer + (1.0 if p == 1 else 0.0) + (1.0 if p == nx else 0.0)
        edge = 0.5 * mid * faces
        edge3[p] = edge
        edge_total = edge_total + edge
        rest_total = rest_total + f3[p]

    def gather3(ref, p):
        mid = ref[p]
        total = cx3[p] * ref[p + 1] + cx3[p - 1] * ref[p - 1]
        total = total + cy3[p] * roll(mid, -1, 0) + roll(cy3[p] * mid, 1, 0)
        return mid, total + cz3[p] * roll(mid, -2, 1) + roll(cz3[p] * mid, 2, 1)

    source, target = ga, gb
    for _ in range(7):
        for p in range(1, nx + 1):
            mid, total = gather3(source, p)
            target[p] = KEEP * mid + w3[p] * (f3[p] + total)
        source, target = target, source
    for p in range(1, nx + 1):
        rest_total = rest_total - edge3[p] * source[p]

    def whole(value):
        return jnp.sum(jnp.sum(value, axis=0, keepdims=True), axis=1, keepdims=True)

    shift = whole(rest_total) / whole(edge_total)
    first_row = jnp.clip(gy - 3, 0, ny - 8)
    rows = pl.ds(first_row, 8)
    no_wrap = iota((8, 128), 0) < 7
    planes = []
    for j in range(10):
        x = 2 * gx - 4 + j
        planes.append((jnp.logical_and(x >= 0, x < n2), jnp.clip(x, 0, n2 - 1)))
    level = []
    for ok, q in planes:
        e3 = source[q // 2 + 1, rows] + shift
        level.append([jnp.where(ok, v2[q + 1, s, rows] + e3, 0.0) for s in range(2)])
    for first, last in ((1, 8), (2, 7)):
        done = list(level)
        for j in range(first, last + 1):
            ok, q = planes[j]
            low, high = level[j]
            inner = cyi[q + 1, rows]
            after = jnp.where(no_wrap, cyo[q + 1, rows], 0.0)
            sums = [inner * high + roll(after * high, 1, 0), inner * low + after * roll(low, -1, 0)]
            for s in range(2):
                mid = level[j][s]
                cz = cz2[q + 1, s, rows]
                total = sums[s] + cz * roll(mid, -1, 1) + roll(cz * mid, 1, 1)
                total = total + cx2[q + 1, s, rows] * level[j + 1][s]
                total = total + cx2[q, s, rows] * level[j - 1][s]
                value = KEEP * mid + w2[q + 1, s, rows] * (f2[q + 1, s, rows] + total)
                done[j] = [jnp.where(ok, value, 0.0)] if s == 0 else done[j] + [jnp.where(ok, value, 0.0)]
        level = done
    copies = pair_copy_matrix()
    at = gy - first_row
    steps = (
        (0, at, None),
        (2, jnp.minimum(at + 1, 7), gy < ny - 1),
        (6, jnp.maximum(at - 1, 0), gy > 0),
    )
    for i in range(6):
        small[8 * i + 4 : 8 * i + 6] = jnp.zeros((2, 128), F32)
        for s in range(2):
            e2[i, s] = level[i + 2][s]
            for j, r, ok in steps:
                line = e2[i, s, pl.ds(r, 1)]
                small[8 * i + j + s : 8 * i + j + s + 1] = (
                    line if ok is None else jnp.where(ok, line, 0.0)
                )
    wide[...] = lane_copy(small[...], copies)
    for i in range(6):
        spread = row_copy(narrow, wide[8 * i : 8 * i + 8])
        for p in (2 * i, 2 * i + 1):
            if 1 <= p <= 10:
                e1a[p] = v1[p] + spread
    for source, target, first, last in ((e1a, e1b, 2, 9), (e1b, e1a, 3, 8)):
        for p in range(first, last + 1):
            mid = source[p]
            total = gathered(
                mid, source[p - 1], source[p + 1], cx1[p - 1], cx1[p], cy1[p], cz1[p]
            )
            target[p] = KEEP * mid + w1[p] * (f1[p] + total)
    row8 = iota((8, 256), 0)
    for i in range(6):
        value = e1a[i + 3]
        wide[8 * i : 8 * i + 8] = jnp.where(row8 == 7, value[8:16], value[0:8])
    doubled = lane_copy(wide[...], copies)
    for i in range(6):
        spread = row_copy(narrow, doubled[8 * i : 8 * i + 8])
        for p in (2 * i, 2 * i + 1):
            e0a[p] = v0x[p] + spread
    for p in range(1, 11):
        mid = e0a[p]
        total = gathered(
            mid, e0a[p - 1], e0a[p + 1], cx0[p], cx0[p + 1], cy0[p + 1], cz0[p + 1]
        )
        e0b[p] = KEEP * mid + w0[p + 1] * (rs[p + 1] + total)
    for p in range(2, 10):
        mid = e0b[p]
        total = gathered(
            mid, e0b[p - 1], e0b[p + 1], cx0[p], cx0[p + 1], cy0[p + 1], cz0[p + 1]
        )
        out_ref[p - 2] = (KEEP * mid + w0[p + 1] * (rs[p + 1] + total))[0:8]


def run(kernel, outs, scratch, where, *operands, space=VMEM, cost=None):
    return pl.pallas_call(
        kernel,
        out_shape=[jax.ShapeDtypeStruct(shape, F32) for shape in outs],
        in_specs=[pl.BlockSpec(memory_space=pltpu.SMEM)]
        + [pl.BlockSpec(memory_space=space)] * len(operands),
        out_specs=[pl.BlockSpec(memory_space=VMEM)] * len(outs),
        scratch_shapes=[VMEM(s, F32) if isinstance(s, tuple) else s for s in scratch],
        compiler_params=PARAMS,
        cost_estimate=cost,
    )(where, *operands)


def body(initial, right_side, phase_map, phase_table):
    nx, ny = lax.axis_size("gx"), lax.axis_size("gy")
    where = jnp.stack([lax.axis_index("gx"), lax.axis_index("gy")]).astype(jnp.int32)

    def pairs(partner):
        return [
            (x * ny + y, px * ny + py)
            for x in range(nx)
            for y in range(ny)
            for px, py in [partner(x, y)]
        ]

    def beyond(at, size):
        other = at + 1 if at % 2 else at - 1
        return other if 0 <= other < size else None

    def far_x(x, y):
        other = beyond(x, nx)
        return (x, y ^ 1) if other is None else (other, y)

    def far_y(x, y):
        other = beyond(y, ny)
        return (x ^ 1, y) if other is None else (x, other)

    both = ("gx", "gy")

    def swap_x(near, far):
        return (
            lax.ppermute(near, both, pairs(lambda x, y: (x ^ 1, y))),
            lax.ppermute(far, both, pairs(far_x)),
        )

    def swap_y(near, far):
        return (
            lax.ppermute(near, both, pairs(lambda x, y: (x, y ^ 1))),
            lax.ppermute(far, both, pairs(far_y)),
        )

    inputs = [
        pltpu.with_memory_space_constraint(value, pltpu.HBM)
        for value in (phase_table, phase_map, initial, right_side)
    ]
    early_cost = pl.CostEstimate(flops=20_000_000, bytes_accessed=4_000_000, transcendentals=0)
    tile0 = (8, 512)
    ring0 = (16, 512)
    ring1 = (16, 256)
    kappa, init, rhs, near, far, yeven, yodd = run(
        start_kernel, [(8,) + tile0] * 7,
        [pltpu.SMEM((3,), F32), VMEM((8,) + tile0, jnp.int32), pltpu.SemaphoreType.DMA((4,))],
        where, *inputs, space=pltpu.HBM,
    )
    yeven, yodd = swap_y(yeven, yodd)
    near, far = swap_x(near, far)
    yodd, yeven, far, near = lax.optimization_barrier((yodd, yeven, far, near))
    cnear, cfar = swap_x(*corner_messages(nx, ny, yeven, yodd))
    ksx, vsx, rsx, cxx, cyx, czx, wix, v1x, v2x, restx, kcx = run(
        functools.partial(early0_kernel, ny),
        [(8,) + ring0] * 3 + [(7,) + ring0] + [(6,) + ring0] * 4
        + [(4,) + ring0, (2,) + tile0, (32, 256)],
        [(4, 16, 128), (32, 512)],
        where, kappa, init, rhs, yeven, yodd, cost=early_cost,
    )
    v0, rs, cx0, cy0, cz0, w0, block, mnear, mfar, meven, modd = run(
        functools.partial(down0_kernel, nx, ny),
        [(8,) + tile0]
        + [(6,) + ring0, (6,) + ring0]
        + [(8,) + ring0] * 3
        + [(3,) + tile0]
        + [(5,) + tile0] * 4,
        [(6,) + ring0] * 2 + [(8,) + ring0, (10,) + ring0, (4, 16, 128), (32, 512), (32, 256)],
        where, near, far, cnear, cfar,
        ksx, vsx, rsx, cxx, cyx, czx, wix, v1x, v2x, restx, kcx,
    )
    meven, modd = swap_y(meven, modd)
    mnear, mfar = swap_x(mnear, mfar)
    modd, meven, mfar, mnear = lax.optimization_barrier((modd, meven, mfar, mnear))
    corner = corner1_message(ny, meven, modd)
    cnear, cfar = swap_x(corner, corner)
    v0x, v1, f1, w1, cx1, cy1, cz1, send = run(
        functools.partial(down1_kernel, nx, ny),
        [(12,) + ring0] + [(12,) + ring1] * 6 + [(ny, 8, 128)],
        [(12,) + ring1, (12,) + ring1, (4, 16, 128), (8, 256)],
        where, block, v0, mnear, mfar, meven, modd, cnear, cfar,
    )
    column = jnp.transpose(lax.all_to_all(send, "gy", 0, 0), (1, 0, 2))

    def chips_apart(j):
        return pairs(lambda x, y: (((x // 2) ^ j) * 2 + x % 2, y))

    mine = {0: column}
    for j in sorted(range(1, nx // 2), key=lambda j: j != 2):
        mine[j] = lax.ppermute(column, both, chips_apart(j))
    mine = [mine[j] for j in range(nx // 2)]
    other = [lax.ppermute(c, both, pairs(lambda x, y: (x ^ 1, y))) for c in mine]
    n2 = 2 * nx
    pair2 = (n2 + 2, 2, ny, 128)
    one2 = (n2 + 2, ny, 128)
    one3 = (nx + 2, ny, 128)
    (out,) = run(
        functools.partial(up_kernel, nx, ny), [(8,) + tile0],
        [pair2, pair2, pair2, one2, one2, pair2, pair2, pair2, pair2, pair2, (6, 2, 8, 128)]
        + [one3] * 9
        + [(48, 128), (48, 256), (12,) + ring1, (12,) + ring1, (4, 16, 128), (12,) + ring0, (12,) + ring0],
        where, *mine, *other, rsx, cxx, cyx, czx, wix, rs, cx0, cy0, cz0, w0,
        v1, f1, w1, cx1, cy1, cz1, v0x,
    )
    return out


def solution(mesh):
    return jax.shard_map(
        body,
        mesh=mesh,
        in_specs=(P("gx", "gy", None), P("gx", "gy", None), P("gx", "gy", None), P()),
        out_specs=P("gx", "gy", None),
        check_vma=False,
    )
```

```python
import functools

import jax
import jax.numpy as jnp
from jax import lax
from jax.experimental import pallas as pl
from jax.experimental.pallas import tpu as pltpu
from jax.sharding import PartitionSpec as P

F32 = jnp.float32
KEEP = 0.2
OMEGA = 0.8
VMEM = pltpu.VMEM
PARAMS = pltpu.CompilerParams(vmem_limit_bytes=48 * 1024 * 1024)


def roll(value, shift, axis):
    return pltpu.roll(value, shift % value.shape[axis], axis)


def iota(shape, dim):
    return lax.broadcasted_iota(jnp.int32, shape, dim)


def pair_sum_matrix():
    return (iota((256, 128), 0) // 2 == iota((256, 128), 1)).astype(F32)


def pair_copy_matrix():
    return (iota((128, 256), 1) // 2 == iota((128, 256), 0)).astype(F32)


def exact_dot(a, b):
    return lax.dot_general(
        a, b, (((1,), (0,)), ((), ())), precision=lax.Precision.HIGHEST, preferred_element_type=F32
    )


def lane_sum(value, matrix):
    width = value.shape[1]
    parts = [exact_dot(value[:, at : at + 256], matrix) for at in range(0, width, 256)]
    return parts[0] if len(parts) == 1 else jnp.concatenate(parts, axis=1)


def lane_copy(value, matrix):
    width = value.shape[1]
    parts = [exact_dot(value[:, at : at + 128], matrix) for at in range(0, width, 128)]
    return parts[0] if len(parts) == 1 else jnp.concatenate(parts, axis=1)


def row_sum(scratch, value):
    rows, width = value.shape
    parts = []
    for c in range(width // 128):
        scratch[c, 0:rows] = value[:, 128 * c : 128 * c + 128]
        first = scratch[c, pl.ds(0, rows // 2, stride=2)]
        parts.append(first + scratch[c, pl.ds(1, rows // 2, stride=2)])
    return parts[0] if len(parts) == 1 else jnp.concatenate(parts, axis=1)


def row_copy(scratch, value):
    rows, width = value.shape
    parts = []
    for c in range(width // 128):
        part = value[:, 128 * c : 128 * c + 128]
        scratch[c, pl.ds(0, rows, stride=2)] = part
        scratch[c, pl.ds(1, rows, stride=2)] = part
        parts.append(scratch[c, 0 : 2 * rows])
    return parts[0] if len(parts) == 1 else jnp.concatenate(parts, axis=1)


def gathered(mid, low, high, cx_low, cx, cy, cz):
    total = cx * high + cx_low * low
    total = total + cy * roll(mid, -1, 0) + roll(cy * mid, 1, 0)
    return total + cz * roll(mid, -1, 1) + roll(cz * mid, 1, 1)


def z_neighbours(mid):
    lane = iota(mid.shape, 1)
    last = mid.shape[1] - 1
    up = jnp.where(lane == last, 0.0, roll(mid, -1, 1))
    down = jnp.where(lane == 0, 0.0, roll(mid, 1, 1))
    return up, down


def diagonal(mid, low, high):
    up, down = z_neighbours(mid)
    total = low + high + roll(mid, -1, 0) + roll(mid, 1, 0) + up + down
    return 3.0 * mid + 0.5 * total


def coupling_y(mid):
    return 0.5 * (mid + roll(mid, -1, 0))


def coupling_z(mid):
    lane = iota(mid.shape, 1)
    return jnp.where(lane == mid.shape[1] - 1, 0.0, 0.5 * (mid + roll(mid, -1, 1)))


def edge_flags(at, grid):
    even = at % 2 == 0
    outside = jnp.logical_or(at == 0, at == grid - 1)
    return even, outside


def start_kernel(
    where_ref, table_hbm, phase_hbm, init_hbm, rhs_hbm,
    kap_ref, init_ref, rhs_ref, near_ref, far_ref, yeven_ref, yodd_ref,
    table_ref, phase_ref, sems,
):
    copies = [
        pltpu.make_async_copy(source, target, sems.at[i])
        for i, (source, target) in enumerate(
            ((table_hbm, table_ref), (phase_hbm, phase_ref), (init_hbm, init_ref), (rhs_hbm, rhs_ref))
        )
    ]
    for copy in copies:
        copy.start()
    for copy in copies:
        copy.wait()
    even = where_ref[0] % 2 == 0
    for x in range(8):
        phase = phase_ref[x]
        kap_ref[x] = jnp.where(
            phase == 0, table_ref[0], jnp.where(phase == 1, table_ref[1], table_ref[2])
        )
    for ref, side in ((near_ref, even), (far_ref, jnp.logical_not(even))):
        deep = jnp.where(side, 5, 0)
        shallow = jnp.where(side, 6, 0)
        for i in range(3):
            ref[i] = kap_ref[deep + i]
            ref[3 + i] = init_ref[deep + i]
        for i in range(2):
            ref[6 + i] = rhs_ref[shallow + i]

    def write(low_ref, high_ref):
        for x in range(8):
            low_ref[x, 0:3] = kap_ref[x, 0:3]
            low_ref[x, 3:6] = init_ref[x, 0:3]
            low_ref[x, 6:8] = rhs_ref[x, 0:2]
            high_ref[x, 0:3] = kap_ref[x, 5:8]
            high_ref[x, 3:6] = init_ref[x, 5:8]
            high_ref[x, 6:8] = rhs_ref[x, 6:8]

    by_parity(where_ref, yeven_ref, yodd_ref, write)


def by_parity(where_ref, even_ref, odd_ref, write):
    even = where_ref[1] % 2 == 0

    @pl.when(even)
    def _():
        write(odd_ref, even_ref)

    @pl.when(jnp.logical_not(even))
    def _():
        write(even_ref, odd_ref)


def y_tiles(where_ref, grid, even_ref, odd_ref, p):
    even, outside = edge_flags(where_ref[1], grid)
    inner = even_ref[p]
    outer = jnp.where(outside, 0.0, odd_ref[p])
    return jnp.where(even, inner, outer), jnp.where(even, outer, inner)


def corner_messages(nx, ny, yeven, yodd):
    even = lax.axis_index("gx") % 2 == 0
    high, low = both_tiles(ny, yeven, yodd)
    top = jnp.concatenate([high[7:8], high[6:7], low[7:8], low[6:7]], axis=0)
    bottom = jnp.concatenate([high[0:2], low[0:2]], axis=0)
    return jnp.where(even, top, bottom), jnp.where(even, bottom, top)


def both_tiles(ny, yeven, yodd):
    at = lax.axis_index("gy")
    even, outside = edge_flags(at, ny)
    outer = jnp.where(outside, 0.0, yodd)
    return jnp.where(even, yeven, outer), jnp.where(even, outer, yeven)


class Planes:
    def __init__(self, middle, outer, first, count):
        self.middle, self.outer, self.first, self.count = middle, outer, first, count

    def find(self, p):
        if p < self.first:
            return self.outer, p
        if p < self.first + self.count:
            return self.middle, p - self.first
        return self.outer, p - self.count

    def __getitem__(self, p):
        ref, at = self.find(p)
        return ref[at]

    def __setitem__(self, p, value):
        ref, at = self.find(p)
        ref[at] = value


def setup0(ks, cx, cy, cz, wi, planes, faces):
    for p in faces:
        cx[p] = 0.5 * (ks[p] + ks[p + 1])
    for p in planes:
        mid = ks[p]
        cy[p] = coupling_y(mid)
        cz[p] = coupling_z(mid)
        diag = diagonal(mid, ks[p - 1], ks[p + 1])
        wi[p] = jnp.where(mid > 0.0, OMEGA / jnp.where(mid > 0.0, diag, 1.0), 0.0)


def sweep0(source, target, rs, cx, cy, cz, wi, planes):
    for p in planes:
        mid = source[p]
        total = gathered(mid, source[p - 1], source[p + 1], cx[p - 1], cx[p], cy[p], cz[p])
        target[p] = KEEP * mid + wi[p] * (rs[p] + total)


def rest0(v2, rs, ks, cx, cy, cz, p):
    mid = v2[p]
    total = gathered(mid, v2[p - 1], v2[p + 1], cx[p - 1], cx[p], cy[p], cz[p])
    diag = diagonal(ks[p], ks[p - 1], ks[p + 1])
    return (rs[p] + total - diag * mid)[0:8]


def add_y_halo(ks, vs, rs, p, high, low):
    zero = jnp.zeros((8, 512), F32)
    ks[p, 8:16] = zero
    vs[p, 8:16] = zero
    rs[p, 8:16] = zero
    ks[p, 8:11] = high[0:3]
    ks[p, 13:16] = low[0:3]
    vs[p, 8:11] = high[3:6]
    vs[p, 13:16] = low[3:6]
    rs[p, 8:10] = high[6:8]
    rs[p, 14:16] = low[6:8]


def early0_kernel(
    ny, where_ref, kap_ref, init_ref, rhs_ref, even_ref, odd_ref,
    ks, vs, rs, cx, cy, cz, wi, v1, v2, rest, kc,
    pair, fine,
):
    for x in range(8):
        ks[x, 0:8] = kap_ref[x]
        vs[x, 0:8] = init_ref[x]
        rs[x, 0:8] = rhs_ref[x]
        add_y_halo(ks, vs, rs, x, *y_tiles(where_ref, ny, even_ref, odd_ref, x))
    ks, vs, rs = (Planes(ref, None, 3, 8) for ref in (ks, vs, rs))
    cx = Planes(cx, None, 3, 7)
    cy, cz, wi, v1 = (Planes(ref, None, 4, 6) for ref in (cy, cz, wi, v1))
    v2 = Planes(v2, None, 5, 4)
    setup0(ks, cx, cy, cz, wi, range(4, 10), range(3, 10))
    sweep0(vs, v1, rs, cx, cy, cz, wi, range(4, 10))
    sweep0(v1, v2, rs, cx, cy, cz, wi, range(5, 9))
    for p in (6, 7):
        rest[p - 6] = rest0(v2, rs, ks, cx, cy, cz, p)
    for x in range(4):
        fine[8 * x : 8 * x + 8] = row_sum(pair, ks[2 * x + 3] + ks[2 * x + 4])
    kc[...] = 0.125 * lane_sum(fine[...], pair_sum_matrix())


def down0_kernel(
    nx, ny, where_ref, near_ref, far_ref, cnear_ref, cfar_ref,
    ks_own, vs_own, rs_own, cx_own, cy_own, cz_own, wi_own, v1_own, v2_own, rest_own, kc,
    v0_ref, rs, cx, cy, cz, wi, block_ref, mnear_ref, mfar_ref, meven_ref, modd_ref,
    ks, vs, v1, v2, pair, fine, coarse,
):
    even, outside = edge_flags(where_ref[0], nx)
    for i in range(3):
        near_at = jnp.where(even, 3 + i, i)
        far_at = jnp.where(even, i, 3 + i)
        for ref, first in ((ks, 0), (vs, 3)):
            ref[near_at, 0:8] = near_ref[first + i]
            ref[far_at, 0:8] = jnp.where(outside, 0.0, far_ref[first + i])
    for i in range(2):
        rs[jnp.where(even, 3 + i, 1 + i), 0:8] = near_ref[6 + i]
        rs[jnp.where(even, 1 + i, 3 + i), 0:8] = jnp.where(outside, 0.0, far_ref[6 + i])
    zero = jnp.zeros((8, 512), F32)
    for p in (0, 5):
        ks[p, 8:16] = zero
        vs[p, 8:16] = zero
        rs[p, 8:16] = zero
    rs[0, 0:8] = zero
    rs[5, 0:8] = zero
    for i in range(2):
        add_y_halo(ks, vs, rs, jnp.where(even, 3 + i, 2 - i), cnear_ref[i], cnear_ref[2 + i])
        add_y_halo(
            ks, vs, rs, jnp.where(even, 2 - i, 3 + i),
            jnp.where(outside, 0.0, cfar_ref[i]), jnp.where(outside, 0.0, cfar_ref[2 + i]),
        )
    ks, vs, rs = (Planes(a, b, 3, 8) for a, b in ((ks_own, ks), (vs_own, vs), (rs_own, rs)))
    cx = Planes(cx_own, cx, 3, 7)
    cy, cz, wi, v1 = (
        Planes(a, b, 4, 6) for a, b in ((cy_own, cy), (cz_own, cz), (wi_own, wi), (v1_own, v1))
    )
    v2 = Planes(v2_own, v2, 5, 4)
    setup0(ks, cx, cy, cz, wi, (1, 2, 3, 10, 11, 12), (0, 1, 2, 10, 11, 12))
    sweep0(vs, v1, rs, cx, cy, cz, wi, (1, 2, 3, 10, 11, 12))
    sweep0(v1, v2, rs, cx, cy, cz, wi, (2, 3, 4, 9, 10, 11))
    for p in range(3, 11, 2):
        both = None
        for q in (p, p + 1):
            rest = rest_own[q - 6] if q in (6, 7) else rest0(v2, rs, ks, cx, cy, cz, q)
            both = rest if both is None else both + rest
            v0_ref[q - 3] = v2[q][0:8]
        at = 2 * (p - 3)
        fine[at : at + 4] = row_sum(pair, both)
    fine[16:24] = row_sum(pair, ks[1] + ks[2])
    fine[24:32] = row_sum(pair, ks[11] + ks[12])
    coarse[...] = lane_sum(fine[...], pair_sum_matrix())
    kept = [0.125 * coarse[16:24]] + [kc[8 * x : 8 * x + 8] for x in range(4)]
    kept.append(0.125 * coarse[24:32])
    for x in range(4):
        half = pl.ds(256 * (x % 2), 256)
        mid = kept[x + 1]
        block_ref[x // 2, 0:4, half] = 0.5 * coarse[4 * x : 4 * x + 4]
        block_ref[x // 2, 4:8, half] = mid[0:4]
        at = 4 * (x // 2)
        block_ref[2, at : at + 4, half] = (OMEGA / diagonal(mid, kept[x], kept[x + 2])[0:4])
    for ref, side in ((mnear_ref, even), (mfar_ref, jnp.logical_not(even))):
        shallow = jnp.where(side, 6, 0)
        for i in range(3):
            ref[i] = block_ref[i]
        for i in range(2):
            ref[3 + i] = v0_ref[shallow + i]

    def write(low_ref, high_ref):
        for i in range(3):
            low_ref[i] = block_ref[i]
            high_ref[i] = block_ref[i]
        for x in range(8):
            at = 2 * (x % 4)
            low_ref[3 + x // 4, at : at + 2] = v0_ref[x, 0:2]
            high_ref[3 + x // 4, at : at + 2] = v0_ref[x, 6:8]

    by_parity(where_ref, meven_ref, modd_ref, write)


def corner1_message(ny, meven, modd):
    high, low = both_tiles(ny, meven, modd)
    rows = [high[4:5, 6:8], low[4:5, 6:8], high[3:4, 0:2], low[3:4, 0:2]]
    return jnp.concatenate([high[0:3], low[0:3], jnp.concatenate(rows, axis=1)], axis=0)


def nearest_messages(ny, meven, modd):
    high, low = both_tiles(ny, meven, modd)

    def message(t, r):
        rows = [high[t, 0:1], high[t, 4:5], high[2, r : r + 1]]
        rows += [low[t, 3:4], low[t, 7:8], low[2, r + 3 : r + 4], high[t, 0:2]]
        return jnp.concatenate(rows, axis=0)

    top, bottom = message(1, 4), message(0, 0)
    even = lax.axis_index("gx") % 2 == 0
    return jnp.where(even, top, bottom), jnp.where(even, bottom, top)


def coarse_kernel(
    nx, ny, where_ref, block_ref, near_ref, far_ref, meven_ref, modd_ref, cnear_ref, cfar_ref,
    send_ref, f1, k1, w1, u1, v1, cx, cy, cz, pair, fine,
):
    even, outside = edge_flags(where_ref[0], nx)
    lanes = (slice(0, 256), slice(256, 512))
    zero = jnp.zeros((12, 256), F32)
    near = [near_ref[i] for i in range(3)]
    far = [jnp.where(outside, 0.0, far_ref[i]) for i in range(3)]
    cnear = cnear_ref[...]
    cfar = jnp.where(outside, 0.0, cfar_ref[...])
    mine = [y_tiles(where_ref, ny, meven_ref, modd_ref, i) for i in range(3)]

    def pick(a, b):
        return [jnp.where(even, p, q) for p, q in zip(a, b)]

    low, high = pick(far, near), pick(near, far)
    corners = {1: (jnp.where(even, cfar, cnear), lanes[1]), 6: (jnp.where(even, cnear, cfar), lanes[0])}
    for p, tiles, x in (
        [(0, low, 2), (1, low, 3)]
        + [(x + 2, [block_ref[i] for i in range(3)], x) for x in range(4)]
        + [(6, high, 0), (7, high, 1)]
    ):
        half, t = lanes[x % 2], x // 2
        for i, (ref, at, row) in enumerate(
            ((f1, t, slice(0, 4)), (k1, t, slice(4, 8)), (w1, 2, slice(4 * t, 4 * t + 4)))
        ):
            ref[p, 4:16] = zero
            ref[p, 0:4] = tiles[at][row, half]
            if 2 <= p <= 5:
                ref[p, 4:8] = mine[at][0][row, half]
                ref[p, 12:16] = mine[at][1][row, half]
            if p in corners:
                rows, side = corners[p]
                ref[p, 4:5] = rows[i : i + 1, side]
                ref[p, 15:16] = rows[3 + i : 4 + i, side]
    for p in range(8):
        u1[p] = w1[p] * f1[p]
        if p < 7:
            cx[p] = 0.5 * (k1[p] + k1[p + 1])
    for p in range(1, 7):
        cy[p] = coupling_y(k1[p])
        cz[p] = coupling_z(k1[p])
        mid = u1[p]
        total = gathered(mid, u1[p - 1], u1[p + 1], cx[p - 1], cx[p], cy[p], cz[p])
        v1[p] = KEEP * mid + w1[p] * (f1[p] + total)
    for p in range(2, 6, 2):
        both = None
        for q in (p, p + 1):
            mid = v1[q]
            total = gathered(mid, v1[q - 1], v1[q + 1], cx[q - 1], cx[q], cy[q], cz[q])
            diag = diagonal(k1[q], k1[q - 1], k1[q + 1])
            rest = (f1[q] + total - diag * mid)[0:8]
            both = rest if both is None else both + rest
        at = p - 2
        fine[at : at + 2] = 0.5 * row_sum(pair, both)[0:2]
        kept = k1[p, 0:8] + k1[p + 1, 0:8]
        fine[4 + at : 6 + at] = 0.125 * row_sum(pair, kept)[0:2]
    tile = lane_sum(fine[...], pair_sum_matrix())
    for i in range(send_ref.shape[0]):
        send_ref[i] = tile


def down1_kernel(
    nx, ny, where_ref, block_ref, v0_ref, near_ref, far_ref, meven_ref, modd_ref,
    cnear_ref, cfar_ref,
    v0x, v1, f1, w1, cx, cy, cz,
    k1, u1,
):
    even, outside = edge_flags(where_ref[0], nx)

    def inside(value):
        return jnp.where(outside, 0.0, value)

    near = [near_ref[i] for i in range(3)]
    far = [inside(far_ref[i]) for i in range(3)]
    cnear = [cnear_ref[i] for i in range(7)]
    cfar = [inside(cfar_ref[i]) for i in range(7)]
    mine = [y_tiles(where_ref, ny, meven_ref, modd_ref, i) for i in range(5)]

    def pick(a, b):
        return [jnp.where(even, p, q) for p, q in zip(a, b)]

    blocks = (
        (pick(far, near), pick(cfar[0:3], cnear[0:3]), pick(cfar[3:6], cnear[3:6])),
        ([block_ref[i] for i in range(3)], [t[0] for t in mine], [t[1] for t in mine]),
        (pick(near, far), pick(cnear[0:3], cfar[0:3]), pick(cnear[3:6], cfar[3:6])),
    )
    zero = jnp.zeros((4, 256), F32)
    for b in range(3):
        for x in range(4):
            p = 4 * b + x
            half = slice(256 * (x % 2), 256 * (x % 2) + 256)
            t = x // 2
            for ref, at, row in (
                (f1, t, slice(0, 4)), (k1, t, slice(4, 8)), (w1, 2, slice(4 * t, 4 * t + 4))
            ):
                ref[p, 0:4] = blocks[b][0][at][row, half]
                ref[p, 4:8] = blocks[b][1][at][row, half]
                ref[p, 8:12] = zero
                ref[p, 12:16] = blocks[b][2][at][row, half]
    blank = jnp.zeros((8, 512), F32)
    for p in range(12):
        v0x[p, 8:16] = blank
    for x in range(8):
        v0x[2 + x, 0:8] = v0_ref[x]
        at = 2 * (x % 4)
        v0x[2 + x, 8:10] = mine[3 + x // 4][0][at : at + 2]
        v0x[2 + x, 14:16] = mine[3 + x // 4][1][at : at + 2]
    near_at = jnp.where(even, 10, 0)
    far_at = jnp.where(even, 0, 10)
    for i in range(2):
        v0x[near_at + i, 0:8] = near_ref[3 + i]
        v0x[far_at + i, 0:8] = inside(far_ref[3 + i])
    low_tile = jnp.where(even, cfar[6], cnear[6])
    high_tile = jnp.where(even, cnear[6], cfar[6])
    for at, tile, row in ((1, low_tile, 0), (10, high_tile, 4)):
        v0x[at, 8:10] = tile[row : row + 2]
        v0x[at, 14:16] = tile[row + 2 : row + 4]
    for p in range(12):
        u1[p] = w1[p] * f1[p]
        if p < 11:
            cx[p] = 0.5 * (k1[p] + k1[p + 1])
        cy[p] = coupling_y(k1[p])
        cz[p] = coupling_z(k1[p])
    for p in range(1, 11):
        mid = u1[p]
        total = gathered(mid, u1[p - 1], u1[p + 1], cx[p - 1], cx[p], cy[p], cz[p])
        v1[p] = KEEP * mid + w1[p] * (f1[p] + total)


def up_kernel(
    nx, ny, where_ref, *refs
):
    half = nx // 2
    columns = (refs[:half], refs[half : 2 * half])
    own, far = refs[nx : nx + 5], refs[nx + 5 : nx + 10]
    rs = Planes(own[0], far[0], 3, 8)
    cx0 = Planes(own[1], far[1], 3, 7)
    cy0, cz0, w0 = (Planes(a, b, 4, 6) for a, b in zip(own[2:], far[2:]))
    up_levels(nx, ny, where_ref, columns, rs, cx0, cy0, cz0, w0, *refs[nx + 10 :])


def up_levels(
    nx, ny, where_ref, columns, rs, cx0, cy0, cz0, w0, v1, f1, w1, cx1, cy1, cz1, v0x, out_ref,
    f2, k2, cx2, cyi, cyo, cz2, w2, d2, u2, v2, e2, f3, k3, cx3, cy3, cz3, w3, edge3, ga, gb,
    small, wide, e1a, e1b, narrow, e0a, e0b,
):
    gx = where_ref[0]
    gy = where_ref[1]
    core = gx % 2
    n2 = 2 * nx
    zero = jnp.zeros((ny, 128), F32)
    row = iota((ny, 128), 0)
    lane = iota((ny, 128), 1)
    last_row = row == ny - 1
    for s in range(2):
        k2[0, s] = zero
        k2[n2 + 1, s] = zero
        u2[0, s] = zero
        u2[n2 + 1, s] = zero
        v2[0, s] = zero
        v2[n2 + 1, s] = zero
    for j in range(nx // 2):
        chip = (gx // 2) ^ j
        for refs, which in ((columns[0], core), (columns[1], 1 - core)):
            for i in range(2):
                p = 4 * chip + 2 * which + i + 1
                for s in range(2):
                    f2[p, s] = refs[j][2 * i + s]
                    k2[p, s] = refs[j][4 + 2 * i + s]
    for p in range(n2 + 1):
        for s in range(2):
            cx2[p, s] = 0.5 * (k2[p, s] + k2[p + 1, s])
    for p in range(1, n2 + 1):
        k_low, k_high = k2[p, 0], k2[p, 1]
        after = jnp.where(last_row, 0.0, roll(k_low, -1, 0))
        before = jnp.where(row == 0, 0.0, roll(k_high, 1, 0))
        cyi[p] = 0.5 * (k_low + k_high)
        cyo[p] = jnp.where(last_row, 0.0, 0.5 * (k_high + after))
        for s, mid, ya, yb in ((0, k_low, k_high, before), (1, k_high, k_low, after)):
            up, down = z_neighbours(mid)
            cz2[p, s] = jnp.where(lane == 127, 0.0, 0.5 * (mid + up))
            diag = 3.0 * mid + 0.5 * (k2[p - 1, s] + k2[p + 1, s] + ya + yb + up + down)
            scale = OMEGA / diag
            d2[p, s] = diag
            w2[p, s] = scale
            u2[p, s] = scale * f2[p, s]

    def gather2(ref, p):
        low, high = ref[p, 0], ref[p, 1]
        sums = []
        for s, mid in ((0, low), (1, high)):
            total = cx2[p, s] * ref[p + 1, s] + cx2[p - 1, s] * ref[p - 1, s]
            total = total + cz2[p, s] * roll(mid, -1, 1) + roll(cz2[p, s] * mid, 1, 1)
            sums.append(total)
        sums[0] = sums[0] + cyi[p] * high + roll(cyo[p] * high, 1, 0)
        sums[1] = sums[1] + cyi[p] * low + cyo[p] * roll(low, -1, 0)
        return (low, high), sums

    def sweep2(source, target):
        for p in range(1, n2 + 1):
            mids, sums = gather2(source, p)
            for s in range(2):
                target[p, s] = KEEP * mids[s] + w2[p, s] * (f2[p, s] + sums[s])

    sweep2(u2, v2)
    even_lane = lane % 2 == 0

    def pair_lanes(value):
        return value + jnp.where(even_lane, roll(value, -1, 1), roll(value, 1, 1))

    k3[0] = zero
    k3[nx + 1] = zero
    ga[0] = zero
    ga[nx + 1] = zero
    gb[0] = zero
    gb[nx + 1] = zero
    for x in range(nx):
        both = None
        kept = None
        for p in (2 * x + 1, 2 * x + 2):
            mids, sums = gather2(v2, p)
            for s in range(2):
                rest = f2[p, s] + sums[s] - d2[p, s] * mids[s]
                both = rest if both is None else both + rest
                kept = k2[p, s] if kept is None else kept + k2[p, s]
        f3[x + 1] = 0.5 * pair_lanes(both)
        k3[x + 1] = 0.125 * pair_lanes(kept)
    for p in range(nx + 1):
        cx3[p] = 0.5 * (k3[p] + k3[p + 1])
    edge_total = zero
    rest_total = zero
    outer = (
        (row == 0).astype(F32) + last_row.astype(F32)
        + (lane < 2).astype(F32) + (lane >= 126).astype(F32)
    )
    for p in range(1, nx + 1):
        mid = k3[p]
        after = jnp.where(last_row, 0.0, roll(mid, -1, 0))
        before = jnp.where(row == 0, 0.0, roll(mid, 1, 0))
        up = jnp.where(lane >= 126, 0.0, roll(mid, -2, 1))
        down = jnp.where(lane < 2, 0.0, roll(mid, 2, 1))
        cy3[p] = jnp.where(last_row, 0.0, 0.5 * (mid + after))
        cz3[p] = jnp.where(lane >= 126, 0.0, 0.5 * (mid + up))
        diag = 3.0 * mid + 0.5 * (k3[p - 1] + k3[p + 1] + after + before + up + down)
        scale = OMEGA / diag
        w3[p] = scale
        ga[p] = scale * f3[p]
        faces = outer + (1.0 if p == 1 else 0.0) + (1.0 if p == nx else 0.0)
        edge = 0.5 * mid * faces
        edge3[p] = edge
        edge_total = edge_total + edge
        rest_total = rest_total + f3[p]

    def gather3(ref, p):
        mid = ref[p]
        total = cx3[p] * ref[p + 1] + cx3[p - 1] * ref[p - 1]
        total = total + cy3[p] * roll(mid, -1, 0) + roll(cy3[p] * mid, 1, 0)
        return mid, total + cz3[p] * roll(mid, -2, 1) + roll(cz3[p] * mid, 2, 1)

    source, target = ga, gb
    for _ in range(7):
        for p in range(1, nx + 1):
            mid, total = gather3(source, p)
            target[p] = KEEP * mid + w3[p] * (f3[p] + total)
        source, target = target, source
    for p in range(1, nx + 1):
        rest_total = rest_total - edge3[p] * source[p]

    def whole(value):
        return jnp.sum(jnp.sum(value, axis=0, keepdims=True), axis=1, keepdims=True)

    shift = whole(rest_total) / whole(edge_total)
    first_row = jnp.clip(gy - 3, 0, ny - 8)
    rows = pl.ds(first_row, 8)
    no_wrap = iota((8, 128), 0) < 7
    planes = []
    for j in range(10):
        x = 2 * gx - 4 + j
        planes.append((jnp.logical_and(x >= 0, x < n2), jnp.clip(x, 0, n2 - 1)))
    level = []
    for ok, q in planes:
        e3 = source[q // 2 + 1, rows] + shift
        level.append([jnp.where(ok, v2[q + 1, s, rows] + e3, 0.0) for s in range(2)])
    for first, last in ((1, 8), (2, 7)):
        done = list(level)
        for j in range(first, last + 1):
            ok, q = planes[j]
            low, high = level[j]
            inner = cyi[q + 1, rows]
            after = jnp.where(no_wrap, cyo[q + 1, rows], 0.0)
            sums = [inner * high + roll(after * high, 1, 0), inner * low + after * roll(low, -1, 0)]
            for s in range(2):
                mid = level[j][s]
                cz = cz2[q + 1, s, rows]
                total = sums[s] + cz * roll(mid, -1, 1) + roll(cz * mid, 1, 1)
                total = total + cx2[q + 1, s, rows] * level[j + 1][s]
                total = total + cx2[q, s, rows] * level[j - 1][s]
                value = KEEP * mid + w2[q + 1, s, rows] * (f2[q + 1, s, rows] + total)
                done[j] = [jnp.where(ok, value, 0.0)] if s == 0 else done[j] + [jnp.where(ok, value, 0.0)]
        level = done
    copies = pair_copy_matrix()
    at = gy - first_row
    steps = (
        (0, at, None),
        (2, jnp.minimum(at + 1, 7), gy < ny - 1),
        (6, jnp.maximum(at - 1, 0), gy > 0),
    )
    for i in range(6):
        small[8 * i + 4 : 8 * i + 6] = jnp.zeros((2, 128), F32)
        for s in range(2):
            e2[i, s] = level[i + 2][s]
            for j, r, ok in steps:
                line = e2[i, s, pl.ds(r, 1)]
                small[8 * i + j + s : 8 * i + j + s + 1] = (
                    line if ok is None else jnp.where(ok, line, 0.0)
                )
    wide[...] = lane_copy(small[...], copies)
    for i in range(6):
        spread = row_copy(narrow, wide[8 * i : 8 * i + 8])
        for p in (2 * i, 2 * i + 1):
            if 1 <= p <= 10:
                e1a[p] = v1[p] + spread
    for source, target, first, last in ((e1a, e1b, 2, 9), (e1b, e1a, 3, 8)):
        for p in range(first, last + 1):
            mid = source[p]
            total = gathered(
                mid, source[p - 1], source[p + 1], cx1[p - 1], cx1[p], cy1[p], cz1[p]
            )
            target[p] = KEEP * mid + w1[p] * (f1[p] + total)
    row8 = iota((8, 256), 0)
    for i in range(6):
        value = e1a[i + 3]
        wide[8 * i : 8 * i + 8] = jnp.where(row8 == 7, value[8:16], value[0:8])
    doubled = lane_copy(wide[...], copies)
    for i in range(6):
        spread = row_copy(narrow, doubled[8 * i : 8 * i + 8])
        for p in (2 * i, 2 * i + 1):
            e0a[p] = v0x[p] + spread
    for p in range(1, 11):
        mid = e0a[p]
        total = gathered(
            mid, e0a[p - 1], e0a[p + 1], cx0[p], cx0[p + 1], cy0[p + 1], cz0[p + 1]
        )
        e0b[p] = KEEP * mid + w0[p + 1] * (rs[p + 1] + total)
    for p in range(2, 10):
        mid = e0b[p]
        total = gathered(
            mid, e0b[p - 1], e0b[p + 1], cx0[p], cx0[p + 1], cy0[p + 1], cz0[p + 1]
        )
        out_ref[p - 2] = (KEEP * mid + w0[p + 1] * (rs[p + 1] + total))[0:8]


def run(kernel, outs, scratch, where, *operands, space=VMEM, cost=None):
    return pl.pallas_call(
        kernel,
        out_shape=[jax.ShapeDtypeStruct(shape, F32) for shape in outs],
        in_specs=[pl.BlockSpec(memory_space=pltpu.SMEM)]
        + [pl.BlockSpec(memory_space=space)] * len(operands),
        out_specs=[pl.BlockSpec(memory_space=VMEM)] * len(outs),
        scratch_shapes=[VMEM(s, F32) if isinstance(s, tuple) else s for s in scratch],
        compiler_params=PARAMS,
        cost_estimate=cost,
    )(where, *operands)


def body(initial, right_side, phase_map, phase_table):
    nx, ny = lax.axis_size("gx"), lax.axis_size("gy")
    where = jnp.stack([lax.axis_index("gx"), lax.axis_index("gy")]).astype(jnp.int32)

    def pairs(partner):
        return [
            (x * ny + y, px * ny + py)
            for x in range(nx)
            for y in range(ny)
            for px, py in [partner(x, y)]
        ]

    def beyond(at, size):
        other = at + 1 if at % 2 else at - 1
        return other if 0 <= other < size else None

    def far_x(x, y):
        other = beyond(x, nx)
        return (x, y ^ 1) if other is None else (other, y)

    def far_y(x, y):
        other = beyond(y, ny)
        return (x ^ 1, y) if other is None else (x, other)

    both = ("gx", "gy")

    def swap_x(near, far):
        return (
            lax.ppermute(near, both, pairs(lambda x, y: (x ^ 1, y))),
            lax.ppermute(far, both, pairs(far_x)),
        )

    def swap_y(near, far):
        return (
            lax.ppermute(near, both, pairs(lambda x, y: (x, y ^ 1))),
            lax.ppermute(far, both, pairs(far_y)),
        )

    inputs = [
        pltpu.with_memory_space_constraint(value, pltpu.HBM)
        for value in (phase_table, phase_map, initial, right_side)
    ]
    early_cost = pl.CostEstimate(flops=20_000_000, bytes_accessed=4_000_000, transcendentals=0)
    tile0 = (8, 512)
    ring0 = (16, 512)
    ring1 = (16, 256)
    kappa, init, rhs, near, far, yeven, yodd = run(
        start_kernel, [(8,) + tile0] * 7,
        [pltpu.SMEM((3,), F32), VMEM((8,) + tile0, jnp.int32), pltpu.SemaphoreType.DMA((4,))],
        where, *inputs, space=pltpu.HBM,
    )
    yeven, yodd = swap_y(yeven, yodd)
    near, far = swap_x(near, far)
    yodd, yeven, far, near = lax.optimization_barrier((yodd, yeven, far, near))
    cnear, cfar = swap_x(*corner_messages(nx, ny, yeven, yodd))
    ksx, vsx, rsx, cxx, cyx, czx, wix, v1x, v2x, restx, kcx = run(
        functools.partial(early0_kernel, ny),
        [(8,) + ring0] * 3 + [(7,) + ring0] + [(6,) + ring0] * 4
        + [(4,) + ring0, (2,) + tile0, (32, 256)],
        [(4, 16, 128), (32, 512)],
        where, kappa, init, rhs, yeven, yodd, cost=early_cost,
    )
    v0, rs, cx0, cy0, cz0, w0, block, mnear, mfar, meven, modd = run(
        functools.partial(down0_kernel, nx, ny),
        [(8,) + tile0]
        + [(6,) + ring0, (6,) + ring0]
        + [(8,) + ring0] * 3
        + [(3,) + tile0]
        + [(5,) + tile0] * 4,
        [(6,) + ring0] * 2 + [(8,) + ring0, (10,) + ring0, (4, 16, 128), (32, 512), (32, 256)],
        where, near, far, cnear, cfar,
        ksx, vsx, rsx, cxx, cyx, czx, wix, v1x, v2x, restx, kcx,
    )
    meven, modd = swap_y(meven, modd)
    mnear, mfar = swap_x(mnear, mfar)
    modd, meven, mfar, mnear = lax.optimization_barrier((modd, meven, mfar, mnear))
    nnear, nfar = swap_x(*nearest_messages(ny, meven, modd))
    corner = corner1_message(ny, meven, modd)
    cnear, cfar = swap_x(corner, corner)
    (send,) = run(
        functools.partial(coarse_kernel, nx, ny), [(ny, 8, 128)],
        [(8,) + ring1] * 8 + [(4, 16, 128), (8, 256)],
        where, block, mnear, mfar, meven, modd, nnear, nfar,
    )
    column = jnp.transpose(lax.all_to_all(send, "gy", 0, 0), (1, 0, 2))
    column, cnear, cfar, v0 = lax.optimization_barrier((column, cnear, cfar, v0))
    v0x, v1, f1, w1, cx1, cy1, cz1 = run(
        functools.partial(down1_kernel, nx, ny),
        [(12,) + ring0] + [(12,) + ring1] * 6,
        [(12,) + ring1, (12,) + ring1],
        where, block, v0, mnear, mfar, meven, modd, cnear, cfar, cost=early_cost,
    )

    def chips_apart(j):
        return pairs(lambda x, y: (((x // 2) ^ j) * 2 + x % 2, y))

    mine = {0: column}
    for j in sorted(range(1, nx // 2), key=lambda j: j != 2):
        mine[j] = lax.ppermute(column, both, chips_apart(j))
    mine = [mine[j] for j in range(nx // 2)]
    other = [lax.ppermute(c, both, pairs(lambda x, y: (x ^ 1, y))) for c in mine]
    n2 = 2 * nx
    pair2 = (n2 + 2, 2, ny, 128)
    one2 = (n2 + 2, ny, 128)
    one3 = (nx + 2, ny, 128)
    (out,) = run(
        functools.partial(up_kernel, nx, ny), [(8,) + tile0],
        [pair2, pair2, pair2, one2, one2, pair2, pair2, pair2, pair2, pair2, (6, 2, 8, 128)]
        + [one3] * 9
        + [(48, 128), (48, 256), (12,) + ring1, (12,) + ring1, (4, 16, 128), (12,) + ring0, (12,) + ring0],
        where, *mine, *other, rsx, cxx, cyx, czx, wix, rs, cx0, cy0, cz0, w0,
        v1, f1, w1, cx1, cy1, cz1, v0x,
    )
    return out


def solution(mesh):
    return jax.shard_map(
        body,
        mesh=mesh,
        in_specs=(P("gx", "gy", None), P("gx", "gy", None), P("gx", "gy", None), P()),
        out_specs=P("gx", "gy", None),
        check_vma=False,
    )
```

```python
import functools

import jax
import jax.numpy as jnp
from jax import lax
from jax.experimental import pallas as pl
from jax.experimental.pallas import tpu as pltpu
from jax.sharding import PartitionSpec as P

F32 = jnp.float32
KEEP = 0.2
OMEGA = 0.8
VMEM = pltpu.VMEM
PARAMS = pltpu.CompilerParams(vmem_limit_bytes=48 * 1024 * 1024)


def roll(value, shift, axis):
    return pltpu.roll(value, shift % value.shape[axis], axis)


def iota(shape, dim):
    return lax.broadcasted_iota(jnp.int32, shape, dim)


def pair_sum_matrix():
    return (iota((256, 128), 0) // 2 == iota((256, 128), 1)).astype(F32)


def pair_copy_matrix():
    return (iota((128, 256), 1) // 2 == iota((128, 256), 0)).astype(F32)


def exact_dot(a, b):
    return lax.dot_general(
        a, b, (((1,), (0,)), ((), ())), precision=lax.Precision.HIGHEST, preferred_element_type=F32
    )


def lane_sum(value, matrix):
    width = value.shape[1]
    parts = [exact_dot(value[:, at : at + 256], matrix) for at in range(0, width, 256)]
    return parts[0] if len(parts) == 1 else jnp.concatenate(parts, axis=1)


def lane_copy(value, matrix):
    width = value.shape[1]
    parts = [exact_dot(value[:, at : at + 128], matrix) for at in range(0, width, 128)]
    return parts[0] if len(parts) == 1 else jnp.concatenate(parts, axis=1)


def row_sum(scratch, value):
    rows, width = value.shape
    parts = []
    for c in range(width // 128):
        scratch[c, 0:rows] = value[:, 128 * c : 128 * c + 128]
        first = scratch[c, pl.ds(0, rows // 2, stride=2)]
        parts.append(first + scratch[c, pl.ds(1, rows // 2, stride=2)])
    return parts[0] if len(parts) == 1 else jnp.concatenate(parts, axis=1)


def row_copy(scratch, value):
    rows, width = value.shape
    parts = []
    for c in range(width // 128):
        part = value[:, 128 * c : 128 * c + 128]
        scratch[c, pl.ds(0, rows, stride=2)] = part
        scratch[c, pl.ds(1, rows, stride=2)] = part
        parts.append(scratch[c, 0 : 2 * rows])
    return parts[0] if len(parts) == 1 else jnp.concatenate(parts, axis=1)


def gathered(mid, low, high, cx_low, cx, cy, cz):
    total = cx * high + cx_low * low
    total = total + cy * roll(mid, -1, 0) + roll(cy * mid, 1, 0)
    return total + cz * roll(mid, -1, 1) + roll(cz * mid, 1, 1)


def z_neighbours(mid):
    lane = iota(mid.shape, 1)
    last = mid.shape[1] - 1
    up = jnp.where(lane == last, 0.0, roll(mid, -1, 1))
    down = jnp.where(lane == 0, 0.0, roll(mid, 1, 1))
    return up, down


def diagonal(mid, low, high):
    up, down = z_neighbours(mid)
    total = low + high + roll(mid, -1, 0) + roll(mid, 1, 0) + up + down
    return 3.0 * mid + 0.5 * total


def coupling_y(mid):
    return 0.5 * (mid + roll(mid, -1, 0))


def coupling_z(mid):
    lane = iota(mid.shape, 1)
    return jnp.where(lane == mid.shape[1] - 1, 0.0, 0.5 * (mid + roll(mid, -1, 1)))


def edge_flags(at, grid):
    even = at % 2 == 0
    outside = jnp.logical_or(at == 0, at == grid - 1)
    return even, outside


def start_kernel(
    where_ref, table_hbm, phase_hbm, init_hbm, rhs_hbm,
    kap_ref, init_ref, rhs_ref, near_ref, far_ref, yeven_ref, yodd_ref,
    table_ref, phase_ref, sems,
):
    copies = [
        pltpu.make_async_copy(source, target, sems.at[i])
        for i, (source, target) in enumerate(
            ((table_hbm, table_ref), (phase_hbm, phase_ref), (init_hbm, init_ref), (rhs_hbm, rhs_ref))
        )
    ]
    for copy in copies:
        copy.start()
    for copy in copies:
        copy.wait()
    even = where_ref[0] % 2 == 0
    for x in range(8):
        phase = phase_ref[x]
        kap_ref[x] = jnp.where(
            phase == 0, table_ref[0], jnp.where(phase == 1, table_ref[1], table_ref[2])
        )
    for ref, side in ((near_ref, even), (far_ref, jnp.logical_not(even))):
        deep = jnp.where(side, 5, 0)
        shallow = jnp.where(side, 6, 0)
        for i in range(3):
            ref[i] = kap_ref[deep + i]
            ref[3 + i] = init_ref[deep + i]
        for i in range(2):
            ref[6 + i] = rhs_ref[shallow + i]

    def write(low_ref, high_ref):
        for x in range(8):
            low_ref[x, 0:3] = kap_ref[x, 0:3]
            low_ref[x, 3:6] = init_ref[x, 0:3]
            low_ref[x, 6:8] = rhs_ref[x, 0:2]
            high_ref[x, 0:3] = kap_ref[x, 5:8]
            high_ref[x, 3:6] = init_ref[x, 5:8]
            high_ref[x, 6:8] = rhs_ref[x, 6:8]

    by_parity(where_ref, yeven_ref, yodd_ref, write)


def by_parity(where_ref, even_ref, odd_ref, write):
    even = where_ref[1] % 2 == 0

    @pl.when(even)
    def _():
        write(odd_ref, even_ref)

    @pl.when(jnp.logical_not(even))
    def _():
        write(even_ref, odd_ref)


def y_tiles(where_ref, grid, even_ref, odd_ref, p):
    even, outside = edge_flags(where_ref[1], grid)
    inner = even_ref[p]
    outer = jnp.where(outside, 0.0, odd_ref[p])
    return jnp.where(even, inner, outer), jnp.where(even, outer, inner)


def corner_messages(nx, ny, yeven, yodd):
    even = lax.axis_index("gx") % 2 == 0
    high, low = both_tiles(ny, yeven, yodd)
    top = jnp.concatenate([high[7:8], high[6:7], low[7:8], low[6:7]], axis=0)
    bottom = jnp.concatenate([high[0:2], low[0:2]], axis=0)
    return jnp.where(even, top, bottom), jnp.where(even, bottom, top)


def both_tiles(ny, yeven, yodd):
    at = lax.axis_index("gy")
    even, outside = edge_flags(at, ny)
    outer = jnp.where(outside, 0.0, yodd)
    return jnp.where(even, yeven, outer), jnp.where(even, outer, yeven)


class Planes:
    def __init__(self, middle, outer, first, count):
        self.middle, self.outer, self.first, self.count = middle, outer, first, count

    def find(self, p):
        if p < self.first:
            return self.outer, p
        if p < self.first + self.count:
            return self.middle, p - self.first
        return self.outer, p - self.count

    def __getitem__(self, p):
        ref, at = self.find(p)
        return ref[at]

    def __setitem__(self, p, value):
        ref, at = self.find(p)
        ref[at] = value


def setup0(ks, cx, cy, cz, wi, planes, faces):
    for p in faces:
        cx[p] = 0.5 * (ks[p] + ks[p + 1])
    for p in planes:
        mid = ks[p]
        cy[p] = coupling_y(mid)
        cz[p] = coupling_z(mid)
        diag = diagonal(mid, ks[p - 1], ks[p + 1])
        wi[p] = jnp.where(mid > 0.0, OMEGA / jnp.where(mid > 0.0, diag, 1.0), 0.0)


def sweep0(source, target, rs, cx, cy, cz, wi, planes):
    for p in planes:
        mid = source[p]
        total = gathered(mid, source[p - 1], source[p + 1], cx[p - 1], cx[p], cy[p], cz[p])
        target[p] = KEEP * mid + wi[p] * (rs[p] + total)


def rest0(v2, rs, ks, cx, cy, cz, p):
    mid = v2[p]
    total = gathered(mid, v2[p - 1], v2[p + 1], cx[p - 1], cx[p], cy[p], cz[p])
    diag = diagonal(ks[p], ks[p - 1], ks[p + 1])
    return (rs[p] + total - diag * mid)[0:8]


def add_y_halo(ks, vs, rs, p, high, low):
    zero = jnp.zeros((8, 512), F32)
    ks[p, 8:16] = zero
    vs[p, 8:16] = zero
    rs[p, 8:16] = zero
    ks[p, 8:11] = high[0:3]
    ks[p, 13:16] = low[0:3]
    vs[p, 8:11] = high[3:6]
    vs[p, 13:16] = low[3:6]
    rs[p, 8:10] = high[6:8]
    rs[p, 14:16] = low[6:8]


def early0_kernel(
    ny, where_ref, kap_ref, init_ref, rhs_ref, even_ref, odd_ref,
    ks, vs, rs, cx, cy, cz, wi, v1, v2, rest, kc,
    pair, fine,
):
    for x in range(8):
        ks[x, 0:8] = kap_ref[x]
        vs[x, 0:8] = init_ref[x]
        rs[x, 0:8] = rhs_ref[x]
        add_y_halo(ks, vs, rs, x, *y_tiles(where_ref, ny, even_ref, odd_ref, x))
    ks, vs, rs = (Planes(ref, None, 3, 8) for ref in (ks, vs, rs))
    cx = Planes(cx, None, 3, 7)
    cy, cz, wi, v1 = (Planes(ref, None, 4, 6) for ref in (cy, cz, wi, v1))
    v2 = Planes(v2, None, 5, 4)
    setup0(ks, cx, cy, cz, wi, range(4, 10), range(3, 10))
    sweep0(vs, v1, rs, cx, cy, cz, wi, range(4, 10))
    sweep0(v1, v2, rs, cx, cy, cz, wi, range(5, 9))
    for p in (6, 7):
        rest[p - 6] = rest0(v2, rs, ks, cx, cy, cz, p)
    for x in range(4):
        fine[8 * x : 8 * x + 8] = row_sum(pair, ks[2 * x + 3] + ks[2 * x + 4])
    kc[...] = 0.125 * lane_sum(fine[...], pair_sum_matrix())


def down0_kernel(
    nx, ny, where_ref, near_ref, far_ref, cnear_ref, cfar_ref,
    ks_own, vs_own, rs_own, cx_own, cy_own, cz_own, wi_own, v1_own, v2_own, rest_own, kc,
    v0_ref, rs, cx, cy, cz, wi, block_ref, mnear_ref, mfar_ref, meven_ref, modd_ref,
    ks, vs, v1, v2, pair, fine, coarse,
):
    even, outside = edge_flags(where_ref[0], nx)
    for i in range(3):
        near_at = jnp.where(even, 3 + i, i)
        far_at = jnp.where(even, i, 3 + i)
        for ref, first in ((ks, 0), (vs, 3)):
            ref[near_at, 0:8] = near_ref[first + i]
            ref[far_at, 0:8] = jnp.where(outside, 0.0, far_ref[first + i])
    for i in range(2):
        rs[jnp.where(even, 3 + i, 1 + i), 0:8] = near_ref[6 + i]
        rs[jnp.where(even, 1 + i, 3 + i), 0:8] = jnp.where(outside, 0.0, far_ref[6 + i])
    zero = jnp.zeros((8, 512), F32)
    for p in (0, 5):
        ks[p, 8:16] = zero
        vs[p, 8:16] = zero
        rs[p, 8:16] = zero
    rs[0, 0:8] = zero
    rs[5, 0:8] = zero
    for i in range(2):
        add_y_halo(ks, vs, rs, jnp.where(even, 3 + i, 2 - i), cnear_ref[i], cnear_ref[2 + i])
        add_y_halo(
            ks, vs, rs, jnp.where(even, 2 - i, 3 + i),
            jnp.where(outside, 0.0, cfar_ref[i]), jnp.where(outside, 0.0, cfar_ref[2 + i]),
        )
    ks, vs, rs = (Planes(a, b, 3, 8) for a, b in ((ks_own, ks), (vs_own, vs), (rs_own, rs)))
    cx = Planes(cx_own, cx, 3, 7)
    cy, cz, wi, v1 = (
        Planes(a, b, 4, 6) for a, b in ((cy_own, cy), (cz_own, cz), (wi_own, wi), (v1_own, v1))
    )
    v2 = Planes(v2_own, v2, 5, 4)
    setup0(ks, cx, cy, cz, wi, (1, 2, 3, 10, 11, 12), (0, 1, 2, 10, 11, 12))
    sweep0(vs, v1, rs, cx, cy, cz, wi, (1, 2, 3, 10, 11, 12))
    sweep0(v1, v2, rs, cx, cy, cz, wi, (2, 3, 4, 9, 10, 11))
    for p in range(3, 11, 2):
        both = None
        for q in (p, p + 1):
            rest = rest_own[q - 6] if q in (6, 7) else rest0(v2, rs, ks, cx, cy, cz, q)
            both = rest if both is None else both + rest
            v0_ref[q - 3] = v2[q][0:8]
        at = 2 * (p - 3)
        fine[at : at + 4] = row_sum(pair, both)
    fine[16:24] = row_sum(pair, ks[1] + ks[2])
    fine[24:32] = row_sum(pair, ks[11] + ks[12])
    coarse[...] = lane_sum(fine[...], pair_sum_matrix())
    kept = [0.125 * coarse[16:24]] + [kc[8 * x : 8 * x + 8] for x in range(4)]
    kept.append(0.125 * coarse[24:32])
    for x in range(4):
        half = pl.ds(256 * (x % 2), 256)
        mid = kept[x + 1]
        block_ref[x // 2, 0:4, half] = 0.5 * coarse[4 * x : 4 * x + 4]
        block_ref[x // 2, 4:8, half] = mid[0:4]
        at = 4 * (x // 2)
        block_ref[2, at : at + 4, half] = (OMEGA / diagonal(mid, kept[x], kept[x + 2])[0:4])
    for ref, side in ((mnear_ref, even), (mfar_ref, jnp.logical_not(even))):
        shallow = jnp.where(side, 6, 0)
        for i in range(3):
            ref[i] = block_ref[i]
        for i in range(2):
            ref[3 + i] = v0_ref[shallow + i]

    def write(low_ref, high_ref):
        for i in range(3):
            low_ref[i] = block_ref[i]
            high_ref[i] = block_ref[i]
        for x in range(8):
            at = 2 * (x % 4)
            low_ref[3 + x // 4, at : at + 2] = v0_ref[x, 0:2]
            high_ref[3 + x // 4, at : at + 2] = v0_ref[x, 6:8]

    by_parity(where_ref, meven_ref, modd_ref, write)


def corner1_message(ny, meven, modd):
    high, low = both_tiles(ny, meven, modd)
    rows = [high[4:5, 6:8], low[4:5, 6:8], high[3:4, 0:2], low[3:4, 0:2]]
    return jnp.concatenate([high[0:3], low[0:3], jnp.concatenate(rows, axis=1)], axis=0)


def down1_kernel(
    nx, ny, where_ref, block_ref, v0_ref, near_ref, far_ref, meven_ref, modd_ref,
    cnear_ref, cfar_ref,
    v0x, v1, f1, w1, cx, cy, cz, send_ref,
    k1, u1, pair, fine,
):
    even, outside = edge_flags(where_ref[0], nx)

    def inside(value):
        return jnp.where(outside, 0.0, value)

    near = [near_ref[i] for i in range(3)]
    far = [inside(far_ref[i]) for i in range(3)]
    cnear = [cnear_ref[i] for i in range(7)]
    cfar = [inside(cfar_ref[i]) for i in range(7)]
    mine = [y_tiles(where_ref, ny, meven_ref, modd_ref, i) for i in range(5)]

    def pick(a, b):
        return [jnp.where(even, p, q) for p, q in zip(a, b)]

    blocks = (
        (pick(far, near), pick(cfar[0:3], cnear[0:3]), pick(cfar[3:6], cnear[3:6])),
        ([block_ref[i] for i in range(3)], [t[0] for t in mine], [t[1] for t in mine]),
        (pick(near, far), pick(cnear[0:3], cfar[0:3]), pick(cnear[3:6], cfar[3:6])),
    )
    zero = jnp.zeros((4, 256), F32)
    for b in range(3):
        for x in range(4):
            p = 4 * b + x
            half = slice(256 * (x % 2), 256 * (x % 2) + 256)
            t = x // 2
            for ref, at, row in (
                (f1, t, slice(0, 4)), (k1, t, slice(4, 8)), (w1, 2, slice(4 * t, 4 * t + 4))
            ):
                ref[p, 0:4] = blocks[b][0][at][row, half]
                ref[p, 4:8] = blocks[b][1][at][row, half]
                ref[p, 8:12] = zero
                ref[p, 12:16] = blocks[b][2][at][row, half]
    blank = jnp.zeros((8, 512), F32)
    for p in range(12):
        v0x[p, 8:16] = blank
    for x in range(8):
        v0x[2 + x, 0:8] = v0_ref[x]
        at = 2 * (x % 4)
        v0x[2 + x, 8:10] = mine[3 + x // 4][0][at : at + 2]
        v0x[2 + x, 14:16] = mine[3 + x // 4][1][at : at + 2]
    near_at = jnp.where(even, 10, 0)
    far_at = jnp.where(even, 0, 10)
    for i in range(2):
        v0x[near_at + i, 0:8] = near_ref[3 + i]
        v0x[far_at + i, 0:8] = inside(far_ref[3 + i])
    low_tile = jnp.where(even, cfar[6], cnear[6])
    high_tile = jnp.where(even, cnear[6], cfar[6])
    for at, tile, row in ((1, low_tile, 0), (10, high_tile, 4)):
        v0x[at, 8:10] = tile[row : row + 2]
        v0x[at, 14:16] = tile[row + 2 : row + 4]
    for p in range(12):
        u1[p] = w1[p] * f1[p]
        if p < 11:
            cx[p] = 0.5 * (k1[p] + k1[p + 1])
        cy[p] = coupling_y(k1[p])
        cz[p] = coupling_z(k1[p])
    for p in range(1, 11):
        mid = u1[p]
        total = gathered(mid, u1[p - 1], u1[p + 1], cx[p - 1], cx[p], cy[p], cz[p])
        v1[p] = KEEP * mid + w1[p] * (f1[p] + total)
    for p in range(4, 8, 2):
        both = None
        for q in (p, p + 1):
            mid = v1[q]
            total = gathered(mid, v1[q - 1], v1[q + 1], cx[q - 1], cx[q], cy[q], cz[q])
            diag = diagonal(k1[q], k1[q - 1], k1[q + 1])
            rest = (f1[q] + total - diag * mid)[0:8]
            both = rest if both is None else both + rest
        at = p - 4
        fine[at : at + 2] = 0.5 * row_sum(pair, both)[0:2]
        kept = k1[p, 0:8] + k1[p + 1, 0:8]
        fine[4 + at : 6 + at] = 0.125 * row_sum(pair, kept)[0:2]
    tile = lane_sum(fine[...], pair_sum_matrix())
    for i in range(send_ref.shape[0]):
        send_ref[i] = tile


def up_kernel(
    nx, ny, where_ref, *refs
):
    half = nx // 2
    columns = (refs[:half], refs[half : 2 * half])
    own, far = refs[nx : nx + 5], refs[nx + 5 : nx + 10]
    rs = Planes(own[0], far[0], 3, 8)
    cx0 = Planes(own[1], far[1], 3, 7)
    cy0, cz0, w0 = (Planes(a, b, 4, 6) for a, b in zip(own[2:], far[2:]))
    up_levels(nx, ny, where_ref, columns, rs, cx0, cy0, cz0, w0, *refs[nx + 10 :])


def up_levels(
    nx, ny, where_ref, columns, rs, cx0, cy0, cz0, w0, v1, f1, w1, cx1, cy1, cz1, v0x, out_ref,
    f2, k2, cx2, cyi, cyo, cz2, w2, d2, u2, v2, e2, f3, k3, cx3, cy3, cz3, w3, edge3, ga, gb,
    small, wide, e1a, e1b, narrow, e0a, e0b,
):
    gx = where_ref[0]
    gy = where_ref[1]
    core = gx % 2
    n2 = 2 * nx
    zero = jnp.zeros((ny, 128), F32)
    row = iota((ny, 128), 0)
    lane = iota((ny, 128), 1)
    last_row = row == ny - 1
    for s in range(2):
        k2[0, s] = zero
        k2[n2 + 1, s] = zero
        u2[0, s] = zero
        u2[n2 + 1, s] = zero
        v2[0, s] = zero
        v2[n2 + 1, s] = zero
    for j in range(nx // 2):
        chip = (gx // 2) ^ j
        for refs, which in ((columns[0], core), (columns[1], 1 - core)):
            for i in range(2):
                p = 4 * chip + 2 * which + i + 1
                for s in range(2):
                    f2[p, s] = refs[j][2 * i + s]
                    k2[p, s] = refs[j][4 + 2 * i + s]
    for p in range(n2 + 1):
        for s in range(2):
            cx2[p, s] = 0.5 * (k2[p, s] + k2[p + 1, s])
    for p in range(1, n2 + 1):
        k_low, k_high = k2[p, 0], k2[p, 1]
        after = jnp.where(last_row, 0.0, roll(k_low, -1, 0))
        before = jnp.where(row == 0, 0.0, roll(k_high, 1, 0))
        cyi[p] = 0.5 * (k_low + k_high)
        cyo[p] = jnp.where(last_row, 0.0, 0.5 * (k_high + after))
        for s, mid, ya, yb in ((0, k_low, k_high, before), (1, k_high, k_low, after)):
            up, down = z_neighbours(mid)
            cz2[p, s] = jnp.where(lane == 127, 0.0, 0.5 * (mid + up))
            diag = 3.0 * mid + 0.5 * (k2[p - 1, s] + k2[p + 1, s] + ya + yb + up + down)
            scale = OMEGA / diag
            d2[p, s] = diag
            w2[p, s] = scale
            u2[p, s] = scale * f2[p, s]

    def gather2(ref, p):
        low, high = ref[p, 0], ref[p, 1]
        sums = []
        for s, mid in ((0, low), (1, high)):
            total = cx2[p, s] * ref[p + 1, s] + cx2[p - 1, s] * ref[p - 1, s]
            total = total + cz2[p, s] * roll(mid, -1, 1) + roll(cz2[p, s] * mid, 1, 1)
            sums.append(total)
        sums[0] = sums[0] + cyi[p] * high + roll(cyo[p] * high, 1, 0)
        sums[1] = sums[1] + cyi[p] * low + cyo[p] * roll(low, -1, 0)
        return (low, high), sums

    def sweep2(source, target):
        for p in range(1, n2 + 1):
            mids, sums = gather2(source, p)
            for s in range(2):
                target[p, s] = KEEP * mids[s] + w2[p, s] * (f2[p, s] + sums[s])

    sweep2(u2, v2)
    even_lane = lane % 2 == 0

    def pair_lanes(value):
        return value + jnp.where(even_lane, roll(value, -1, 1), roll(value, 1, 1))

    k3[0] = zero
    k3[nx + 1] = zero
    ga[0] = zero
    ga[nx + 1] = zero
    gb[0] = zero
    gb[nx + 1] = zero
    for x in range(nx):
        both = None
        kept = None
        for p in (2 * x + 1, 2 * x + 2):
            mids, sums = gather2(v2, p)
            for s in range(2):
                rest = f2[p, s] + sums[s] - d2[p, s] * mids[s]
                both = rest if both is None else both + rest
                kept = k2[p, s] if kept is None else kept + k2[p, s]
        f3[x + 1] = 0.5 * pair_lanes(both)
        k3[x + 1] = 0.125 * pair_lanes(kept)
    for p in range(nx + 1):
        cx3[p] = 0.5 * (k3[p] + k3[p + 1])
    edge_total = zero
    rest_total = zero
    outer = (
        (row == 0).astype(F32) + last_row.astype(F32)
        + (lane < 2).astype(F32) + (lane >= 126).astype(F32)
    )
    for p in range(1, nx + 1):
        mid = k3[p]
        after = jnp.where(last_row, 0.0, roll(mid, -1, 0))
        before = jnp.where(row == 0, 0.0, roll(mid, 1, 0))
        up = jnp.where(lane >= 126, 0.0, roll(mid, -2, 1))
        down = jnp.where(lane < 2, 0.0, roll(mid, 2, 1))
        cy3[p] = jnp.where(last_row, 0.0, 0.5 * (mid + after))
        cz3[p] = jnp.where(lane >= 126, 0.0, 0.5 * (mid + up))
        diag = 3.0 * mid + 0.5 * (k3[p - 1] + k3[p + 1] + after + before + up + down)
        scale = OMEGA / diag
        w3[p] = scale
        ga[p] = scale * f3[p]
        faces = outer + (1.0 if p == 1 else 0.0) + (1.0 if p == nx else 0.0)
        edge = 0.5 * mid * faces
        edge3[p] = edge
        edge_total = edge_total + edge
        rest_total = rest_total + f3[p]

    def gather3(ref, p):
        mid = ref[p]
        total = cx3[p] * ref[p + 1] + cx3[p - 1] * ref[p - 1]
        total = total + cy3[p] * roll(mid, -1, 0) + roll(cy3[p] * mid, 1, 0)
        return mid, total + cz3[p] * roll(mid, -2, 1) + roll(cz3[p] * mid, 2, 1)

    source, target = ga, gb
    for _ in range(7):
        for p in range(1, nx + 1):
            mid, total = gather3(source, p)
            target[p] = KEEP * mid + w3[p] * (f3[p] + total)
        source, target = target, source
    for p in range(1, nx + 1):
        rest_total = rest_total - edge3[p] * source[p]

    def whole(value):
        return jnp.sum(jnp.sum(value, axis=0, keepdims=True), axis=1, keepdims=True)

    shift = whole(rest_total) / whole(edge_total)
    first_row = jnp.clip(gy - 3, 0, ny - 8)
    rows = pl.ds(first_row, 8)
    no_wrap = iota((8, 128), 0) < 7
    planes = []
    for j in range(10):
        x = 2 * gx - 4 + j
        planes.append((jnp.logical_and(x >= 0, x < n2), jnp.clip(x, 0, n2 - 1)))
    level = []
    for ok, q in planes:
        e3 = source[q // 2 + 1, rows] + shift
        level.append([jnp.where(ok, v2[q + 1, s, rows] + e3, 0.0) for s in range(2)])
    for first, last in ((1, 8), (2, 7)):
        done = list(level)
        for j in range(first, last + 1):
            ok, q = planes[j]
            low, high = level[j]
            inner = cyi[q + 1, rows]
            after = jnp.where(no_wrap, cyo[q + 1, rows], 0.0)
            sums = [inner * high + roll(after * high, 1, 0), inner * low + after * roll(low, -1, 0)]
            for s in range(2):
                mid = level[j][s]
                cz = cz2[q + 1, s, rows]
                total = sums[s] + cz * roll(mid, -1, 1) + roll(cz * mid, 1, 1)
                total = total + cx2[q + 1, s, rows] * level[j + 1][s]
                total = total + cx2[q, s, rows] * level[j - 1][s]
                value = KEEP * mid + w2[q + 1, s, rows] * (f2[q + 1, s, rows] + total)
                done[j] = [jnp.where(ok, value, 0.0)] if s == 0 else done[j] + [jnp.where(ok, value, 0.0)]
        level = done
    copies = pair_copy_matrix()
    at = gy - first_row
    steps = (
        (0, at, None),
        (2, jnp.minimum(at + 1, 7), gy < ny - 1),
        (6, jnp.maximum(at - 1, 0), gy > 0),
    )
    for i in range(6):
        small[8 * i + 4 : 8 * i + 6] = jnp.zeros((2, 128), F32)
        for s in range(2):
            e2[i, s] = level[i + 2][s]
            for j, r, ok in steps:
                line = e2[i, s, pl.ds(r, 1)]
                small[8 * i + j + s : 8 * i + j + s + 1] = (
                    line if ok is None else jnp.where(ok, line, 0.0)
                )
    wide[...] = lane_copy(small[...], copies)
    for i in range(6):
        spread = row_copy(narrow, wide[8 * i : 8 * i + 8])
        for p in (2 * i, 2 * i + 1):
            if 1 <= p <= 10:
                e1a[p] = v1[p] + spread
    for source, target, first, last in ((e1a, e1b, 2, 9), (e1b, e1a, 3, 8)):
        for p in range(first, last + 1):
            mid = source[p]
            total = gathered(
                mid, source[p - 1], source[p + 1], cx1[p - 1], cx1[p], cy1[p], cz1[p]
            )
            target[p] = KEEP * mid + w1[p] * (f1[p] + total)
    row8 = iota((8, 256), 0)
    for i in range(6):
        value = e1a[i + 3]
        wide[8 * i : 8 * i + 8] = jnp.where(row8 == 7, value[8:16], value[0:8])
    doubled = lane_copy(wide[...], copies)
    for i in range(6):
        spread = row_copy(narrow, doubled[8 * i : 8 * i + 8])
        for p in (2 * i, 2 * i + 1):
            e0a[p] = v0x[p] + spread
    for p in range(1, 11):
        mid = e0a[p]
        total = gathered(
            mid, e0a[p - 1], e0a[p + 1], cx0[p], cx0[p + 1], cy0[p + 1], cz0[p + 1]
        )
        e0b[p] = KEEP * mid + w0[p + 1] * (rs[p + 1] + total)
    for p in range(2, 10):
        mid = e0b[p]
        total = gathered(
            mid, e0b[p - 1], e0b[p + 1], cx0[p], cx0[p + 1], cy0[p + 1], cz0[p + 1]
        )
        out_ref[p - 2] = (KEEP * mid + w0[p + 1] * (rs[p + 1] + total))[0:8]


def run(kernel, outs, scratch, where, *operands, space=VMEM, cost=None):
    return pl.pallas_call(
        kernel,
        out_shape=[jax.ShapeDtypeStruct(shape, F32) for shape in outs],
        in_specs=[pl.BlockSpec(memory_space=pltpu.SMEM)]
        + [pl.BlockSpec(memory_space=space)] * len(operands),
        out_specs=[pl.BlockSpec(memory_space=VMEM)] * len(outs),
        scratch_shapes=[VMEM(s, F32) if isinstance(s, tuple) else s for s in scratch],
        compiler_params=PARAMS,
        cost_estimate=cost,
    )(where, *operands)


def body(initial, right_side, phase_map, phase_table):
    nx, ny = lax.axis_size("gx"), lax.axis_size("gy")
    where = jnp.stack([lax.axis_index("gx"), lax.axis_index("gy")]).astype(jnp.int32)

    def pairs(partner):
        return [
            (x * ny + y, px * ny + py)
            for x in range(nx)
            for y in range(ny)
            for px, py in [partner(x, y)]
        ]

    def beyond(at, size):
        other = at + 1 if at % 2 else at - 1
        return other if 0 <= other < size else None

    def far_x(x, y):
        other = beyond(x, nx)
        return (x, y ^ 1) if other is None else (other, y)

    def far_y(x, y):
        other = beyond(y, ny)
        return (x ^ 1, y) if other is None else (x, other)

    both = ("gx", "gy")

    def swap_x(near, far):
        return (
            lax.ppermute(near, both, pairs(lambda x, y: (x ^ 1, y))),
            lax.ppermute(far, both, pairs(far_x)),
        )

    def swap_y(near, far):
        return (
            lax.ppermute(near, both, pairs(lambda x, y: (x, y ^ 1))),
            lax.ppermute(far, both, pairs(far_y)),
        )

    inputs = [
        pltpu.with_memory_space_constraint(value, pltpu.HBM)
        for value in (phase_table, phase_map, initial, right_side)
    ]
    early_cost = pl.CostEstimate(flops=20_000_000, bytes_accessed=4_000_000, transcendentals=0)
    tile0 = (8, 512)
    ring0 = (16, 512)
    ring1 = (16, 256)
    kappa, init, rhs, near, far, yeven, yodd = run(
        start_kernel, [(8,) + tile0] * 7,
        [pltpu.SMEM((3,), F32), VMEM((8,) + tile0, jnp.int32), pltpu.SemaphoreType.DMA((4,))],
        where, *inputs, space=pltpu.HBM,
    )
    yeven, yodd = swap_y(yeven, yodd)
    near, far = swap_x(near, far)
    yodd, far, yeven, near = lax.optimization_barrier((yodd, far, yeven, near))
    cnear, cfar = swap_x(*corner_messages(nx, ny, yeven, yodd))
    ksx, vsx, rsx, cxx, cyx, czx, wix, v1x, v2x, restx, kcx = run(
        functools.partial(early0_kernel, ny),
        [(8,) + ring0] * 3 + [(7,) + ring0] + [(6,) + ring0] * 4
        + [(4,) + ring0, (2,) + tile0, (32, 256)],
        [(4, 16, 128), (32, 512)],
        where, kappa, init, rhs, yeven, yodd, cost=early_cost,
    )
    v0, rs, cx0, cy0, cz0, w0, block, mnear, mfar, meven, modd = run(
        functools.partial(down0_kernel, nx, ny),
        [(8,) + tile0]
        + [(6,) + ring0, (6,) + ring0]
        + [(8,) + ring0] * 3
        + [(3,) + tile0]
        + [(5,) + tile0] * 4,
        [(6,) + ring0] * 2 + [(8,) + ring0, (10,) + ring0, (4, 16, 128), (32, 512), (32, 256)],
        where, near, far, cnear, cfar,
        ksx, vsx, rsx, cxx, cyx, czx, wix, v1x, v2x, restx, kcx,
    )
    meven, modd = swap_y(meven, modd)
    mnear, mfar = swap_x(mnear, mfar)
    modd, mfar, meven, mnear = lax.optimization_barrier((modd, mfar, meven, mnear))
    corner = corner1_message(ny, meven, modd)
    cnear, cfar = swap_x(corner, corner)
    v0x, v1, f1, w1, cx1, cy1, cz1, send = run(
        functools.partial(down1_kernel, nx, ny),
        [(12,) + ring0] + [(12,) + ring1] * 6 + [(ny, 8, 128)],
        [(12,) + ring1, (12,) + ring1, (4, 16, 128), (8, 256)],
        where, block, v0, mnear, mfar, meven, modd, cnear, cfar,
    )
    column = jnp.transpose(lax.all_to_all(send, "gy", 0, 0), (1, 0, 2))

    def chips_apart(j):
        return pairs(lambda x, y: (((x // 2) ^ j) * 2 + x % 2, y))

    mine = {0: column}
    for j in sorted(range(1, nx // 2), key=lambda j: j != 2):
        mine[j] = lax.ppermute(column, both, chips_apart(j))
    mine = [mine[j] for j in range(nx // 2)]
    other = [lax.ppermute(c, both, pairs(lambda x, y: (x ^ 1, y))) for c in mine]
    n2 = 2 * nx
    pair2 = (n2 + 2, 2, ny, 128)
    one2 = (n2 + 2, ny, 128)
    one3 = (nx + 2, ny, 128)
    (out,) = run(
        functools.partial(up_kernel, nx, ny), [(8,) + tile0],
        [pair2, pair2, pair2, one2, one2, pair2, pair2, pair2, pair2, pair2, (6, 2, 8, 128)]
        + [one3] * 9
        + [(48, 128), (48, 256), (12,) + ring1, (12,) + ring1, (4, 16, 128), (12,) + ring0, (12,) + ring0],
        where, *mine, *other, rsx, cxx, cyx, czx, wix, rs, cx0, cy0, cz0, w0,
        v1, f1, w1, cx1, cy1, cz1, v0x,
    )
    return out


def solution(mesh):
    return jax.shard_map(
        body,
        mesh=mesh,
        in_specs=(P("gx", "gy", None), P("gx", "gy", None), P("gx", "gy", None), P()),
        out_specs=P("gx", "gy", None),
        check_vma=False,
    )
```

```python
import functools

import jax
import jax.numpy as jnp
from jax import lax
from jax.experimental import pallas as pl
from jax.experimental.pallas import tpu as pltpu
from jax.sharding import PartitionSpec as P

F32 = jnp.float32
KEEP = 0.2
OMEGA = 0.8
VMEM = pltpu.VMEM
PARAMS = pltpu.CompilerParams(vmem_limit_bytes=48 * 1024 * 1024)


def roll(value, shift, axis):
    return pltpu.roll(value, shift % value.shape[axis], axis)


def iota(shape, dim):
    return lax.broadcasted_iota(jnp.int32, shape, dim)


def pair_sum_matrix():
    return (iota((256, 128), 0) // 2 == iota((256, 128), 1)).astype(F32)


def pair_copy_matrix():
    return (iota((128, 256), 1) // 2 == iota((128, 256), 0)).astype(F32)


def exact_dot(a, b):
    return lax.dot_general(
        a, b, (((1,), (0,)), ((), ())), precision=lax.Precision.HIGHEST, preferred_element_type=F32
    )


def lane_sum(value, matrix):
    width = value.shape[1]
    parts = [exact_dot(value[:, at : at + 256], matrix) for at in range(0, width, 256)]
    return parts[0] if len(parts) == 1 else jnp.concatenate(parts, axis=1)


def lane_copy(value, matrix):
    width = value.shape[1]
    parts = [exact_dot(value[:, at : at + 128], matrix) for at in range(0, width, 128)]
    return parts[0] if len(parts) == 1 else jnp.concatenate(parts, axis=1)


def row_sum(scratch, value):
    rows, width = value.shape
    parts = []
    for c in range(width // 128):
        scratch[c, 0:rows] = value[:, 128 * c : 128 * c + 128]
        first = scratch[c, pl.ds(0, rows // 2, stride=2)]
        parts.append(first + scratch[c, pl.ds(1, rows // 2, stride=2)])
    return parts[0] if len(parts) == 1 else jnp.concatenate(parts, axis=1)


def row_copy(scratch, value):
    rows, width = value.shape
    parts = []
    for c in range(width // 128):
        part = value[:, 128 * c : 128 * c + 128]
        scratch[c, pl.ds(0, rows, stride=2)] = part
        scratch[c, pl.ds(1, rows, stride=2)] = part
        parts.append(scratch[c, 0 : 2 * rows])
    return parts[0] if len(parts) == 1 else jnp.concatenate(parts, axis=1)


def gathered(mid, low, high, cx_low, cx, cy, cz):
    total = cx * high + cx_low * low
    total = total + cy * roll(mid, -1, 0) + roll(cy * mid, 1, 0)
    return total + cz * roll(mid, -1, 1) + roll(cz * mid, 1, 1)


def z_neighbours(mid):
    lane = iota(mid.shape, 1)
    last = mid.shape[1] - 1
    up = jnp.where(lane == last, 0.0, roll(mid, -1, 1))
    down = jnp.where(lane == 0, 0.0, roll(mid, 1, 1))
    return up, down


def diagonal(mid, low, high):
    up, down = z_neighbours(mid)
    total = low + high + roll(mid, -1, 0) + roll(mid, 1, 0) + up + down
    return 3.0 * mid + 0.5 * total


def coupling_y(mid):
    return 0.5 * (mid + roll(mid, -1, 0))


def coupling_z(mid):
    lane = iota(mid.shape, 1)
    return jnp.where(lane == mid.shape[1] - 1, 0.0, 0.5 * (mid + roll(mid, -1, 1)))


def edge_flags(at, grid):
    even = at % 2 == 0
    outside = jnp.logical_or(at == 0, at == grid - 1)
    return even, outside


def start_kernel(
    where_ref, table_hbm, phase_hbm, init_hbm, rhs_hbm,
    kap_ref, init_ref, rhs_ref, near_ref, far_ref, yeven_ref, yodd_ref,
    table_ref, phase_ref, sems,
):
    copies = [
        pltpu.make_async_copy(source, target, sems.at[i])
        for i, (source, target) in enumerate(
            ((table_hbm, table_ref), (phase_hbm, phase_ref), (init_hbm, init_ref), (rhs_hbm, rhs_ref))
        )
    ]
    for copy in copies:
        copy.start()
    for copy in copies:
        copy.wait()
    even = where_ref[0] % 2 == 0
    for x in range(8):
        phase = phase_ref[x]
        kap_ref[x] = jnp.where(
            phase == 0, table_ref[0], jnp.where(phase == 1, table_ref[1], table_ref[2])
        )
    for ref, side in ((near_ref, even), (far_ref, jnp.logical_not(even))):
        deep = jnp.where(side, 5, 0)
        shallow = jnp.where(side, 6, 0)
        for i in range(3):
            ref[i] = kap_ref[deep + i]
            ref[3 + i] = init_ref[deep + i]
        for i in range(2):
            ref[6 + i] = rhs_ref[shallow + i]

    def write(low_ref, high_ref):
        for x in range(8):
            low_ref[x, 0:3] = kap_ref[x, 0:3]
            low_ref[x, 3:6] = init_ref[x, 0:3]
            low_ref[x, 6:8] = rhs_ref[x, 0:2]
            high_ref[x, 0:3] = kap_ref[x, 5:8]
            high_ref[x, 3:6] = init_ref[x, 5:8]
            high_ref[x, 6:8] = rhs_ref[x, 6:8]

    by_parity(where_ref, yeven_ref, yodd_ref, write)


def by_parity(where_ref, even_ref, odd_ref, write):
    even = where_ref[1] % 2 == 0

    @pl.when(even)
    def _():
        write(odd_ref, even_ref)

    @pl.when(jnp.logical_not(even))
    def _():
        write(even_ref, odd_ref)


def y_tiles(where_ref, grid, even_ref, odd_ref, p):
    even, outside = edge_flags(where_ref[1], grid)
    inner = even_ref[p]
    outer = jnp.where(outside, 0.0, odd_ref[p])
    return jnp.where(even, inner, outer), jnp.where(even, outer, inner)


def corner_messages(nx, ny, yeven, yodd):
    even = lax.axis_index("gx") % 2 == 0
    high, low = both_tiles(ny, yeven, yodd)
    top = jnp.concatenate([high[7:8], high[6:7], low[7:8], low[6:7]], axis=0)
    bottom = jnp.concatenate([high[0:2], low[0:2]], axis=0)
    return jnp.where(even, top, bottom), jnp.where(even, bottom, top)


def both_tiles(ny, yeven, yodd):
    at = lax.axis_index("gy")
    even, outside = edge_flags(at, ny)
    outer = jnp.where(outside, 0.0, yodd)
    return jnp.where(even, yeven, outer), jnp.where(even, outer, yeven)


class Planes:
    def __init__(self, middle, outer, first, count):
        self.middle, self.outer, self.first, self.count = middle, outer, first, count

    def find(self, p):
        if p < self.first:
            return self.outer, p
        if p < self.first + self.count:
            return self.middle, p - self.first
        return self.outer, p - self.count

    def __getitem__(self, p):
        ref, at = self.find(p)
        return ref[at]

    def __setitem__(self, p, value):
        ref, at = self.find(p)
        ref[at] = value


def setup0(ks, cx, cy, cz, wi, planes, faces):
    for p in faces:
        cx[p] = 0.5 * (ks[p] + ks[p + 1])
    for p in planes:
        mid = ks[p]
        cy[p] = coupling_y(mid)
        cz[p] = coupling_z(mid)
        diag = diagonal(mid, ks[p - 1], ks[p + 1])
        wi[p] = jnp.where(mid > 0.0, OMEGA / jnp.where(mid > 0.0, diag, 1.0), 0.0)


def sweep0(source, target, rs, cx, cy, cz, wi, planes):
    for p in planes:
        mid = source[p]
        total = gathered(mid, source[p - 1], source[p + 1], cx[p - 1], cx[p], cy[p], cz[p])
        target[p] = KEEP * mid + wi[p] * (rs[p] + total)


def rest0(v2, rs, ks, cx, cy, cz, p):
    mid = v2[p]
    total = gathered(mid, v2[p - 1], v2[p + 1], cx[p - 1], cx[p], cy[p], cz[p])
    diag = diagonal(ks[p], ks[p - 1], ks[p + 1])
    return (rs[p] + total - diag * mid)[0:8]


def add_y_halo(ks, vs, rs, p, high, low):
    zero = jnp.zeros((8, 512), F32)
    ks[p, 8:16] = zero
    vs[p, 8:16] = zero
    rs[p, 8:16] = zero
    ks[p, 8:11] = high[0:3]
    ks[p, 13:16] = low[0:3]
    vs[p, 8:11] = high[3:6]
    vs[p, 13:16] = low[3:6]
    rs[p, 8:10] = high[6:8]
    rs[p, 14:16] = low[6:8]


def early0_kernel(
    ny, where_ref, kap_ref, init_ref, rhs_ref, even_ref, odd_ref,
    ks, vs, rs, cx, cy, cz, wi, v1, v2, rest, kc,
    pair, fine,
):
    for x in range(8):
        ks[x, 0:8] = kap_ref[x]
        vs[x, 0:8] = init_ref[x]
        rs[x, 0:8] = rhs_ref[x]
        add_y_halo(ks, vs, rs, x, *y_tiles(where_ref, ny, even_ref, odd_ref, x))
    ks, vs, rs = (Planes(ref, None, 3, 8) for ref in (ks, vs, rs))
    cx = Planes(cx, None, 3, 7)
    cy, cz, wi, v1 = (Planes(ref, None, 4, 6) for ref in (cy, cz, wi, v1))
    v2 = Planes(v2, None, 5, 4)
    setup0(ks, cx, cy, cz, wi, range(4, 10), range(3, 10))
    sweep0(vs, v1, rs, cx, cy, cz, wi, range(4, 10))
    sweep0(v1, v2, rs, cx, cy, cz, wi, range(5, 9))
    for p in (6, 7):
        rest[p - 6] = rest0(v2, rs, ks, cx, cy, cz, p)
    for x in range(4):
        fine[8 * x : 8 * x + 8] = row_sum(pair, ks[2 * x + 3] + ks[2 * x + 4])
    kc[...] = 0.125 * lane_sum(fine[...], pair_sum_matrix())


def down0_kernel(
    nx, ny, where_ref, near_ref, far_ref, cnear_ref, cfar_ref,
    ks_own, vs_own, rs_own, cx_own, cy_own, cz_own, wi_own, v1_own, v2_own, rest_own, kc,
    v0_ref, rs, cx, cy, cz, wi, block_ref, mnear_ref, mfar_ref,
    ks, vs, v1, v2, pair, fine, coarse,
):
    even, outside = edge_flags(where_ref[0], nx)
    for i in range(3):
        near_at = jnp.where(even, 3 + i, i)
        far_at = jnp.where(even, i, 3 + i)
        for ref, first in ((ks, 0), (vs, 3)):
            ref[near_at, 0:8] = near_ref[first + i]
            ref[far_at, 0:8] = jnp.where(outside, 0.0, far_ref[first + i])
    for i in range(2):
        rs[jnp.where(even, 3 + i, 1 + i), 0:8] = near_ref[6 + i]
        rs[jnp.where(even, 1 + i, 3 + i), 0:8] = jnp.where(outside, 0.0, far_ref[6 + i])
    zero = jnp.zeros((8, 512), F32)
    for p in (0, 5):
        ks[p, 8:16] = zero
        vs[p, 8:16] = zero
        rs[p, 8:16] = zero
    rs[0, 0:8] = zero
    rs[5, 0:8] = zero
    for i in range(2):
        add_y_halo(ks, vs, rs, jnp.where(even, 3 + i, 2 - i), cnear_ref[i], cnear_ref[2 + i])
        add_y_halo(
            ks, vs, rs, jnp.where(even, 2 - i, 3 + i),
            jnp.where(outside, 0.0, cfar_ref[i]), jnp.where(outside, 0.0, cfar_ref[2 + i]),
        )
    ks, vs, rs = (Planes(a, b, 3, 8) for a, b in ((ks_own, ks), (vs_own, vs), (rs_own, rs)))
    cx = Planes(cx_own, cx, 3, 7)
    cy, cz, wi, v1 = (
        Planes(a, b, 4, 6) for a, b in ((cy_own, cy), (cz_own, cz), (wi_own, wi), (v1_own, v1))
    )
    v2 = Planes(v2_own, v2, 5, 4)
    setup0(ks, cx, cy, cz, wi, (1, 2, 3, 10, 11, 12), (0, 1, 2, 10, 11, 12))
    sweep0(vs, v1, rs, cx, cy, cz, wi, (1, 2, 3, 10, 11, 12))
    sweep0(v1, v2, rs, cx, cy, cz, wi, (2, 3, 4, 9, 10, 11))
    for p in range(3, 11, 2):
        both = None
        for q in (p, p + 1):
            rest = rest_own[q - 6] if q in (6, 7) else rest0(v2, rs, ks, cx, cy, cz, q)
            both = rest if both is None else both + rest
            v0_ref[q - 3] = v2[q][0:8]
        at = 2 * (p - 3)
        fine[at : at + 4] = row_sum(pair, both)
    fine[16:24] = row_sum(pair, ks[1] + ks[2])
    fine[24:32] = row_sum(pair, ks[11] + ks[12])
    coarse[...] = lane_sum(fine[...], pair_sum_matrix())
    kept = [0.125 * coarse[16:24]] + [kc[8 * x : 8 * x + 8] for x in range(4)]
    kept.append(0.125 * coarse[24:32])
    for x in range(4):
        half = pl.ds(256 * (x % 2), 256)
        mid = kept[x + 1]
        block_ref[x // 2, 0:4, half] = 0.5 * coarse[4 * x : 4 * x + 4]
        block_ref[x // 2, 4:8, half] = mid[0:4]
        at = 4 * (x // 2)
        block_ref[2, at : at + 4, half] = (OMEGA / diagonal(mid, kept[x], kept[x + 2])[0:4])
    for ref, side in ((mnear_ref, even), (mfar_ref, jnp.logical_not(even))):
        shallow = jnp.where(side, 6, 0)
        for i in range(3):
            ref[i] = block_ref[i]
        for i in range(2):
            ref[3 + i] = v0_ref[shallow + i]


def corner1_message(ny, meven, modd):
    return jnp.concatenate(both_tiles(ny, meven, modd), axis=0)


def down1_kernel(
    nx, ny, where_ref, block_ref, v0_ref, near_ref, far_ref, meven_ref, modd_ref,
    cnear_ref, cfar_ref,
    v0x, v1, f1, w1, cx, cy, cz, send_ref, veven_ref, vodd_ref,
    k1, u1, pair, fine,
):
    even, outside = edge_flags(where_ref[0], nx)

    def inside(value):
        return jnp.where(outside, 0.0, value)

    near = [near_ref[i] for i in range(3)]
    far = [inside(far_ref[i]) for i in range(3)]
    cnear = [cnear_ref[i] for i in range(6)]
    cfar = [inside(cfar_ref[i]) for i in range(6)]
    mine = [y_tiles(where_ref, ny, meven_ref, modd_ref, i) for i in range(3)]

    def pick(a, b):
        return [jnp.where(even, p, q) for p, q in zip(a, b)]

    blocks = (
        (pick(far, near), pick(cfar[0:3], cnear[0:3]), pick(cfar[3:6], cnear[3:6])),
        ([block_ref[i] for i in range(3)], [t[0] for t in mine], [t[1] for t in mine]),
        (pick(near, far), pick(cnear[0:3], cfar[0:3]), pick(cnear[3:6], cfar[3:6])),
    )
    zero = jnp.zeros((4, 256), F32)
    for b in range(3):
        for x in range(4):
            p = 4 * b + x
            half = slice(256 * (x % 2), 256 * (x % 2) + 256)
            t = x // 2
            for ref, at, row in (
                (f1, t, slice(0, 4)), (k1, t, slice(4, 8)), (w1, 2, slice(4 * t, 4 * t + 4))
            ):
                ref[p, 0:4] = blocks[b][0][at][row, half]
                ref[p, 4:8] = blocks[b][1][at][row, half]
                ref[p, 8:12] = zero
                ref[p, 12:16] = blocks[b][2][at][row, half]
    blank = jnp.zeros((8, 512), F32)
    for p in range(12):
        v0x[p, 8:16] = blank
    for x in range(8):
        v0x[2 + x, 0:8] = v0_ref[x]
    near_at = jnp.where(even, 10, 0)
    far_at = jnp.where(even, 0, 10)
    for i in range(2):
        v0x[near_at + i, 0:8] = near_ref[3 + i]
        v0x[far_at + i, 0:8] = inside(far_ref[3 + i])

    def write(low_ref, high_ref):
        for q in range(10):
            at = 2 * (q % 4)
            low_ref[q // 4, at : at + 2] = v0x[q + 1, 0:2]
            high_ref[q // 4, at : at + 2] = v0x[q + 1, 6:8]
        for ref in (low_ref, high_ref):
            ref[2, 4:8] = jnp.zeros((4, 512), F32)

    by_parity(where_ref, veven_ref, vodd_ref, write)
    for p in range(12):
        u1[p] = w1[p] * f1[p]
        if p < 11:
            cx[p] = 0.5 * (k1[p] + k1[p + 1])
        cy[p] = coupling_y(k1[p])
        cz[p] = coupling_z(k1[p])
    for p in range(1, 11):
        mid = u1[p]
        total = gathered(mid, u1[p - 1], u1[p + 1], cx[p - 1], cx[p], cy[p], cz[p])
        v1[p] = KEEP * mid + w1[p] * (f1[p] + total)
    for p in range(4, 8, 2):
        both = None
        for q in (p, p + 1):
            mid = v1[q]
            total = gathered(mid, v1[q - 1], v1[q + 1], cx[q - 1], cx[q], cy[q], cz[q])
            diag = diagonal(k1[q], k1[q - 1], k1[q + 1])
            rest = (f1[q] + total - diag * mid)[0:8]
            both = rest if both is None else both + rest
        at = p - 4
        fine[at : at + 2] = 0.5 * row_sum(pair, both)[0:2]
        kept = k1[p, 0:8] + k1[p + 1, 0:8]
        fine[4 + at : 6 + at] = 0.125 * row_sum(pair, kept)[0:2]
    tile = lane_sum(fine[...], pair_sum_matrix())
    for i in range(send_ref.shape[0]):
        send_ref[i] = tile


def up_kernel(
    nx, ny, where_ref, *refs
):
    half = nx // 2
    columns = (refs[:half], refs[half : 2 * half])
    own, far = refs[nx : nx + 5], refs[nx + 5 : nx + 10]
    rs = Planes(own[0], far[0], 3, 8)
    cx0 = Planes(own[1], far[1], 3, 7)
    cy0, cz0, w0 = (Planes(a, b, 4, 6) for a, b in zip(own[2:], far[2:]))
    up_levels(nx, ny, where_ref, columns, rs, cx0, cy0, cz0, w0, *refs[nx + 10 :])


def up_levels(
    nx, ny, where_ref, columns, rs, cx0, cy0, cz0, w0, v1, f1, w1, cx1, cy1, cz1, v0x, veven_ref, vodd_ref,
    out_ref,
    f2, k2, cx2, cyi, cyo, cz2, w2, d2, u2, v2, e2, f3, k3, cx3, cy3, cz3, w3, edge3, ga, gb,
    small, wide, e1a, e1b, narrow, e0a, e0b,
):
    gx = where_ref[0]
    gy = where_ref[1]
    core = gx % 2
    n2 = 2 * nx
    zero = jnp.zeros((ny, 128), F32)
    row = iota((ny, 128), 0)
    lane = iota((ny, 128), 1)
    last_row = row == ny - 1
    for s in range(2):
        k2[0, s] = zero
        k2[n2 + 1, s] = zero
        u2[0, s] = zero
        u2[n2 + 1, s] = zero
        v2[0, s] = zero
        v2[n2 + 1, s] = zero
    for j in range(nx // 2):
        chip = (gx // 2) ^ j
        for refs, which in ((columns[0], core), (columns[1], 1 - core)):
            for i in range(2):
                p = 4 * chip + 2 * which + i + 1
                for s in range(2):
                    f2[p, s] = refs[j][2 * i + s]
                    k2[p, s] = refs[j][4 + 2 * i + s]
    for p in range(n2 + 1):
        for s in range(2):
            cx2[p, s] = 0.5 * (k2[p, s] + k2[p + 1, s])
    for p in range(1, n2 + 1):
        k_low, k_high = k2[p, 0], k2[p, 1]
        after = jnp.where(last_row, 0.0, roll(k_low, -1, 0))
        before = jnp.where(row == 0, 0.0, roll(k_high, 1, 0))
        cyi[p] = 0.5 * (k_low + k_high)
        cyo[p] = jnp.where(last_row, 0.0, 0.5 * (k_high + after))
        for s, mid, ya, yb in ((0, k_low, k_high, before), (1, k_high, k_low, after)):
            up, down = z_neighbours(mid)
            cz2[p, s] = jnp.where(lane == 127, 0.0, 0.5 * (mid + up))
            diag = 3.0 * mid + 0.5 * (k2[p - 1, s] + k2[p + 1, s] + ya + yb + up + down)
            scale = OMEGA / diag
            d2[p, s] = diag
            w2[p, s] = scale
            u2[p, s] = scale * f2[p, s]

    def gather2(ref, p):
        low, high = ref[p, 0], ref[p, 1]
        sums = []
        for s, mid in ((0, low), (1, high)):
            total = cx2[p, s] * ref[p + 1, s] + cx2[p - 1, s] * ref[p - 1, s]
            total = total + cz2[p, s] * roll(mid, -1, 1) + roll(cz2[p, s] * mid, 1, 1)
            sums.append(total)
        sums[0] = sums[0] + cyi[p] * high + roll(cyo[p] * high, 1, 0)
        sums[1] = sums[1] + cyi[p] * low + cyo[p] * roll(low, -1, 0)
        return (low, high), sums

    def sweep2(source, target):
        for p in range(1, n2 + 1):
            mids, sums = gather2(source, p)
            for s in range(2):
                target[p, s] = KEEP * mids[s] + w2[p, s] * (f2[p, s] + sums[s])

    sweep2(u2, v2)
    even_lane = lane % 2 == 0

    def pair_lanes(value):
        return value + jnp.where(even_lane, roll(value, -1, 1), roll(value, 1, 1))

    k3[0] = zero
    k3[nx + 1] = zero
    ga[0] = zero
    ga[nx + 1] = zero
    gb[0] = zero
    gb[nx + 1] = zero
    for x in range(nx):
        both = None
        kept = None
        for p in (2 * x + 1, 2 * x + 2):
            mids, sums = gather2(v2, p)
            for s in range(2):
                rest = f2[p, s] + sums[s] - d2[p, s] * mids[s]
                both = rest if both is None else both + rest
                kept = k2[p, s] if kept is None else kept + k2[p, s]
        f3[x + 1] = 0.5 * pair_lanes(both)
        k3[x + 1] = 0.125 * pair_lanes(kept)
    for p in range(nx + 1):
        cx3[p] = 0.5 * (k3[p] + k3[p + 1])
    edge_total = zero
    rest_total = zero
    outer = (
        (row == 0).astype(F32) + last_row.astype(F32)
        + (lane < 2).astype(F32) + (lane >= 126).astype(F32)
    )
    for p in range(1, nx + 1):
        mid = k3[p]
        after = jnp.where(last_row, 0.0, roll(mid, -1, 0))
        before = jnp.where(row == 0, 0.0, roll(mid, 1, 0))
        up = jnp.where(lane >= 126, 0.0, roll(mid, -2, 1))
        down = jnp.where(lane < 2, 0.0, roll(mid, 2, 1))
        cy3[p] = jnp.where(last_row, 0.0, 0.5 * (mid + after))
        cz3[p] = jnp.where(lane >= 126, 0.0, 0.5 * (mid + up))
        diag = 3.0 * mid + 0.5 * (k3[p - 1] + k3[p + 1] + after + before + up + down)
        scale = OMEGA / diag
        w3[p] = scale
        ga[p] = scale * f3[p]
        faces = outer + (1.0 if p == 1 else 0.0) + (1.0 if p == nx else 0.0)
        edge = 0.5 * mid * faces
        edge3[p] = edge
        edge_total = edge_total + edge
        rest_total = rest_total + f3[p]

    def gather3(ref, p):
        mid = ref[p]
        total = cx3[p] * ref[p + 1] + cx3[p - 1] * ref[p - 1]
        total = total + cy3[p] * roll(mid, -1, 0) + roll(cy3[p] * mid, 1, 0)
        return mid, total + cz3[p] * roll(mid, -2, 1) + roll(cz3[p] * mid, 2, 1)

    source, target = ga, gb
    for _ in range(7):
        for p in range(1, nx + 1):
            mid, total = gather3(source, p)
            target[p] = KEEP * mid + w3[p] * (f3[p] + total)
        source, target = target, source
    for p in range(1, nx + 1):
        rest_total = rest_total - edge3[p] * source[p]

    def whole(value):
        return jnp.sum(jnp.sum(value, axis=0, keepdims=True), axis=1, keepdims=True)

    shift = whole(rest_total) / whole(edge_total)
    first_row = jnp.clip(gy - 3, 0, ny - 8)
    rows = pl.ds(first_row, 8)
    no_wrap = iota((8, 128), 0) < 7
    planes = []
    for j in range(10):
        x = 2 * gx - 4 + j
        planes.append((jnp.logical_and(x >= 0, x < n2), jnp.clip(x, 0, n2 - 1)))
    level = []
    for ok, q in planes:
        e3 = source[q // 2 + 1, rows] + shift
        level.append([jnp.where(ok, v2[q + 1, s, rows] + e3, 0.0) for s in range(2)])
    for first, last in ((1, 8), (2, 7)):
        done = list(level)
        for j in range(first, last + 1):
            ok, q = planes[j]
            low, high = level[j]
            inner = cyi[q + 1, rows]
            after = jnp.where(no_wrap, cyo[q + 1, rows], 0.0)
            sums = [inner * high + roll(after * high, 1, 0), inner * low + after * roll(low, -1, 0)]
            for s in range(2):
                mid = level[j][s]
                cz = cz2[q + 1, s, rows]
                total = sums[s] + cz * roll(mid, -1, 1) + roll(cz * mid, 1, 1)
                total = total + cx2[q + 1, s, rows] * level[j + 1][s]
                total = total + cx2[q, s, rows] * level[j - 1][s]
                value = KEEP * mid + w2[q + 1, s, rows] * (f2[q + 1, s, rows] + total)
                done[j] = [jnp.where(ok, value, 0.0)] if s == 0 else done[j] + [jnp.where(ok, value, 0.0)]
        level = done
    copies = pair_copy_matrix()
    at = gy - first_row
    steps = (
        (0, at, None),
        (2, jnp.minimum(at + 1, 7), gy < ny - 1),
        (6, jnp.maximum(at - 1, 0), gy > 0),
    )
    for i in range(6):
        small[8 * i + 4 : 8 * i + 6] = jnp.zeros((2, 128), F32)
        for s in range(2):
            e2[i, s] = level[i + 2][s]
            for j, r, ok in steps:
                line = e2[i, s, pl.ds(r, 1)]
                small[8 * i + j + s : 8 * i + j + s + 1] = (
                    line if ok is None else jnp.where(ok, line, 0.0)
                )
    wide[...] = lane_copy(small[...], copies)
    for i in range(6):
        spread = row_copy(narrow, wide[8 * i : 8 * i + 8])
        for p in (2 * i, 2 * i + 1):
            if 1 <= p <= 10:
                e1a[p] = v1[p] + spread
    for source, target, first, last in ((e1a, e1b, 2, 9), (e1b, e1a, 3, 8)):
        for p in range(first, last + 1):
            mid = source[p]
            total = gathered(
                mid, source[p - 1], source[p + 1], cx1[p - 1], cx1[p], cy1[p], cz1[p]
            )
            target[p] = KEEP * mid + w1[p] * (f1[p] + total)
    row8 = iota((8, 256), 0)
    for i in range(6):
        value = e1a[i + 3]
        wide[8 * i : 8 * i + 8] = jnp.where(row8 == 7, value[8:16], value[0:8])
    doubled = lane_copy(wide[...], copies)
    for i in range(6):
        spread = row_copy(narrow, doubled[8 * i : 8 * i + 8])
        for p in (2 * i, 2 * i + 1):
            e0a[p] = v0x[p] + spread
    tiles = [y_tiles(where_ref, ny, veven_ref, vodd_ref, i) for i in range(3)]
    for q in range(10):
        at = 2 * (q % 4)
        above, below = (tile[at : at + 2] for tile in tiles[q // 4])
        e0a[q + 1, 8:10] = e0a[q + 1, 8:10] + above
        e0a[q + 1, 14:16] = e0a[q + 1, 14:16] + below
    for p in range(1, 11):
        mid = e0a[p]
        total = gathered(
            mid, e0a[p - 1], e0a[p + 1], cx0[p], cx0[p + 1], cy0[p + 1], cz0[p + 1]
        )
        e0b[p] = KEEP * mid + w0[p + 1] * (rs[p + 1] + total)
    for p in range(2, 10):
        mid = e0b[p]
        total = gathered(
            mid, e0b[p - 1], e0b[p + 1], cx0[p], cx0[p + 1], cy0[p + 1], cz0[p + 1]
        )
        out_ref[p - 2] = (KEEP * mid + w0[p + 1] * (rs[p + 1] + total))[0:8]


def run(kernel, outs, scratch, where, *operands, space=VMEM, cost=None):
    return pl.pallas_call(
        kernel,
        out_shape=[jax.ShapeDtypeStruct(shape, F32) for shape in outs],
        in_specs=[pl.BlockSpec(memory_space=pltpu.SMEM)]
        + [pl.BlockSpec(memory_space=space)] * len(operands),
        out_specs=[pl.BlockSpec(memory_space=VMEM)] * len(outs),
        scratch_shapes=[VMEM(s, F32) if isinstance(s, tuple) else s for s in scratch],
        compiler_params=PARAMS,
        cost_estimate=cost,
    )(where, *operands)


def body(initial, right_side, phase_map, phase_table):
    nx, ny = lax.axis_size("gx"), lax.axis_size("gy")
    where = jnp.stack([lax.axis_index("gx"), lax.axis_index("gy")]).astype(jnp.int32)

    def pairs(partner):
        return [
            (x * ny + y, px * ny + py)
            for x in range(nx)
            for y in range(ny)
            for px, py in [partner(x, y)]
        ]

    def beyond(at, size):
        other = at + 1 if at % 2 else at - 1
        return other if 0 <= other < size else None

    def far_x(x, y):
        other = beyond(x, nx)
        return (x, y ^ 1) if other is None else (other, y)

    def far_y(x, y):
        other = beyond(y, ny)
        return (x ^ 1, y) if other is None else (x, other)

    both = ("gx", "gy")

    def swap_x(near, far):
        return (
            lax.ppermute(near, both, pairs(lambda x, y: (x ^ 1, y))),
            lax.ppermute(far, both, pairs(far_x)),
        )

    def swap_y(near, far):
        return (
            lax.ppermute(near, both, pairs(lambda x, y: (x, y ^ 1))),
            lax.ppermute(far, both, pairs(far_y)),
        )

    inputs = [
        pltpu.with_memory_space_constraint(value, pltpu.HBM)
        for value in (phase_table, phase_map, initial, right_side)
    ]
    early_cost = pl.CostEstimate(flops=20_000_000, bytes_accessed=4_000_000, transcendentals=0)
    tile0 = (8, 512)
    ring0 = (16, 512)
    ring1 = (16, 256)
    kappa, init, rhs, near, far, yeven, yodd = run(
        start_kernel, [(8,) + tile0] * 7,
        [pltpu.SMEM((3,), F32), VMEM((8,) + tile0, jnp.int32), pltpu.SemaphoreType.DMA((4,))],
        where, *inputs, space=pltpu.HBM,
    )
    yeven, yodd = swap_y(yeven, yodd)
    near, far = swap_x(near, far)
    yodd, yeven, far, near = lax.optimization_barrier((yodd, yeven, far, near))
    cnear, cfar = swap_x(*corner_messages(nx, ny, yeven, yodd))
    ksx, vsx, rsx, cxx, cyx, czx, wix, v1x, v2x, restx, kcx = run(
        functools.partial(early0_kernel, ny),
        [(8,) + ring0] * 3 + [(7,) + ring0] + [(6,) + ring0] * 4
        + [(4,) + ring0, (2,) + tile0, (32, 256)],
        [(4, 16, 128), (32, 512)],
        where, kappa, init, rhs, yeven, yodd, cost=early_cost,
    )
    v0, rs, cx0, cy0, cz0, w0, block, mnear, mfar = run(
        functools.partial(down0_kernel, nx, ny),
        [(8,) + tile0]
        + [(6,) + ring0, (6,) + ring0]
        + [(8,) + ring0] * 3
        + [(3,) + tile0]
        + [(5,) + tile0] * 2,
        [(6,) + ring0] * 2 + [(8,) + ring0, (10,) + ring0, (4, 16, 128), (32, 512), (32, 256)],
        where, near, far, cnear, cfar,
        ksx, vsx, rsx, cxx, cyx, czx, wix, v1x, v2x, restx, kcx,
    )
    meven, modd = swap_y(block, block)
    mnear, mfar = swap_x(mnear, mfar)
    modd, meven, mfar, mnear = lax.optimization_barrier((modd, meven, mfar, mnear))
    corner = corner1_message(ny, meven, modd)
    cnear, cfar = swap_x(corner, corner)
    v0x, v1, f1, w1, cx1, cy1, cz1, send, veven, vodd = run(
        functools.partial(down1_kernel, nx, ny),
        [(12,) + ring0] + [(12,) + ring1] * 6
        + [(ny, 8, 128), (3,) + tile0, (3,) + tile0],
        [(12,) + ring1, (12,) + ring1, (4, 16, 128), (8, 256)],
        where, block, v0, mnear, mfar, meven, modd, cnear, cfar,
    )
    column = jnp.transpose(lax.all_to_all(send, "gy", 0, 0), (1, 0, 2))
    column, veven, vodd = lax.optimization_barrier((column, veven, vodd))

    def chips_apart(j):
        return pairs(lambda x, y: (((x // 2) ^ j) * 2 + x % 2, y))

    mine = {0: column}
    for j in sorted(range(1, nx // 2), key=lambda j: j != 2):
        mine[j] = lax.ppermute(column, both, chips_apart(j))
    mine = [mine[j] for j in range(nx // 2)]
    veven, vodd = swap_y(veven, vodd)
    mine[-1], veven, vodd = lax.optimization_barrier((mine[-1], veven, vodd))
    other = [lax.ppermute(c, both, pairs(lambda x, y: (x ^ 1, y))) for c in mine]
    n2 = 2 * nx
    pair2 = (n2 + 2, 2, ny, 128)
    one2 = (n2 + 2, ny, 128)
    one3 = (nx + 2, ny, 128)
    (out,) = run(
        functools.partial(up_kernel, nx, ny), [(8,) + tile0],
        [pair2, pair2, pair2, one2, one2, pair2, pair2, pair2, pair2, pair2, (6, 2, 8, 128)]
        + [one3] * 9
        + [(48, 128), (48, 256), (12,) + ring1, (12,) + ring1, (4, 16, 128), (12,) + ring0, (12,) + ring0],
        where, *mine, *other, rsx, cxx, cyx, czx, wix, rs, cx0, cy0, cz0, w0,
        v1, f1, w1, cx1, cy1, cz1, v0x, veven, vodd,
    )
    return out


def solution(mesh):
    return jax.shard_map(
        body,
        mesh=mesh,
        in_specs=(P("gx", "gy", None), P("gx", "gy", None), P("gx", "gy", None), P()),
        out_specs=P("gx", "gy", None),
        check_vma=False,
    )
```

```python
import functools

import jax
import jax.numpy as jnp
from jax import lax
from jax.experimental import pallas as pl
from jax.experimental.pallas import tpu as pltpu
from jax.sharding import PartitionSpec as P

F32 = jnp.float32
KEEP = 0.2
OMEGA = 0.8
VMEM = pltpu.VMEM
PARAMS = pltpu.CompilerParams(vmem_limit_bytes=48 * 1024 * 1024)


def roll(value, shift, axis):
    return pltpu.roll(value, shift % value.shape[axis], axis)


def iota(shape, dim):
    return lax.broadcasted_iota(jnp.int32, shape, dim)


def pair_sum_matrix():
    return (iota((256, 128), 0) // 2 == iota((256, 128), 1)).astype(F32)


def pair_copy_matrix():
    return (iota((128, 256), 1) // 2 == iota((128, 256), 0)).astype(F32)


def exact_dot(a, b):
    return lax.dot_general(
        a, b, (((1,), (0,)), ((), ())), precision=lax.Precision.HIGHEST, preferred_element_type=F32
    )


def lane_sum(value, matrix):
    width = value.shape[1]
    parts = [exact_dot(value[:, at : at + 256], matrix) for at in range(0, width, 256)]
    return parts[0] if len(parts) == 1 else jnp.concatenate(parts, axis=1)


def lane_copy(value, matrix):
    width = value.shape[1]
    parts = [exact_dot(value[:, at : at + 128], matrix) for at in range(0, width, 128)]
    return parts[0] if len(parts) == 1 else jnp.concatenate(parts, axis=1)


def row_sum(scratch, value):
    rows, width = value.shape
    parts = []
    for c in range(width // 128):
        scratch[c, 0:rows] = value[:, 128 * c : 128 * c + 128]
        first = scratch[c, pl.ds(0, rows // 2, stride=2)]
        parts.append(first + scratch[c, pl.ds(1, rows // 2, stride=2)])
    return parts[0] if len(parts) == 1 else jnp.concatenate(parts, axis=1)


def row_copy(scratch, value):
    rows, width = value.shape
    parts = []
    for c in range(width // 128):
        part = value[:, 128 * c : 128 * c + 128]
        scratch[c, pl.ds(0, rows, stride=2)] = part
        scratch[c, pl.ds(1, rows, stride=2)] = part
        parts.append(scratch[c, 0 : 2 * rows])
    return parts[0] if len(parts) == 1 else jnp.concatenate(parts, axis=1)


def gathered(mid, low, high, cx_low, cx, cy, cz):
    total = cx * high + cx_low * low
    total = total + cy * roll(mid, -1, 0) + roll(cy * mid, 1, 0)
    return total + cz * roll(mid, -1, 1) + roll(cz * mid, 1, 1)


def z_neighbours(mid):
    lane = iota(mid.shape, 1)
    last = mid.shape[1] - 1
    up = jnp.where(lane == last, 0.0, roll(mid, -1, 1))
    down = jnp.where(lane == 0, 0.0, roll(mid, 1, 1))
    return up, down


def diagonal(mid, low, high):
    up, down = z_neighbours(mid)
    total = low + high + roll(mid, -1, 0) + roll(mid, 1, 0) + up + down
    return 3.0 * mid + 0.5 * total


def coupling_y(mid):
    return 0.5 * (mid + roll(mid, -1, 0))


def coupling_z(mid):
    lane = iota(mid.shape, 1)
    return jnp.where(lane == mid.shape[1] - 1, 0.0, 0.5 * (mid + roll(mid, -1, 1)))


def edge_flags(at, grid):
    even = at % 2 == 0
    outside = jnp.logical_or(at == 0, at == grid - 1)
    return even, outside


def start_kernel(
    where_ref, table_hbm, phase_hbm, init_hbm, rhs_hbm,
    kap_ref, init_ref, rhs_ref, near_ref, far_ref, yeven_ref, yodd_ref,
    table_ref, phase_ref, sems,
):
    copies = [
        pltpu.make_async_copy(source, target, sems.at[i])
        for i, (source, target) in enumerate(
            ((table_hbm, table_ref), (phase_hbm, phase_ref), (init_hbm, init_ref), (rhs_hbm, rhs_ref))
        )
    ]
    for copy in copies:
        copy.start()
    for copy in copies:
        copy.wait()
    even = where_ref[0] % 2 == 0
    for x in range(8):
        phase = phase_ref[x]
        kap_ref[x] = jnp.where(
            phase == 0, table_ref[0], jnp.where(phase == 1, table_ref[1], table_ref[2])
        )
    for ref, side in ((near_ref, even), (far_ref, jnp.logical_not(even))):
        deep = jnp.where(side, 5, 0)
        shallow = jnp.where(side, 6, 0)
        for i in range(3):
            ref[i] = kap_ref[deep + i]
            ref[3 + i] = init_ref[deep + i]
        for i in range(2):
            ref[6 + i] = rhs_ref[shallow + i]

    def write(low_ref, high_ref):
        for x in range(8):
            low_ref[x, 0:3] = kap_ref[x, 0:3]
            low_ref[x, 3:6] = init_ref[x, 0:3]
            low_ref[x, 6:8] = rhs_ref[x, 0:2]
            high_ref[x, 0:3] = kap_ref[x, 5:8]
            high_ref[x, 3:6] = init_ref[x, 5:8]
            high_ref[x, 6:8] = rhs_ref[x, 6:8]

    by_parity(where_ref, yeven_ref, yodd_ref, write)


def by_parity(where_ref, even_ref, odd_ref, write):
    even = where_ref[1] % 2 == 0

    @pl.when(even)
    def _():
        write(odd_ref, even_ref)

    @pl.when(jnp.logical_not(even))
    def _():
        write(even_ref, odd_ref)


def y_tiles(where_ref, grid, even_ref, odd_ref, p):
    even, outside = edge_flags(where_ref[1], grid)
    inner = even_ref[p]
    outer = jnp.where(outside, 0.0, odd_ref[p])
    return jnp.where(even, inner, outer), jnp.where(even, outer, inner)


def corner_messages(nx, ny, yeven, yodd):
    even = lax.axis_index("gx") % 2 == 0
    high, low = both_tiles(ny, yeven, yodd)
    top = jnp.concatenate([high[7:8], high[6:7], low[7:8], low[6:7]], axis=0)
    bottom = jnp.concatenate([high[0:2], low[0:2]], axis=0)
    return jnp.where(even, top, bottom), jnp.where(even, bottom, top)


def both_tiles(ny, yeven, yodd):
    at = lax.axis_index("gy")
    even, outside = edge_flags(at, ny)
    outer = jnp.where(outside, 0.0, yodd)
    return jnp.where(even, yeven, outer), jnp.where(even, outer, yeven)


class Planes:
    def __init__(self, middle, outer, first, count):
        self.middle, self.outer, self.first, self.count = middle, outer, first, count

    def find(self, p):
        if p < self.first:
            return self.outer, p
        if p < self.first + self.count:
            return self.middle, p - self.first
        return self.outer, p - self.count

    def __getitem__(self, p):
        ref, at = self.find(p)
        return ref[at]

    def __setitem__(self, p, value):
        ref, at = self.find(p)
        ref[at] = value


def setup0(ks, cx, cy, cz, wi, planes, faces):
    for p in faces:
        cx[p] = 0.5 * (ks[p] + ks[p + 1])
    for p in planes:
        mid = ks[p]
        cy[p] = coupling_y(mid)
        cz[p] = coupling_z(mid)
        diag = diagonal(mid, ks[p - 1], ks[p + 1])
        wi[p] = jnp.where(mid > 0.0, OMEGA / jnp.where(mid > 0.0, diag, 1.0), 0.0)


def sweep0(source, target, rs, cx, cy, cz, wi, planes):
    for p in planes:
        mid = source[p]
        total = gathered(mid, source[p - 1], source[p + 1], cx[p - 1], cx[p], cy[p], cz[p])
        target[p] = KEEP * mid + wi[p] * (rs[p] + total)


def rest0(v2, rs, ks, cx, cy, cz, p):
    mid = v2[p]
    total = gathered(mid, v2[p - 1], v2[p + 1], cx[p - 1], cx[p], cy[p], cz[p])
    diag = diagonal(ks[p], ks[p - 1], ks[p + 1])
    return (rs[p] + total - diag * mid)[0:8]


def add_y_halo(ks, vs, rs, p, high, low):
    zero = jnp.zeros((8, 512), F32)
    ks[p, 8:16] = zero
    vs[p, 8:16] = zero
    rs[p, 8:16] = zero
    ks[p, 8:11] = high[0:3]
    ks[p, 13:16] = low[0:3]
    vs[p, 8:11] = high[3:6]
    vs[p, 13:16] = low[3:6]
    rs[p, 8:10] = high[6:8]
    rs[p, 14:16] = low[6:8]


def early0_kernel(
    ny, where_ref, kap_ref, init_ref, rhs_ref, even_ref, odd_ref,
    ks, vs, rs, cx, cy, cz, wi, v1, v2, rest, kc,
    pair, fine,
):
    for x in range(8):
        ks[x, 0:8] = kap_ref[x]
        vs[x, 0:8] = init_ref[x]
        rs[x, 0:8] = rhs_ref[x]
        add_y_halo(ks, vs, rs, x, *y_tiles(where_ref, ny, even_ref, odd_ref, x))
    ks, vs, rs = (Planes(ref, None, 3, 8) for ref in (ks, vs, rs))
    cx = Planes(cx, None, 3, 7)
    cy, cz, wi, v1 = (Planes(ref, None, 4, 6) for ref in (cy, cz, wi, v1))
    v2 = Planes(v2, None, 5, 4)
    setup0(ks, cx, cy, cz, wi, range(4, 10), range(3, 10))
    sweep0(vs, v1, rs, cx, cy, cz, wi, range(4, 10))
    sweep0(v1, v2, rs, cx, cy, cz, wi, range(5, 9))
    for p in (6, 7):
        rest[p - 6] = rest0(v2, rs, ks, cx, cy, cz, p)
    for x in range(4):
        fine[8 * x : 8 * x + 8] = row_sum(pair, ks[2 * x + 3] + ks[2 * x + 4])
    kc[...] = 0.125 * lane_sum(fine[...], pair_sum_matrix())


def down0_kernel(
    nx, ny, where_ref, near_ref, far_ref, cnear_ref, cfar_ref,
    ks_own, vs_own, rs_own, cx_own, cy_own, cz_own, wi_own, v1_own, v2_own, rest_own, kc,
    v0_ref, rs, cx, cy, cz, wi, block_ref, mnear_ref, mfar_ref, meven_ref, modd_ref,
    ks, vs, v1, v2, pair, fine, coarse,
):
    even, outside = edge_flags(where_ref[0], nx)
    for i in range(3):
        near_at = jnp.where(even, 3 + i, i)
        far_at = jnp.where(even, i, 3 + i)
        for ref, first in ((ks, 0), (vs, 3)):
            ref[near_at, 0:8] = near_ref[first + i]
            ref[far_at, 0:8] = jnp.where(outside, 0.0, far_ref[first + i])
    for i in range(2):
        rs[jnp.where(even, 3 + i, 1 + i), 0:8] = near_ref[6 + i]
        rs[jnp.where(even, 1 + i, 3 + i), 0:8] = jnp.where(outside, 0.0, far_ref[6 + i])
    zero = jnp.zeros((8, 512), F32)
    for p in (0, 5):
        ks[p, 8:16] = zero
        vs[p, 8:16] = zero
        rs[p, 8:16] = zero
    rs[0, 0:8] = zero
    rs[5, 0:8] = zero
    for i in range(2):
        add_y_halo(ks, vs, rs, jnp.where(even, 3 + i, 2 - i), cnear_ref[i], cnear_ref[2 + i])
        add_y_halo(
            ks, vs, rs, jnp.where(even, 2 - i, 3 + i),
            jnp.where(outside, 0.0, cfar_ref[i]), jnp.where(outside, 0.0, cfar_ref[2 + i]),
        )
    ks, vs, rs = (Planes(a, b, 3, 8) for a, b in ((ks_own, ks), (vs_own, vs), (rs_own, rs)))
    cx = Planes(cx_own, cx, 3, 7)
    cy, cz, wi, v1 = (
        Planes(a, b, 4, 6) for a, b in ((cy_own, cy), (cz_own, cz), (wi_own, wi), (v1_own, v1))
    )
    v2 = Planes(v2_own, v2, 5, 4)
    setup0(ks, cx, cy, cz, wi, (1, 2, 3, 10, 11, 12), (0, 1, 2, 10, 11, 12))
    sweep0(vs, v1, rs, cx, cy, cz, wi, (1, 2, 3, 10, 11, 12))
    sweep0(v1, v2, rs, cx, cy, cz, wi, (2, 3, 4, 9, 10, 11))
    for p in range(3, 11, 2):
        both = None
        for q in (p, p + 1):
            rest = rest_own[q - 6] if q in (6, 7) else rest0(v2, rs, ks, cx, cy, cz, q)
            both = rest if both is None else both + rest
            v0_ref[q - 3] = v2[q][0:8]
        at = 2 * (p - 3)
        fine[at : at + 4] = row_sum(pair, both)
    fine[16:24] = row_sum(pair, ks[1] + ks[2])
    fine[24:32] = row_sum(pair, ks[11] + ks[12])
    coarse[...] = lane_sum(fine[...], pair_sum_matrix())
    kept = [0.125 * coarse[16:24]] + [kc[8 * x : 8 * x + 8] for x in range(4)]
    kept.append(0.125 * coarse[24:32])
    for x in range(4):
        half = pl.ds(256 * (x % 2), 256)
        mid = kept[x + 1]
        block_ref[x // 2, 0:4, half] = 0.5 * coarse[4 * x : 4 * x + 4]
        block_ref[x // 2, 4:8, half] = mid[0:4]
        at = 4 * (x // 2)
        block_ref[2, at : at + 4, half] = (OMEGA / diagonal(mid, kept[x], kept[x + 2])[0:4])
    for ref, side in ((mnear_ref, even), (mfar_ref, jnp.logical_not(even))):
        shallow = jnp.where(side, 6, 0)
        for i in range(3):
            ref[i] = block_ref[i]
        for i in range(2):
            ref[3 + i] = v0_ref[shallow + i]

    def write(low_ref, high_ref):
        for i in range(3):
            low_ref[i] = block_ref[i]
            high_ref[i] = block_ref[i]
        for x in range(8):
            at = 2 * (x % 4)
            low_ref[3 + x // 4, at : at + 2] = v0_ref[x, 0:2]
            high_ref[3 + x // 4, at : at + 2] = v0_ref[x, 6:8]

    by_parity(where_ref, meven_ref, modd_ref, write)


def corner1_message(ny, meven, modd):
    high, low = both_tiles(ny, meven, modd)
    rows = [high[4:5, 6:8], low[4:5, 6:8], high[3:4, 0:2], low[3:4, 0:2]]
    return jnp.concatenate([high[0:3], low[0:3], jnp.concatenate(rows, axis=1)], axis=0)


def down1_kernel(
    nx, ny, where_ref, block_ref, v0_ref, near_ref, far_ref, meven_ref, modd_ref,
    cnear_ref, cfar_ref,
    v0x, v1, f1, w1, cx, cy, cz, send_ref,
    k1, u1, pair, fine,
):
    even, outside = edge_flags(where_ref[0], nx)

    def inside(value):
        return jnp.where(outside, 0.0, value)

    near = [near_ref[i] for i in range(3)]
    far = [inside(far_ref[i]) for i in range(3)]
    cnear = [cnear_ref[i] for i in range(7)]
    cfar = [inside(cfar_ref[i]) for i in range(7)]
    mine = [y_tiles(where_ref, ny, meven_ref, modd_ref, i) for i in range(5)]

    def pick(a, b):
        return [jnp.where(even, p, q) for p, q in zip(a, b)]

    blocks = (
        (pick(far, near), pick(cfar[0:3], cnear[0:3]), pick(cfar[3:6], cnear[3:6])),
        ([block_ref[i] for i in range(3)], [t[0] for t in mine], [t[1] for t in mine]),
        (pick(near, far), pick(cnear[0:3], cfar[0:3]), pick(cnear[3:6], cfar[3:6])),
    )
    zero = jnp.zeros((4, 256), F32)
    for b in range(3):
        for x in range(4):
            p = 4 * b + x
            half = slice(256 * (x % 2), 256 * (x % 2) + 256)
            t = x // 2
            for ref, at, row in (
                (f1, t, slice(0, 4)), (k1, t, slice(4, 8)), (w1, 2, slice(4 * t, 4 * t + 4))
            ):
                ref[p, 0:4] = blocks[b][0][at][row, half]
                ref[p, 4:8] = blocks[b][1][at][row, half]
                ref[p, 8:12] = zero
                ref[p, 12:16] = blocks[b][2][at][row, half]
    blank = jnp.zeros((8, 512), F32)
    for p in range(12):
        v0x[p, 8:16] = blank
    for x in range(8):
        v0x[2 + x, 0:8] = v0_ref[x]
        at = 2 * (x % 4)
        v0x[2 + x, 8:10] = mine[3 + x // 4][0][at : at + 2]
        v0x[2 + x, 14:16] = mine[3 + x // 4][1][at : at + 2]
    near_at = jnp.where(even, 10, 0)
    far_at = jnp.where(even, 0, 10)
    for i in range(2):
        v0x[near_at + i, 0:8] = near_ref[3 + i]
        v0x[far_at + i, 0:8] = inside(far_ref[3 + i])
    low_tile = jnp.where(even, cfar[6], cnear[6])
    high_tile = jnp.where(even, cnear[6], cfar[6])
    for at, tile, row in ((1, low_tile, 0), (10, high_tile, 4)):
        v0x[at, 8:10] = tile[row : row + 2]
        v0x[at, 14:16] = tile[row + 2 : row + 4]
    for p in range(12):
        u1[p] = w1[p] * f1[p]
        if p < 11:
            cx[p] = 0.5 * (k1[p] + k1[p + 1])
        cy[p] = coupling_y(k1[p])
        cz[p] = coupling_z(k1[p])
    for p in range(1, 11):
        mid = u1[p]
        total = gathered(mid, u1[p - 1], u1[p + 1], cx[p - 1], cx[p], cy[p], cz[p])
        v1[p] = KEEP * mid + w1[p] * (f1[p] + total)
    for p in range(4, 8, 2):
        both = None
        for q in (p, p + 1):
            mid = v1[q]
            total = gathered(mid, v1[q - 1], v1[q + 1], cx[q - 1], cx[q], cy[q], cz[q])
            diag = diagonal(k1[q], k1[q - 1], k1[q + 1])
            rest = (f1[q] + total - diag * mid)[0:8]
            both = rest if both is None else both + rest
        at = p - 4
        fine[at : at + 2] = 0.5 * row_sum(pair, both)[0:2]
        kept = k1[p, 0:8] + k1[p + 1, 0:8]
        fine[4 + at : 6 + at] = 0.125 * row_sum(pair, kept)[0:2]
    tile = lane_sum(fine[...], pair_sum_matrix())
    for i in range(send_ref.shape[0]):
        send_ref[i] = tile


def up_kernel(
    nx, ny, where_ref, *refs
):
    half = nx // 2
    columns = (refs[:half], refs[half : 2 * half])
    own, far = refs[nx : nx + 5], refs[nx + 5 : nx + 10]
    rs = Planes(own[0], far[0], 3, 8)
    cx0 = Planes(own[1], far[1], 3, 7)
    cy0, cz0, w0 = (Planes(a, b, 4, 6) for a, b in zip(own[2:], far[2:]))
    up_levels(nx, ny, where_ref, columns, rs, cx0, cy0, cz0, w0, *refs[nx + 10 :])


def up_levels(
    nx, ny, where_ref, columns, rs, cx0, cy0, cz0, w0, v1, f1, w1, cx1, cy1, cz1, v0x, out_ref,
    f2, k2, cx2, cyi, cyo, cz2, w2, d2, u2, v2, e2, f3, k3, cx3, cy3, cz3, w3, edge3, ga, gb,
    small, wide, e1a, e1b, narrow, e0a, e0b,
):
    gx = where_ref[0]
    gy = where_ref[1]
    core = gx % 2
    n2 = 2 * nx
    zero = jnp.zeros((ny, 128), F32)
    row = iota((ny, 128), 0)
    lane = iota((ny, 128), 1)
    last_row = row == ny - 1
    for s in range(2):
        k2[0, s] = zero
        k2[n2 + 1, s] = zero
        u2[0, s] = zero
        u2[n2 + 1, s] = zero
        v2[0, s] = zero
        v2[n2 + 1, s] = zero
    for j in range(nx // 2):
        chip = (gx // 2) ^ j
        for refs, which in ((columns[0], core), (columns[1], 1 - core)):
            for i in range(2):
                p = 4 * chip + 2 * which + i + 1
                for s in range(2):
                    f2[p, s] = refs[j][2 * i + s]
                    k2[p, s] = refs[j][4 + 2 * i + s]
    for p in range(n2 + 1):
        for s in range(2):
            cx2[p, s] = 0.5 * (k2[p, s] + k2[p + 1, s])
    for p in range(1, n2 + 1):
        k_low, k_high = k2[p, 0], k2[p, 1]
        after = jnp.where(last_row, 0.0, roll(k_low, -1, 0))
        before = jnp.where(row == 0, 0.0, roll(k_high, 1, 0))
        cyi[p] = 0.5 * (k_low + k_high)
        cyo[p] = jnp.where(last_row, 0.0, 0.5 * (k_high + after))
        for s, mid, ya, yb in ((0, k_low, k_high, before), (1, k_high, k_low, after)):
            up, down = z_neighbours(mid)
            cz2[p, s] = jnp.where(lane == 127, 0.0, 0.5 * (mid + up))
            diag = 3.0 * mid + 0.5 * (k2[p - 1, s] + k2[p + 1, s] + ya + yb + up + down)
            scale = OMEGA / diag
            d2[p, s] = diag
            w2[p, s] = scale
            u2[p, s] = scale * f2[p, s]

    def gather2(ref, p):
        low, high = ref[p, 0], ref[p, 1]
        sums = []
        for s, mid in ((0, low), (1, high)):
            total = cx2[p, s] * ref[p + 1, s] + cx2[p - 1, s] * ref[p - 1, s]
            total = total + cz2[p, s] * roll(mid, -1, 1) + roll(cz2[p, s] * mid, 1, 1)
            sums.append(total)
        sums[0] = sums[0] + cyi[p] * high + roll(cyo[p] * high, 1, 0)
        sums[1] = sums[1] + cyi[p] * low + cyo[p] * roll(low, -1, 0)
        return (low, high), sums

    def sweep2(source, target):
        for p in range(1, n2 + 1):
            mids, sums = gather2(source, p)
            for s in range(2):
                target[p, s] = KEEP * mids[s] + w2[p, s] * (f2[p, s] + sums[s])

    sweep2(u2, v2)
    even_lane = lane % 2 == 0

    def pair_lanes(value):
        return value + jnp.where(even_lane, roll(value, -1, 1), roll(value, 1, 1))

    k3[0] = zero
    k3[nx + 1] = zero
    ga[0] = zero
    ga[nx + 1] = zero
    gb[0] = zero
    gb[nx + 1] = zero
    for x in range(nx):
        both = None
        kept = None
        for p in (2 * x + 1, 2 * x + 2):
            mids, sums = gather2(v2, p)
            for s in range(2):
                rest = f2[p, s] + sums[s] - d2[p, s] * mids[s]
                both = rest if both is None else both + rest
                kept = k2[p, s] if kept is None else kept + k2[p, s]
        f3[x + 1] = 0.5 * pair_lanes(both)
        k3[x + 1] = 0.125 * pair_lanes(kept)
    for p in range(nx + 1):
        cx3[p] = 0.5 * (k3[p] + k3[p + 1])
    edge_total = zero
    rest_total = zero
    outer = (
        (row == 0).astype(F32) + last_row.astype(F32)
        + (lane < 2).astype(F32) + (lane >= 126).astype(F32)
    )
    for p in range(1, nx + 1):
        mid = k3[p]
        after = jnp.where(last_row, 0.0, roll(mid, -1, 0))
        before = jnp.where(row == 0, 0.0, roll(mid, 1, 0))
        up = jnp.where(lane >= 126, 0.0, roll(mid, -2, 1))
        down = jnp.where(lane < 2, 0.0, roll(mid, 2, 1))
        cy3[p] = jnp.where(last_row, 0.0, 0.5 * (mid + after))
        cz3[p] = jnp.where(lane >= 126, 0.0, 0.5 * (mid + up))
        diag = 3.0 * mid + 0.5 * (k3[p - 1] + k3[p + 1] + after + before + up + down)
        scale = OMEGA / diag
        w3[p] = scale
        ga[p] = scale * f3[p]
        faces = outer + (1.0 if p == 1 else 0.0) + (1.0 if p == nx else 0.0)
        edge = 0.5 * mid * faces
        edge3[p] = edge
        edge_total = edge_total + edge
        rest_total = rest_total + f3[p]

    def gather3(ref, p):
        mid = ref[p]
        total = cx3[p] * ref[p + 1] + cx3[p - 1] * ref[p - 1]
        total = total + cy3[p] * roll(mid, -1, 0) + roll(cy3[p] * mid, 1, 0)
        return mid, total + cz3[p] * roll(mid, -2, 1) + roll(cz3[p] * mid, 2, 1)

    source, target = ga, gb
    for _ in range(7):
        for p in range(1, nx + 1):
            mid, total = gather3(source, p)
            target[p] = KEEP * mid + w3[p] * (f3[p] + total)
        source, target = target, source
    for p in range(1, nx + 1):
        rest_total = rest_total - edge3[p] * source[p]

    def whole(value):
        return jnp.sum(jnp.sum(value, axis=0, keepdims=True), axis=1, keepdims=True)

    shift = whole(rest_total) / whole(edge_total)
    first_row = jnp.clip(gy - 3, 0, ny - 8)
    rows = pl.ds(first_row, 8)
    no_wrap = iota((8, 128), 0) < 7
    planes = []
    for j in range(10):
        x = 2 * gx - 4 + j
        planes.append((jnp.logical_and(x >= 0, x < n2), jnp.clip(x, 0, n2 - 1)))
    level = []
    for ok, q in planes:
        e3 = source[q // 2 + 1, rows] + shift
        level.append([jnp.where(ok, v2[q + 1, s, rows] + e3, 0.0) for s in range(2)])
    for first, last in ((1, 8), (2, 7)):
        done = list(level)
        for j in range(first, last + 1):
            ok, q = planes[j]
            low, high = level[j]
            inner = cyi[q + 1, rows]
            after = jnp.where(no_wrap, cyo[q + 1, rows], 0.0)
            sums = [inner * high + roll(after * high, 1, 0), inner * low + after * roll(low, -1, 0)]
            for s in range(2):
                mid = level[j][s]
                cz = cz2[q + 1, s, rows]
                total = sums[s] + cz * roll(mid, -1, 1) + roll(cz * mid, 1, 1)
                total = total + cx2[q + 1, s, rows] * level[j + 1][s]
                total = total + cx2[q, s, rows] * level[j - 1][s]
                value = KEEP * mid + w2[q + 1, s, rows] * (f2[q + 1, s, rows] + total)
                done[j] = [jnp.where(ok, value, 0.0)] if s == 0 else done[j] + [jnp.where(ok, value, 0.0)]
        level = done
    copies = pair_copy_matrix()
    at = gy - first_row
    steps = (
        (0, at, None),
        (2, jnp.minimum(at + 1, 7), gy < ny - 1),
        (6, jnp.maximum(at - 1, 0), gy > 0),
    )
    for i in range(6):
        small[8 * i + 4 : 8 * i + 6] = jnp.zeros((2, 128), F32)
        for s in range(2):
            e2[i, s] = level[i + 2][s]
            for j, r, ok in steps:
                line = e2[i, s, pl.ds(r, 1)]
                small[8 * i + j + s : 8 * i + j + s + 1] = (
                    line if ok is None else jnp.where(ok, line, 0.0)
                )
    wide[...] = lane_copy(small[...], copies)
    for i in range(6):
        spread = row_copy(narrow, wide[8 * i : 8 * i + 8])
        for p in (2 * i, 2 * i + 1):
            if 1 <= p <= 10:
                e1a[p] = v1[p] + spread
    for source, target, first, last in ((e1a, e1b, 2, 9), (e1b, e1a, 3, 8)):
        for p in range(first, last + 1):
            mid = source[p]
            total = gathered(
                mid, source[p - 1], source[p + 1], cx1[p - 1], cx1[p], cy1[p], cz1[p]
            )
            target[p] = KEEP * mid + w1[p] * (f1[p] + total)
    row8 = iota((8, 256), 0)
    for i in range(6):
        value = e1a[i + 3]
        wide[8 * i : 8 * i + 8] = jnp.where(row8 == 7, value[8:16], value[0:8])
    doubled = lane_copy(wide[...], copies)
    for i in range(6):
        spread = row_copy(narrow, doubled[8 * i : 8 * i + 8])
        for p in (2 * i, 2 * i + 1):
            e0a[p] = v0x[p] + spread
    for p in range(1, 11):
        mid = e0a[p]
        total = gathered(
            mid, e0a[p - 1], e0a[p + 1], cx0[p], cx0[p + 1], cy0[p + 1], cz0[p + 1]
        )
        e0b[p] = KEEP * mid + w0[p + 1] * (rs[p + 1] + total)
    for p in range(2, 10):
        mid = e0b[p]
        total = gathered(
            mid, e0b[p - 1], e0b[p + 1], cx0[p], cx0[p + 1], cy0[p + 1], cz0[p + 1]
        )
        out_ref[p - 2] = (KEEP * mid + w0[p + 1] * (rs[p + 1] + total))[0:8]


def run(kernel, outs, scratch, where, *operands, space=VMEM, cost=None):
    return pl.pallas_call(
        kernel,
        out_shape=[jax.ShapeDtypeStruct(shape, F32) for shape in outs],
        in_specs=[pl.BlockSpec(memory_space=pltpu.SMEM)]
        + [pl.BlockSpec(memory_space=space)] * len(operands),
        out_specs=[pl.BlockSpec(memory_space=VMEM)] * len(outs),
        scratch_shapes=[VMEM(s, F32) if isinstance(s, tuple) else s for s in scratch],
        compiler_params=PARAMS,
        cost_estimate=cost,
    )(where, *operands)


def body(initial, right_side, phase_map, phase_table):
    nx, ny = lax.axis_size("gx"), lax.axis_size("gy")
    where = jnp.stack([lax.axis_index("gx"), lax.axis_index("gy")]).astype(jnp.int32)

    def pairs(partner):
        return [
            (x * ny + y, px * ny + py)
            for x in range(nx)
            for y in range(ny)
            for px, py in [partner(x, y)]
        ]

    def beyond(at, size):
        other = at + 1 if at % 2 else at - 1
        return other if 0 <= other < size else None

    def far_x(x, y):
        other = beyond(x, nx)
        return (x, y ^ 1) if other is None else (other, y)

    def far_y(x, y):
        other = beyond(y, ny)
        return (x ^ 1, y) if other is None else (x, other)

    both = ("gx", "gy")

    def swap_x(near, far):
        return (
            lax.ppermute(near, both, pairs(lambda x, y: (x ^ 1, y))),
            lax.ppermute(far, both, pairs(far_x)),
        )

    def swap_y(near, far):
        return (
            lax.ppermute(near, both, pairs(lambda x, y: (x, y ^ 1))),
            lax.ppermute(far, both, pairs(far_y)),
        )

    inputs = [
        pltpu.with_memory_space_constraint(value, pltpu.HBM)
        for value in (phase_table, phase_map, initial, right_side)
    ]
    early_cost = pl.CostEstimate(flops=20_000_000, bytes_accessed=4_000_000, transcendentals=0)
    tile0 = (8, 512)
    ring0 = (16, 512)
    ring1 = (16, 256)
    kappa, init, rhs, near, far, yeven, yodd = run(
        start_kernel, [(8,) + tile0] * 7,
        [pltpu.SMEM((3,), F32), VMEM((8,) + tile0, jnp.int32), pltpu.SemaphoreType.DMA((4,))],
        where, *inputs, space=pltpu.HBM,
    )
    yeven, yodd = swap_y(yeven, yodd)
    near, far = swap_x(near, far)
    yeven, yodd, far, near = lax.optimization_barrier((yeven, yodd, far, near))
    cnear, cfar = swap_x(*corner_messages(nx, ny, yeven, yodd))
    ksx, vsx, rsx, cxx, cyx, czx, wix, v1x, v2x, restx, kcx = run(
        functools.partial(early0_kernel, ny),
        [(8,) + ring0] * 3 + [(7,) + ring0] + [(6,) + ring0] * 4
        + [(4,) + ring0, (2,) + tile0, (32, 256)],
        [(4, 16, 128), (32, 512)],
        where, kappa, init, rhs, yeven, yodd, cost=early_cost,
    )
    v0, rs, cx0, cy0, cz0, w0, block, mnear, mfar, meven, modd = run(
        functools.partial(down0_kernel, nx, ny),
        [(8,) + tile0]
        + [(6,) + ring0, (6,) + ring0]
        + [(8,) + ring0] * 3
        + [(3,) + tile0]
        + [(5,) + tile0] * 4,
        [(6,) + ring0] * 2 + [(8,) + ring0, (10,) + ring0, (4, 16, 128), (32, 512), (32, 256)],
        where, near, far, cnear, cfar,
        ksx, vsx, rsx, cxx, cyx, czx, wix, v1x, v2x, restx, kcx,
    )
    meven, modd = swap_y(meven, modd)
    mnear, mfar = swap_x(mnear, mfar)
    meven, modd, mfar, mnear = lax.optimization_barrier((meven, modd, mfar, mnear))
    corner = corner1_message(ny, meven, modd)
    cnear, cfar = swap_x(corner, corner)
    v0x, v1, f1, w1, cx1, cy1, cz1, send = run(
        functools.partial(down1_kernel, nx, ny),
        [(12,) + ring0] + [(12,) + ring1] * 6 + [(ny, 8, 128)],
        [(12,) + ring1, (12,) + ring1, (4, 16, 128), (8, 256)],
        where, block, v0, mnear, mfar, meven, modd, cnear, cfar,
    )
    column = jnp.transpose(lax.all_to_all(send, "gy", 0, 0), (1, 0, 2))

    def chips_apart(j):
        return pairs(lambda x, y: (((x // 2) ^ j) * 2 + x % 2, y))

    mine = {0: column}
    for j in sorted(range(1, nx // 2), key=lambda j: j != 2):
        mine[j] = lax.ppermute(column, both, chips_apart(j))
    mine = [mine[j] for j in range(nx // 2)]
    other = [lax.ppermute(c, both, pairs(lambda x, y: (x ^ 1, y))) for c in mine]
    n2 = 2 * nx
    pair2 = (n2 + 2, 2, ny, 128)
    one2 = (n2 + 2, ny, 128)
    one3 = (nx + 2, ny, 128)
    (out,) = run(
        functools.partial(up_kernel, nx, ny), [(8,) + tile0],
        [pair2, pair2, pair2, one2, one2, pair2, pair2, pair2, pair2, pair2, (6, 2, 8, 128)]
        + [one3] * 9
        + [(48, 128), (48, 256), (12,) + ring1, (12,) + ring1, (4, 16, 128), (12,) + ring0, (12,) + ring0],
        where, *mine, *other, rsx, cxx, cyx, czx, wix, rs, cx0, cy0, cz0, w0,
        v1, f1, w1, cx1, cy1, cz1, v0x,
    )
    return out


def solution(mesh):
    return jax.shard_map(
        body,
        mesh=mesh,
        in_specs=(P("gx", "gy", None), P("gx", "gy", None), P("gx", "gy", None), P()),
        out_specs=P("gx", "gy", None),
        check_vma=False,
    )
```
